32 devices in a mesh: dp: 8 (over y, x, core), tensor: 4 (over z).
Axes of the slice: x: 2, y: 2, z: 4, core: 2. Of those that a mesh axis runs over, the one named last changes fastest.
Arguments:
- hidden: bfloat16 [8, 1024, 1024], P('dp', 'tensor'), may hold values from -6 to 6
- seg_ids: int32 [8, 1024], P('dp', 'tensor'), may hold values from 0 to 4, as said below
- cotangent: bfloat16 [8, 1024, 1024], P('dp', 'tensor'), may hold values from -6 to 6
- norm_gain: bfloat16 [1024], P('dp'), may hold values from 0.099609375 to 1.8984375
- w_in_z: bfloat16 [1024, 2048], P('dp', 'tensor'), may hold values from -0.1875 to 0.1875
- w_in_x: bfloat16 [1024, 2048], P('dp', 'tensor'), may hold values from -0.1875 to 0.1875
- w_in_bc: bfloat16 [1024, 256], P('dp'), may hold values from -0.1875 to 0.1875
- w_in_dt: bfloat16 [1024, 32], P('dp', 'tensor'), may hold values from -0.1875 to 0.1875
- conv_x: float32 [4, 2048], P(None, 'tensor'), may hold values from -3 to 3
- conv_x_bias: float32 [2048], P('tensor'), may hold values from -1.75 to 1.75
- conv_bc: float32 [4, 256], replicated, may hold values from -3 to 3
- conv_bc_bias: float32 [256], replicated, may hold values from -1.75 to 1.75
- dt_bias: float32 [32], P('tensor'), may hold values from -5 to -1
- a_log: float32 [32], P('tensor'), may hold values from 0 to 2.77
- d_skip: float32 [32], P('tensor'), may hold values from 0.5 to 1.5
- gate_gain: float32 [2048], P('tensor'), may hold values from 0.1 to 1.9
- w_out: bfloat16 [1024, 2048], P('dp', 'tensor'), may hold values from -0.125 to 0.125
Outputs:
- layer_out: bfloat16 [8, 1024, 1024], P('dp', 'tensor')
- grad_hidden: bfloat16 [8, 1024, 1024], P('dp', 'tensor')
- grad_norm_gain: float32 [1024], P('dp')
- grad_w_in_z: float32 [1024, 2048], P('dp', 'tensor')
- grad_w_in_x: float32 [1024, 2048], P('dp', 'tensor')
- grad_w_in_bc: float32 [1024, 256], P('dp')
- grad_w_in_dt: float32 [1024, 32], P('dp', 'tensor')
- grad_conv_x: float32 [4, 2048], P(None, 'tensor')
- grad_conv_x_bias: float32 [2048], P('tensor')
- grad_conv_bc: float32 [4, 256], replicated
- grad_conv_bc_bias: float32 [256], replicated
- grad_dt_bias: float32 [32], P('tensor')
- grad_a_log: float32 [32], P('tensor')
- grad_d_skip: float32 [32], P('tensor')
- grad_gate_gain: float32 [2048], P('tensor')
- grad_w_out: float32 [1024, 2048], P('dp', 'tensor')
The draws below stay inside these ranges and needn't reach their ends.
Inputs may be any that keep to these rules, and one draw needn't show every extreme that they name: `seg_ids`: within a row the ids never fall; ids restart in each row and are compared within a row only; id 0 marks padding, which comes after all documents of its row; in every draw some row is a single document of 1024 positions, and other rows are filled to between 128 and 1024 positions.
All inputs are finite; a program needn't handle non-finite values.
Results may differ from the reference program's by a relative error of at most 0.011.
Values may be sent and summed in bfloat16 or wider, within the bound.
No kernel may reach another device: no remote copies, remote signals or barrier semaphores. Data moves between devices by JAX's collectives and lax.ppermute only.
A program may use at most 128 MiB of HBM per device.

```python
import jax
import jax.numpy as jnp
from jax import lax

D = 1024
DI = 2048
H = 32
N = 128
CONV = 4
GROUP = 256
ROW_LEN = 1024
ROWS = 8


def draw_seg_ids(key, part):
    key = jax.random.fold_in(key, 11)
    fill_key, whole_key, cut_key = jax.random.split(key, 3)
    fill_counts = jax.random.randint(fill_key, (ROWS,), ROW_LEN // 8, ROW_LEN + 1)
    whole_row = jax.random.randint(whole_key, (), 0, ROWS)
    row_number = jnp.arange(ROWS)
    is_whole = row_number == whole_row
    fill_counts = jnp.where(is_whole, ROW_LEN, fill_counts)
    quarter = fill_counts // 4
    cut_keys = jax.random.split(cut_key, 3)
    positions = jnp.arange(ROW_LEN)[None, :]
    seg_values = jnp.ones((ROWS, ROW_LEN), jnp.int32)
    for cut_number in range(3):
        cut_points = jax.random.randint(cut_keys[cut_number], (ROWS,), (cut_number + 1) * quarter, (cut_number + 2) * quarter)
        cut_points = jnp.where(is_whole, ROW_LEN, cut_points)
        seg_values = seg_values + (positions >= cut_points[:, None]).astype(jnp.int32)
    return jnp.where(positions < fill_counts[:, None], seg_values, 0).astype(jnp.int32)


def block_scale(stream_key, shape, pieces, least, top_value):
    def one(position, shards_of):
        heights = jax.random.uniform(jax.random.fold_in(jax.random.fold_in(stream_key, 6), position), (shards_of,), jnp.float32, least / len(pieces), top_value / len(pieces))
        return jnp.repeat(jnp.exp(heights), shape[position] // shards_of).reshape((-1,) + (1,) * (len(shape) - position - 1))

    level = one(*pieces[0])
    for cut in pieces[1:]:
        level = level * one(*cut)
    return level


def bell_draw(stream_key, extent, width, reach, cuts=(), held_as=jnp.bfloat16):
    array = jax.random.normal(stream_key, extent, jnp.float32) * width
    if len(cuts) > 0:
        array = block_scale(stream_key, extent, cuts, -0.22, 0.18) * array
    return jnp.clip(array, min=-reach, max=reach).astype(held_as)


def setup_inputs(seed: int = 0) -> dict:
    splits = jax.random.split(jax.random.key(seed), 18)
    return {
        "hidden": bell_draw(splits[0], (ROWS, ROW_LEN, D), 1.0, 6.0, ((0, 8), (1, 4))),
        "seg_ids": draw_seg_ids(jax.random.fold_in(splits[17], 71), 0),
        "cotangent": bell_draw(splits[2], (ROWS, ROW_LEN, D), 1.0, 6.0, ((0, 8), (1, 4))),
        "norm_gain": jnp.clip(1.0 + 0.18 * jax.random.normal(splits[3], (D,), jnp.float32), 0.099609375, 1.8984375).astype(jnp.bfloat16),
        "w_in_z": bell_draw(splits[4], (D, DI), D ** -0.5, 0.1875, ((0, 8), (1, 4))),
        "w_in_x": bell_draw(splits[5], (D, DI), D ** -0.5, 0.1875, ((0, 8), (1, 4))),
        "w_in_bc": bell_draw(splits[6], (D, 2 * N), D ** -0.5, 0.1875, ((0, 8),)),
        "w_in_dt": bell_draw(splits[7], (D, H), D ** -0.5, 0.1875, ((0, 8), (1, 4))),
        "conv_x": bell_draw(splits[8], (CONV, DI), CONV ** -0.5, 3.0, ((1, 4),), jnp.float32),
        "conv_x_bias": bell_draw(splits[9], (DI,), 0.3, 1.75, ((0, 4),), jnp.float32),
        "conv_bc": bell_draw(splits[10], (CONV, 2 * N), CONV ** -0.5, 3.0, (), jnp.float32),
        "conv_bc_bias": bell_draw(splits[11], (2 * N,), 0.3, 1.75, (), jnp.float32),
        "dt_bias": jnp.clip(-5.0 + 4.0 * jax.random.uniform(splits[12], (H,), jnp.float32) ** block_scale(splits[12], (H,), ((0, 4),), -0.2, 0.2), -5.0, -1.0),
        "a_log": jnp.clip(2.77 * jax.random.uniform(splits[13], (H,), jnp.float32) ** block_scale(splits[13], (H,), ((0, 4),), -0.2, 0.2), 0.0, 2.77),
        "d_skip": jnp.clip(0.5 + 1.0 * jax.random.uniform(splits[14], (H,), jnp.float32) ** block_scale(splits[14], (H,), ((0, 4),), -0.2, 0.2), 0.5, 1.5),
        "gate_gain": jnp.clip(1.0 + 0.18 * jax.random.normal(splits[15], (DI,), jnp.float32), 0.1, 1.9),
        "w_out": bell_draw(splits[16], (D, DI), DI ** -0.5, 0.125, ((0, 8), (1, 4))),
    }


full_precision = lax.Precision.HIGHEST
norm_epsilon = 1e-05

@jax.custom_vjp
def low(v):
    return lax.optimization_barrier(v.astype(jnp.bfloat16)).astype(jnp.float32)

@jax.custom_vjp
def low_back(v):
    return v

def low_keep(v):
    return (low(v), None)

def low_pass(kept, grad):
    return (grad,)

def back_keep(v):
    return (v, None)

def back_low(kept, grad):
    return (low(grad),)
low.defvjp(low_keep, low_pass)
low_back.defvjp(back_keep, back_low)

def causal_conv(values, seg_row, kernel, conv_bias):
    length = values.shape[0]
    padded = jnp.pad(values, ((CONV - 1, 0), (0, 0)))
    seg_padded = jnp.pad(seg_row, (CONV - 1, 0), constant_values=-1)
    summed = conv_bias[None, :] + jnp.zeros_like(values)
    for offset in range(CONV):
        matches = (seg_padded[offset:offset + length] == seg_row).astype(jnp.float32)
        summed = summed + kernel[offset][None, :] * padded[offset:offset + length] * matches[:, None]
    return jax.nn.silu(summed)

def block_step(carry_state, inputs):
    x_block, dt_block, decay_block, b_block, c_block, seg_block, prev_seg = inputs
    block_len = seg_block.shape[0]
    head_count = dt_block.shape[1]
    x_heads = x_block.reshape(block_len, head_count, -1)
    cumulative = jnp.cumsum(decay_block, axis=0)
    places = jnp.arange(block_len)
    keep_mask = (places[:, None] >= places[None, :]) & (seg_block[:, None] == seg_block[None, :])
    spread_mask = keep_mask[:, :, None]
    decays = jnp.where(spread_mask, jnp.exp(jnp.where(spread_mask, cumulative[:, None, :] - cumulative[None, :, :], -60.0)), 0.0)
    scores = jnp.dot(c_block, b_block.T, precision=full_precision)
    weighted = x_heads * dt_block[:, :, None]
    y_inner = jnp.einsum('tsh,shp->thp', scores[:, :, None] * decays, weighted, precision=full_precision)
    from_prev = (seg_block == prev_seg).astype(jnp.float32)
    carried = jnp.einsum('tn,hpn->thp', c_block, carry_state, precision=full_precision)
    y_outer = carried * (jnp.exp(cumulative) * from_prev[:, None])[:, :, None]
    last_seg = seg_block[block_len - 1]
    to_end = jnp.exp(cumulative[block_len - 1][None, :] - cumulative) * (seg_block == last_seg).astype(jnp.float32)[:, None]
    new_state = jnp.einsum('shp,sn->hpn', weighted * to_end[:, :, None], b_block, precision=full_precision)
    survive = jnp.exp(cumulative[block_len - 1]) * (last_seg == prev_seg).astype(jnp.float32)
    new_state = new_state + carry_state * survive[:, None, None]
    return (new_state, (y_inner + y_outer).reshape(block_len, -1))

def scan_row(x_row, dt_row, decay_row, b_row, c_row, seg_row):
    length = seg_row.shape[0]
    blocks = length // GROUP
    head_count = dt_row.shape[1]
    head_size = x_row.shape[1] // head_count

    def to_blocks(source):
        return source.reshape((blocks, GROUP) + source.shape[1:])
    seg_blocks = to_blocks(seg_row)
    prev_segs = jnp.concatenate([jnp.full((1,), -1, jnp.int32), seg_blocks[:-1, GROUP - 1].astype(jnp.int32)])
    initial = jnp.zeros((head_count, head_size, N), jnp.float32)
    final_state, outputs = lax.scan(jax.checkpoint(block_step), initial, (to_blocks(x_row), to_blocks(dt_row), to_blocks(decay_row), to_blocks(b_row), to_blocks(c_row), seg_blocks, prev_segs))
    return outputs.reshape(length, -1)

def mixer_core(z_proj, x_proj, bc_proj, dt_proj, seg_row, conv_x, conv_x_bias, conv_bc, conv_bc_bias, dt_bias, a_log, d_skip):
    x_conv = causal_conv(x_proj, seg_row, conv_x, conv_x_bias)
    bc_conv = causal_conv(bc_proj, seg_row, conv_bc, conv_bc_bias)
    dt_row = jax.nn.softplus(dt_proj + dt_bias[None, :])
    decay_row = -dt_row * jnp.exp(a_log)[None, :]
    scanned = scan_row(x_conv, dt_row, decay_row, bc_conv[:, :N], bc_conv[:, N:], seg_row)
    head_count = dt_row.shape[1]
    length = x_conv.shape[0]
    skipped = (x_conv.reshape(length, head_count, -1) * d_skip[None, :, None]).reshape(length, -1)
    return (scanned + skipped) * jax.nn.silu(z_proj)

def layer_row(hidden_row, seg_row, weights):
    norm_gain, w_in_z, w_in_x, w_in_bc, w_in_dt, conv_x, conv_x_bias, conv_bc, conv_bc_bias, dt_bias, a_log, d_skip, gate_gain, w_out = weights
    inverse = lax.rsqrt(lax.optimization_barrier(jnp.mean(hidden_row * hidden_row, axis=1, keepdims=True)) + norm_epsilon)
    normed = low(hidden_row * inverse * norm_gain[None, :])
    z_proj = low_back(jnp.dot(normed, w_in_z, precision=full_precision))
    x_proj = low_back(jnp.dot(normed, w_in_x, precision=full_precision))
    bc_proj = low_back(jnp.dot(normed, w_in_bc, precision=full_precision))
    dt_proj = low_back(jnp.dot(normed, w_in_dt, precision=full_precision))
    gated = mixer_core(z_proj, x_proj, bc_proj, dt_proj, seg_row, conv_x, conv_x_bias, conv_bc, conv_bc_bias, dt_bias, a_log, d_skip)
    gate_inverse = lax.rsqrt(lax.optimization_barrier(jnp.mean(gated * gated, axis=1, keepdims=True)) + norm_epsilon)
    live = (seg_row > 0).astype(jnp.float32)
    normed_out = low(gated * gate_inverse * gate_gain[None, :] * live[:, None])
    return hidden_row + jnp.dot(normed_out, w_out.T, precision=full_precision)

def reference(hidden, seg_ids, cotangent, norm_gain, w_in_z, w_in_x, w_in_bc, w_in_dt, conv_x, conv_x_bias, conv_bc, conv_bc_bias, dt_bias, a_log, d_skip, gate_gain, w_out):
    weights = tuple((weight_arg.astype(jnp.float32) for weight_arg in (norm_gain, w_in_z, w_in_x, w_in_bc, w_in_dt, conv_x, conv_x_bias, conv_bc, conv_bc_bias, dt_bias, a_log, d_skip, gate_gain, w_out)))

    def row_step(totals, row_inputs):
        hidden_row, seg_row, cot_row = row_inputs

        def forward(hidden_in, weight_in):
            return layer_row(hidden_in, seg_row, weight_in)
        result, pullback = jax.vjp(forward, hidden_row.astype(jnp.float32), weights)
        hidden_grad, weight_grads = pullback(cot_row.astype(jnp.float32))
        totals = jax.tree.map(jnp.add, totals, weight_grads)
        return (totals, (result.astype(jnp.bfloat16), hidden_grad.astype(jnp.bfloat16)))
    initial_totals = tuple((jnp.zeros_like(weight_arg) for weight_arg in weights))
    totals, row_results = lax.scan(row_step, initial_totals, (hidden, seg_ids, cotangent))
    layer_out, grad_hidden = row_results
    return (layer_out, grad_hidden, totals[0], totals[1], totals[2], totals[3], totals[4], totals[5], totals[6], totals[7], totals[8], totals[9], totals[10], totals[11], totals[12], totals[13])
```

```python
import functools

import jax
import jax.numpy as jnp
from jax import lax
from jax.experimental import pallas as pl
from jax.experimental.pallas import tpu as pltpu
from jax.sharding import PartitionSpec as P

N = 128
CONV = 4
Q = 256
LANES = 128
HALO = 8
EPS = 1e-05
NEG = -1e30
F32 = jnp.float32
BF16 = jnp.bfloat16
VMEM_LIMIT = 52 * 1024 * 1024


def dot(a, b):
    return jnp.dot(a, b, preferred_element_type=F32)


def dot_nt(a, b):
    return lax.dot_general(a, b, (((1,), (1,)), ((), ())), preferred_element_type=F32)


def dot_tn(a, b):
    return lax.dot_general(a, b, (((0,), (0,)), ((), ())), preferred_element_type=F32)


def dot_exact(a, b):
    return jnp.dot(a, b, preferred_element_type=F32, precision=lax.Precision.HIGHEST)


def spread(cols, heads, size):
    rows = cols.shape[0]
    per = LANES // size
    lane = lax.broadcasted_iota(jnp.int32, (rows, LANES), 1)
    parts = []
    for first in range(0, heads, per):
        part = jnp.broadcast_to(cols[:, first : first + 1], (rows, LANES))
        for extra in range(1, per):
            part = jnp.where(lane < extra * size, part, cols[:, first + extra : first + extra + 1])
        parts.append(part)
    return jnp.concatenate(parts, axis=1)


def head_sums(values, heads, size):
    width = heads * size
    channel = lax.broadcasted_iota(jnp.int32, (width, LANES), 0)
    column = lax.broadcasted_iota(jnp.int32, (width, LANES), 1)
    first = column * size
    picks = jnp.where((channel >= first) & (channel < first + size), 1.0, 0.0).astype(BF16)
    high = values.astype(BF16)
    low = (values - high.astype(F32)).astype(BF16)
    return dot(high, picks) + dot(low, picks)


def widen(tile, width):
    return jnp.concatenate([tile] * (width // tile.shape[1]), axis=1)


def softplus(v):
    return jnp.maximum(v, 0.0) + jnp.log1p(jnp.exp(-jnp.abs(v)))


def sigmoid(v):
    return 1.0 / (1.0 + jnp.exp(-v))


def as_row(column):
    rows = column.shape[0]
    return jnp.broadcast_to(column, (rows, LANES)).T[:8]


def triangle(lower):
    row = lax.broadcasted_iota(jnp.int32, (Q, Q), 0)
    col = lax.broadcasted_iota(jnp.int32, (Q, Q), 1)
    return row >= col if lower else row <= col


def block_masks(window, seg_row):
    seg = window[HALO : HALO + Q]
    before = window[HALO - 1 : HALO]
    last = window[HALO + Q - 1 : HALO + Q]
    from_prev = (seg == before).astype(F32)
    same_last = (seg == last).astype(F32)
    passes = (last == before).astype(F32)
    keep = (widen(seg, Q) == seg_row) & triangle(True)
    bias = jnp.where(keep, 0.0, NEG)
    return seg, from_prev, same_last, passes, bias


def conv_forward(buffer, window, seg, kernel, conv_bias, width):
    total = conv_bias + kernel[CONV - 1 : CONV] * buffer[HALO : HALO + Q, :]
    for back in range(1, CONV):
        match = (window[HALO - back : HALO - back + Q] == seg).astype(F32)
        tap = kernel[CONV - 1 - back : CONV - back]
        total = total + tap * (buffer[HALO - back : HALO - back + Q, :] * widen(match, width))
    return total


def conv_backward(buffer, window, seg, kernel, values, width):
    here = buffer[0:Q, :]
    total = kernel[CONV - 1 : CONV] * here
    taps = [jnp.sum(values * here, axis=0, keepdims=True)]
    for ahead in range(1, CONV):
        match = (window[HALO + ahead : HALO + ahead + Q] == seg).astype(F32)
        moved = buffer[ahead : ahead + Q, :] * widen(match, width)
        total = total + kernel[CONV - 1 - ahead : CONV - ahead] * moved
        taps.append(jnp.sum(values * moved, axis=0, keepdims=True))
    return total, taps


def forward_kernel(
    heads,
    size,
    hidden_ref,
    gain_ref,
    window_ref,
    seg_row_ref,
    weights_ref,
    kernel_x_ref,
    kernel_bc_ref,
    head_ref,
    channel_ref,
    tokens_ref,
    z_ref,
    mixed_ref,
    x_ref,
    pre_ref,
    bcdt_ref,
    pre_bc_ref,
    state_ref,
    scaled_ref,
    part_ref,
    square_ref,
    x_buffer,
    bc_buffer,
    carry,
):
    step = pl.program_id(0)
    width = heads * size
    rest = 2 * N + LANES

    @pl.when(step == 0)
    def _():
        x_buffer[0:HALO, :] = jnp.zeros((HALO, width), F32)
        bc_buffer[0:HALO, :] = jnp.zeros((HALO, 2 * N), F32)
        carry[...] = jnp.zeros((N, width), F32)

    window = window_ref[pl.ds(pl.multiple_of(step * Q, Q), Q + 2 * HALO), :]
    seg, from_prev, same_last, passes, bias = block_masks(window, seg_row_ref[0:1, :])

    hidden = hidden_ref[...].astype(F32)
    inverse = lax.rsqrt(jnp.mean(hidden * hidden, axis=1, keepdims=True) + EPS)
    tokens = (hidden * inverse * gain_ref[0:1, :]).astype(BF16)
    tokens_ref[...] = tokens
    x_proj = dot(tokens, weights_ref[:, width : 2 * width])
    z_proj = dot(tokens, weights_ref[:, 2 * width : 3 * width])
    bcdt = dot(tokens, weights_ref[:, 3 * width : 3 * width + rest])
    z_ref[...] = z_proj
    x_ref[...] = x_proj
    bcdt_ref[...] = bcdt

    x_buffer[HALO : HALO + Q, :] = x_proj
    bc_buffer[HALO : HALO + Q, :] = bcdt[:, : 2 * N]
    pre = conv_forward(
        x_buffer, window, seg, kernel_x_ref[...], kernel_x_ref[CONV : CONV + 1, :], width
    )
    pre_bc = conv_forward(
        bc_buffer, window, seg, kernel_bc_ref[...], kernel_bc_ref[CONV : CONV + 1, :], 2 * N
    )
    x_buffer[0:HALO, :] = x_buffer[Q : Q + HALO, :]
    bc_buffer[0:HALO, :] = bc_buffer[Q : Q + HALO, :]
    pre_ref[...] = pre
    pre_bc_ref[...] = pre_bc
    x_conv = pre * sigmoid(pre)
    bc_conv = (pre_bc * sigmoid(pre_bc)).astype(BF16)
    b_in = bc_conv[:, :N]
    c_in = bc_conv[:, N:]

    dt = softplus(bcdt[:, 2 * N :] + head_ref[0:1, :])
    decay = -dt * jnp.exp(head_ref[1:2, :])
    total = dot_exact(triangle(True).astype(F32), decay)
    total_t = total.T
    weighted = x_conv * spread(dt, heads, size)
    scores = dot_nt(c_in, b_in)
    before = carry[...]
    state_ref[0] = before

    per = LANES // size
    lane = lax.broadcasted_iota(jnp.int32, (Q, LANES), 1)
    inner = []
    for first in range(0, heads, per):
        group = weighted[:, first * size : first * size + LANES]
        summed = jnp.zeros((Q, LANES), F32)
        for extra in range(per):
            h = first + extra
            shape = jnp.exp(total[:, h : h + 1] - total_t[h : h + 1, :] + bias)
            mine = (lane >= extra * size) & (lane < (extra + 1) * size)
            summed = summed + dot(
                (scores * shape).astype(BF16), jnp.where(mine, group, 0.0).astype(BF16)
            )
        inner.append(summed)
    scanned = jnp.concatenate(inner, axis=1)
    scanned = scanned + dot(c_in, before.astype(BF16)) * spread(
        jnp.exp(total) * from_prev, heads, size
    )
    last = total[Q - 1 : Q, :]
    to_end = jnp.exp(last - total) * same_last
    carry[...] = dot_tn(
        b_in, (weighted * spread(to_end, heads, size)).astype(BF16)
    ) + before * spread(jnp.exp(last) * passes, heads, size)

    mixed = scanned + channel_ref[1:2, :] * x_conv
    mixed_ref[...] = mixed
    gated = mixed * (z_proj * sigmoid(z_proj))
    scaled = (gated * channel_ref[0:1, :]).astype(BF16)
    scaled_ref[...] = scaled
    part_ref[...] = dot_nt(scaled, weights_ref[:, :width]).astype(BF16)
    square_ref[...] = as_row(jnp.sum(gated * gated, axis=1, keepdims=True))


def gradient_kernel(width, cot_ref, weights_ref, scaled_ref, window_ref, grad_ref, along_ref):
    step = pl.program_id(0)
    window = window_ref[pl.ds(pl.multiple_of(step * Q, Q), Q + 2 * HALO), :]
    live = (window[HALO : HALO + Q] > 0).astype(F32)
    grad = dot(cot_ref[...], weights_ref[...]) * widen(live, width)
    grad_ref[...] = grad
    along_ref[...] = as_row(jnp.sum(scaled_ref[...].astype(F32) * grad, axis=1, keepdims=True))


def backward_kernel(
    heads,
    size,
    full_inner,
    stat_ref,
    hidden_ref,
    window_ref,
    seg_row_ref,
    weights_ref,
    kernel_x_ref,
    kernel_bc_ref,
    head_ref,
    channel_ref,
    z_ref,
    mixed_ref,
    x_ref,
    pre_ref,
    bcdt_ref,
    pre_bc_ref,
    state_ref,
    grad_ref,
    proj_ref,
    part_ref,
    out_ref,
    sum_x_ref,
    sum_bc_ref,
    sum_head_ref,
    sum_gain_ref,
    x_buffer,
    bc_buffer,
    carry,
    tail,
):
    turn = pl.program_id(0)
    step = pl.num_programs(0) - 1 - turn
    width = heads * size

    @pl.when(turn == 0)
    def _():
        x_buffer[...] = jnp.zeros((Q + HALO, width), F32)
        bc_buffer[...] = jnp.zeros((Q + HALO, 2 * N), F32)
        carry[...] = jnp.zeros((N, width), F32)
        tail[...] = jnp.zeros((8, LANES), F32)
        sum_x_ref[...] = jnp.zeros((8, width), F32)
        sum_bc_ref[...] = jnp.zeros((8, 2 * N), F32)
        sum_head_ref[...] = jnp.zeros((8, LANES), F32)
        sum_gain_ref[...] = jnp.zeros(sum_gain_ref.shape, F32)

    window = window_ref[pl.ds(pl.multiple_of(step * Q, Q), Q + 2 * HALO), :]
    seg, from_prev, same_last, passes, bias = block_masks(window, seg_row_ref[0:1, :])
    live = (seg[:, 0:1] > 0).astype(F32)

    stat = stat_ref[...].T
    gate_inverse = lax.rsqrt(stat[:, 0:1] / full_inner + EPS)
    along = stat[:, 1:2] * (gate_inverse * gate_inverse * gate_inverse / full_inner)

    gain = channel_ref[0:1, :]
    skip = channel_ref[1:2, :]
    z_proj = z_ref[...]
    mixed = mixed_ref[...]
    grad_out = grad_ref[...]
    gate = sigmoid(z_proj)
    opened = z_proj * gate
    gated = mixed * opened
    normal = gated * gate_inverse
    sum_gate = jnp.sum(grad_out * normal, axis=0, keepdims=True)
    out_ref[...] = (normal * gain * live).astype(BF16)
    grad_gated = grad_out * gain * gate_inverse - gated * along
    grad_z = grad_gated * mixed * (gate * (1.0 + z_proj * (1.0 - gate)))
    dy = grad_gated * opened

    pre = pre_ref[...]
    gate_x = sigmoid(pre)
    x_conv = pre * gate_x
    pre_bc = pre_bc_ref[...]
    gate_bc = sigmoid(pre_bc)
    bc_conv = (pre_bc * gate_bc).astype(BF16)
    b_in = bc_conv[:, :N]
    c_in = bc_conv[:, N:]
    bcdt = bcdt_ref[...]
    raw = bcdt[:, 2 * N :] + head_ref[0:1, :]
    dt = softplus(raw)
    rate = jnp.exp(head_ref[1:2, :])
    decay = -dt * rate
    total = dot_exact(triangle(True).astype(F32), decay)
    total_t = total.T
    dt_wide = spread(dt, heads, size)
    weighted = x_conv * dt_wide
    scores = dot_nt(c_in, b_in)
    before = state_ref[0]
    before_low = before.astype(BF16)
    last = total[Q - 1 : Q, :]
    to_end = spread(jnp.exp(last - total) * same_last, heads, size)
    from_start = spread(jnp.exp(total) * from_prev, heads, size)
    after = carry[...]
    after_low = after.astype(BF16)

    dy_low = dy.astype(BF16)
    weighted_low = weighted.astype(BF16)
    dy_start = (dy * from_start).astype(BF16)
    grad_c = dot_nt(dy_start, before_low)
    carried = dot(c_in, before_low)
    returned = dot(b_in, after_low)
    grad_weighted = to_end * returned
    weighted_end = (weighted * to_end).astype(BF16)
    grad_b = dot_nt(weighted_end, after_low)
    new_after = dot_tn(c_in, dy_start) + after * spread(jnp.exp(last) * passes, heads, size)
    carry[...] = new_after

    per = LANES // size
    lane = lax.broadcasted_iota(jnp.int32, (Q, LANES), 1)
    grad_scores = jnp.zeros((Q, Q), F32)
    inner = []
    none = jnp.zeros((Q, LANES), BF16)
    for first in range(0, heads, per):
        at = first * size
        dy_group = dy_low[:, at : at + LANES]
        weighted_group = weighted_low[:, at : at + LANES]
        summed = jnp.zeros((Q, LANES), F32)
        for extra in range(per):
            h = first + extra
            shape = jnp.exp(total[:, h : h + 1] - total_t[h : h + 1, :] + bias)
            mine = (lane >= extra * size) & (lane < (extra + 1) * size)
            dy_mine = jnp.where(mine, dy_group, none)
            grad_scores = grad_scores + dot_nt(dy_mine, weighted_group) * shape
            summed = summed + dot_tn((scores * shape).astype(BF16), dy_mine)
        inner.append(summed)
    grad_inner = jnp.concatenate(inner, axis=1)
    grad_weighted = grad_weighted + grad_inner
    grad_scores = grad_scores.astype(BF16)
    grad_c = grad_c + dot(grad_scores, b_in)
    grad_b = grad_b + dot_tn(grad_scores, c_in)

    scanned = mixed - skip * x_conv - carried * from_start
    pairs = head_sums(
        dy_low.astype(F32) * scanned
        + dy_start.astype(F32) * carried
        - weighted_low.astype(F32) * grad_inner
        - weighted_end.astype(F32) * returned,
        heads,
        size,
    )
    grad_decay = dot_exact(triangle(False).astype(F32), pairs) + tail[0:1, :]
    kept = jnp.sum(new_after.astype(BF16).astype(F32) * before, axis=0, keepdims=True)
    kept = jnp.broadcast_to(kept, (8, width))
    tail[...] = head_sums(kept, heads, size)
    grad_dt = head_sums(grad_weighted * x_conv, heads, size) - grad_decay * rate
    grad_raw = grad_dt * sigmoid(raw)
    sum_head_ref[0:1, :] += jnp.sum(grad_raw, axis=0, keepdims=True)
    sum_head_ref[1:2, :] += jnp.sum(grad_decay * decay, axis=0, keepdims=True)

    grad_x = grad_weighted * dt_wide + skip * dy
    sum_skip = jnp.sum(dy * x_conv, axis=0, keepdims=True)
    grad_pre = grad_x * (gate_x * (1.0 + pre * (1.0 - gate_x)))
    x_buffer[Q : Q + HALO, :] = x_buffer[0:HALO, :]
    x_buffer[0:Q, :] = grad_pre
    grad_proj, taps = conv_backward(
        x_buffer, window, seg, kernel_x_ref[...], x_ref[...], width
    )
    sum_bias = jnp.sum(grad_pre, axis=0, keepdims=True)
    blank = jnp.zeros((1, width), F32)
    sum_x_ref[...] += jnp.concatenate(
        [taps[3], taps[2], taps[1], taps[0], sum_bias, sum_gate, sum_skip, blank], axis=0
    )

    grad_pre_bc = jnp.concatenate([grad_b, grad_c], axis=1) * (
        gate_bc * (1.0 + pre_bc * (1.0 - gate_bc))
    )
    bc_buffer[Q : Q + HALO, :] = bc_buffer[0:HALO, :]
    bc_buffer[0:Q, :] = grad_pre_bc
    grad_bc, taps_bc = conv_backward(
        bc_buffer, window, seg, kernel_bc_ref[...], bcdt[:, : 2 * N], 2 * N
    )
    sum_bias_bc = jnp.sum(grad_pre_bc, axis=0, keepdims=True)
    blank_bc = jnp.zeros((3, 2 * N), F32)
    sum_bc_ref[...] += jnp.concatenate(
        [taps_bc[3], taps_bc[2], taps_bc[1], taps_bc[0], sum_bias_bc, blank_bc], axis=0
    )

    grads = jnp.concatenate(
        [
            grad_proj.astype(BF16),
            grad_z.astype(BF16),
            grad_bc.astype(BF16),
            grad_raw.astype(BF16),
        ],
        axis=1,
    )
    proj_ref[...] = grads
    part = dot_nt(grads, weights_ref[:, width:])
    part_ref[...] = part.astype(BF16)
    hidden = hidden_ref[...].astype(F32)
    inverse = lax.rsqrt(jnp.mean(hidden * hidden, axis=1, keepdims=True) + EPS)
    sum_gain_ref[0:1, :] += jnp.sum(part * (hidden * inverse), axis=0, keepdims=True)


def whole(shape):
    return pl.BlockSpec(shape, lambda i: (0,) * len(shape))


def run_forward(heads, size, hidden, gain, window, seg_row, weights, kernel_x, kernel_bc, head, channel):
    length, features = hidden.shape
    width = heads * size
    blocks = length // Q
    rest = 2 * N + LANES

    def rows(columns):
        return pl.BlockSpec((Q, columns), lambda i: (i, 0))

    def made(columns, dtype):
        return jax.ShapeDtypeStruct((length, columns), dtype)

    return pl.pallas_call(
        functools.partial(forward_kernel, heads, size),
        grid=(blocks,),
        in_specs=[
            rows(features),
            whole(gain.shape),
            whole(window.shape),
            pl.BlockSpec((8, Q), lambda i: (0, i)),
            whole(weights.shape),
            whole(kernel_x.shape),
            whole(kernel_bc.shape),
            whole(head.shape),
            whole(channel.shape),
        ],
        out_specs=[
            rows(features),
            rows(width),
            rows(width),
            rows(width),
            rows(width),
            rows(rest),
            rows(2 * N),
            pl.BlockSpec((1, N, width), lambda i: (i, 0, 0)),
            rows(width),
            rows(features),
            pl.BlockSpec((8, Q), lambda i: (0, i)),
        ],
        out_shape=[
            made(features, BF16),
            made(width, F32),
            made(width, F32),
            made(width, F32),
            made(width, F32),
            made(rest, F32),
            made(2 * N, F32),
            jax.ShapeDtypeStruct((blocks, N, width), F32),
            made(width, BF16),
            made(features, BF16),
            jax.ShapeDtypeStruct((8, length), F32),
        ],
        scratch_shapes=[
            pltpu.VMEM((Q + HALO, width), F32),
            pltpu.VMEM((Q + HALO, 2 * N), F32),
            pltpu.VMEM((N, width), F32),
        ],
        compiler_params=pltpu.CompilerParams(vmem_limit_bytes=VMEM_LIMIT),
        name="forward",
    )(hidden, gain, window, seg_row, weights, kernel_x, kernel_bc, head, channel)


def run_gradient(cot, weights, scaled, window):
    length, features = cot.shape
    width = scaled.shape[1]
    return pl.pallas_call(
        functools.partial(gradient_kernel, width),
        grid=(length // Q,),
        in_specs=[
            pl.BlockSpec((Q, features), lambda i: (i, 0)),
            pl.BlockSpec((features, width), lambda i: (0, 0)),
            pl.BlockSpec((Q, width), lambda i: (i, 0)),
            whole(window.shape),
        ],
        out_specs=[
            pl.BlockSpec((Q, width), lambda i: (i, 0)),
            pl.BlockSpec((8, Q), lambda i: (0, i)),
        ],
        out_shape=[
            jax.ShapeDtypeStruct((length, width), F32),
            jax.ShapeDtypeStruct((8, length), F32),
        ],
        compiler_params=pltpu.CompilerParams(vmem_limit_bytes=VMEM_LIMIT),
        name="out_gradient",
    )(cot, weights, scaled, window)


def run_backward(
    heads, size, full_inner, stat, hidden, window, seg_row, weights, kernel_x, kernel_bc, head, channel,
    z_proj, mixed, x_proj, pre, bcdt, pre_bc, states, grad_out,
):
    length, features = hidden.shape
    width = heads * size
    blocks = length // Q
    rest = 2 * N + LANES
    total = 2 * width + rest

    def rows(columns):
        return pl.BlockSpec((Q, columns), lambda i: (blocks - 1 - i, 0))

    def made(columns, dtype):
        return jax.ShapeDtypeStruct((length, columns), dtype)

    across = pl.BlockSpec((8, Q), lambda i: (0, blocks - 1 - i))
    sums = [(8, width), (8, 2 * N), (8, LANES), (8, features)]
    return pl.pallas_call(
        functools.partial(backward_kernel, heads, size, full_inner),
        grid=(blocks,),
        in_specs=[
            across,
            rows(features),
            whole(window.shape),
            across,
            whole(weights.shape),
            whole(kernel_x.shape),
            whole(kernel_bc.shape),
            whole(head.shape),
            whole(channel.shape),
            rows(width),
            rows(width),
            rows(width),
            rows(width),
            rows(rest),
            rows(2 * N),
            pl.BlockSpec((1, N, width), lambda i: (blocks - 1 - i, 0, 0)),
            rows(width),
        ],
        out_specs=[rows(total), rows(features), rows(width)] + [whole(shape) for shape in sums],
        out_shape=[made(total, BF16), made(features, BF16), made(width, BF16)]
        + [jax.ShapeDtypeStruct(shape, F32) for shape in sums],
        scratch_shapes=[
            pltpu.VMEM((Q + HALO, width), F32),
            pltpu.VMEM((Q + HALO, 2 * N), F32),
            pltpu.VMEM((N, width), F32),
            pltpu.VMEM((8, LANES), F32),
        ],
        compiler_params=pltpu.CompilerParams(vmem_limit_bytes=VMEM_LIMIT),
        name="backward",
    )(
        stat, hidden, window, seg_row, weights, kernel_x, kernel_bc, head, channel,
        z_proj, mixed, x_proj, pre, bcdt, pre_bc, states, grad_out,
    )


def pad_lanes(values):
    return jnp.pad(values, ((0, 0), (0, LANES - values.shape[1])))


def shards(
    hidden,
    seg_ids,
    cotangent,
    norm_gain,
    w_in_z,
    w_in_x,
    w_in_bc,
    w_in_dt,
    conv_x,
    conv_x_bias,
    conv_bc,
    conv_bc_bias,
    dt_bias,
    a_log,
    d_skip,
    gate_gain,
    w_out,
):
    heads = dt_bias.shape[0]
    width = gate_gain.shape[0]
    size = width // heads
    full_inner = width * lax.axis_size("tensor")
    features = hidden.shape[2]
    hidden_local = hidden[0]

    packed = jnp.concatenate([w_out, w_in_x, w_in_z, w_in_bc, pad_lanes(w_in_dt)], axis=1)
    hidden_full = lax.all_gather(hidden_local, "tensor", axis=0, tiled=True)
    weights = lax.all_gather(packed, "dp", axis=0, tiled=True)
    gain_full = lax.all_gather(norm_gain, "dp", axis=0, tiled=True)
    seg_full = lax.all_gather(seg_ids[0], "tensor", axis=0, tiled=True)
    cot_full = lax.all_gather(cotangent[0], "tensor", axis=0, tiled=True)

    gain = gain_full.astype(F32)[None, :]
    window = jnp.broadcast_to(
        jnp.pad(seg_full, (HALO, HALO), constant_values=-1)[:, None],
        (seg_full.shape[0] + 2 * HALO, LANES),
    )
    seg_row = jnp.broadcast_to(seg_full[None, :], (8, seg_full.shape[0]))
    kernel_x = jnp.concatenate([conv_x, conv_x_bias[None, :]], axis=0)
    kernel_bc = jnp.concatenate([conv_bc, conv_bc_bias[None, :]], axis=0)
    head = pad_lanes(jnp.stack([dt_bias, a_log]))
    channel = jnp.stack([gate_gain, jnp.repeat(d_skip, size)])

    (
        tokens, z_proj, mixed, x_proj, pre, bcdt, pre_bc, states, scaled, out_part, square,
    ) = run_forward(
        heads, size, hidden_full, gain, window, seg_row, weights, kernel_x, kernel_bc, head, channel
    )
    out_sum = lax.psum_scatter(out_part, "tensor", scatter_dimension=0, tiled=True)
    grad_out, along = run_gradient(cot_full, weights, scaled, window)
    stat = lax.psum(jnp.stack([square[0], along[0]]), "tensor")
    stat_full = jnp.pad(stat, ((0, 6), (0, 0)))

    grads, in_part, normed_out, sum_x, sum_bc, sum_head, sum_gain = run_backward(
        heads, size, full_inner, stat_full, hidden_full, window, seg_row, weights, kernel_x,
        kernel_bc, head, channel, z_proj, mixed, x_proj, pre, bcdt, pre_bc, states, grad_out,
    )
    in_sum = lax.psum_scatter(in_part, "tensor", scatter_dimension=0, tiled=True)

    grad_weights = dot_tn(tokens, grads).astype(BF16)
    grad_w_out = dot_tn(cot_full, normed_out).astype(BF16)
    sum_weights = lax.psum_scatter(
        jnp.concatenate([grad_w_out, grad_weights], axis=1), "dp", scatter_dimension=0, tiled=True
    )
    shared = lax.psum(
        (sum_gain[0], sum_bc, sum_weights[:, 3 * width : 3 * width + 2 * N].astype(F32)),
        "tensor",
    )
    gain_bc, sum_bc, grad_bc = shared
    small = lax.psum((sum_x, sum_head, gain_bc, sum_bc), "dp")
    sum_x, sum_head, sum_gain, sum_bc = small
    local_features = norm_gain.shape[0]
    grad_norm_gain = lax.dynamic_slice_in_dim(
        sum_gain, lax.axis_index("dp") * local_features, local_features, 0
    )

    local = hidden_local.shape[0]
    place = lax.axis_index("tensor") * local
    hidden_rows = hidden_local.astype(F32)
    live = (seg_ids[0] > 0).astype(F32)[:, None]
    square_here = lax.dynamic_slice_in_dim(stat[0], place, local, 0)[:, None]
    out_scale = lax.rsqrt(square_here / full_inner + EPS) * live
    layer_out = (hidden_rows + out_sum.astype(F32) * out_scale).astype(BF16)

    inverse = lax.rsqrt(jnp.mean(hidden_rows * hidden_rows, axis=1, keepdims=True) + EPS)
    unit = hidden_rows * inverse
    grad_scaled = in_sum.astype(F32) * gain
    grad_hidden = (
        cotangent[0].astype(F32)
        + inverse * (grad_scaled - unit * jnp.mean(grad_scaled * unit, axis=1, keepdims=True))
    ).astype(BF16)

    sum_weights = sum_weights.astype(F32)
    return (
        layer_out[None],
        grad_hidden[None],
        grad_norm_gain,
        sum_weights[:, 2 * width : 3 * width],
        sum_weights[:, width : 2 * width],
        grad_bc,
        sum_weights[:, 3 * width + 2 * N : 3 * width + 2 * N + heads],
        sum_x[0:CONV],
        sum_x[CONV],
        sum_bc[0:CONV],
        sum_bc[CONV],
        sum_head[0, :heads],
        sum_head[1, :heads],
        jnp.sum(sum_x[CONV + 2].reshape(heads, size), axis=1),
        sum_x[CONV + 1],
        sum_weights[:, :width],
    )


def solution(mesh):
    in_specs = (
        P("dp", "tensor", None),
        P("dp", "tensor"),
        P("dp", "tensor", None),
        P("dp"),
        P("dp", "tensor"),
        P("dp", "tensor"),
        P("dp", None),
        P("dp", "tensor"),
        P(None, "tensor"),
        P("tensor"),
        P(),
        P(),
        P("tensor"),
        P("tensor"),
        P("tensor"),
        P("tensor"),
        P("dp", "tensor"),
    )
    out_specs = (
        P("dp", "tensor", None),
        P("dp", "tensor", None),
        P("dp"),
        P("dp", "tensor"),
        P("dp", "tensor"),
        P("dp", None),
        P("dp", "tensor"),
        P(None, "tensor"),
        P("tensor"),
        P(),
        P(),
        P("tensor"),
        P("tensor"),
        P("tensor"),
        P("tensor"),
        P("dp", "tensor"),
    )
    return jax.shard_map(shards, mesh=mesh, in_specs=in_specs, out_specs=out_specs, check_vma=False)
```

```python
import functools

import jax
import jax.numpy as jnp
from jax import lax
from jax.experimental import pallas as pl
from jax.experimental.pallas import tpu as pltpu
from jax.sharding import PartitionSpec as P

N = 128
CONV = 4
Q = 256
LANES = 128
HALO = 8
EPS = 1e-05
NEG = -1e30
F32 = jnp.float32
BF16 = jnp.bfloat16
VMEM_LIMIT = 52 * 1024 * 1024


def dot(a, b):
    return jnp.dot(a, b, preferred_element_type=F32)


def dot_nt(a, b):
    return lax.dot_general(a, b, (((1,), (1,)), ((), ())), preferred_element_type=F32)


def dot_tn(a, b):
    return lax.dot_general(a, b, (((0,), (0,)), ((), ())), preferred_element_type=F32)


def dot_exact(a, b):
    return jnp.dot(a, b, preferred_element_type=F32, precision=lax.Precision.HIGHEST)


def spread(cols, heads, size):
    rows = cols.shape[0]
    per = LANES // size
    lane = lax.broadcasted_iota(jnp.int32, (rows, LANES), 1)
    parts = []
    for first in range(0, heads, per):
        part = jnp.broadcast_to(cols[:, first : first + 1], (rows, LANES))
        for extra in range(1, per):
            part = jnp.where(lane < extra * size, part, cols[:, first + extra : first + extra + 1])
        parts.append(part)
    return jnp.concatenate(parts, axis=1)


def head_sums(values, heads, size):
    width = heads * size
    channel = lax.broadcasted_iota(jnp.int32, (width, LANES), 0)
    column = lax.broadcasted_iota(jnp.int32, (width, LANES), 1)
    first = column * size
    picks = jnp.where((channel >= first) & (channel < first + size), 1.0, 0.0).astype(BF16)
    high = values.astype(BF16)
    low = (values - high.astype(F32)).astype(BF16)
    return dot(high, picks) + dot(low, picks)


def widen(tile, width):
    return jnp.concatenate([tile] * (width // tile.shape[1]), axis=1)


def softplus(v):
    return jnp.maximum(v, 0.0) + jnp.log1p(jnp.exp(-jnp.abs(v)))


def sigmoid(v):
    return 1.0 / (1.0 + jnp.exp(-v))


def as_row(column):
    rows = column.shape[0]
    return jnp.broadcast_to(column, (rows, LANES)).T[:8]


def triangle(lower):
    row = lax.broadcasted_iota(jnp.int32, (Q, Q), 0)
    col = lax.broadcasted_iota(jnp.int32, (Q, Q), 1)
    return row >= col if lower else row <= col


def block_masks(window, seg_row):
    seg = window[HALO : HALO + Q]
    before = window[HALO - 1 : HALO]
    last = window[HALO + Q - 1 : HALO + Q]
    from_prev = (seg == before).astype(F32)
    same_last = (seg == last).astype(F32)
    passes = (last == before).astype(F32)
    keep = (widen(seg, Q) == seg_row) & triangle(True)
    bias = jnp.where(keep, 0.0, NEG)
    return seg, from_prev, same_last, passes, bias


def conv_forward(buffer, window, seg, kernel, conv_bias, width):
    total = conv_bias + kernel[CONV - 1 : CONV] * buffer[HALO : HALO + Q, :]
    for back in range(1, CONV):
        match = (window[HALO - back : HALO - back + Q] == seg).astype(F32)
        tap = kernel[CONV - 1 - back : CONV - back]
        total = total + tap * (buffer[HALO - back : HALO - back + Q, :] * widen(match, width))
    return total


def conv_backward(buffer, window, seg, kernel, values, width):
    here = buffer[0:Q, :]
    total = kernel[CONV - 1 : CONV] * here
    taps = [jnp.sum(values * here, axis=0, keepdims=True)]
    for ahead in range(1, CONV):
        match = (window[HALO + ahead : HALO + ahead + Q] == seg).astype(F32)
        moved = buffer[ahead : ahead + Q, :] * widen(match, width)
        total = total + kernel[CONV - 1 - ahead : CONV - ahead] * moved
        taps.append(jnp.sum(values * moved, axis=0, keepdims=True))
    return total, taps


def pick_block(place, near_refs, block):
    reach = len(near_refs) // 2
    away = pl.program_id(0) - place
    for index, ref in enumerate(near_refs):

        @pl.when(away == index - reach)
        def _():
            block[...] = ref[...]


def forward_kernel(
    heads,
    size,
    near,
    place_ref,
    *refs,
):
    near_refs, refs = refs[:near], refs[near:]
    forward_body(heads, size, place_ref[0], near_refs, *refs)


def forward_body(
    heads,
    size,
    place,
    near_refs,
    window_ref,
    seg_row_ref,
    weights_ref,
    kernel_x_ref,
    kernel_bc_ref,
    head_ref,
    channel_ref,
    hidden_ref,
    tokens_ref,
    z_ref,
    mixed_ref,
    x_ref,
    pre_ref,
    bcdt_ref,
    pre_bc_ref,
    state_ref,
    scaled_ref,
    part_ref,
    square_ref,
    gain_ref,
    x_buffer,
    bc_buffer,
    carry,
):
    step = pl.program_id(0)
    width = heads * size
    rest = 2 * N + LANES

    @pl.when(step == 0)
    def _():
        x_buffer[0:HALO, :] = jnp.zeros((HALO, width), F32)
        bc_buffer[0:HALO, :] = jnp.zeros((HALO, 2 * N), F32)
        carry[...] = jnp.zeros((N, width), F32)
        tail_columns = weights_ref[:, 3 * width + 2 * N :].astype(F32).T
        gain_ref[...] = jnp.broadcast_to(tail_columns[heads : heads + 1], gain_ref.shape)

    pick_block(place, near_refs, hidden_ref)
    window = window_ref[pl.ds(pl.multiple_of(step * Q, Q), Q + 2 * HALO), :]
    seg, from_prev, same_last, passes, bias = block_masks(window, seg_row_ref[0:1, :])

    hidden = hidden_ref[...].astype(F32)
    inverse = lax.rsqrt(jnp.mean(hidden * hidden, axis=1, keepdims=True) + EPS)
    tokens = (hidden * inverse * gain_ref[0:1, :]).astype(BF16)
    tokens_ref[...] = tokens
    x_proj = dot(tokens, weights_ref[:, width : 2 * width])
    z_proj = dot(tokens, weights_ref[:, 2 * width : 3 * width])
    bcdt = dot(tokens, weights_ref[:, 3 * width : 3 * width + rest])
    z_ref[...] = z_proj
    x_ref[...] = x_proj
    bcdt_ref[...] = bcdt

    x_buffer[HALO : HALO + Q, :] = x_proj
    bc_buffer[HALO : HALO + Q, :] = bcdt[:, : 2 * N]
    pre = conv_forward(
        x_buffer, window, seg, kernel_x_ref[...], kernel_x_ref[CONV : CONV + 1, :], width
    )
    pre_bc = conv_forward(
        bc_buffer, window, seg, kernel_bc_ref[...], kernel_bc_ref[CONV : CONV + 1, :], 2 * N
    )
    x_buffer[0:HALO, :] = x_buffer[Q : Q + HALO, :]
    bc_buffer[0:HALO, :] = bc_buffer[Q : Q + HALO, :]
    pre_ref[...] = pre
    pre_bc_ref[...] = pre_bc
    x_conv = pre * sigmoid(pre)
    bc_conv = (pre_bc * sigmoid(pre_bc)).astype(BF16)
    b_in = bc_conv[:, :N]
    c_in = bc_conv[:, N:]

    dt = softplus(bcdt[:, 2 * N :] + head_ref[0:1, :])
    decay = -dt * jnp.exp(head_ref[1:2, :])
    total = dot_exact(triangle(True).astype(F32), decay)
    total_t = total.T
    weighted = x_conv * spread(dt, heads, size)
    scores = dot_nt(c_in, b_in)
    before = carry[...]
    state_ref[0] = before

    per = LANES // size
    lane = lax.broadcasted_iota(jnp.int32, (Q, LANES), 1)
    inner = []
    for first in range(0, heads, per):
        group = weighted[:, first * size : first * size + LANES]
        summed = jnp.zeros((Q, LANES), F32)
        for extra in range(per):
            h = first + extra
            shape = jnp.exp(total[:, h : h + 1] - total_t[h : h + 1, :] + bias)
            mine = (lane >= extra * size) & (lane < (extra + 1) * size)
            summed = summed + dot(
                (scores * shape).astype(BF16), jnp.where(mine, group, 0.0).astype(BF16)
            )
        inner.append(summed)
    scanned = jnp.concatenate(inner, axis=1)
    scanned = scanned + dot(c_in, before.astype(BF16)) * spread(
        jnp.exp(total) * from_prev, heads, size
    )
    last = total[Q - 1 : Q, :]
    to_end = jnp.exp(last - total) * same_last
    carry[...] = dot_tn(
        b_in, (weighted * spread(to_end, heads, size)).astype(BF16)
    ) + before * spread(jnp.exp(last) * passes, heads, size)

    mixed = scanned + channel_ref[1:2, :] * x_conv
    mixed_ref[...] = mixed
    gated = mixed * (z_proj * sigmoid(z_proj))
    scaled = (gated * channel_ref[0:1, :]).astype(BF16)
    scaled_ref[...] = scaled
    part_ref[...] = dot_nt(scaled, weights_ref[:, :width]).astype(BF16)
    square_ref[...] = as_row(jnp.sum(gated * gated, axis=1, keepdims=True))


def gradient_kernel(width, near, place_ref, *refs):
    near_refs, refs = refs[:near], refs[near:]
    weights_ref, scaled_ref, window_ref, cot_ref, grad_ref, along_ref = refs
    step = pl.program_id(0)
    pick_block(place_ref[0], near_refs, cot_ref)
    window = window_ref[pl.ds(pl.multiple_of(step * Q, Q), Q + 2 * HALO), :]
    live = (window[HALO : HALO + Q] > 0).astype(F32)
    grad = dot(cot_ref[...], weights_ref[...]) * widen(live, width)
    grad_ref[...] = grad
    along_ref[...] = as_row(jnp.sum(scaled_ref[...].astype(F32) * grad, axis=1, keepdims=True))


def backward_kernel(
    heads,
    size,
    full_inner,
    stat_ref,
    hidden_ref,
    window_ref,
    seg_row_ref,
    weights_ref,
    kernel_x_ref,
    kernel_bc_ref,
    head_ref,
    channel_ref,
    z_ref,
    mixed_ref,
    x_ref,
    pre_ref,
    bcdt_ref,
    pre_bc_ref,
    state_ref,
    grad_ref,
    proj_ref,
    part_ref,
    sum_x_ref,
    sum_bc_ref,
    sum_head_ref,
    sum_gain_ref,
    x_buffer,
    bc_buffer,
    carry,
    tail,
):
    turn = pl.program_id(0)
    step = pl.num_programs(0) - 1 - turn
    width = heads * size

    @pl.when(turn == 0)
    def _():
        x_buffer[...] = jnp.zeros((Q + HALO, width), F32)
        bc_buffer[...] = jnp.zeros((Q + HALO, 2 * N), F32)
        carry[...] = jnp.zeros((N, width), F32)
        tail[...] = jnp.zeros((8, LANES), F32)
        sum_x_ref[...] = jnp.zeros((8, width), F32)
        sum_bc_ref[...] = jnp.zeros((8, 2 * N), F32)
        sum_head_ref[...] = jnp.zeros((8, LANES), F32)
        sum_gain_ref[...] = jnp.zeros(sum_gain_ref.shape, F32)

    window = window_ref[pl.ds(pl.multiple_of(step * Q, Q), Q + 2 * HALO), :]
    seg, from_prev, same_last, passes, bias = block_masks(window, seg_row_ref[0:1, :])
    stat = stat_ref[...].T
    gate_inverse = lax.rsqrt(stat[:, 0:1] / full_inner + EPS)
    along = stat[:, 1:2] * (gate_inverse * gate_inverse * gate_inverse / full_inner)

    gain = channel_ref[0:1, :]
    skip = channel_ref[1:2, :]
    z_proj = z_ref[...]
    mixed = mixed_ref[...]
    grad_out = grad_ref[...]
    gate = sigmoid(z_proj)
    opened = z_proj * gate
    gated = mixed * opened
    normal = gated * gate_inverse
    sum_gate = jnp.sum(grad_out * normal, axis=0, keepdims=True)
    grad_gated = grad_out * gain * gate_inverse - gated * along
    grad_z = grad_gated * mixed * (gate * (1.0 + z_proj * (1.0 - gate)))
    dy = grad_gated * opened

    pre = pre_ref[...]
    gate_x = sigmoid(pre)
    x_conv = pre * gate_x
    pre_bc = pre_bc_ref[...]
    gate_bc = sigmoid(pre_bc)
    bc_conv = (pre_bc * gate_bc).astype(BF16)
    b_in = bc_conv[:, :N]
    c_in = bc_conv[:, N:]
    bcdt = bcdt_ref[...]
    raw = bcdt[:, 2 * N :] + head_ref[0:1, :]
    dt = softplus(raw)
    rate = jnp.exp(head_ref[1:2, :])
    decay = -dt * rate
    total = dot_exact(triangle(True).astype(F32), decay)
    total_t = total.T
    dt_wide = spread(dt, heads, size)
    weighted = x_conv * dt_wide
    scores = dot_nt(c_in, b_in)
    before = state_ref[0]
    before_low = before.astype(BF16)
    last = total[Q - 1 : Q, :]
    to_end = spread(jnp.exp(last - total) * same_last, heads, size)
    from_start = spread(jnp.exp(total) * from_prev, heads, size)
    after = carry[...]
    after_low = after.astype(BF16)

    dy_low = dy.astype(BF16)
    weighted_low = weighted.astype(BF16)
    dy_start = (dy * from_start).astype(BF16)
    grad_c = dot_nt(dy_start, before_low)
    carried = dot(c_in, before_low)
    returned = dot(b_in, after_low)
    grad_weighted = to_end * returned
    weighted_end = (weighted * to_end).astype(BF16)
    grad_b = dot_nt(weighted_end, after_low)
    new_after = dot_tn(c_in, dy_start) + after * spread(jnp.exp(last) * passes, heads, size)
    carry[...] = new_after

    per = LANES // size
    lane = lax.broadcasted_iota(jnp.int32, (Q, LANES), 1)
    grad_scores = jnp.zeros((Q, Q), F32)
    inner = []
    none = jnp.zeros((Q, LANES), BF16)
    for first in range(0, heads, per):
        at = first * size
        dy_group = dy_low[:, at : at + LANES]
        weighted_group = weighted_low[:, at : at + LANES]
        summed = jnp.zeros((Q, LANES), F32)
        for extra in range(per):
            h = first + extra
            shape = jnp.exp(total[:, h : h + 1] - total_t[h : h + 1, :] + bias)
            mine = (lane >= extra * size) & (lane < (extra + 1) * size)
            dy_mine = jnp.where(mine, dy_group, none)
            grad_scores = grad_scores + dot_nt(dy_mine, weighted_group) * shape
            summed = summed + dot_tn((scores * shape).astype(BF16), dy_mine)
        inner.append(summed)
    grad_inner = jnp.concatenate(inner, axis=1)
    grad_weighted = grad_weighted + grad_inner
    grad_scores = grad_scores.astype(BF16)
    grad_c = grad_c + dot(grad_scores, b_in)
    grad_b = grad_b + dot_tn(grad_scores, c_in)

    scanned = mixed - skip * x_conv - carried * from_start
    pairs = head_sums(
        dy_low.astype(F32) * scanned
        + dy_start.astype(F32) * carried
        - weighted_low.astype(F32) * grad_inner
        - weighted_end.astype(F32) * returned,
        heads,
        size,
    )
    grad_decay = dot_exact(triangle(False).astype(F32), pairs) + tail[0:1, :]
    kept = jnp.sum(new_after.astype(BF16).astype(F32) * before, axis=0, keepdims=True)
    kept = jnp.broadcast_to(kept, (8, width))
    tail[...] = head_sums(kept, heads, size)
    grad_dt = head_sums(grad_weighted * x_conv, heads, size) - grad_decay * rate
    grad_raw = grad_dt * sigmoid(raw)
    sum_head_ref[0:1, :] += jnp.sum(grad_raw, axis=0, keepdims=True)
    sum_head_ref[1:2, :] += jnp.sum(grad_decay * decay, axis=0, keepdims=True)

    grad_x = grad_weighted * dt_wide + skip * dy
    sum_skip = jnp.sum(dy * x_conv, axis=0, keepdims=True)
    grad_pre = grad_x * (gate_x * (1.0 + pre * (1.0 - gate_x)))
    x_buffer[Q : Q + HALO, :] = x_buffer[0:HALO, :]
    x_buffer[0:Q, :] = grad_pre
    grad_proj, taps = conv_backward(
        x_buffer, window, seg, kernel_x_ref[...], x_ref[...], width
    )
    sum_bias = jnp.sum(grad_pre, axis=0, keepdims=True)
    blank = jnp.zeros((1, width), F32)
    sum_x_ref[...] += jnp.concatenate(
        [taps[3], taps[2], taps[1], taps[0], sum_bias, sum_gate, sum_skip, blank], axis=0
    )

    grad_pre_bc = jnp.concatenate([grad_b, grad_c], axis=1) * (
        gate_bc * (1.0 + pre_bc * (1.0 - gate_bc))
    )
    bc_buffer[Q : Q + HALO, :] = bc_buffer[0:HALO, :]
    bc_buffer[0:Q, :] = grad_pre_bc
    grad_bc, taps_bc = conv_backward(
        bc_buffer, window, seg, kernel_bc_ref[...], bcdt[:, : 2 * N], 2 * N
    )
    sum_bias_bc = jnp.sum(grad_pre_bc, axis=0, keepdims=True)
    blank_bc = jnp.zeros((3, 2 * N), F32)
    sum_bc_ref[...] += jnp.concatenate(
        [taps_bc[3], taps_bc[2], taps_bc[1], taps_bc[0], sum_bias_bc, blank_bc], axis=0
    )

    grads = jnp.concatenate(
        [
            grad_proj.astype(BF16),
            grad_z.astype(BF16),
            grad_bc.astype(BF16),
            grad_raw.astype(BF16),
        ],
        axis=1,
    )
    proj_ref[...] = grads
    part = dot_nt(grads, weights_ref[:, width:])
    part_ref[...] = part.astype(BF16)
    hidden = hidden_ref[...].astype(F32)
    inverse = lax.rsqrt(jnp.mean(hidden * hidden, axis=1, keepdims=True) + EPS)
    sum_gain_ref[0:1, :] += jnp.sum(part * (hidden * inverse), axis=0, keepdims=True)


def whole(shape):
    return pl.BlockSpec(shape, lambda i: (0,) * len(shape))


def scalar():
    return pl.BlockSpec(memory_space=pltpu.SMEM)


def run_forward(heads, size, place, near, window, seg_row, weights, kernel_x, kernel_bc, head, channel):
    length, features = seg_row.shape[1], near[0].shape[1]
    width = heads * size
    blocks = length // Q
    rest = 2 * N + LANES

    def rows(columns):
        return pl.BlockSpec((Q, columns), lambda i: (i, 0))

    def made(columns, dtype):
        return jax.ShapeDtypeStruct((length, columns), dtype)

    return pl.pallas_call(
        functools.partial(forward_kernel, heads, size, len(near)),
        grid=(blocks,),
        in_specs=[
            scalar(),
            *[whole(block.shape) for block in near],
            whole(window.shape),
            pl.BlockSpec((8, Q), lambda i: (0, i)),
            whole(weights.shape),
            whole(kernel_x.shape),
            whole(kernel_bc.shape),
            whole(head.shape),
            whole(channel.shape),
        ],
        out_specs=[
            rows(features),
            rows(features),
            rows(width),
            rows(width),
            rows(width),
            rows(width),
            rows(rest),
            rows(2 * N),
            pl.BlockSpec((1, N, width), lambda i: (i, 0, 0)),
            rows(width),
            rows(features),
            pl.BlockSpec((8, Q), lambda i: (0, i)),
            whole((8, features)),
        ],
        out_shape=[
            made(features, BF16),
            made(features, BF16),
            made(width, F32),
            made(width, F32),
            made(width, F32),
            made(width, F32),
            made(rest, F32),
            made(2 * N, F32),
            jax.ShapeDtypeStruct((blocks, N, width), F32),
            made(width, BF16),
            made(features, BF16),
            jax.ShapeDtypeStruct((8, length), F32),
            jax.ShapeDtypeStruct((8, features), F32),
        ],
        scratch_shapes=[
            pltpu.VMEM((Q + HALO, width), F32),
            pltpu.VMEM((Q + HALO, 2 * N), F32),
            pltpu.VMEM((N, width), F32),
        ],
        compiler_params=pltpu.CompilerParams(vmem_limit_bytes=VMEM_LIMIT),
        name="forward",
    )(place, *near, window, seg_row, weights, kernel_x, kernel_bc, head, channel)


def run_gradient(place, near, weights, scaled, window):
    features = near[0].shape[1]
    length, width = scaled.shape
    return pl.pallas_call(
        functools.partial(gradient_kernel, width, len(near)),
        grid=(length // Q,),
        in_specs=[
            scalar(),
            *[whole(block.shape) for block in near],
            pl.BlockSpec((features, width), lambda i: (0, 0)),
            pl.BlockSpec((Q, width), lambda i: (i, 0)),
            whole(window.shape),
        ],
        out_specs=[
            pl.BlockSpec((Q, features), lambda i: (i, 0)),
            pl.BlockSpec((Q, width), lambda i: (i, 0)),
            pl.BlockSpec((8, Q), lambda i: (0, i)),
        ],
        out_shape=[
            jax.ShapeDtypeStruct((length, features), BF16),
            jax.ShapeDtypeStruct((length, width), F32),
            jax.ShapeDtypeStruct((8, length), F32),
        ],
        compiler_params=pltpu.CompilerParams(vmem_limit_bytes=VMEM_LIMIT),
        name="out_gradient",
    )(place, *near, weights, scaled, window)


def run_backward(
    heads, size, full_inner, stat, hidden, window, seg_row, weights, kernel_x, kernel_bc, head, channel,
    z_proj, mixed, x_proj, pre, bcdt, pre_bc, states, grad_out,
):
    length, features = hidden.shape
    width = heads * size
    blocks = length // Q
    rest = 2 * N + LANES
    total = 2 * width + rest

    def rows(columns):
        return pl.BlockSpec((Q, columns), lambda i: (blocks - 1 - i, 0))

    def made(columns, dtype):
        return jax.ShapeDtypeStruct((length, columns), dtype)

    across = pl.BlockSpec((8, Q), lambda i: (0, blocks - 1 - i))
    sums = [(8, width), (8, 2 * N), (8, LANES), (8, features)]
    return pl.pallas_call(
        functools.partial(backward_kernel, heads, size, full_inner),
        grid=(blocks,),
        in_specs=[
            across,
            rows(features),
            whole(window.shape),
            across,
            whole(weights.shape),
            whole(kernel_x.shape),
            whole(kernel_bc.shape),
            whole(head.shape),
            whole(channel.shape),
            rows(width),
            rows(width),
            rows(width),
            rows(width),
            rows(rest),
            rows(2 * N),
            pl.BlockSpec((1, N, width), lambda i: (blocks - 1 - i, 0, 0)),
            rows(width),
        ],
        out_specs=[rows(total), rows(features)] + [whole(shape) for shape in sums],
        out_shape=[made(total, BF16), made(features, BF16)]
        + [jax.ShapeDtypeStruct(shape, F32) for shape in sums],
        scratch_shapes=[
            pltpu.VMEM((Q + HALO, width), F32),
            pltpu.VMEM((Q + HALO, 2 * N), F32),
            pltpu.VMEM((N, width), F32),
            pltpu.VMEM((8, LANES), F32),
        ],
        compiler_params=pltpu.CompilerParams(vmem_limit_bytes=VMEM_LIMIT),
        name="backward",
    )(
        stat, hidden, window, seg_row, weights, kernel_x, kernel_bc, head, channel,
        z_proj, mixed, x_proj, pre, bcdt, pre_bc, states, grad_out,
    )


def pad_lanes(values):
    return jnp.pad(values, ((0, 0), (0, LANES - values.shape[1])))


def line_gather(block, axis):
    n = lax.axis_size(axis)
    from_left, from_right = [], []
    right = left = block
    for step in range(1, n):
        right = lax.ppermute(right, axis, [(i, i + 1) for i in range(step - 1, n - 1)])
        left = lax.ppermute(left, axis, [(i, i - 1) for i in range(1, n - step + 1)])
        from_left.append(right)
        from_right.append(left)
    return from_left[::-1] + [block] + from_right


def line_scatter(part, axis):
    n = lax.axis_size(axis)
    place = lax.axis_index(axis)
    count = part.shape[0] // n

    def block(index):
        start = jnp.clip(index, 0, n - 1) * count
        return lax.dynamic_slice_in_dim(part, start, count, 0)

    right = left = None
    for step in range(1, n):
        send_right = block(n - step + place)
        send_left = block(step + place - n)
        if step > 1:
            send_right = (send_right.astype(F32) + right.astype(F32)).astype(part.dtype)
            send_left = (send_left.astype(F32) + left.astype(F32)).astype(part.dtype)
        right = lax.ppermute(send_right, axis, [(i, i + 1) for i in range(step)])
        left = lax.ppermute(send_left, axis, [(n - 1 - i, n - 2 - i) for i in range(step)])
    return block(place).astype(F32) + right.astype(F32) + left.astype(F32)


def around(values, axis):
    n = lax.axis_size(axis)
    return [values] + [
        lax.ppermute(values, axis, [(i, (i - k) % n) for i in range(n)]) for k in range(1, n)
    ]


def sum_around(values, axis):
    return functools.reduce(jnp.add, around(values, axis))


def sum_pairwise(values, axis):
    n = lax.axis_size(axis)
    if n & (n - 1):
        return lax.psum(values, axis)
    bit = 1
    while bit < n:
        values = values + lax.ppermute(values, axis, [(i, i ^ bit) for i in range(n)])
        bit *= 2
    return values


def shards(
    hidden,
    seg_ids,
    cotangent,
    norm_gain,
    w_in_z,
    w_in_x,
    w_in_bc,
    w_in_dt,
    conv_x,
    conv_x_bias,
    conv_bc,
    conv_bc_bias,
    dt_bias,
    a_log,
    d_skip,
    gate_gain,
    w_out,
):
    heads = dt_bias.shape[0]
    width = gate_gain.shape[0]
    size = width // heads
    full_inner = width * lax.axis_size("tensor")
    features = hidden.shape[2]
    hidden_local = hidden[0]

    steps = jnp.pad(
        jnp.concatenate([w_in_dt, norm_gain[:, None]], axis=1), ((0, 0), (0, LANES - heads - 1))
    )
    packed = jnp.concatenate([w_out, w_in_x, w_in_z, w_in_bc, steps], axis=1)
    n = lax.axis_size("tensor")
    axis_place = lax.axis_index("tensor")
    place = axis_place[None]
    near_hidden = line_gather(hidden_local, "tensor")
    weights = lax.all_gather(packed, "dp", axis=0, tiled=True)
    seg_stack = around(seg_ids[0], "tensor")
    count = seg_ids.shape[1]
    seg_full = lax.dynamic_slice_in_dim(
        jnp.concatenate(seg_stack + seg_stack), (n - axis_place) * count, n * count, 0
    )
    cot_local, _, _ = lax.optimization_barrier((cotangent[0], near_hidden[0], near_hidden[-1]))
    near_cot = line_gather(cot_local, "tensor")

    window = jnp.broadcast_to(
        jnp.pad(seg_full, (HALO, HALO), constant_values=-1)[:, None],
        (seg_full.shape[0] + 2 * HALO, LANES),
    )
    seg_row = jnp.broadcast_to(seg_full[None, :], (8, seg_full.shape[0]))
    kernel_x = jnp.concatenate([conv_x, conv_x_bias[None, :]], axis=0)
    kernel_bc = jnp.concatenate([conv_bc, conv_bc_bias[None, :]], axis=0)
    head = pad_lanes(jnp.stack([dt_bias, a_log]))
    channel = jnp.stack([gate_gain, jnp.repeat(d_skip, size)])

    (
        hidden_full, tokens, z_proj, mixed, x_proj, pre, bcdt, pre_bc, states, scaled, out_part,
        square, gain,
    ) = run_forward(
        heads, size, place, near_hidden, window, seg_row, weights, kernel_x, kernel_bc, head, channel
    )
    out_sum = line_scatter(out_part, "tensor")
    cot_full, grad_out, along = run_gradient(place, near_cot, weights, scaled, window)
    stat = sum_around(jnp.stack([square[0], along[0]]), "tensor")
    stat_full = jnp.pad(stat, ((0, 6), (0, 0)))
    out_scale = lax.rsqrt(stat[0] / full_inner + EPS) * (seg_full > 0).astype(F32)
    normed_out = (scaled.astype(F32) * out_scale[:, None]).astype(BF16)
    grad_w_out = lax.psum_scatter(
        dot_tn(cot_full, normed_out).astype(BF16), "dp", scatter_dimension=0, tiled=True
    )

    grads, in_part, sum_x, sum_bc, sum_head, sum_gain = run_backward(
        heads, size, full_inner, stat_full, hidden_full, window, seg_row, weights, kernel_x,
        kernel_bc, head, channel, z_proj, mixed, x_proj, pre, bcdt, pre_bc, states, grad_out,
    )
    in_sum = line_scatter(in_part, "tensor")

    sum_weights = lax.psum_scatter(
        dot_tn(tokens, grads).astype(BF16), "dp", scatter_dimension=0, tiled=True
    )
    sum_bc_weights = sum_weights[:, 2 * width : 2 * width + 2 * N]
    grad_bc = sum(part.astype(F32) for part in around(sum_bc_weights, "tensor"))
    own = jnp.concatenate([sum_x.reshape(-1, LANES), sum_head])
    both = jnp.concatenate([sum_gain[0].reshape(-1, LANES), sum_bc.reshape(-1, LANES)])
    both = sum_around(both, "tensor")
    small = sum_pairwise(jnp.concatenate([own, both]), "dp")
    cuts = [sum_x.size // LANES, 8, features // LANES]
    sum_x = small[: cuts[0]].reshape(8, width)
    sum_head = small[cuts[0] : cuts[0] + 8]
    sum_gain = small[cuts[0] + 8 : cuts[0] + 8 + cuts[2]].reshape(features)
    sum_bc = small[cuts[0] + 8 + cuts[2] :].reshape(8, 2 * N)
    local_features = norm_gain.shape[0]
    grad_norm_gain = lax.dynamic_slice_in_dim(
        sum_gain, lax.axis_index("dp") * local_features, local_features, 0
    )

    local = hidden_local.shape[0]
    hidden_rows = hidden_local.astype(F32)
    scale_here = lax.dynamic_slice_in_dim(out_scale, axis_place * local, local, 0)[:, None]
    layer_out = (hidden_rows + out_sum * scale_here).astype(BF16)

    inverse = lax.rsqrt(jnp.mean(hidden_rows * hidden_rows, axis=1, keepdims=True) + EPS)
    unit = hidden_rows * inverse
    grad_scaled = in_sum * gain[0:1]
    grad_hidden = (
        cotangent[0].astype(F32)
        + inverse * (grad_scaled - unit * jnp.mean(grad_scaled * unit, axis=1, keepdims=True))
    ).astype(BF16)

    sum_weights = sum_weights.astype(F32)
    return (
        layer_out[None],
        grad_hidden[None],
        grad_norm_gain,
        sum_weights[:, width : 2 * width],
        sum_weights[:, :width],
        grad_bc,
        sum_weights[:, 2 * width + 2 * N : 2 * width + 2 * N + heads],
        sum_x[0:CONV],
        sum_x[CONV],
        sum_bc[0:CONV],
        sum_bc[CONV],
        sum_head[0, :heads],
        sum_head[1, :heads],
        jnp.sum(sum_x[CONV + 2].reshape(heads, size), axis=1),
        sum_x[CONV + 1],
        grad_w_out.astype(F32),
    )


def solution(mesh):
    in_specs = (
        P("dp", "tensor", None),
        P("dp", "tensor"),
        P("dp", "tensor", None),
        P("dp"),
        P("dp", "tensor"),
        P("dp", "tensor"),
        P("dp", None),
        P("dp", "tensor"),
        P(None, "tensor"),
        P("tensor"),
        P(),
        P(),
        P("tensor"),
        P("tensor"),
        P("tensor"),
        P("tensor"),
        P("dp", "tensor"),
    )
    out_specs = (
        P("dp", "tensor", None),
        P("dp", "tensor", None),
        P("dp"),
        P("dp", "tensor"),
        P("dp", "tensor"),
        P("dp", None),
        P("dp", "tensor"),
        P(None, "tensor"),
        P("tensor"),
        P(),
        P(),
        P("tensor"),
        P("tensor"),
        P("tensor"),
        P("tensor"),
        P("dp", "tensor"),
    )
    return jax.shard_map(shards, mesh=mesh, in_specs=in_specs, out_specs=out_specs, check_vma=False)
```

```python
import functools

import jax
import jax.numpy as jnp
from jax import lax
from jax.experimental import pallas as pl
from jax.experimental.pallas import tpu as pltpu
from jax.sharding import PartitionSpec as P

N = 128
CONV = 4
Q = 256
LANES = 128
HALO = 8
EPS = 1e-05
NEG = -1e30
F32 = jnp.float32
BF16 = jnp.bfloat16
VMEM_LIMIT = 52 * 1024 * 1024


def dot(a, b):
    return jnp.dot(a, b, preferred_element_type=F32)


def dot_nt(a, b):
    return lax.dot_general(a, b, (((1,), (1,)), ((), ())), preferred_element_type=F32)


def dot_tn(a, b):
    return lax.dot_general(a, b, (((0,), (0,)), ((), ())), preferred_element_type=F32)


def dot_exact(a, b):
    return jnp.dot(a, b, preferred_element_type=F32, precision=lax.Precision.HIGHEST)


def spread(cols, heads, size):
    rows = cols.shape[0]
    per = LANES // size
    lane = lax.broadcasted_iota(jnp.int32, (rows, LANES), 1)
    parts = []
    for first in range(0, heads, per):
        part = jnp.broadcast_to(cols[:, first : first + 1], (rows, LANES))
        for extra in range(1, per):
            part = jnp.where(lane < extra * size, part, cols[:, first + extra : first + extra + 1])
        parts.append(part)
    return jnp.concatenate(parts, axis=1)


def head_sums(values, heads, size):
    width = heads * size
    channel = lax.broadcasted_iota(jnp.int32, (width, LANES), 0)
    column = lax.broadcasted_iota(jnp.int32, (width, LANES), 1)
    first = column * size
    picks = jnp.where((channel >= first) & (channel < first + size), 1.0, 0.0).astype(BF16)
    high = values.astype(BF16)
    low = (values - high.astype(F32)).astype(BF16)
    return dot(high, picks) + dot(low, picks)


def widen(tile, width):
    return jnp.concatenate([tile] * (width // tile.shape[1]), axis=1)


def softplus(v):
    return jnp.maximum(v, 0.0) + jnp.log1p(jnp.exp(-jnp.abs(v)))


def sigmoid(v):
    return 1.0 / (1.0 + jnp.exp(-v))


def as_row(column):
    rows = column.shape[0]
    return jnp.broadcast_to(column, (rows, LANES)).T[:8]


def triangle(lower):
    row = lax.broadcasted_iota(jnp.int32, (Q, Q), 0)
    col = lax.broadcasted_iota(jnp.int32, (Q, Q), 1)
    return row >= col if lower else row <= col


def block_masks(window, seg_row):
    seg = window[HALO : HALO + Q]
    before = window[HALO - 1 : HALO]
    last = window[HALO + Q - 1 : HALO + Q]
    from_prev = (seg == before).astype(F32)
    same_last = (seg == last).astype(F32)
    passes = (last == before).astype(F32)
    keep = (widen(seg, Q) == seg_row) & triangle(True)
    bias = jnp.where(keep, 0.0, NEG)
    return seg, from_prev, same_last, passes, bias


def conv_forward(buffer, window, seg, kernel, conv_bias, width):
    total = conv_bias + kernel[CONV - 1 : CONV] * buffer[HALO : HALO + Q, :]
    for back in range(1, CONV):
        match = (window[HALO - back : HALO - back + Q] == seg).astype(F32)
        tap = kernel[CONV - 1 - back : CONV - back]
        total = total + tap * (buffer[HALO - back : HALO - back + Q, :] * widen(match, width))
    return total


def conv_backward(buffer, window, seg, kernel, values, width):
    here = buffer[0:Q, :]
    total = kernel[CONV - 1 : CONV] * here
    taps = [jnp.sum(values * here, axis=0, keepdims=True)]
    for ahead in range(1, CONV):
        match = (window[HALO + ahead : HALO + ahead + Q] == seg).astype(F32)
        moved = buffer[ahead : ahead + Q, :] * widen(match, width)
        total = total + kernel[CONV - 1 - ahead : CONV - ahead] * moved
        taps.append(jnp.sum(values * moved, axis=0, keepdims=True))
    return total, taps


def pick_block(place, near_refs, block):
    reach = len(near_refs) // 2
    away = pl.program_id(0) - place
    for index, ref in enumerate(near_refs):

        @pl.when(away == index - reach)
        def _():
            block[...] = ref[...]


def forward_kernel(
    heads,
    size,
    near,
    place_ref,
    *refs,
):
    near_refs, refs = refs[:near], refs[near:]
    forward_body(heads, size, place_ref[0], near_refs, *refs)


def forward_body(
    heads,
    size,
    place,
    near_refs,
    window_ref,
    seg_row_ref,
    weights_ref,
    kernel_x_ref,
    kernel_bc_ref,
    head_ref,
    channel_ref,
    hidden_ref,
    tokens_ref,
    z_ref,
    mixed_ref,
    x_ref,
    pre_ref,
    bcdt_ref,
    pre_bc_ref,
    state_ref,
    scaled_ref,
    part_ref,
    square_ref,
    gain_ref,
    x_buffer,
    bc_buffer,
    carry,
):
    step = pl.program_id(0)
    width = heads * size
    rest = 2 * N + LANES

    @pl.when(step == 0)
    def _():
        x_buffer[0:HALO, :] = jnp.zeros((HALO, width), F32)
        bc_buffer[0:HALO, :] = jnp.zeros((HALO, 2 * N), F32)
        carry[...] = jnp.zeros((N, width), F32)
        tail_columns = weights_ref[:, 3 * width + 2 * N :].astype(F32).T
        gain_ref[...] = jnp.broadcast_to(tail_columns[heads : heads + 1], gain_ref.shape)

    pick_block(place, near_refs, hidden_ref)
    window = window_ref[pl.ds(pl.multiple_of(step * Q, Q), Q + 2 * HALO), :]
    seg, from_prev, same_last, passes, bias = block_masks(window, seg_row_ref[0:1, :])

    hidden = hidden_ref[...].astype(F32)
    inverse = lax.rsqrt(jnp.mean(hidden * hidden, axis=1, keepdims=True) + EPS)
    tokens = (hidden * inverse * gain_ref[0:1, :]).astype(BF16)
    tokens_ref[...] = tokens
    x_proj = dot(tokens, weights_ref[:, width : 2 * width])
    z_proj = dot(tokens, weights_ref[:, 2 * width : 3 * width])
    bcdt = dot(tokens, weights_ref[:, 3 * width : 3 * width + rest])
    z_ref[...] = z_proj
    x_ref[...] = x_proj
    bcdt_ref[...] = bcdt

    x_buffer[HALO : HALO + Q, :] = x_proj
    bc_buffer[HALO : HALO + Q, :] = bcdt[:, : 2 * N]
    pre = conv_forward(
        x_buffer, window, seg, kernel_x_ref[...], kernel_x_ref[CONV : CONV + 1, :], width
    )
    pre_bc = conv_forward(
        bc_buffer, window, seg, kernel_bc_ref[...], kernel_bc_ref[CONV : CONV + 1, :], 2 * N
    )
    x_buffer[0:HALO, :] = x_buffer[Q : Q + HALO, :]
    bc_buffer[0:HALO, :] = bc_buffer[Q : Q + HALO, :]
    pre_ref[...] = pre
    pre_bc_ref[...] = pre_bc
    x_conv = pre * sigmoid(pre)
    bc_conv = (pre_bc * sigmoid(pre_bc)).astype(BF16)
    b_in = bc_conv[:, :N]
    c_in = bc_conv[:, N:]

    dt = softplus(bcdt[:, 2 * N :] + head_ref[0:1, :])
    decay = -dt * jnp.exp(head_ref[1:2, :])
    total = dot_exact(triangle(True).astype(F32), decay)
    total_t = total.T
    weighted = x_conv * spread(dt, heads, size)
    scores = dot_nt(c_in, b_in)
    before = carry[...]
    state_ref[0] = before

    per = LANES // size
    lane = lax.broadcasted_iota(jnp.int32, (Q, LANES), 1)
    inner = []
    for first in range(0, heads, per):
        group = weighted[:, first * size : first * size + LANES]
        summed = jnp.zeros((Q, LANES), F32)
        for extra in range(per):
            h = first + extra
            shape = jnp.exp(total[:, h : h + 1] - total_t[h : h + 1, :] + bias)
            mine = (lane >= extra * size) & (lane < (extra + 1) * size)
            summed = summed + dot(
                (scores * shape).astype(BF16), jnp.where(mine, group, 0.0).astype(BF16)
            )
        inner.append(summed)
    scanned = jnp.concatenate(inner, axis=1)
    scanned = scanned + dot(c_in, before.astype(BF16)) * spread(
        jnp.exp(total) * from_prev, heads, size
    )
    last = total[Q - 1 : Q, :]
    to_end = jnp.exp(last - total) * same_last
    carry[...] = dot_tn(
        b_in, (weighted * spread(to_end, heads, size)).astype(BF16)
    ) + before * spread(jnp.exp(last) * passes, heads, size)

    mixed = scanned + channel_ref[1:2, :] * x_conv
    mixed_ref[...] = mixed
    gated = mixed * (z_proj * sigmoid(z_proj))
    scaled = (gated * channel_ref[0:1, :]).astype(BF16)
    scaled_ref[...] = scaled
    part_ref[...] = dot_nt(scaled, weights_ref[:, :width]).astype(BF16)
    square_ref[...] = as_row(jnp.sum(gated * gated, axis=1, keepdims=True))


def gradient_kernel(width, cot_ref, weights_ref, scaled_ref, window_ref, grad_ref, along_ref):
    step = pl.program_id(0)
    window = window_ref[pl.ds(pl.multiple_of(step * Q, Q), Q + 2 * HALO), :]
    live = (window[HALO : HALO + Q] > 0).astype(F32)
    grad = dot(cot_ref[...], weights_ref[...]) * widen(live, width)
    grad_ref[...] = grad
    along_ref[...] = as_row(jnp.sum(scaled_ref[...].astype(F32) * grad, axis=1, keepdims=True))


def backward_kernel(
    heads,
    size,
    full_inner,
    stat_ref,
    hidden_ref,
    window_ref,
    seg_row_ref,
    weights_ref,
    kernel_x_ref,
    kernel_bc_ref,
    head_ref,
    channel_ref,
    z_ref,
    mixed_ref,
    x_ref,
    pre_ref,
    bcdt_ref,
    pre_bc_ref,
    state_ref,
    grad_ref,
    proj_ref,
    part_ref,
    out_ref,
    sum_x_ref,
    sum_bc_ref,
    sum_head_ref,
    sum_gain_ref,
    x_buffer,
    bc_buffer,
    carry,
    tail,
):
    turn = pl.program_id(0)
    step = pl.num_programs(0) - 1 - turn
    width = heads * size

    @pl.when(turn == 0)
    def _():
        x_buffer[...] = jnp.zeros((Q + HALO, width), F32)
        bc_buffer[...] = jnp.zeros((Q + HALO, 2 * N), F32)
        carry[...] = jnp.zeros((N, width), F32)
        tail[...] = jnp.zeros((8, LANES), F32)
        sum_x_ref[...] = jnp.zeros((8, width), F32)
        sum_bc_ref[...] = jnp.zeros((8, 2 * N), F32)
        sum_head_ref[...] = jnp.zeros((8, LANES), F32)
        sum_gain_ref[...] = jnp.zeros(sum_gain_ref.shape, F32)

    window = window_ref[pl.ds(pl.multiple_of(step * Q, Q), Q + 2 * HALO), :]
    seg, from_prev, same_last, passes, bias = block_masks(window, seg_row_ref[0:1, :])
    live = (seg[:, 0:1] > 0).astype(F32)
    stat = stat_ref[...].T
    gate_inverse = lax.rsqrt(stat[:, 0:1] / full_inner + EPS)
    along = stat[:, 1:2] * (gate_inverse * gate_inverse * gate_inverse / full_inner)

    gain = channel_ref[0:1, :]
    skip = channel_ref[1:2, :]
    z_proj = z_ref[...]
    mixed = mixed_ref[...]
    grad_out = grad_ref[...]
    gate = sigmoid(z_proj)
    opened = z_proj * gate
    gated = mixed * opened
    normal = gated * gate_inverse
    sum_gate = jnp.sum(grad_out * normal, axis=0, keepdims=True)
    out_ref[...] = (normal * gain * live).astype(BF16)
    grad_gated = grad_out * gain * gate_inverse - gated * along
    grad_z = grad_gated * mixed * (gate * (1.0 + z_proj * (1.0 - gate)))
    dy = grad_gated * opened

    pre = pre_ref[...]
    gate_x = sigmoid(pre)
    x_conv = pre * gate_x
    pre_bc = pre_bc_ref[...]
    gate_bc = sigmoid(pre_bc)
    bc_conv = (pre_bc * gate_bc).astype(BF16)
    b_in = bc_conv[:, :N]
    c_in = bc_conv[:, N:]
    bcdt = bcdt_ref[...]
    raw = bcdt[:, 2 * N :] + head_ref[0:1, :]
    dt = softplus(raw)
    rate = jnp.exp(head_ref[1:2, :])
    decay = -dt * rate
    total = dot_exact(triangle(True).astype(F32), decay)
    total_t = total.T
    dt_wide = spread(dt, heads, size)
    weighted = x_conv * dt_wide
    scores = dot_nt(c_in, b_in)
    before = state_ref[0]
    before_low = before.astype(BF16)
    last = total[Q - 1 : Q, :]
    to_end = spread(jnp.exp(last - total) * same_last, heads, size)
    from_start = spread(jnp.exp(total) * from_prev, heads, size)
    after = carry[...]
    after_low = after.astype(BF16)

    dy_low = dy.astype(BF16)
    weighted_low = weighted.astype(BF16)
    dy_start = (dy * from_start).astype(BF16)
    grad_c = dot_nt(dy_start, before_low)
    carried = dot(c_in, before_low)
    returned = dot(b_in, after_low)
    grad_weighted = to_end * returned
    weighted_end = (weighted * to_end).astype(BF16)
    grad_b = dot_nt(weighted_end, after_low)
    new_after = dot_tn(c_in, dy_start) + after * spread(jnp.exp(last) * passes, heads, size)
    carry[...] = new_after

    per = LANES // size
    lane = lax.broadcasted_iota(jnp.int32, (Q, LANES), 1)
    grad_scores = jnp.zeros((Q, Q), F32)
    inner = []
    none = jnp.zeros((Q, LANES), BF16)
    for first in range(0, heads, per):
        at = first * size
        dy_group = dy_low[:, at : at + LANES]
        weighted_group = weighted_low[:, at : at + LANES]
        summed = jnp.zeros((Q, LANES), F32)
        for extra in range(per):
            h = first + extra
            shape = jnp.exp(total[:, h : h + 1] - total_t[h : h + 1, :] + bias)
            mine = (lane >= extra * size) & (lane < (extra + 1) * size)
            dy_mine = jnp.where(mine, dy_group, none)
            grad_scores = grad_scores + dot_nt(dy_mine, weighted_group) * shape
            summed = summed + dot_tn((scores * shape).astype(BF16), dy_mine)
        inner.append(summed)
    grad_inner = jnp.concatenate(inner, axis=1)
    grad_weighted = grad_weighted + grad_inner
    grad_scores = grad_scores.astype(BF16)
    grad_c = grad_c + dot(grad_scores, b_in)
    grad_b = grad_b + dot_tn(grad_scores, c_in)

    scanned = mixed - skip * x_conv - carried * from_start
    pairs = head_sums(
        dy_low.astype(F32) * scanned
        + dy_start.astype(F32) * carried
        - weighted_low.astype(F32) * grad_inner
        - weighted_end.astype(F32) * returned,
        heads,
        size,
    )
    grad_decay = dot_exact(triangle(False).astype(F32), pairs) + tail[0:1, :]
    kept = jnp.sum(new_after.astype(BF16).astype(F32) * before, axis=0, keepdims=True)
    kept = jnp.broadcast_to(kept, (8, width))
    tail[...] = head_sums(kept, heads, size)
    grad_dt = head_sums(grad_weighted * x_conv, heads, size) - grad_decay * rate
    grad_raw = grad_dt * sigmoid(raw)
    sum_head_ref[0:1, :] += jnp.sum(grad_raw, axis=0, keepdims=True)
    sum_head_ref[1:2, :] += jnp.sum(grad_decay * decay, axis=0, keepdims=True)

    grad_x = grad_weighted * dt_wide + skip * dy
    sum_skip = jnp.sum(dy * x_conv, axis=0, keepdims=True)
    grad_pre = grad_x * (gate_x * (1.0 + pre * (1.0 - gate_x)))
    x_buffer[Q : Q + HALO, :] = x_buffer[0:HALO, :]
    x_buffer[0:Q, :] = grad_pre
    grad_proj, taps = conv_backward(
        x_buffer, window, seg, kernel_x_ref[...], x_ref[...], width
    )
    sum_bias = jnp.sum(grad_pre, axis=0, keepdims=True)
    blank = jnp.zeros((1, width), F32)
    sum_x_ref[...] += jnp.concatenate(
        [taps[3], taps[2], taps[1], taps[0], sum_bias, sum_gate, sum_skip, blank], axis=0
    )

    grad_pre_bc = jnp.concatenate([grad_b, grad_c], axis=1) * (
        gate_bc * (1.0 + pre_bc * (1.0 - gate_bc))
    )
    bc_buffer[Q : Q + HALO, :] = bc_buffer[0:HALO, :]
    bc_buffer[0:Q, :] = grad_pre_bc
    grad_bc, taps_bc = conv_backward(
        bc_buffer, window, seg, kernel_bc_ref[...], bcdt[:, : 2 * N], 2 * N
    )
    sum_bias_bc = jnp.sum(grad_pre_bc, axis=0, keepdims=True)
    blank_bc = jnp.zeros((3, 2 * N), F32)
    sum_bc_ref[...] += jnp.concatenate(
        [taps_bc[3], taps_bc[2], taps_bc[1], taps_bc[0], sum_bias_bc, blank_bc], axis=0
    )

    grads = jnp.concatenate(
        [
            grad_proj.astype(BF16),
            grad_z.astype(BF16),
            grad_bc.astype(BF16),
            grad_raw.astype(BF16),
        ],
        axis=1,
    )
    proj_ref[...] = grads
    part = dot_nt(grads, weights_ref[:, width:])
    part_ref[...] = part.astype(BF16)
    hidden = hidden_ref[...].astype(F32)
    inverse = lax.rsqrt(jnp.mean(hidden * hidden, axis=1, keepdims=True) + EPS)
    sum_gain_ref[0:1, :] += jnp.sum(part * (hidden * inverse), axis=0, keepdims=True)


def cost(micros):
    return pl.CostEstimate(flops=int(micros * 1e9), bytes_accessed=1 << 20, transcendentals=0)


def whole(shape):
    return pl.BlockSpec(shape, lambda i: (0,) * len(shape))


def scalar():
    return pl.BlockSpec(memory_space=pltpu.SMEM)


def run_forward(heads, size, place, near, window, seg_row, weights, kernel_x, kernel_bc, head, channel):
    length, features = seg_row.shape[1], near[0].shape[1]
    width = heads * size
    blocks = length // Q
    rest = 2 * N + LANES

    def rows(columns):
        return pl.BlockSpec((Q, columns), lambda i: (i, 0))

    def made(columns, dtype):
        return jax.ShapeDtypeStruct((length, columns), dtype)

    return pl.pallas_call(
        functools.partial(forward_kernel, heads, size, len(near)),
        grid=(blocks,),
        in_specs=[
            scalar(),
            *[whole(block.shape) for block in near],
            whole(window.shape),
            pl.BlockSpec((8, Q), lambda i: (0, i)),
            whole(weights.shape),
            whole(kernel_x.shape),
            whole(kernel_bc.shape),
            whole(head.shape),
            whole(channel.shape),
        ],
        out_specs=[
            rows(features),
            rows(features),
            rows(width),
            rows(width),
            rows(width),
            rows(width),
            rows(rest),
            rows(2 * N),
            pl.BlockSpec((1, N, width), lambda i: (i, 0, 0)),
            rows(width),
            rows(features),
            pl.BlockSpec((8, Q), lambda i: (0, i)),
            whole((8, features)),
        ],
        out_shape=[
            made(features, BF16),
            made(features, BF16),
            made(width, F32),
            made(width, F32),
            made(width, F32),
            made(width, F32),
            made(rest, F32),
            made(2 * N, F32),
            jax.ShapeDtypeStruct((blocks, N, width), F32),
            made(width, BF16),
            made(features, BF16),
            jax.ShapeDtypeStruct((8, length), F32),
            jax.ShapeDtypeStruct((8, features), F32),
        ],
        scratch_shapes=[
            pltpu.VMEM((Q + HALO, width), F32),
            pltpu.VMEM((Q + HALO, 2 * N), F32),
            pltpu.VMEM((N, width), F32),
        ],
        compiler_params=pltpu.CompilerParams(vmem_limit_bytes=VMEM_LIMIT),
        cost_estimate=cost(20),
        name="forward",
    )(place, *near, window, seg_row, weights, kernel_x, kernel_bc, head, channel)


def run_gradient(cot, weights, scaled, window):
    length, features = cot.shape
    width = scaled.shape[1]
    return pl.pallas_call(
        functools.partial(gradient_kernel, width),
        grid=(length // Q,),
        in_specs=[
            pl.BlockSpec((Q, features), lambda i: (i, 0)),
            pl.BlockSpec((features, width), lambda i: (0, 0)),
            pl.BlockSpec((Q, width), lambda i: (i, 0)),
            whole(window.shape),
        ],
        out_specs=[
            pl.BlockSpec((Q, width), lambda i: (i, 0)),
            pl.BlockSpec((8, Q), lambda i: (0, i)),
        ],
        out_shape=[
            jax.ShapeDtypeStruct((length, width), F32),
            jax.ShapeDtypeStruct((8, length), F32),
        ],
        compiler_params=pltpu.CompilerParams(vmem_limit_bytes=VMEM_LIMIT),
        cost_estimate=cost(5),
        name="out_gradient",
    )(cot, weights, scaled, window)


def weights_kernel(width, cot_ref, normed_ref, tokens_ref, grads_ref, first_ref, second_ref):
    tokens = tokens_ref[...]
    first_ref[:, :width] = dot_tn(cot_ref[...], normed_ref[...]).astype(BF16)
    first_ref[:, width:] = dot_tn(tokens, grads_ref[:, 2 * width :]).astype(BF16)
    second_ref[...] = dot_tn(tokens, grads_ref[:, : 2 * width]).astype(BF16)


def run_weights(cot, normed, tokens, grads):
    length, features = tokens.shape
    width = normed.shape[1]
    columns = [grads.shape[1] - width, 2 * width]
    return pl.pallas_call(
        functools.partial(weights_kernel, width),
        grid=(features // Q,),
        in_specs=[
            pl.BlockSpec((length, Q), lambda i: (0, i)),
            whole(normed.shape),
            pl.BlockSpec((length, Q), lambda i: (0, i)),
            whole(grads.shape),
        ],
        out_specs=[pl.BlockSpec((Q, count), lambda i: (i, 0)) for count in columns],
        out_shape=[jax.ShapeDtypeStruct((features, count), BF16) for count in columns],
        compiler_params=pltpu.CompilerParams(vmem_limit_bytes=VMEM_LIMIT),
        cost_estimate=cost(7),
        name="weight_gradients",
    )(cot, normed, tokens, grads)


def run_backward(
    heads, size, full_inner, stat, hidden, window, seg_row, weights, kernel_x, kernel_bc, head, channel,
    z_proj, mixed, x_proj, pre, bcdt, pre_bc, states, grad_out,
):
    length, features = hidden.shape
    width = heads * size
    blocks = length // Q
    rest = 2 * N + LANES
    total = 2 * width + rest

    def rows(columns):
        return pl.BlockSpec((Q, columns), lambda i: (blocks - 1 - i, 0))

    def made(columns, dtype):
        return jax.ShapeDtypeStruct((length, columns), dtype)

    across = pl.BlockSpec((8, Q), lambda i: (0, blocks - 1 - i))
    sums = [(8, width), (8, 2 * N), (8, LANES), (8, features)]
    return pl.pallas_call(
        functools.partial(backward_kernel, heads, size, full_inner),
        grid=(blocks,),
        in_specs=[
            across,
            rows(features),
            whole(window.shape),
            across,
            whole(weights.shape),
            whole(kernel_x.shape),
            whole(kernel_bc.shape),
            whole(head.shape),
            whole(channel.shape),
            rows(width),
            rows(width),
            rows(width),
            rows(width),
            rows(rest),
            rows(2 * N),
            pl.BlockSpec((1, N, width), lambda i: (blocks - 1 - i, 0, 0)),
            rows(width),
        ],
        out_specs=[rows(total), rows(features), rows(width)] + [whole(shape) for shape in sums],
        out_shape=[made(total, BF16), made(features, BF16), made(width, BF16)]
        + [jax.ShapeDtypeStruct(shape, F32) for shape in sums],
        scratch_shapes=[
            pltpu.VMEM((Q + HALO, width), F32),
            pltpu.VMEM((Q + HALO, 2 * N), F32),
            pltpu.VMEM((N, width), F32),
            pltpu.VMEM((8, LANES), F32),
        ],
        compiler_params=pltpu.CompilerParams(vmem_limit_bytes=VMEM_LIMIT),
        cost_estimate=cost(27),
        name="backward",
    )(
        stat, hidden, window, seg_row, weights, kernel_x, kernel_bc, head, channel,
        z_proj, mixed, x_proj, pre, bcdt, pre_bc, states, grad_out,
    )


def pad_lanes(values):
    return jnp.pad(values, ((0, 0), (0, LANES - values.shape[1])))


def line_gather(block, axis):
    n = lax.axis_size(axis)
    from_left, from_right = [], []
    right = left = block
    for step in range(1, n):
        right = lax.ppermute(right, axis, [(i, i + 1) for i in range(step - 1, n - 1)])
        left = lax.ppermute(left, axis, [(i, i - 1) for i in range(1, n - step + 1)])
        from_left.append(right)
        from_right.append(left)
    return from_left[::-1] + [block] + from_right


def line_scatter(part, axis):
    n = lax.axis_size(axis)
    place = lax.axis_index(axis)
    count = part.shape[0] // n

    def block(index):
        start = jnp.clip(index, 0, n - 1) * count
        return lax.dynamic_slice_in_dim(part, start, count, 0)

    right = left = None
    for step in range(1, n):
        send_right = block(n - step + place)
        send_left = block(step + place - n)
        if step > 1:
            send_right = (send_right.astype(F32) + right.astype(F32)).astype(part.dtype)
            send_left = (send_left.astype(F32) + left.astype(F32)).astype(part.dtype)
        right = lax.ppermute(send_right, axis, [(i, i + 1) for i in range(step)])
        left = lax.ppermute(send_left, axis, [(n - 1 - i, n - 2 - i) for i in range(step)])
    return block(place).astype(F32) + right.astype(F32) + left.astype(F32)


def cube_scatter(part, axis, upward):
    n = lax.axis_size(axis)
    if n & (n - 1):
        return lax.psum_scatter(part, axis, scatter_dimension=0, tiled=True).astype(F32)
    place = lax.axis_index(axis)
    rows, columns = part.shape
    bits = list(range(n.bit_length() - 1))
    order = bits if upward else bits[:1] + bits[:0:-1]
    left = bits[::-1]
    part = part.reshape((2,) * len(bits) + (rows // n, columns))
    for bit in order:
        dim = left.index(bit)
        mine = (place >> bit) & 1
        keep = lax.dynamic_index_in_dim(part, mine, dim, keepdims=False)
        send = lax.dynamic_index_in_dim(part, 1 - mine, dim, keepdims=False)
        other = lax.ppermute(send, axis, [(i, i ^ (1 << bit)) for i in range(n)])
        part = keep.astype(F32) + other.astype(F32)
        left.remove(bit)
        if left:
            part = part.astype(BF16)
    return part


def around(values, axis):
    n = lax.axis_size(axis)
    return [values] + [
        lax.ppermute(values, axis, [(i, (i - k) % n) for i in range(n)]) for k in range(1, n)
    ]


def sum_around(values, axis):
    return functools.reduce(jnp.add, around(values, axis))


def sum_pairwise(values, axis):
    n = lax.axis_size(axis)
    if n & (n - 1):
        return lax.psum(values, axis)
    bit = 1
    while bit < n:
        values = values + lax.ppermute(values, axis, [(i, i ^ bit) for i in range(n)])
        bit *= 2
    return values


def shards(
    hidden,
    seg_ids,
    cotangent,
    norm_gain,
    w_in_z,
    w_in_x,
    w_in_bc,
    w_in_dt,
    conv_x,
    conv_x_bias,
    conv_bc,
    conv_bc_bias,
    dt_bias,
    a_log,
    d_skip,
    gate_gain,
    w_out,
):
    heads = dt_bias.shape[0]
    width = gate_gain.shape[0]
    size = width // heads
    full_inner = width * lax.axis_size("tensor")
    features = hidden.shape[2]
    hidden_local = hidden[0]

    steps = jnp.pad(
        jnp.concatenate([w_in_dt, norm_gain[:, None]], axis=1), ((0, 0), (0, LANES - heads - 1))
    )
    packed = jnp.concatenate([w_out, w_in_x, w_in_z, w_in_bc, steps], axis=1)
    n = lax.axis_size("tensor")
    axis_place = lax.axis_index("tensor")
    place = axis_place[None]
    near_hidden = line_gather(hidden_local, "tensor")
    weights = lax.all_gather(packed, "dp", axis=0, tiled=True)
    seg_stack = around(seg_ids[0], "tensor")
    count = seg_ids.shape[1]
    seg_full = lax.dynamic_slice_in_dim(
        jnp.concatenate(seg_stack + seg_stack), (n - axis_place) * count, n * count, 0
    )
    cot_local, _ = lax.optimization_barrier((cotangent[0], weights))
    cot_full = lax.all_gather(cot_local, "tensor", axis=0, tiled=True)

    window = jnp.broadcast_to(
        jnp.pad(seg_full, (HALO, HALO), constant_values=-1)[:, None],
        (seg_full.shape[0] + 2 * HALO, LANES),
    )
    seg_row = jnp.broadcast_to(seg_full[None, :], (8, seg_full.shape[0]))
    kernel_x = jnp.concatenate([conv_x, conv_x_bias[None, :]], axis=0)
    kernel_bc = jnp.concatenate([conv_bc, conv_bc_bias[None, :]], axis=0)
    head = pad_lanes(jnp.stack([dt_bias, a_log]))
    channel = jnp.stack([gate_gain, jnp.repeat(d_skip, size)])

    (
        hidden_full, tokens, z_proj, mixed, x_proj, pre, bcdt, pre_bc, states, scaled, out_part,
        square, gain,
    ) = run_forward(
        heads, size, place, near_hidden, window, seg_row, weights, kernel_x, kernel_bc, head, channel
    )
    out_part, _ = lax.optimization_barrier((out_part, cot_full))
    out_sum = lax.psum_scatter(out_part, "tensor", scatter_dimension=0, tiled=True)
    grad_out, along = run_gradient(cot_full, weights, scaled, window)
    stat = sum_around(jnp.stack([square[0], along[0]]), "tensor")
    stat_full = jnp.pad(stat, ((0, 6), (0, 0)))
    out_scale = lax.rsqrt(stat[0] / full_inner + EPS) * (seg_full > 0).astype(F32)

    grads, in_part, normed_out, sum_x, sum_bc, sum_head, sum_gain = run_backward(
        heads, size, full_inner, stat_full, hidden_full, window, seg_row, weights, kernel_x,
        kernel_bc, head, channel, z_proj, mixed, x_proj, pre, bcdt, pre_bc, states, grad_out,
    )
    in_sum = line_scatter(in_part, "tensor")

    first, second = run_weights(cot_full, normed_out, tokens, grads)
    first = cube_scatter(first, "dp", True)
    second = cube_scatter(second, "dp", False)
    grad_bc = sum_around(first[:, width : width + 2 * N], "tensor")
    own = jnp.concatenate([sum_x.reshape(-1, LANES), sum_head])
    both = jnp.concatenate([sum_gain[0].reshape(-1, LANES), sum_bc.reshape(-1, LANES)])
    both = sum_around(both, "tensor")
    small = sum_pairwise(jnp.concatenate([own, both]), "dp")
    cuts = [sum_x.size // LANES, 8, features // LANES]
    sum_x = small[: cuts[0]].reshape(8, width)
    sum_head = small[cuts[0] : cuts[0] + 8]
    sum_gain = small[cuts[0] + 8 : cuts[0] + 8 + cuts[2]].reshape(features)
    sum_bc = small[cuts[0] + 8 + cuts[2] :].reshape(8, 2 * N)
    local_features = norm_gain.shape[0]
    grad_norm_gain = lax.dynamic_slice_in_dim(
        sum_gain, lax.axis_index("dp") * local_features, local_features, 0
    )

    local = hidden_local.shape[0]
    hidden_rows = hidden_local.astype(F32)
    scale_here = lax.dynamic_slice_in_dim(out_scale, axis_place * local, local, 0)[:, None]
    layer_out = (hidden_rows + out_sum.astype(F32) * scale_here).astype(BF16)

    inverse = lax.rsqrt(jnp.mean(hidden_rows * hidden_rows, axis=1, keepdims=True) + EPS)
    unit = hidden_rows * inverse
    grad_scaled = in_sum * gain[0:1]
    grad_hidden = (
        cotangent[0].astype(F32)
        + inverse * (grad_scaled - unit * jnp.mean(grad_scaled * unit, axis=1, keepdims=True))
    ).astype(BF16)

    return (
        layer_out[None],
        grad_hidden[None],
        grad_norm_gain,
        second[:, width:],
        second[:, :width],
        grad_bc,
        first[:, width + 2 * N : width + 2 * N + heads],
        sum_x[0:CONV],
        sum_x[CONV],
        sum_bc[0:CONV],
        sum_bc[CONV],
        sum_head[0, :heads],
        sum_head[1, :heads],
        jnp.sum(sum_x[CONV + 2].reshape(heads, size), axis=1),
        sum_x[CONV + 1],
        first[:, :width],
    )


def solution(mesh):
    in_specs = (
        P("dp", "tensor", None),
        P("dp", "tensor"),
        P("dp", "tensor", None),
        P("dp"),
        P("dp", "tensor"),
        P("dp", "tensor"),
        P("dp", None),
        P("dp", "tensor"),
        P(None, "tensor"),
        P("tensor"),
        P(),
        P(),
        P("tensor"),
        P("tensor"),
        P("tensor"),
        P("tensor"),
        P("dp", "tensor"),
    )
    out_specs = (
        P("dp", "tensor", None),
        P("dp", "tensor", None),
        P("dp"),
        P("dp", "tensor"),
        P("dp", "tensor"),
        P("dp", None),
        P("dp", "tensor"),
        P(None, "tensor"),
        P("tensor"),
        P(),
        P(),
        P("tensor"),
        P("tensor"),
        P("tensor"),
        P("tensor"),
        P("dp", "tensor"),
    )
    return jax.shard_map(shards, mesh=mesh, in_specs=in_specs, out_specs=out_specs, check_vma=False)
```

```python
import functools

import jax
import jax.numpy as jnp
from jax import lax
from jax.experimental import pallas as pl
from jax.experimental.pallas import tpu as pltpu
from jax.sharding import PartitionSpec as P

N = 128
CONV = 4
Q = 256
LANES = 128
HALO = 8
EPS = 1e-05
NEG = -1e30
F32 = jnp.float32
BF16 = jnp.bfloat16
VMEM_LIMIT = 52 * 1024 * 1024


def dot(a, b):
    return jnp.dot(a, b, preferred_element_type=F32)


def dot_nt(a, b):
    return lax.dot_general(a, b, (((1,), (1,)), ((), ())), preferred_element_type=F32)


def dot_tn(a, b):
    return lax.dot_general(a, b, (((0,), (0,)), ((), ())), preferred_element_type=F32)


def dot_exact(a, b):
    return jnp.dot(a, b, preferred_element_type=F32, precision=lax.Precision.HIGHEST)


def spread(cols, heads, size):
    rows = cols.shape[0]
    per = LANES // size
    lane = lax.broadcasted_iota(jnp.int32, (rows, LANES), 1)
    parts = []
    for first in range(0, heads, per):
        part = jnp.broadcast_to(cols[:, first : first + 1], (rows, LANES))
        for extra in range(1, per):
            part = jnp.where(lane < extra * size, part, cols[:, first + extra : first + extra + 1])
        parts.append(part)
    return jnp.concatenate(parts, axis=1)


def head_sums(values, heads, size):
    width = heads * size
    channel = lax.broadcasted_iota(jnp.int32, (width, LANES), 0)
    column = lax.broadcasted_iota(jnp.int32, (width, LANES), 1)
    first = column * size
    picks = jnp.where((channel >= first) & (channel < first + size), 1.0, 0.0).astype(BF16)
    high = values.astype(BF16)
    low = (values - high.astype(F32)).astype(BF16)
    return dot(high, picks) + dot(low, picks)


def widen(tile, width):
    return jnp.concatenate([tile] * (width // tile.shape[1]), axis=1)


def softplus(v):
    return jnp.maximum(v, 0.0) + jnp.log1p(jnp.exp(-jnp.abs(v)))


def sigmoid(v):
    return 1.0 / (1.0 + jnp.exp(-v))


def as_row(column):
    rows = column.shape[0]
    return jnp.broadcast_to(column, (rows, LANES)).T[:8]


def triangle(lower):
    row = lax.broadcasted_iota(jnp.int32, (Q, Q), 0)
    col = lax.broadcasted_iota(jnp.int32, (Q, Q), 1)
    return row >= col if lower else row <= col


def block_masks(window, seg_row):
    seg = window[HALO : HALO + Q]
    before = window[HALO - 1 : HALO]
    last = window[HALO + Q - 1 : HALO + Q]
    from_prev = (seg == before).astype(F32)
    same_last = (seg == last).astype(F32)
    passes = (last == before).astype(F32)
    keep = (widen(seg, Q) == seg_row) & triangle(True)
    bias = jnp.where(keep, 0.0, NEG)
    return seg, from_prev, same_last, passes, bias


def conv_forward(buffer, window, seg, kernel, conv_bias, width):
    total = conv_bias + kernel[CONV - 1 : CONV] * buffer[HALO : HALO + Q, :]
    for back in range(1, CONV):
        match = (window[HALO - back : HALO - back + Q] == seg).astype(F32)
        tap = kernel[CONV - 1 - back : CONV - back]
        total = total + tap * (buffer[HALO - back : HALO - back + Q, :] * widen(match, width))
    return total


def conv_backward(buffer, window, seg, kernel, values, width):
    here = buffer[0:Q, :]
    total = kernel[CONV - 1 : CONV] * here
    taps = [jnp.sum(values * here, axis=0, keepdims=True)]
    for ahead in range(1, CONV):
        match = (window[HALO + ahead : HALO + ahead + Q] == seg).astype(F32)
        moved = buffer[ahead : ahead + Q, :] * widen(match, width)
        total = total + kernel[CONV - 1 - ahead : CONV - ahead] * moved
        taps.append(jnp.sum(values * moved, axis=0, keepdims=True))
    return total, taps


def pick_block(place, near_refs, block):
    reach = len(near_refs) // 2
    away = pl.program_id(0) - place
    for index, ref in enumerate(near_refs):

        @pl.when(away == index - reach)
        def _():
            block[...] = ref[...]


def project_kernel(heads, size, near, place_ref, *refs):
    near_refs, refs = refs[:near], refs[near:]
    weights_ref, hidden_ref, tokens_ref, z_ref, x_ref, bcdt_ref, gain_ref = refs
    width = heads * size

    @pl.when(pl.program_id(0) == 0)
    def _():
        tail_columns = weights_ref[:, 3 * width + 2 * N :].astype(F32).T
        gain_ref[...] = jnp.broadcast_to(tail_columns[heads : heads + 1], gain_ref.shape)

    pick_block(place_ref[0], near_refs, hidden_ref)
    hidden = hidden_ref[...].astype(F32)
    inverse = lax.rsqrt(jnp.mean(hidden * hidden, axis=1, keepdims=True) + EPS)
    tokens = (hidden * inverse * gain_ref[0:1, :]).astype(BF16)
    tokens_ref[...] = tokens
    x_ref[...] = dot(tokens, weights_ref[:, width : 2 * width])
    z_ref[...] = dot(tokens, weights_ref[:, 2 * width : 3 * width])
    bcdt_ref[...] = dot(tokens, weights_ref[:, 3 * width :])


def forward_kernel(
    heads,
    size,
    window_ref,
    seg_row_ref,
    weights_ref,
    kernel_x_ref,
    kernel_bc_ref,
    head_ref,
    channel_ref,
    z_ref,
    x_ref,
    bcdt_ref,
    mixed_ref,
    pre_ref,
    pre_bc_ref,
    state_ref,
    scaled_ref,
    part_ref,
    square_ref,
    x_buffer,
    bc_buffer,
    carry,
):
    step = pl.program_id(0)
    width = heads * size

    @pl.when(step == 0)
    def _():
        x_buffer[0:HALO, :] = jnp.zeros((HALO, width), F32)
        bc_buffer[0:HALO, :] = jnp.zeros((HALO, 2 * N), F32)
        carry[...] = jnp.zeros((N, width), F32)

    window = window_ref[pl.ds(pl.multiple_of(step * Q, Q), Q + 2 * HALO), :]
    seg, from_prev, same_last, passes, bias = block_masks(window, seg_row_ref[0:1, :])
    z_proj = z_ref[...]
    bcdt = bcdt_ref[...]
    x_buffer[HALO : HALO + Q, :] = x_ref[...]
    bc_buffer[HALO : HALO + Q, :] = bcdt[:, : 2 * N]
    pre = conv_forward(
        x_buffer, window, seg, kernel_x_ref[...], kernel_x_ref[CONV : CONV + 1, :], width
    )
    pre_bc = conv_forward(
        bc_buffer, window, seg, kernel_bc_ref[...], kernel_bc_ref[CONV : CONV + 1, :], 2 * N
    )
    x_buffer[0:HALO, :] = x_buffer[Q : Q + HALO, :]
    bc_buffer[0:HALO, :] = bc_buffer[Q : Q + HALO, :]
    pre_ref[...] = pre
    pre_bc_ref[...] = pre_bc
    x_conv = pre * sigmoid(pre)
    bc_conv = (pre_bc * sigmoid(pre_bc)).astype(BF16)
    b_in = bc_conv[:, :N]
    c_in = bc_conv[:, N:]

    dt = softplus(bcdt[:, 2 * N :] + head_ref[0:1, :])
    decay = -dt * jnp.exp(head_ref[1:2, :])
    total = dot_exact(triangle(True).astype(F32), decay)
    total_t = total.T
    weighted = x_conv * spread(dt, heads, size)
    scores = dot_nt(c_in, b_in)
    before = carry[...]
    state_ref[0] = before

    per = LANES // size
    lane = lax.broadcasted_iota(jnp.int32, (Q, LANES), 1)
    inner = []
    for first in range(0, heads, per):
        group = weighted[:, first * size : first * size + LANES]
        summed = jnp.zeros((Q, LANES), F32)
        for extra in range(per):
            h = first + extra
            shape = jnp.exp(total[:, h : h + 1] - total_t[h : h + 1, :] + bias)
            mine = (lane >= extra * size) & (lane < (extra + 1) * size)
            summed = summed + dot(
                (scores * shape).astype(BF16), jnp.where(mine, group, 0.0).astype(BF16)
            )
        inner.append(summed)
    scanned = jnp.concatenate(inner, axis=1)
    scanned = scanned + dot(c_in, before.astype(BF16)) * spread(
        jnp.exp(total) * from_prev, heads, size
    )
    last = total[Q - 1 : Q, :]
    to_end = jnp.exp(last - total) * same_last
    carry[...] = dot_tn(
        b_in, (weighted * spread(to_end, heads, size)).astype(BF16)
    ) + before * spread(jnp.exp(last) * passes, heads, size)

    mixed = scanned + channel_ref[1:2, :] * x_conv
    mixed_ref[...] = mixed
    gated = mixed * (z_proj * sigmoid(z_proj))
    scaled = (gated * channel_ref[0:1, :]).astype(BF16)
    scaled_ref[...] = scaled
    part_ref[...] = dot_nt(scaled, weights_ref[...]).astype(BF16)
    square_ref[...] = as_row(jnp.sum(gated * gated, axis=1, keepdims=True))


def gradient_kernel(width, near, place_ref, *refs):
    near_refs, refs = refs[:near], refs[near:]
    weights_ref, scaled_ref, window_ref, cot_ref, grad_ref, along_ref = refs
    step = pl.program_id(0)
    pick_block(place_ref[0], near_refs, cot_ref)
    window = window_ref[pl.ds(pl.multiple_of(step * Q, Q), Q + 2 * HALO), :]
    live = (window[HALO : HALO + Q] > 0).astype(F32)
    grad = dot(cot_ref[...], weights_ref[...]) * widen(live, width)
    grad_ref[...] = grad
    along_ref[...] = as_row(jnp.sum(scaled_ref[...].astype(F32) * grad, axis=1, keepdims=True))


def backward_kernel(
    heads,
    size,
    full_inner,
    stat_ref,
    hidden_ref,
    window_ref,
    seg_row_ref,
    weights_ref,
    kernel_x_ref,
    kernel_bc_ref,
    head_ref,
    channel_ref,
    z_ref,
    mixed_ref,
    x_ref,
    pre_ref,
    bcdt_ref,
    pre_bc_ref,
    state_ref,
    grad_ref,
    proj_ref,
    part_ref,
    out_ref,
    sum_x_ref,
    sum_bc_ref,
    sum_head_ref,
    sum_gain_ref,
    x_buffer,
    bc_buffer,
    carry,
    tail,
):
    turn = pl.program_id(0)
    step = pl.num_programs(0) - 1 - turn
    width = heads * size

    @pl.when(turn == 0)
    def _():
        x_buffer[...] = jnp.zeros((Q + HALO, width), F32)
        bc_buffer[...] = jnp.zeros((Q + HALO, 2 * N), F32)
        carry[...] = jnp.zeros((N, width), F32)
        tail[...] = jnp.zeros((8, LANES), F32)
        sum_x_ref[...] = jnp.zeros((8, width), F32)
        sum_bc_ref[...] = jnp.zeros((8, 2 * N), F32)
        sum_head_ref[...] = jnp.zeros((8, LANES), F32)
        sum_gain_ref[...] = jnp.zeros(sum_gain_ref.shape, F32)

    window = window_ref[pl.ds(pl.multiple_of(step * Q, Q), Q + 2 * HALO), :]
    seg, from_prev, same_last, passes, bias = block_masks(window, seg_row_ref[0:1, :])
    live = (seg[:, 0:1] > 0).astype(F32)
    stat = stat_ref[...].T
    gate_inverse = lax.rsqrt(stat[:, 0:1] / full_inner + EPS)
    along = stat[:, 1:2] * (gate_inverse * gate_inverse * gate_inverse / full_inner)

    gain = channel_ref[0:1, :]
    skip = channel_ref[1:2, :]
    z_proj = z_ref[...]
    mixed = mixed_ref[...]
    grad_out = grad_ref[...]
    gate = sigmoid(z_proj)
    opened = z_proj * gate
    gated = mixed * opened
    normal = gated * gate_inverse
    sum_gate = jnp.sum(grad_out * normal, axis=0, keepdims=True)
    out_ref[...] = (normal * gain * live).astype(BF16)
    grad_gated = grad_out * gain * gate_inverse - gated * along
    grad_z = grad_gated * mixed * (gate * (1.0 + z_proj * (1.0 - gate)))
    dy = grad_gated * opened

    pre = pre_ref[...]
    gate_x = sigmoid(pre)
    x_conv = pre * gate_x
    pre_bc = pre_bc_ref[...]
    gate_bc = sigmoid(pre_bc)
    bc_conv = (pre_bc * gate_bc).astype(BF16)
    b_in = bc_conv[:, :N]
    c_in = bc_conv[:, N:]
    bcdt = bcdt_ref[...]
    raw = bcdt[:, 2 * N :] + head_ref[0:1, :]
    dt = softplus(raw)
    rate = jnp.exp(head_ref[1:2, :])
    decay = -dt * rate
    total = dot_exact(triangle(True).astype(F32), decay)
    total_t = total.T
    dt_wide = spread(dt, heads, size)
    weighted = x_conv * dt_wide
    scores = dot_nt(c_in, b_in)
    before = state_ref[0]
    before_low = before.astype(BF16)
    last = total[Q - 1 : Q, :]
    to_end = spread(jnp.exp(last - total) * same_last, heads, size)
    from_start = spread(jnp.exp(total) * from_prev, heads, size)
    after = carry[...]
    after_low = after.astype(BF16)

    dy_low = dy.astype(BF16)
    weighted_low = weighted.astype(BF16)
    dy_start = (dy * from_start).astype(BF16)
    grad_c = dot_nt(dy_start, before_low)
    carried = dot(c_in, before_low)
    returned = dot(b_in, after_low)
    grad_weighted = to_end * returned
    weighted_end = (weighted * to_end).astype(BF16)
    grad_b = dot_nt(weighted_end, after_low)
    new_after = dot_tn(c_in, dy_start) + after * spread(jnp.exp(last) * passes, heads, size)
    carry[...] = new_after

    per = LANES // size
    lane = lax.broadcasted_iota(jnp.int32, (Q, LANES), 1)
    grad_scores = jnp.zeros((Q, Q), F32)
    inner = []
    none = jnp.zeros((Q, LANES), BF16)
    for first in range(0, heads, per):
        at = first * size
        dy_group = dy_low[:, at : at + LANES]
        weighted_group = weighted_low[:, at : at + LANES]
        summed = jnp.zeros((Q, LANES), F32)
        for extra in range(per):
            h = first + extra
            shape = jnp.exp(total[:, h : h + 1] - total_t[h : h + 1, :] + bias)
            mine = (lane >= extra * size) & (lane < (extra + 1) * size)
            dy_mine = jnp.where(mine, dy_group, none)
            grad_scores = grad_scores + dot_nt(dy_mine, weighted_group) * shape
            summed = summed + dot_tn((scores * shape).astype(BF16), dy_mine)
        inner.append(summed)
    grad_inner = jnp.concatenate(inner, axis=1)
    grad_weighted = grad_weighted + grad_inner
    grad_scores = grad_scores.astype(BF16)
    grad_c = grad_c + dot(grad_scores, b_in)
    grad_b = grad_b + dot_tn(grad_scores, c_in)

    scanned = mixed - skip * x_conv - carried * from_start
    pairs = head_sums(
        dy_low.astype(F32) * scanned
        + dy_start.astype(F32) * carried
        - weighted_low.astype(F32) * grad_inner
        - weighted_end.astype(F32) * returned,
        heads,
        size,
    )
    grad_decay = dot_exact(triangle(False).astype(F32), pairs) + tail[0:1, :]
    kept = jnp.sum(new_after.astype(BF16).astype(F32) * before, axis=0, keepdims=True)
    kept = jnp.broadcast_to(kept, (8, width))
    tail[...] = head_sums(kept, heads, size)
    grad_dt = head_sums(grad_weighted * x_conv, heads, size) - grad_decay * rate
    grad_raw = grad_dt * sigmoid(raw)
    sum_head_ref[0:1, :] += jnp.sum(grad_raw, axis=0, keepdims=True)
    sum_head_ref[1:2, :] += jnp.sum(grad_decay * decay, axis=0, keepdims=True)

    grad_x = grad_weighted * dt_wide + skip * dy
    sum_skip = jnp.sum(dy * x_conv, axis=0, keepdims=True)
    grad_pre = grad_x * (gate_x * (1.0 + pre * (1.0 - gate_x)))
    x_buffer[Q : Q + HALO, :] = x_buffer[0:HALO, :]
    x_buffer[0:Q, :] = grad_pre
    grad_proj, taps = conv_backward(
        x_buffer, window, seg, kernel_x_ref[...], x_ref[...], width
    )
    sum_bias = jnp.sum(grad_pre, axis=0, keepdims=True)
    blank = jnp.zeros((1, width), F32)
    sum_x_ref[...] += jnp.concatenate(
        [taps[3], taps[2], taps[1], taps[0], sum_bias, sum_gate, sum_skip, blank], axis=0
    )

    grad_pre_bc = jnp.concatenate([grad_b, grad_c], axis=1) * (
        gate_bc * (1.0 + pre_bc * (1.0 - gate_bc))
    )
    bc_buffer[Q : Q + HALO, :] = bc_buffer[0:HALO, :]
    bc_buffer[0:Q, :] = grad_pre_bc
    grad_bc, taps_bc = conv_backward(
        bc_buffer, window, seg, kernel_bc_ref[...], bcdt[:, : 2 * N], 2 * N
    )
    sum_bias_bc = jnp.sum(grad_pre_bc, axis=0, keepdims=True)
    blank_bc = jnp.zeros((3, 2 * N), F32)
    sum_bc_ref[...] += jnp.concatenate(
        [taps_bc[3], taps_bc[2], taps_bc[1], taps_bc[0], sum_bias_bc, blank_bc], axis=0
    )

    grads = jnp.concatenate(
        [
            grad_proj.astype(BF16),
            grad_z.astype(BF16),
            grad_bc.astype(BF16),
            grad_raw.astype(BF16),
        ],
        axis=1,
    )
    proj_ref[...] = grads
    part = dot_nt(grads, weights_ref[:, width:])
    part_ref[...] = part.astype(BF16)
    hidden = hidden_ref[...].astype(F32)
    inverse = lax.rsqrt(jnp.mean(hidden * hidden, axis=1, keepdims=True) + EPS)
    sum_gain_ref[0:1, :] += jnp.sum(part * (hidden * inverse), axis=0, keepdims=True)


def cost(micros):
    return pl.CostEstimate(flops=int(micros * 1e9), bytes_accessed=1 << 20, transcendentals=0)


def whole(shape):
    return pl.BlockSpec(shape, lambda i: (0,) * len(shape))


def scalar():
    return pl.BlockSpec(memory_space=pltpu.SMEM)


def run_project(heads, size, place, near, weights):
    features = near[0].shape[1]
    blocks = len(near) // 2 + 1
    length = blocks * Q
    width = heads * size
    rest = 2 * N + LANES

    def rows(columns):
        return pl.BlockSpec((Q, columns), lambda i: (i, 0))

    def made(columns, dtype):
        return jax.ShapeDtypeStruct((length, columns), dtype)

    return pl.pallas_call(
        functools.partial(project_kernel, heads, size, len(near)),
        grid=(blocks,),
        in_specs=[scalar(), *[whole(block.shape) for block in near], whole(weights.shape)],
        out_specs=[
            rows(features),
            rows(features),
            rows(width),
            rows(width),
            rows(rest),
            whole((8, features)),
        ],
        out_shape=[
            made(features, BF16),
            made(features, BF16),
            made(width, F32),
            made(width, F32),
            made(rest, F32),
            jax.ShapeDtypeStruct((8, features), F32),
        ],
        compiler_params=pltpu.CompilerParams(vmem_limit_bytes=VMEM_LIMIT),
        cost_estimate=cost(8),
        name="project",
    )(place, *near, weights)


def run_forward(
    heads, size, window, seg_row, weights, kernel_x, kernel_bc, head, channel, z_proj, x_proj, bcdt
):
    length, features = seg_row.shape[1], weights.shape[0]
    width = heads * size
    blocks = length // Q

    def rows(columns):
        return pl.BlockSpec((Q, columns), lambda i: (i, 0))

    def made(columns, dtype):
        return jax.ShapeDtypeStruct((length, columns), dtype)

    across = pl.BlockSpec((8, Q), lambda i: (0, i))
    return pl.pallas_call(
        functools.partial(forward_kernel, heads, size),
        grid=(blocks,),
        in_specs=[
            whole(window.shape),
            across,
            whole((features, width)),
            whole(kernel_x.shape),
            whole(kernel_bc.shape),
            whole(head.shape),
            whole(channel.shape),
            rows(width),
            rows(width),
            rows(bcdt.shape[1]),
        ],
        out_specs=[
            rows(width),
            rows(width),
            rows(2 * N),
            pl.BlockSpec((1, N, width), lambda i: (i, 0, 0)),
            rows(width),
            rows(features),
            across,
        ],
        out_shape=[
            made(width, F32),
            made(width, F32),
            made(2 * N, F32),
            jax.ShapeDtypeStruct((blocks, N, width), F32),
            made(width, BF16),
            made(features, BF16),
            jax.ShapeDtypeStruct((8, length), F32),
        ],
        scratch_shapes=[
            pltpu.VMEM((Q + HALO, width), F32),
            pltpu.VMEM((Q + HALO, 2 * N), F32),
            pltpu.VMEM((N, width), F32),
        ],
        compiler_params=pltpu.CompilerParams(vmem_limit_bytes=VMEM_LIMIT),
        cost_estimate=cost(14),
        name="forward",
    )(window, seg_row, weights, kernel_x, kernel_bc, head, channel, z_proj, x_proj, bcdt)


def run_gradient(place, near, weights, scaled, window):
    features = near[0].shape[1]
    length, width = scaled.shape
    return pl.pallas_call(
        functools.partial(gradient_kernel, width, len(near)),
        grid=(length // Q,),
        in_specs=[
            scalar(),
            *[whole(block.shape) for block in near],
            whole((features, width)),
            pl.BlockSpec((Q, width), lambda i: (i, 0)),
            whole(window.shape),
        ],
        out_specs=[
            pl.BlockSpec((Q, features), lambda i: (i, 0)),
            pl.BlockSpec((Q, width), lambda i: (i, 0)),
            pl.BlockSpec((8, Q), lambda i: (0, i)),
        ],
        out_shape=[
            jax.ShapeDtypeStruct((length, features), BF16),
            jax.ShapeDtypeStruct((length, width), F32),
            jax.ShapeDtypeStruct((8, length), F32),
        ],
        compiler_params=pltpu.CompilerParams(vmem_limit_bytes=VMEM_LIMIT),
        cost_estimate=cost(5),
        name="out_gradient",
    )(place, *near, weights, scaled, window)


def weights_kernel(width, cot_ref, normed_ref, tokens_ref, grads_ref, first_ref, second_ref):
    tokens = tokens_ref[...]
    first_ref[:, :width] = dot_tn(cot_ref[...], normed_ref[...]).astype(BF16)
    first_ref[:, width:] = dot_tn(tokens, grads_ref[:, 2 * width :]).astype(BF16)
    second_ref[...] = dot_tn(tokens, grads_ref[:, : 2 * width]).astype(BF16)


def run_weights(cot, normed, tokens, grads):
    length, features = tokens.shape
    width = normed.shape[1]
    columns = [grads.shape[1] - width, 2 * width]
    return pl.pallas_call(
        functools.partial(weights_kernel, width),
        grid=(features // Q,),
        in_specs=[
            pl.BlockSpec((length, Q), lambda i: (0, i)),
            whole(normed.shape),
            pl.BlockSpec((length, Q), lambda i: (0, i)),
            whole(grads.shape),
        ],
        out_specs=[pl.BlockSpec((Q, count), lambda i: (i, 0)) for count in columns],
        out_shape=[jax.ShapeDtypeStruct((features, count), BF16) for count in columns],
        compiler_params=pltpu.CompilerParams(vmem_limit_bytes=VMEM_LIMIT),
        cost_estimate=cost(7),
        name="weight_gradients",
    )(cot, normed, tokens, grads)


def run_backward(
    heads, size, full_inner, stat, hidden, window, seg_row, weights, kernel_x, kernel_bc, head, channel,
    z_proj, mixed, x_proj, pre, bcdt, pre_bc, states, grad_out,
):
    length, features = hidden.shape
    width = heads * size
    blocks = length // Q
    rest = 2 * N + LANES
    total = 2 * width + rest

    def rows(columns):
        return pl.BlockSpec((Q, columns), lambda i: (blocks - 1 - i, 0))

    def made(columns, dtype):
        return jax.ShapeDtypeStruct((length, columns), dtype)

    across = pl.BlockSpec((8, Q), lambda i: (0, blocks - 1 - i))
    sums = [(8, width), (8, 2 * N), (8, LANES), (8, features)]
    return pl.pallas_call(
        functools.partial(backward_kernel, heads, size, full_inner),
        grid=(blocks,),
        in_specs=[
            across,
            rows(features),
            whole(window.shape),
            across,
            whole(weights.shape),
            whole(kernel_x.shape),
            whole(kernel_bc.shape),
            whole(head.shape),
            whole(channel.shape),
            rows(width),
            rows(width),
            rows(width),
            rows(width),
            rows(rest),
            rows(2 * N),
            pl.BlockSpec((1, N, width), lambda i: (blocks - 1 - i, 0, 0)),
            rows(width),
        ],
        out_specs=[rows(total), rows(features), rows(width)] + [whole(shape) for shape in sums],
        out_shape=[made(total, BF16), made(features, BF16), made(width, BF16)]
        + [jax.ShapeDtypeStruct(shape, F32) for shape in sums],
        scratch_shapes=[
            pltpu.VMEM((Q + HALO, width), F32),
            pltpu.VMEM((Q + HALO, 2 * N), F32),
            pltpu.VMEM((N, width), F32),
            pltpu.VMEM((8, LANES), F32),
        ],
        compiler_params=pltpu.CompilerParams(vmem_limit_bytes=VMEM_LIMIT),
        cost_estimate=cost(27),
        name="backward",
    )(
        stat, hidden, window, seg_row, weights, kernel_x, kernel_bc, head, channel,
        z_proj, mixed, x_proj, pre, bcdt, pre_bc, states, grad_out,
    )


def pad_lanes(values):
    return jnp.pad(values, ((0, 0), (0, LANES - values.shape[1])))


def line_gather(block, axis):
    n = lax.axis_size(axis)
    from_left, from_right = [], []
    right = left = block
    for step in range(1, n):
        right = lax.ppermute(right, axis, [(i, i + 1) for i in range(step - 1, n - 1)])
        left = lax.ppermute(left, axis, [(i, i - 1) for i in range(1, n - step + 1)])
        from_left.append(right)
        from_right.append(left)
    return from_left[::-1] + [block] + from_right


def cube_scatter(part, axis, upward):
    n = lax.axis_size(axis)
    if n & (n - 1):
        return lax.psum_scatter(part, axis, scatter_dimension=0, tiled=True).astype(F32)
    place = lax.axis_index(axis)
    rows, columns = part.shape
    bits = list(range(n.bit_length() - 1))
    order = bits if upward else bits[:1] + bits[:0:-1]
    left = bits[::-1]
    part = part.reshape((2,) * len(bits) + (rows // n, columns))
    for bit in order:
        dim = left.index(bit)
        mine = (place >> bit) & 1
        keep = lax.dynamic_index_in_dim(part, mine, dim, keepdims=False)
        send = lax.dynamic_index_in_dim(part, 1 - mine, dim, keepdims=False)
        other = lax.ppermute(send, axis, [(i, i ^ (1 << bit)) for i in range(n)])
        part = keep.astype(F32) + other.astype(F32)
        left.remove(bit)
        if left:
            part = part.astype(BF16)
    return part


def around(values, axis):
    n = lax.axis_size(axis)
    return [values] + [
        lax.ppermute(values, axis, [(i, (i - k) % n) for i in range(n)]) for k in range(1, n)
    ]


def sum_around(values, axis):
    return functools.reduce(jnp.add, around(values, axis))


def sum_pairwise(values, axis):
    n = lax.axis_size(axis)
    if n & (n - 1):
        return lax.psum(values, axis)
    bit = 1
    while bit < n:
        values = values + lax.ppermute(values, axis, [(i, i ^ bit) for i in range(n)])
        bit *= 2
    return values


def shards(
    hidden,
    seg_ids,
    cotangent,
    norm_gain,
    w_in_z,
    w_in_x,
    w_in_bc,
    w_in_dt,
    conv_x,
    conv_x_bias,
    conv_bc,
    conv_bc_bias,
    dt_bias,
    a_log,
    d_skip,
    gate_gain,
    w_out,
):
    heads = dt_bias.shape[0]
    width = gate_gain.shape[0]
    size = width // heads
    full_inner = width * lax.axis_size("tensor")
    features = hidden.shape[2]
    hidden_local = hidden[0]

    steps = jnp.pad(
        jnp.concatenate([w_in_dt, norm_gain[:, None]], axis=1), ((0, 0), (0, LANES - heads - 1))
    )
    packed = jnp.concatenate([w_out, w_in_x, w_in_z, w_in_bc, steps], axis=1)
    n = lax.axis_size("tensor")
    axis_place = lax.axis_index("tensor")
    place = axis_place[None]
    near_hidden = line_gather(hidden_local, "tensor")
    weights = lax.all_gather(packed, "dp", axis=0, tiled=True)
    seg_stack = around(seg_ids[0], "tensor")
    count = seg_ids.shape[1]
    seg_full = lax.dynamic_slice_in_dim(
        jnp.concatenate(seg_stack + seg_stack), (n - axis_place) * count, n * count, 0
    )
    cot_local, _, _ = lax.optimization_barrier((cotangent[0], near_hidden[0], near_hidden[-1]))
    near_cot = line_gather(cot_local, "tensor")

    window = jnp.broadcast_to(
        jnp.pad(seg_full, (HALO, HALO), constant_values=-1)[:, None],
        (seg_full.shape[0] + 2 * HALO, LANES),
    )
    seg_row = jnp.broadcast_to(seg_full[None, :], (8, seg_full.shape[0]))
    kernel_x = jnp.concatenate([conv_x, conv_x_bias[None, :]], axis=0)
    kernel_bc = jnp.concatenate([conv_bc, conv_bc_bias[None, :]], axis=0)
    head = pad_lanes(jnp.stack([dt_bias, a_log]))
    channel = jnp.stack([gate_gain, jnp.repeat(d_skip, size)])

    hidden_full, tokens, z_proj, x_proj, bcdt, gain = run_project(
        heads, size, place, near_hidden, weights
    )
    bcdt, _, _ = lax.optimization_barrier((bcdt, near_cot[n - 2], near_cot[n]))
    mixed, pre, pre_bc, states, scaled, out_part, square = run_forward(
        heads, size, window, seg_row, weights, kernel_x, kernel_bc, head, channel, z_proj, x_proj,
        bcdt,
    )
    cot_full, grad_out, along = run_gradient(place, near_cot, weights, scaled, window)
    out_part, _ = lax.optimization_barrier((out_part, along))
    out_sum = lax.psum_scatter(out_part, "tensor", scatter_dimension=0, tiled=True)
    stat = sum_around(jnp.stack([square[0], along[0]]), "tensor")
    stat_full = jnp.pad(stat, ((0, 6), (0, 0)))
    out_scale = lax.rsqrt(stat[0] / full_inner + EPS) * (seg_full > 0).astype(F32)

    grads, in_part, normed_out, sum_x, sum_bc, sum_head, sum_gain = run_backward(
        heads, size, full_inner, stat_full, hidden_full, window, seg_row, weights, kernel_x,
        kernel_bc, head, channel, z_proj, mixed, x_proj, pre, bcdt, pre_bc, states, grad_out,
    )
    in_sum = lax.psum_scatter(in_part, "tensor", scatter_dimension=0, tiled=True)

    first, second = run_weights(cot_full, normed_out, tokens, grads)
    first = cube_scatter(first, "dp", True)
    second = cube_scatter(second, "dp", False)
    own = jnp.concatenate([sum_x.reshape(-1, LANES), sum_head])
    both = jnp.concatenate([sum_gain[0].reshape(-1, LANES), sum_bc.reshape(-1, LANES)])
    small = sum_pairwise(jnp.concatenate([own, both]), "dp")
    sum_x = small[: own.shape[0] - 8].reshape(8, width)
    sum_head = small[own.shape[0] - 8 : own.shape[0]]
    grad_bc = first[:, width : width + 2 * N]
    shared = jnp.concatenate([small[own.shape[0] :], grad_bc.reshape(-1, LANES)])
    shared = sum_around(shared, "tensor")
    gain_rows = features // LANES
    sum_gain = shared[:gain_rows].reshape(features)
    sum_bc = shared[gain_rows : both.shape[0]].reshape(8, 2 * N)
    grad_bc = shared[both.shape[0] :].reshape(grad_bc.shape)
    local_features = norm_gain.shape[0]
    grad_norm_gain = lax.dynamic_slice_in_dim(
        sum_gain, lax.axis_index("dp") * local_features, local_features, 0
    )

    local = hidden_local.shape[0]
    hidden_rows = hidden_local.astype(F32)
    scale_here = lax.dynamic_slice_in_dim(out_scale, axis_place * local, local, 0)[:, None]
    layer_out = (hidden_rows + out_sum.astype(F32) * scale_here).astype(BF16)

    inverse = lax.rsqrt(jnp.mean(hidden_rows * hidden_rows, axis=1, keepdims=True) + EPS)
    unit = hidden_rows * inverse
    grad_scaled = in_sum.astype(F32) * gain[0:1]
    grad_hidden = (
        cotangent[0].astype(F32)
        + inverse * (grad_scaled - unit * jnp.mean(grad_scaled * unit, axis=1, keepdims=True))
    ).astype(BF16)

    return (
        layer_out[None],
        grad_hidden[None],
        grad_norm_gain,
        second[:, width:],
        second[:, :width],
        grad_bc,
        first[:, width + 2 * N : width + 2 * N + heads],
        sum_x[0:CONV],
        sum_x[CONV],
        sum_bc[0:CONV],
        sum_bc[CONV],
        sum_head[0, :heads],
        sum_head[1, :heads],
        jnp.sum(sum_x[CONV + 2].reshape(heads, size), axis=1),
        sum_x[CONV + 1],
        first[:, :width],
    )


def solution(mesh):
    in_specs = (
        P("dp", "tensor", None),
        P("dp", "tensor"),
        P("dp", "tensor", None),
        P("dp"),
        P("dp", "tensor"),
        P("dp", "tensor"),
        P("dp", None),
        P("dp", "tensor"),
        P(None, "tensor"),
        P("tensor"),
        P(),
        P(),
        P("tensor"),
        P("tensor"),
        P("tensor"),
        P("tensor"),
        P("dp", "tensor"),
    )
    out_specs = (
        P("dp", "tensor", None),
        P("dp", "tensor", None),
        P("dp"),
        P("dp", "tensor"),
        P("dp", "tensor"),
        P("dp", None),
        P("dp", "tensor"),
        P(None, "tensor"),
        P("tensor"),
        P(),
        P(),
        P("tensor"),
        P("tensor"),
        P("tensor"),
        P("tensor"),
        P("dp", "tensor"),
    )
    return jax.shard_map(shards, mesh=mesh, in_specs=in_specs, out_specs=out_specs, check_vma=False)
```

```python
import functools

import jax
import jax.numpy as jnp
from jax import lax
from jax.experimental import pallas as pl
from jax.experimental.pallas import tpu as pltpu
from jax.sharding import PartitionSpec as P

N = 128
CONV = 4
Q = 256
LANES = 128
HALO = 8
EPS = 1e-05
NEG = -1e30
F32 = jnp.float32
BF16 = jnp.bfloat16
VMEM_LIMIT = 52 * 1024 * 1024


def dot(a, b):
    return jnp.dot(a, b, preferred_element_type=F32)


def dot_nt(a, b):
    return lax.dot_general(a, b, (((1,), (1,)), ((), ())), preferred_element_type=F32)


def dot_tn(a, b):
    return lax.dot_general(a, b, (((0,), (0,)), ((), ())), preferred_element_type=F32)


def dot_exact(a, b):
    return jnp.dot(a, b, preferred_element_type=F32, precision=lax.Precision.HIGHEST)


def spread(cols, heads, size):
    rows = cols.shape[0]
    per = LANES // size
    lane = lax.broadcasted_iota(jnp.int32, (rows, LANES), 1)
    parts = []
    for first in range(0, heads, per):
        part = jnp.broadcast_to(cols[:, first : first + 1], (rows, LANES))
        for extra in range(1, per):
            part = jnp.where(lane < extra * size, part, cols[:, first + extra : first + extra + 1])
        parts.append(part)
    return jnp.concatenate(parts, axis=1)


def head_sums(values, heads, size):
    width = heads * size
    channel = lax.broadcasted_iota(jnp.int32, (width, LANES), 0)
    column = lax.broadcasted_iota(jnp.int32, (width, LANES), 1)
    first = column * size
    picks = jnp.where((channel >= first) & (channel < first + size), 1.0, 0.0).astype(BF16)
    high = values.astype(BF16)
    low = (values - high.astype(F32)).astype(BF16)
    return dot(high, picks) + dot(low, picks)


def widen(tile, width):
    return jnp.concatenate([tile] * (width // tile.shape[1]), axis=1)


def softplus(v):
    return jnp.maximum(v, 0.0) + jnp.log1p(jnp.exp(-jnp.abs(v)))


def sigmoid(v):
    return 1.0 / (1.0 + jnp.exp(-v))


def as_row(column):
    rows = column.shape[0]
    return jnp.broadcast_to(column, (rows, LANES)).T[:8]


def triangle(lower):
    row = lax.broadcasted_iota(jnp.int32, (Q, Q), 0)
    col = lax.broadcasted_iota(jnp.int32, (Q, Q), 1)
    return row >= col if lower else row <= col


def block_masks(window, seg_row):
    seg = window[HALO : HALO + Q]
    before = window[HALO - 1 : HALO]
    last = window[HALO + Q - 1 : HALO + Q]
    from_prev = (seg == before).astype(F32)
    same_last = (seg == last).astype(F32)
    passes = (last == before).astype(F32)
    keep = (widen(seg, Q) == seg_row) & triangle(True)
    bias = jnp.where(keep, 0.0, NEG)
    return seg, from_prev, same_last, passes, bias


def conv_forward(buffer, window, seg, kernel, conv_bias, width):
    total = conv_bias + kernel[CONV - 1 : CONV] * buffer[HALO : HALO + Q, :]
    for back in range(1, CONV):
        match = (window[HALO - back : HALO - back + Q] == seg).astype(F32)
        tap = kernel[CONV - 1 - back : CONV - back]
        total = total + tap * (buffer[HALO - back : HALO - back + Q, :] * widen(match, width))
    return total


def conv_backward(buffer, window, seg, kernel, values, width):
    here = buffer[0:Q, :]
    total = kernel[CONV - 1 : CONV] * here
    taps = [jnp.sum(values * here, axis=0, keepdims=True)]
    for ahead in range(1, CONV):
        match = (window[HALO + ahead : HALO + ahead + Q] == seg).astype(F32)
        moved = buffer[ahead : ahead + Q, :] * widen(match, width)
        total = total + kernel[CONV - 1 - ahead : CONV - ahead] * moved
        taps.append(jnp.sum(values * moved, axis=0, keepdims=True))
    return total, taps


def pick_block(place, near_refs, block):
    reach = len(near_refs) // 2
    away = pl.program_id(0) - place
    for index, ref in enumerate(near_refs):

        @pl.when(away == index - reach)
        def _():
            block[...] = ref[...]


def project_kernel(heads, size, near, place_ref, *refs):
    near_refs, refs = refs[:near], refs[near:]
    weights_ref, hidden_ref, tokens_ref, z_ref, x_ref, bcdt_ref, gain_ref = refs
    width = heads * size

    @pl.when(pl.program_id(0) == 0)
    def _():
        tail_columns = weights_ref[:, 3 * width + 2 * N :].astype(F32).T
        gain_ref[...] = jnp.broadcast_to(tail_columns[heads : heads + 1], gain_ref.shape)

    pick_block(place_ref[0], near_refs, hidden_ref)
    hidden = hidden_ref[...].astype(F32)
    inverse = lax.rsqrt(jnp.mean(hidden * hidden, axis=1, keepdims=True) + EPS)
    tokens = (hidden * inverse * gain_ref[0:1, :]).astype(BF16)
    tokens_ref[...] = tokens
    x_ref[...] = dot(tokens, weights_ref[:, width : 2 * width])
    z_ref[...] = dot(tokens, weights_ref[:, 2 * width : 3 * width])
    bcdt_ref[...] = dot(tokens, weights_ref[:, 3 * width :])


def forward_kernel(
    heads,
    size,
    window_ref,
    seg_row_ref,
    weights_ref,
    kernel_x_ref,
    kernel_bc_ref,
    head_ref,
    channel_ref,
    z_ref,
    x_ref,
    bcdt_ref,
    mixed_ref,
    pre_ref,
    pre_bc_ref,
    state_ref,
    scaled_ref,
    part_ref,
    square_ref,
    x_buffer,
    bc_buffer,
    carry,
):
    step = pl.program_id(0)
    width = heads * size

    @pl.when(step == 0)
    def _():
        x_buffer[0:HALO, :] = jnp.zeros((HALO, width), F32)
        bc_buffer[0:HALO, :] = jnp.zeros((HALO, 2 * N), F32)
        carry[...] = jnp.zeros((N, width), F32)

    window = window_ref[pl.ds(pl.multiple_of(step * Q, Q), Q + 2 * HALO), :]
    seg, from_prev, same_last, passes, bias = block_masks(window, seg_row_ref[0:1, :])
    z_proj = z_ref[...]
    bcdt = bcdt_ref[...]
    x_buffer[HALO : HALO + Q, :] = x_ref[...]
    bc_buffer[HALO : HALO + Q, :] = bcdt[:, : 2 * N]
    pre = conv_forward(
        x_buffer, window, seg, kernel_x_ref[...], kernel_x_ref[CONV : CONV + 1, :], width
    )
    pre_bc = conv_forward(
        bc_buffer, window, seg, kernel_bc_ref[...], kernel_bc_ref[CONV : CONV + 1, :], 2 * N
    )
    x_buffer[0:HALO, :] = x_buffer[Q : Q + HALO, :]
    bc_buffer[0:HALO, :] = bc_buffer[Q : Q + HALO, :]
    pre_ref[...] = pre
    pre_bc_ref[...] = pre_bc
    x_conv = pre * sigmoid(pre)
    bc_conv = (pre_bc * sigmoid(pre_bc)).astype(BF16)
    b_in = bc_conv[:, :N]
    c_in = bc_conv[:, N:]

    dt = softplus(bcdt[:, 2 * N :] + head_ref[0:1, :])
    decay = -dt * jnp.exp(head_ref[1:2, :])
    total = dot_exact(triangle(True).astype(F32), decay)
    total_t = total.T
    weighted = x_conv * spread(dt, heads, size)
    scores = dot_nt(c_in, b_in)
    before = carry[...]
    state_ref[0] = before

    per = LANES // size
    lane = lax.broadcasted_iota(jnp.int32, (Q, LANES), 1)
    inner = []
    for first in range(0, heads, per):
        group = weighted[:, first * size : first * size + LANES]
        summed = jnp.zeros((Q, LANES), F32)
        for extra in range(per):
            h = first + extra
            shape = jnp.exp(total[:, h : h + 1] - total_t[h : h + 1, :] + bias)
            mine = (lane >= extra * size) & (lane < (extra + 1) * size)
            summed = summed + dot(
                (scores * shape).astype(BF16), jnp.where(mine, group, 0.0).astype(BF16)
            )
        inner.append(summed)
    scanned = jnp.concatenate(inner, axis=1)
    scanned = scanned + dot(c_in, before.astype(BF16)) * spread(
        jnp.exp(total) * from_prev, heads, size
    )
    last = total[Q - 1 : Q, :]
    to_end = jnp.exp(last - total) * same_last
    carry[...] = dot_tn(
        b_in, (weighted * spread(to_end, heads, size)).astype(BF16)
    ) + before * spread(jnp.exp(last) * passes, heads, size)

    mixed = scanned + channel_ref[1:2, :] * x_conv
    mixed_ref[...] = mixed
    gated = mixed * (z_proj * sigmoid(z_proj))
    scaled = (gated * channel_ref[0:1, :]).astype(BF16)
    scaled_ref[...] = scaled
    part_ref[...] = dot_nt(scaled, weights_ref[...]).astype(BF16)
    square_ref[...] = as_row(jnp.sum(gated * gated, axis=1, keepdims=True))


def gradient_kernel(width, near, place_ref, *refs):
    near_refs, refs = refs[:near], refs[near:]
    weights_ref, scaled_ref, window_ref, cot_ref, grad_ref, along_ref = refs
    step = pl.program_id(0)
    pick_block(place_ref[0], near_refs, cot_ref)
    window = window_ref[pl.ds(pl.multiple_of(step * Q, Q), Q + 2 * HALO), :]
    live = (window[HALO : HALO + Q] > 0).astype(F32)
    grad = dot(cot_ref[...], weights_ref[...]) * widen(live, width)
    grad_ref[...] = grad
    along_ref[...] = as_row(jnp.sum(scaled_ref[...].astype(F32) * grad, axis=1, keepdims=True))


def backward_kernel(
    heads,
    size,
    full_inner,
    stat_ref,
    hidden_ref,
    window_ref,
    seg_row_ref,
    weights_ref,
    kernel_x_ref,
    kernel_bc_ref,
    head_ref,
    channel_ref,
    z_ref,
    mixed_ref,
    x_ref,
    pre_ref,
    bcdt_ref,
    pre_bc_ref,
    state_ref,
    grad_ref,
    proj_ref,
    left_ref,
    right_ref,
    out_ref,
    sum_x_ref,
    sum_bc_ref,
    sum_head_ref,
    sum_gain_ref,
    x_buffer,
    bc_buffer,
    carry,
    tail,
):
    turn = pl.program_id(0)
    step = pl.num_programs(0) - 1 - turn
    width = heads * size

    @pl.when(turn == 0)
    def _():
        x_buffer[...] = jnp.zeros((Q + HALO, width), F32)
        bc_buffer[...] = jnp.zeros((Q + HALO, 2 * N), F32)
        carry[...] = jnp.zeros((N, width), F32)
        tail[...] = jnp.zeros((8, LANES), F32)
        sum_x_ref[...] = jnp.zeros((8, width), F32)
        sum_bc_ref[...] = jnp.zeros((8, 2 * N), F32)
        sum_head_ref[...] = jnp.zeros((8, LANES), F32)
        sum_gain_ref[...] = jnp.zeros(sum_gain_ref.shape, F32)

    window = window_ref[pl.ds(pl.multiple_of(step * Q, Q), Q + 2 * HALO), :]
    seg, from_prev, same_last, passes, bias = block_masks(window, seg_row_ref[0:1, :])
    live = (seg[:, 0:1] > 0).astype(F32)
    stat = stat_ref[...].T
    gate_inverse = lax.rsqrt(stat[:, 0:1] / full_inner + EPS)
    along = stat[:, 1:2] * (gate_inverse * gate_inverse * gate_inverse / full_inner)

    gain = channel_ref[0:1, :]
    skip = channel_ref[1:2, :]
    z_proj = z_ref[...]
    mixed = mixed_ref[...]
    grad_out = grad_ref[...]
    gate = sigmoid(z_proj)
    opened = z_proj * gate
    gated = mixed * opened
    normal = gated * gate_inverse
    sum_gate = jnp.sum(grad_out * normal, axis=0, keepdims=True)
    out_ref[...] = (normal * gain * live).astype(BF16)
    grad_gated = grad_out * gain * gate_inverse - gated * along
    grad_z = grad_gated * mixed * (gate * (1.0 + z_proj * (1.0 - gate)))
    dy = grad_gated * opened

    pre = pre_ref[...]
    gate_x = sigmoid(pre)
    x_conv = pre * gate_x
    pre_bc = pre_bc_ref[...]
    gate_bc = sigmoid(pre_bc)
    bc_conv = (pre_bc * gate_bc).astype(BF16)
    b_in = bc_conv[:, :N]
    c_in = bc_conv[:, N:]
    bcdt = bcdt_ref[...]
    raw = bcdt[:, 2 * N :] + head_ref[0:1, :]
    dt = softplus(raw)
    rate = jnp.exp(head_ref[1:2, :])
    decay = -dt * rate
    total = dot_exact(triangle(True).astype(F32), decay)
    total_t = total.T
    dt_wide = spread(dt, heads, size)
    weighted = x_conv * dt_wide
    scores = dot_nt(c_in, b_in)
    before = state_ref[0]
    before_low = before.astype(BF16)
    last = total[Q - 1 : Q, :]
    to_end = spread(jnp.exp(last - total) * same_last, heads, size)
    from_start = spread(jnp.exp(total) * from_prev, heads, size)
    after = carry[...]
    after_low = after.astype(BF16)

    dy_low = dy.astype(BF16)
    weighted_low = weighted.astype(BF16)
    dy_start = (dy * from_start).astype(BF16)
    grad_c = dot_nt(dy_start, before_low)
    carried = dot(c_in, before_low)
    returned = dot(b_in, after_low)
    grad_weighted = to_end * returned
    weighted_end = (weighted * to_end).astype(BF16)
    grad_b = dot_nt(weighted_end, after_low)
    new_after = dot_tn(c_in, dy_start) + after * spread(jnp.exp(last) * passes, heads, size)
    carry[...] = new_after

    per = LANES // size
    lane = lax.broadcasted_iota(jnp.int32, (Q, LANES), 1)
    grad_scores = jnp.zeros((Q, Q), F32)
    inner = []
    none = jnp.zeros((Q, LANES), BF16)
    for first in range(0, heads, per):
        at = first * size
        dy_group = dy_low[:, at : at + LANES]
        weighted_group = weighted_low[:, at : at + LANES]
        summed = jnp.zeros((Q, LANES), F32)
        for extra in range(per):
            h = first + extra
            shape = jnp.exp(total[:, h : h + 1] - total_t[h : h + 1, :] + bias)
            mine = (lane >= extra * size) & (lane < (extra + 1) * size)
            dy_mine = jnp.where(mine, dy_group, none)
            grad_scores = grad_scores + dot_nt(dy_mine, weighted_group) * shape
            summed = summed + dot_tn((scores * shape).astype(BF16), dy_mine)
        inner.append(summed)
    grad_inner = jnp.concatenate(inner, axis=1)
    grad_weighted = grad_weighted + grad_inner
    grad_scores = grad_scores.astype(BF16)
    grad_c = grad_c + dot(grad_scores, b_in)
    grad_b = grad_b + dot_tn(grad_scores, c_in)

    scanned = mixed - skip * x_conv - carried * from_start
    pairs = head_sums(
        dy_low.astype(F32) * scanned
        + dy_start.astype(F32) * carried
        - weighted_low.astype(F32) * grad_inner
        - weighted_end.astype(F32) * returned,
        heads,
        size,
    )
    grad_decay = dot_exact(triangle(False).astype(F32), pairs) + tail[0:1, :]
    kept = jnp.sum(new_after.astype(BF16).astype(F32) * before, axis=0, keepdims=True)
    kept = jnp.broadcast_to(kept, (8, width))
    tail[...] = head_sums(kept, heads, size)
    grad_dt = head_sums(grad_weighted * x_conv, heads, size) - grad_decay * rate
    grad_raw = grad_dt * sigmoid(raw)
    sum_head_ref[0:1, :] += jnp.sum(grad_raw, axis=0, keepdims=True)
    sum_head_ref[1:2, :] += jnp.sum(grad_decay * decay, axis=0, keepdims=True)

    grad_x = grad_weighted * dt_wide + skip * dy
    sum_skip = jnp.sum(dy * x_conv, axis=0, keepdims=True)
    grad_pre = grad_x * (gate_x * (1.0 + pre * (1.0 - gate_x)))
    x_buffer[Q : Q + HALO, :] = x_buffer[0:HALO, :]
    x_buffer[0:Q, :] = grad_pre
    grad_proj, taps = conv_backward(
        x_buffer, window, seg, kernel_x_ref[...], x_ref[...], width
    )
    sum_bias = jnp.sum(grad_pre, axis=0, keepdims=True)
    blank = jnp.zeros((1, width), F32)
    sum_x_ref[...] += jnp.concatenate(
        [taps[3], taps[2], taps[1], taps[0], sum_bias, sum_gate, sum_skip, blank], axis=0
    )

    grad_pre_bc = jnp.concatenate([grad_b, grad_c], axis=1) * (
        gate_bc * (1.0 + pre_bc * (1.0 - gate_bc))
    )
    bc_buffer[Q : Q + HALO, :] = bc_buffer[0:HALO, :]
    bc_buffer[0:Q, :] = grad_pre_bc
    grad_bc, taps_bc = conv_backward(
        bc_buffer, window, seg, kernel_bc_ref[...], bcdt[:, : 2 * N], 2 * N
    )
    sum_bias_bc = jnp.sum(grad_pre_bc, axis=0, keepdims=True)
    blank_bc = jnp.zeros((3, 2 * N), F32)
    sum_bc_ref[...] += jnp.concatenate(
        [taps_bc[3], taps_bc[2], taps_bc[1], taps_bc[0], sum_bias_bc, blank_bc], axis=0
    )

    grads = jnp.concatenate(
        [
            grad_proj.astype(BF16),
            grad_z.astype(BF16),
            grad_bc.astype(BF16),
            grad_raw.astype(BF16),
        ],
        axis=1,
    )
    proj_ref[...] = grads
    part = dot_nt(grads, weights_ref[:, width:])
    left_ref[...] = part[:, : part.shape[1] // 2].astype(BF16)
    right_ref[...] = part[:, part.shape[1] // 2 :].astype(BF16)
    hidden = hidden_ref[...].astype(F32)
    inverse = lax.rsqrt(jnp.mean(hidden * hidden, axis=1, keepdims=True) + EPS)
    sum_gain_ref[0:1, :] += jnp.sum(part * (hidden * inverse), axis=0, keepdims=True)


def cost(micros):
    return pl.CostEstimate(flops=int(micros * 1e9), bytes_accessed=1 << 20, transcendentals=0)


def whole(shape):
    return pl.BlockSpec(shape, lambda i: (0,) * len(shape))


def scalar():
    return pl.BlockSpec(memory_space=pltpu.SMEM)


def run_project(heads, size, place, near, weights):
    features = near[0].shape[1]
    blocks = len(near) // 2 + 1
    length = blocks * Q
    width = heads * size
    rest = 2 * N + LANES

    def rows(columns):
        return pl.BlockSpec((Q, columns), lambda i: (i, 0))

    def made(columns, dtype):
        return jax.ShapeDtypeStruct((length, columns), dtype)

    return pl.pallas_call(
        functools.partial(project_kernel, heads, size, len(near)),
        grid=(blocks,),
        in_specs=[scalar(), *[whole(block.shape) for block in near], whole(weights.shape)],
        out_specs=[
            rows(features),
            rows(features),
            rows(width),
            rows(width),
            rows(rest),
            whole((8, features)),
        ],
        out_shape=[
            made(features, BF16),
            made(features, BF16),
            made(width, F32),
            made(width, F32),
            made(rest, F32),
            jax.ShapeDtypeStruct((8, features), F32),
        ],
        compiler_params=pltpu.CompilerParams(vmem_limit_bytes=VMEM_LIMIT),
        cost_estimate=cost(8),
        name="project",
    )(place, *near, weights)


def run_forward(
    heads, size, window, seg_row, weights, kernel_x, kernel_bc, head, channel, z_proj, x_proj, bcdt
):
    length, features = seg_row.shape[1], weights.shape[0]
    width = heads * size
    blocks = length // Q

    def rows(columns):
        return pl.BlockSpec((Q, columns), lambda i: (i, 0))

    def made(columns, dtype):
        return jax.ShapeDtypeStruct((length, columns), dtype)

    across = pl.BlockSpec((8, Q), lambda i: (0, i))
    return pl.pallas_call(
        functools.partial(forward_kernel, heads, size),
        grid=(blocks,),
        in_specs=[
            whole(window.shape),
            across,
            whole((features, width)),
            whole(kernel_x.shape),
            whole(kernel_bc.shape),
            whole(head.shape),
            whole(channel.shape),
            rows(width),
            rows(width),
            rows(bcdt.shape[1]),
        ],
        out_specs=[
            rows(width),
            rows(width),
            rows(2 * N),
            pl.BlockSpec((1, N, width), lambda i: (i, 0, 0)),
            rows(width),
            rows(features),
            across,
        ],
        out_shape=[
            made(width, F32),
            made(width, F32),
            made(2 * N, F32),
            jax.ShapeDtypeStruct((blocks, N, width), F32),
            made(width, BF16),
            made(features, BF16),
            jax.ShapeDtypeStruct((8, length), F32),
        ],
        scratch_shapes=[
            pltpu.VMEM((Q + HALO, width), F32),
            pltpu.VMEM((Q + HALO, 2 * N), F32),
            pltpu.VMEM((N, width), F32),
        ],
        compiler_params=pltpu.CompilerParams(vmem_limit_bytes=VMEM_LIMIT),
        cost_estimate=cost(14),
        name="forward",
    )(window, seg_row, weights, kernel_x, kernel_bc, head, channel, z_proj, x_proj, bcdt)


def run_gradient(place, near, weights, scaled, window):
    features = near[0].shape[1]
    length, width = scaled.shape
    return pl.pallas_call(
        functools.partial(gradient_kernel, width, len(near)),
        grid=(length // Q,),
        in_specs=[
            scalar(),
            *[whole(block.shape) for block in near],
            whole((features, width)),
            pl.BlockSpec((Q, width), lambda i: (i, 0)),
            whole(window.shape),
        ],
        out_specs=[
            pl.BlockSpec((Q, features), lambda i: (i, 0)),
            pl.BlockSpec((Q, width), lambda i: (i, 0)),
            pl.BlockSpec((8, Q), lambda i: (0, i)),
        ],
        out_shape=[
            jax.ShapeDtypeStruct((length, features), BF16),
            jax.ShapeDtypeStruct((length, width), F32),
            jax.ShapeDtypeStruct((8, length), F32),
        ],
        compiler_params=pltpu.CompilerParams(vmem_limit_bytes=VMEM_LIMIT),
        cost_estimate=cost(5),
        name="out_gradient",
    )(place, *near, weights, scaled, window)


def weights_kernel(width, cot_ref, normed_ref, tokens_ref, grads_ref, first_ref, second_ref):
    tokens = tokens_ref[...]
    first_ref[:, :width] = dot_tn(cot_ref[...], normed_ref[...]).astype(BF16)
    first_ref[:, width:] = dot_tn(tokens, grads_ref[:, 2 * width :]).astype(BF16)
    second_ref[...] = dot_tn(tokens, grads_ref[:, : 2 * width]).astype(BF16)


def run_weights(cot, normed, tokens, grads):
    length, features = tokens.shape
    width = normed.shape[1]
    columns = [grads.shape[1] - width, 2 * width]
    return pl.pallas_call(
        functools.partial(weights_kernel, width),
        grid=(features // Q,),
        in_specs=[
            pl.BlockSpec((length, Q), lambda i: (0, i)),
            whole(normed.shape),
            pl.BlockSpec((length, Q), lambda i: (0, i)),
            whole(grads.shape),
        ],
        out_specs=[pl.BlockSpec((Q, count), lambda i: (i, 0)) for count in columns],
        out_shape=[jax.ShapeDtypeStruct((features, count), BF16) for count in columns],
        compiler_params=pltpu.CompilerParams(vmem_limit_bytes=VMEM_LIMIT),
        cost_estimate=cost(7),
        name="weight_gradients",
    )(cot, normed, tokens, grads)


def run_backward(
    heads, size, full_inner, stat, hidden, window, seg_row, weights, kernel_x, kernel_bc, head, channel,
    z_proj, mixed, x_proj, pre, bcdt, pre_bc, states, grad_out,
):
    length, features = hidden.shape
    width = heads * size
    blocks = length // Q
    rest = 2 * N + LANES
    total = 2 * width + rest

    def rows(columns):
        return pl.BlockSpec((Q, columns), lambda i: (blocks - 1 - i, 0))

    def made(columns, dtype):
        return jax.ShapeDtypeStruct((length, columns), dtype)

    across = pl.BlockSpec((8, Q), lambda i: (0, blocks - 1 - i))
    sums = [(8, width), (8, 2 * N), (8, LANES), (8, features)]
    return pl.pallas_call(
        functools.partial(backward_kernel, heads, size, full_inner),
        grid=(blocks,),
        in_specs=[
            across,
            rows(features),
            whole(window.shape),
            across,
            whole(weights.shape),
            whole(kernel_x.shape),
            whole(kernel_bc.shape),
            whole(head.shape),
            whole(channel.shape),
            rows(width),
            rows(width),
            rows(width),
            rows(width),
            rows(rest),
            rows(2 * N),
            pl.BlockSpec((1, N, width), lambda i: (blocks - 1 - i, 0, 0)),
            rows(width),
        ],
        out_specs=[rows(total), rows(features // 2), rows(features // 2), rows(width)]
        + [whole(shape) for shape in sums],
        out_shape=[made(total, BF16), made(features // 2, BF16), made(features // 2, BF16), made(width, BF16)]
        + [jax.ShapeDtypeStruct(shape, F32) for shape in sums],
        scratch_shapes=[
            pltpu.VMEM((Q + HALO, width), F32),
            pltpu.VMEM((Q + HALO, 2 * N), F32),
            pltpu.VMEM((N, width), F32),
            pltpu.VMEM((8, LANES), F32),
        ],
        compiler_params=pltpu.CompilerParams(vmem_limit_bytes=VMEM_LIMIT),
        cost_estimate=cost(27),
        name="backward",
    )(
        stat, hidden, window, seg_row, weights, kernel_x, kernel_bc, head, channel,
        z_proj, mixed, x_proj, pre, bcdt, pre_bc, states, grad_out,
    )


def finish_kernel(left_ref, right_ref, hidden_ref, cot_ref, gain_ref, out_ref):
    grad = jnp.concatenate([left_ref[...], right_ref[...]], axis=1).astype(F32)
    grad = grad * gain_ref[0:1, :]
    hidden = hidden_ref[...].astype(F32)
    inverse = lax.rsqrt(jnp.mean(hidden * hidden, axis=1, keepdims=True) + EPS)
    unit = hidden * inverse
    along = jnp.mean(grad * unit, axis=1, keepdims=True)
    out_ref[...] = (cot_ref[...].astype(F32) + inverse * (grad - unit * along)).astype(BF16)


def run_finish(in_sums, hidden, cot, gain):
    length, features = hidden.shape
    rows = pl.BlockSpec((length // 2, features), lambda i: (i, 0))
    halves = pl.BlockSpec((length // 2, features // 2), lambda i: (i, 0))
    return pl.pallas_call(
        finish_kernel,
        grid=(2,),
        in_specs=[halves, halves, rows, rows, whole(gain.shape)],
        out_specs=rows,
        out_shape=jax.ShapeDtypeStruct(hidden.shape, BF16),
        compiler_params=pltpu.CompilerParams(vmem_limit_bytes=VMEM_LIMIT),
        name="finish",
    )(*in_sums, hidden, cot, gain)


def pad_lanes(values):
    return jnp.pad(values, ((0, 0), (0, LANES - values.shape[1])))


def after(value, *others):
    return lax.optimization_barrier((value, *others))[0]


def line_step(right, left, step, axis):
    n = lax.axis_size(axis)
    return (
        lax.ppermute(right, axis, [(i, i + 1) for i in range(step - 1, n - 1)]),
        lax.ppermute(left, axis, [(i, i - 1) for i in range(1, n - step + 1)]),
    )


def line_order(block, moved):
    return [pair[0] for pair in moved[::-1]] + [block] + [pair[1] for pair in moved]


def line_gather(block, axis):
    right = left = block
    moved = []
    for step in range(1, lax.axis_size(axis)):
        right, left = line_step(right, left, step, axis)
        moved.append((right, left))
    return line_order(block, moved)


def cube_scatter(part, axis, upward):
    n = lax.axis_size(axis)
    if n & (n - 1):
        part = lax.psum_scatter(part, axis, scatter_dimension=0, tiled=True).astype(F32)
        return part, part
    first = None
    place = lax.axis_index(axis)
    rows, columns = part.shape
    bits = list(range(n.bit_length() - 1))
    order = bits if upward else bits[:1] + bits[:0:-1]
    left = bits[::-1]
    part = part.reshape((2,) * len(bits) + (rows // n, columns))
    for bit in order:
        dim = left.index(bit)
        mine = (place >> bit) & 1
        keep = lax.dynamic_index_in_dim(part, mine, dim, keepdims=False)
        send = lax.dynamic_index_in_dim(part, 1 - mine, dim, keepdims=False)
        other = lax.ppermute(send, axis, [(i, i ^ (1 << bit)) for i in range(n)])
        first = other if first is None else first
        part = keep.astype(F32) + other.astype(F32)
        left.remove(bit)
        if left:
            part = part.astype(BF16)
    return part, first


def around(values, axis):
    n = lax.axis_size(axis)
    return [values] + [
        lax.ppermute(values, axis, [(i, (i - k) % n) for i in range(n)]) for k in range(1, n)
    ]


def sum_around(values, axis):
    return functools.reduce(jnp.add, around(values, axis))


def sum_pairwise(values, axis):
    n = lax.axis_size(axis)
    if n & (n - 1):
        return lax.psum(values, axis)
    bit = 1
    while bit < n:
        values = values + lax.ppermute(values, axis, [(i, i ^ bit) for i in range(n)])
        bit *= 2
    return values


def shards(
    hidden,
    seg_ids,
    cotangent,
    norm_gain,
    w_in_z,
    w_in_x,
    w_in_bc,
    w_in_dt,
    conv_x,
    conv_x_bias,
    conv_bc,
    conv_bc_bias,
    dt_bias,
    a_log,
    d_skip,
    gate_gain,
    w_out,
):
    heads = dt_bias.shape[0]
    width = gate_gain.shape[0]
    size = width // heads
    full_inner = width * lax.axis_size("tensor")
    features = hidden.shape[2]
    hidden_local = hidden[0]

    steps = jnp.pad(
        jnp.concatenate([w_in_dt, norm_gain[:, None]], axis=1), ((0, 0), (0, LANES - heads - 1))
    )
    packed = jnp.concatenate([w_out, w_in_x, w_in_z, w_in_bc, steps], axis=1)
    n = lax.axis_size("tensor")
    axis_place = lax.axis_index("tensor")
    place = axis_place[None]
    near_hidden = line_gather(hidden_local, "tensor")
    weights = lax.all_gather(packed, "dp", axis=0, tiled=True)
    seg_stack = around(seg_ids[0], "tensor")
    count = seg_ids.shape[1]
    seg_full = lax.dynamic_slice_in_dim(
        jnp.concatenate(seg_stack + seg_stack), (n - axis_place) * count, n * count, 0
    )
    window = jnp.broadcast_to(
        jnp.pad(seg_full, (HALO, HALO), constant_values=-1)[:, None],
        (seg_full.shape[0] + 2 * HALO, LANES),
    )
    seg_row = jnp.broadcast_to(seg_full[None, :], (8, seg_full.shape[0]))
    kernel_x = jnp.concatenate([conv_x, conv_x_bias[None, :]], axis=0)
    kernel_bc = jnp.concatenate([conv_bc, conv_bc_bias[None, :]], axis=0)
    head = pad_lanes(jnp.stack([dt_bias, a_log]))
    channel = jnp.stack([gate_gain, jnp.repeat(d_skip, size)])

    hidden_full, tokens, z_proj, x_proj, bcdt, gain = run_project(
        heads, size, place, near_hidden, weights
    )
    right = left = after(cotangent[0], near_hidden[0], near_hidden[-1])
    moved = []
    right, left = line_step(right, left, 1, "tensor")
    moved.append((right, left))
    bcdt = after(bcdt, right, left)
    right, left = line_step(after(right, gain), after(left, gain), 2, "tensor")
    moved.append((right, left))
    mixed, pre, pre_bc, states, scaled, out_part, square = run_forward(
        heads, size, window, seg_row, weights, kernel_x, kernel_bc, head, channel, z_proj, x_proj,
        bcdt,
    )
    for step in range(3, n):
        right, left = line_step(after(right, square), after(left, square), step, "tensor")
        moved.append((right, left))
    near_cot = line_order(cotangent[0], moved)
    cot_full, grad_out, along = run_gradient(place, near_cot, weights, scaled, window)
    out_sum = lax.psum_scatter(
        after(out_part, along), "tensor", scatter_dimension=0, tiled=True
    )
    stat = sum_around(jnp.stack([square[0], along[0]]), "tensor")
    stat_full = jnp.pad(stat, ((0, 6), (0, 0)))
    out_scale = lax.rsqrt(stat[0] / full_inner + EPS) * (seg_full > 0).astype(F32)

    grads, *in_parts, normed_out, sum_x, sum_bc, sum_head, sum_gain = run_backward(
        heads, size, full_inner, stat_full, hidden_full, window, seg_row, weights, kernel_x,
        kernel_bc, head, channel, z_proj, mixed, x_proj, pre, bcdt, pre_bc, states, grad_out,
    )
    in_sums = [
        lax.psum_scatter(half, "tensor", scatter_dimension=0, tiled=True)
        for half in in_parts
    ]
    first, second = run_weights(cot_full, normed_out, tokens, after(grads, out_sum))
    first, _ = cube_scatter(first, "dp", True)
    second, arrived = cube_scatter(second, "dp", False)
    own = jnp.concatenate([sum_x.reshape(-1, LANES), sum_head])
    both = jnp.concatenate([sum_gain[0].reshape(-1, LANES), sum_bc.reshape(-1, LANES)])
    small = sum_pairwise(after(jnp.concatenate([own, both]), arrived), "dp")
    sum_x = small[: own.shape[0] - 8].reshape(8, width)
    sum_head = small[own.shape[0] - 8 : own.shape[0]]
    grad_bc = first[:, width : width + 2 * N]
    shared = jnp.concatenate([small[own.shape[0] :], grad_bc.reshape(-1, LANES)])
    shared = sum_around(shared, "tensor")
    gain_rows = features // LANES
    sum_gain = shared[:gain_rows].reshape(features)
    sum_bc = shared[gain_rows : both.shape[0]].reshape(8, 2 * N)
    grad_bc = shared[both.shape[0] :].reshape(grad_bc.shape)
    local_features = norm_gain.shape[0]
    grad_norm_gain = lax.dynamic_slice_in_dim(
        sum_gain, lax.axis_index("dp") * local_features, local_features, 0
    )

    local = hidden_local.shape[0]
    hidden_rows = hidden_local.astype(F32)
    scale_here = lax.dynamic_slice_in_dim(out_scale, axis_place * local, local, 0)[:, None]
    layer_out = (hidden_rows + out_sum.astype(F32) * scale_here).astype(BF16)

    grad_hidden = run_finish(in_sums, hidden_local, cotangent[0], after(gain, shared))

    return (
        layer_out[None],
        grad_hidden[None],
        grad_norm_gain,
        second[:, width:],
        second[:, :width],
        grad_bc,
        first[:, width + 2 * N : width + 2 * N + heads],
        sum_x[0:CONV],
        sum_x[CONV],
        sum_bc[0:CONV],
        sum_bc[CONV],
        sum_head[0, :heads],
        sum_head[1, :heads],
        jnp.sum(sum_x[CONV + 2].reshape(heads, size), axis=1),
        sum_x[CONV + 1],
        first[:, :width],
    )


def solution(mesh):
    in_specs = (
        P("dp", "tensor", None),
        P("dp", "tensor"),
        P("dp", "tensor", None),
        P("dp"),
        P("dp", "tensor"),
        P("dp", "tensor"),
        P("dp", None),
        P("dp", "tensor"),
        P(None, "tensor"),
        P("tensor"),
        P(),
        P(),
        P("tensor"),
        P("tensor"),
        P("tensor"),
        P("tensor"),
        P("dp", "tensor"),
    )
    out_specs = (
        P("dp", "tensor", None),
        P("dp", "tensor", None),
        P("dp"),
        P("dp", "tensor"),
        P("dp", "tensor"),
        P("dp", None),
        P("dp", "tensor"),
        P(None, "tensor"),
        P("tensor"),
        P(),
        P(),
        P("tensor"),
        P("tensor"),
        P("tensor"),
        P("tensor"),
        P("dp", "tensor"),
    )
    return jax.shard_map(shards, mesh=mesh, in_specs=in_specs, out_specs=out_specs, check_vma=False)
```

```python
import functools

import jax
import jax.numpy as jnp
from jax import lax
from jax.experimental import pallas as pl
from jax.experimental.pallas import tpu as pltpu
from jax.sharding import PartitionSpec as P

N = 128
CONV = 4
Q = 256
LANES = 128
HALO = 8
EPS = 1e-05
NEG = -1e30
F32 = jnp.float32
BF16 = jnp.bfloat16
VMEM_LIMIT = 52 * 1024 * 1024


def dot(a, b):
    return jnp.dot(a, b, preferred_element_type=F32)


def dot_nt(a, b):
    return lax.dot_general(a, b, (((1,), (1,)), ((), ())), preferred_element_type=F32)


def dot_tn(a, b):
    return lax.dot_general(a, b, (((0,), (0,)), ((), ())), preferred_element_type=F32)


def dot_exact(a, b):
    return jnp.dot(a, b, preferred_element_type=F32, precision=lax.Precision.HIGHEST)


def spread(cols, heads, size):
    rows = cols.shape[0]
    per = LANES // size
    lane = lax.broadcasted_iota(jnp.int32, (rows, LANES), 1)
    parts = []
    for first in range(0, heads, per):
        part = jnp.broadcast_to(cols[:, first : first + 1], (rows, LANES))
        for extra in range(1, per):
            part = jnp.where(lane < extra * size, part, cols[:, first + extra : first + extra + 1])
        parts.append(part)
    return jnp.concatenate(parts, axis=1)


def head_sums(values, heads, size):
    width = heads * size
    channel = lax.broadcasted_iota(jnp.int32, (width, LANES), 0)
    column = lax.broadcasted_iota(jnp.int32, (width, LANES), 1)
    first = column * size
    picks = jnp.where((channel >= first) & (channel < first + size), 1.0, 0.0).astype(BF16)
    high = values.astype(BF16)
    low = (values - high.astype(F32)).astype(BF16)
    return dot(high, picks) + dot(low, picks)


def widen(tile, width):
    return jnp.concatenate([tile] * (width // tile.shape[1]), axis=1)


def softplus(v):
    return jnp.maximum(v, 0.0) + jnp.log1p(jnp.exp(-jnp.abs(v)))


def sigmoid(v):
    return 1.0 / (1.0 + jnp.exp(-v))


def as_row(column):
    rows = column.shape[0]
    return jnp.broadcast_to(column, (rows, LANES)).T[:8]


def triangle(lower):
    row = lax.broadcasted_iota(jnp.int32, (Q, Q), 0)
    col = lax.broadcasted_iota(jnp.int32, (Q, Q), 1)
    return row >= col if lower else row <= col


def block_masks(window, seg_row):
    seg = window[HALO : HALO + Q]
    before = window[HALO - 1 : HALO]
    last = window[HALO + Q - 1 : HALO + Q]
    from_prev = (seg == before).astype(F32)
    same_last = (seg == last).astype(F32)
    passes = (last == before).astype(F32)
    keep = (widen(seg, Q) == seg_row) & triangle(True)
    bias = jnp.where(keep, 0.0, NEG)
    return seg, from_prev, same_last, passes, bias


def conv_forward(buffer, window, seg, kernel, conv_bias, width):
    total = conv_bias + kernel[CONV - 1 : CONV] * buffer[HALO : HALO + Q, :]
    for back in range(1, CONV):
        match = (window[HALO - back : HALO - back + Q] == seg).astype(F32)
        tap = kernel[CONV - 1 - back : CONV - back]
        total = total + tap * (buffer[HALO - back : HALO - back + Q, :] * widen(match, width))
    return total


def conv_backward(buffer, window, seg, kernel, values, width):
    here = buffer[0:Q, :]
    total = kernel[CONV - 1 : CONV] * here
    taps = [jnp.sum(values * here, axis=0, keepdims=True)]
    for ahead in range(1, CONV):
        match = (window[HALO + ahead : HALO + ahead + Q] == seg).astype(F32)
        moved = buffer[ahead : ahead + Q, :] * widen(match, width)
        total = total + kernel[CONV - 1 - ahead : CONV - ahead] * moved
        taps.append(jnp.sum(values * moved, axis=0, keepdims=True))
    return total, taps


def pick_block(place, near_refs, block):
    reach = len(near_refs) // 2
    away = pl.program_id(0) - place
    for index, ref in enumerate(near_refs):

        @pl.when(away == index - reach)
        def _():
            block[...] = ref[...]


def project_kernel(heads, size, near, place_ref, *refs):
    near_refs, refs = refs[:near], refs[near:]
    weights_ref, hidden_ref, tokens_ref, z_ref, x_ref, bcdt_ref, gain_ref = refs
    width = heads * size

    @pl.when(pl.program_id(0) == 0)
    def _():
        tail_columns = weights_ref[:, 3 * width + 2 * N :].astype(F32).T
        gain_ref[...] = jnp.broadcast_to(tail_columns[heads : heads + 1], gain_ref.shape)

    pick_block(place_ref[0], near_refs, hidden_ref)
    hidden = hidden_ref[...].astype(F32)
    inverse = lax.rsqrt(jnp.mean(hidden * hidden, axis=1, keepdims=True) + EPS)
    tokens = (hidden * inverse * gain_ref[0:1, :]).astype(BF16)
    tokens_ref[...] = tokens
    x_ref[...] = dot(tokens, weights_ref[:, width : 2 * width])
    z_ref[...] = dot(tokens, weights_ref[:, 2 * width : 3 * width])
    bcdt_ref[...] = dot(tokens, weights_ref[:, 3 * width :])


def forward_kernel(
    heads,
    size,
    window_ref,
    seg_row_ref,
    weights_ref,
    kernel_x_ref,
    kernel_bc_ref,
    head_ref,
    channel_ref,
    z_ref,
    x_ref,
    bcdt_ref,
    mixed_ref,
    pre_ref,
    pre_bc_ref,
    state_ref,
    scaled_ref,
    part_ref,
    square_ref,
    x_buffer,
    bc_buffer,
    carry,
):
    step = pl.program_id(0)
    width = heads * size

    @pl.when(step == 0)
    def _():
        x_buffer[0:HALO, :] = jnp.zeros((HALO, width), F32)
        bc_buffer[0:HALO, :] = jnp.zeros((HALO, 2 * N), F32)
        carry[...] = jnp.zeros((N, width), F32)

    window = window_ref[pl.ds(pl.multiple_of(step * Q, Q), Q + 2 * HALO), :]
    seg, from_prev, same_last, passes, bias = block_masks(window, seg_row_ref[0:1, :])
    z_proj = z_ref[...]
    bcdt = bcdt_ref[...]
    x_buffer[HALO : HALO + Q, :] = x_ref[...]
    bc_buffer[HALO : HALO + Q, :] = bcdt[:, : 2 * N]
    pre = conv_forward(
        x_buffer, window, seg, kernel_x_ref[...], kernel_x_ref[CONV : CONV + 1, :], width
    )
    pre_bc = conv_forward(
        bc_buffer, window, seg, kernel_bc_ref[...], kernel_bc_ref[CONV : CONV + 1, :], 2 * N
    )
    x_buffer[0:HALO, :] = x_buffer[Q : Q + HALO, :]
    bc_buffer[0:HALO, :] = bc_buffer[Q : Q + HALO, :]
    pre_ref[...] = pre
    pre_bc_ref[...] = pre_bc
    x_conv = pre * sigmoid(pre)
    bc_conv = (pre_bc * sigmoid(pre_bc)).astype(BF16)
    b_in = bc_conv[:, :N]
    c_in = bc_conv[:, N:]

    dt = softplus(bcdt[:, 2 * N :] + head_ref[0:1, :])
    decay = -dt * jnp.exp(head_ref[1:2, :])
    total = dot_exact(triangle(True).astype(F32), decay)
    total_t = total.T
    weighted = x_conv * spread(dt, heads, size)
    scores = dot_nt(c_in, b_in)
    before = carry[...]
    state_ref[0] = before

    per = LANES // size
    lane = lax.broadcasted_iota(jnp.int32, (Q, LANES), 1)
    inner = []
    for first in range(0, heads, per):
        group = weighted[:, first * size : first * size + LANES]
        summed = jnp.zeros((Q, LANES), F32)
        for extra in range(per):
            h = first + extra
            shape = jnp.exp(total[:, h : h + 1] - total_t[h : h + 1, :] + bias)
            mine = (lane >= extra * size) & (lane < (extra + 1) * size)
            summed = summed + dot(
                (scores * shape).astype(BF16), jnp.where(mine, group, 0.0).astype(BF16)
            )
        inner.append(summed)
    scanned = jnp.concatenate(inner, axis=1)
    scanned = scanned + dot(c_in, before.astype(BF16)) * spread(
        jnp.exp(total) * from_prev, heads, size
    )
    last = total[Q - 1 : Q, :]
    to_end = jnp.exp(last - total) * same_last
    carry[...] = dot_tn(
        b_in, (weighted * spread(to_end, heads, size)).astype(BF16)
    ) + before * spread(jnp.exp(last) * passes, heads, size)

    mixed = scanned + channel_ref[1:2, :] * x_conv
    mixed_ref[...] = mixed
    gated = mixed * (z_proj * sigmoid(z_proj))
    scaled = (gated * channel_ref[0:1, :]).astype(BF16)
    scaled_ref[...] = scaled
    part_ref[...] = dot_nt(scaled, weights_ref[...]).astype(BF16)
    square_ref[...] = as_row(jnp.sum(gated * gated, axis=1, keepdims=True))


def gradient_kernel(width, near, place_ref, *refs):
    near_refs, refs = refs[:near], refs[near:]
    weights_ref, scaled_ref, window_ref, cot_ref, grad_ref, along_ref = refs
    step = pl.program_id(0)
    pick_block(place_ref[0], near_refs, cot_ref)
    window = window_ref[pl.ds(pl.multiple_of(step * Q, Q), Q + 2 * HALO), :]
    live = (window[HALO : HALO + Q] > 0).astype(F32)
    grad = dot(cot_ref[...], weights_ref[...]) * widen(live, width)
    grad_ref[...] = grad
    along_ref[...] = as_row(jnp.sum(scaled_ref[...].astype(F32) * grad, axis=1, keepdims=True))


def backward_kernel(
    heads,
    size,
    full_inner,
    stat_ref,
    hidden_ref,
    window_ref,
    seg_row_ref,
    weights_ref,
    kernel_x_ref,
    kernel_bc_ref,
    head_ref,
    channel_ref,
    z_ref,
    mixed_ref,
    x_ref,
    pre_ref,
    bcdt_ref,
    pre_bc_ref,
    state_ref,
    grad_ref,
    proj_ref,
    part_ref,
    out_ref,
    sum_x_ref,
    sum_bc_ref,
    sum_head_ref,
    sum_gain_ref,
    x_buffer,
    bc_buffer,
    carry,
    tail,
):
    turn = pl.program_id(0)
    step = pl.num_programs(0) - 1 - turn
    width = heads * size

    @pl.when(turn == 0)
    def _():
        x_buffer[...] = jnp.zeros((Q + HALO, width), F32)
        bc_buffer[...] = jnp.zeros((Q + HALO, 2 * N), F32)
        carry[...] = jnp.zeros((N, width), F32)
        tail[...] = jnp.zeros((8, LANES), F32)
        sum_x_ref[...] = jnp.zeros((8, width), F32)
        sum_bc_ref[...] = jnp.zeros((8, 2 * N), F32)
        sum_head_ref[...] = jnp.zeros((8, LANES), F32)
        sum_gain_ref[...] = jnp.zeros(sum_gain_ref.shape, F32)

    window = window_ref[pl.ds(pl.multiple_of(step * Q, Q), Q + 2 * HALO), :]
    seg, from_prev, same_last, passes, bias = block_masks(window, seg_row_ref[0:1, :])
    live = (seg[:, 0:1] > 0).astype(F32)
    stat = stat_ref[...].T
    gate_inverse = lax.rsqrt(stat[:, 0:1] / full_inner + EPS)
    along = stat[:, 1:2] * (gate_inverse * gate_inverse * gate_inverse / full_inner)

    gain = channel_ref[0:1, :]
    skip = channel_ref[1:2, :]
    z_proj = z_ref[...]
    mixed = mixed_ref[...]
    grad_out = grad_ref[...]
    gate = sigmoid(z_proj)
    opened = z_proj * gate
    gated = mixed * opened
    normal = gated * gate_inverse
    sum_gate = jnp.sum(grad_out * normal, axis=0, keepdims=True)
    out_ref[...] = (normal * gain * live).astype(BF16)
    grad_gated = grad_out * gain * gate_inverse - gated * along
    grad_z = grad_gated * mixed * (gate * (1.0 + z_proj * (1.0 - gate)))
    dy = grad_gated * opened

    pre = pre_ref[...]
    gate_x = sigmoid(pre)
    x_conv = pre * gate_x
    pre_bc = pre_bc_ref[...]
    gate_bc = sigmoid(pre_bc)
    bc_conv = (pre_bc * gate_bc).astype(BF16)
    b_in = bc_conv[:, :N]
    c_in = bc_conv[:, N:]
    bcdt = bcdt_ref[...]
    raw = bcdt[:, 2 * N :] + head_ref[0:1, :]
    dt = softplus(raw)
    rate = jnp.exp(head_ref[1:2, :])
    decay = -dt * rate
    total = dot_exact(triangle(True).astype(F32), decay)
    total_t = total.T
    dt_wide = spread(dt, heads, size)
    weighted = x_conv * dt_wide
    scores = dot_nt(c_in, b_in)
    before = state_ref[0]
    before_low = before.astype(BF16)
    last = total[Q - 1 : Q, :]
    to_end = spread(jnp.exp(last - total) * same_last, heads, size)
    from_start = spread(jnp.exp(total) * from_prev, heads, size)
    after = carry[...]
    after_low = after.astype(BF16)

    dy_low = dy.astype(BF16)
    weighted_low = weighted.astype(BF16)
    dy_start = (dy * from_start).astype(BF16)
    grad_c = dot_nt(dy_start, before_low)
    carried = dot(c_in, before_low)
    returned = dot(b_in, after_low)
    grad_weighted = to_end * returned
    weighted_end = (weighted * to_end).astype(BF16)
    grad_b = dot_nt(weighted_end, after_low)
    new_after = dot_tn(c_in, dy_start) + after * spread(jnp.exp(last) * passes, heads, size)
    carry[...] = new_after

    per = LANES // size
    lane = lax.broadcasted_iota(jnp.int32, (Q, LANES), 1)
    grad_scores = jnp.zeros((Q, Q), F32)
    inner = []
    none = jnp.zeros((Q, LANES), BF16)
    for first in range(0, heads, per):
        at = first * size
        dy_group = dy_low[:, at : at + LANES]
        weighted_group = weighted_low[:, at : at + LANES]
        summed = jnp.zeros((Q, LANES), F32)
        for extra in range(per):
            h = first + extra
            shape = jnp.exp(total[:, h : h + 1] - total_t[h : h + 1, :] + bias)
            mine = (lane >= extra * size) & (lane < (extra + 1) * size)
            dy_mine = jnp.where(mine, dy_group, none)
            grad_scores = grad_scores + dot_nt(dy_mine, weighted_group) * shape
            summed = summed + dot_tn((scores * shape).astype(BF16), dy_mine)
        inner.append(summed)
    grad_inner = jnp.concatenate(inner, axis=1)
    grad_weighted = grad_weighted + grad_inner
    grad_scores = grad_scores.astype(BF16)
    grad_c = grad_c + dot(grad_scores, b_in)
    grad_b = grad_b + dot_tn(grad_scores, c_in)

    scanned = mixed - skip * x_conv - carried * from_start
    pairs = head_sums(
        dy_low.astype(F32) * scanned
        + dy_start.astype(F32) * carried
        - weighted_low.astype(F32) * grad_inner
        - weighted_end.astype(F32) * returned,
        heads,
        size,
    )
    grad_decay = dot_exact(triangle(False).astype(F32), pairs) + tail[0:1, :]
    kept = jnp.sum(new_after.astype(BF16).astype(F32) * before, axis=0, keepdims=True)
    kept = jnp.broadcast_to(kept, (8, width))
    tail[...] = head_sums(kept, heads, size)
    grad_dt = head_sums(grad_weighted * x_conv, heads, size) - grad_decay * rate
    grad_raw = grad_dt * sigmoid(raw)
    sum_head_ref[0:1, :] += jnp.sum(grad_raw, axis=0, keepdims=True)
    sum_head_ref[1:2, :] += jnp.sum(grad_decay * decay, axis=0, keepdims=True)

    grad_x = grad_weighted * dt_wide + skip * dy
    sum_skip = jnp.sum(dy * x_conv, axis=0, keepdims=True)
    grad_pre = grad_x * (gate_x * (1.0 + pre * (1.0 - gate_x)))
    x_buffer[Q : Q + HALO, :] = x_buffer[0:HALO, :]
    x_buffer[0:Q, :] = grad_pre
    grad_proj, taps = conv_backward(
        x_buffer, window, seg, kernel_x_ref[...], x_ref[...], width
    )
    sum_bias = jnp.sum(grad_pre, axis=0, keepdims=True)
    blank = jnp.zeros((1, width), F32)
    sum_x_ref[...] += jnp.concatenate(
        [taps[3], taps[2], taps[1], taps[0], sum_bias, sum_gate, sum_skip, blank], axis=0
    )

    grad_pre_bc = jnp.concatenate([grad_b, grad_c], axis=1) * (
        gate_bc * (1.0 + pre_bc * (1.0 - gate_bc))
    )
    bc_buffer[Q : Q + HALO, :] = bc_buffer[0:HALO, :]
    bc_buffer[0:Q, :] = grad_pre_bc
    grad_bc, taps_bc = conv_backward(
        bc_buffer, window, seg, kernel_bc_ref[...], bcdt[:, : 2 * N], 2 * N
    )
    sum_bias_bc = jnp.sum(grad_pre_bc, axis=0, keepdims=True)
    blank_bc = jnp.zeros((3, 2 * N), F32)
    sum_bc_ref[...] += jnp.concatenate(
        [taps_bc[3], taps_bc[2], taps_bc[1], taps_bc[0], sum_bias_bc, blank_bc], axis=0
    )

    grads = jnp.concatenate(
        [
            grad_proj.astype(BF16),
            grad_z.astype(BF16),
            grad_bc.astype(BF16),
            grad_raw.astype(BF16),
        ],
        axis=1,
    )
    proj_ref[...] = grads
    part = dot_nt(grads, weights_ref[:, width:])
    part_ref[...] = part.astype(BF16)
    hidden = hidden_ref[...].astype(F32)
    inverse = lax.rsqrt(jnp.mean(hidden * hidden, axis=1, keepdims=True) + EPS)
    sum_gain_ref[0:1, :] += jnp.sum(part * (hidden * inverse), axis=0, keepdims=True)


def cost(micros):
    return pl.CostEstimate(flops=int(micros * 1e9), bytes_accessed=1 << 20, transcendentals=0)


def whole(shape):
    return pl.BlockSpec(shape, lambda i: (0,) * len(shape))


def scalar():
    return pl.BlockSpec(memory_space=pltpu.SMEM)


def run_project(heads, size, place, near, weights):
    features = near[0].shape[1]
    blocks = len(near) // 2 + 1
    length = blocks * Q
    width = heads * size
    rest = 2 * N + LANES

    def rows(columns):
        return pl.BlockSpec((Q, columns), lambda i: (i, 0))

    def made(columns, dtype):
        return jax.ShapeDtypeStruct((length, columns), dtype)

    return pl.pallas_call(
        functools.partial(project_kernel, heads, size, len(near)),
        grid=(blocks,),
        in_specs=[scalar(), *[whole(block.shape) for block in near], whole(weights.shape)],
        out_specs=[
            rows(features),
            rows(features),
            rows(width),
            rows(width),
            rows(rest),
            whole((8, features)),
        ],
        out_shape=[
            made(features, BF16),
            made(features, BF16),
            made(width, F32),
            made(width, F32),
            made(rest, F32),
            jax.ShapeDtypeStruct((8, features), F32),
        ],
        compiler_params=pltpu.CompilerParams(vmem_limit_bytes=VMEM_LIMIT),
        cost_estimate=cost(8),
        name="project",
    )(place, *near, weights)


def run_forward(
    heads, size, window, seg_row, weights, kernel_x, kernel_bc, head, channel, z_proj, x_proj, bcdt
):
    length, features = seg_row.shape[1], weights.shape[0]
    width = heads * size
    blocks = length // Q

    def rows(columns):
        return pl.BlockSpec((Q, columns), lambda i: (i, 0))

    def made(columns, dtype):
        return jax.ShapeDtypeStruct((length, columns), dtype)

    across = pl.BlockSpec((8, Q), lambda i: (0, i))
    return pl.pallas_call(
        functools.partial(forward_kernel, heads, size),
        grid=(blocks,),
        in_specs=[
            whole(window.shape),
            across,
            whole((features, width)),
            whole(kernel_x.shape),
            whole(kernel_bc.shape),
            whole(head.shape),
            whole(channel.shape),
            rows(width),
            rows(width),
            rows(bcdt.shape[1]),
        ],
        out_specs=[
            rows(width),
            rows(width),
            rows(2 * N),
            pl.BlockSpec((1, N, width), lambda i: (i, 0, 0)),
            rows(width),
            rows(features),
            across,
        ],
        out_shape=[
            made(width, F32),
            made(width, F32),
            made(2 * N, F32),
            jax.ShapeDtypeStruct((blocks, N, width), F32),
            made(width, BF16),
            made(features, BF16),
            jax.ShapeDtypeStruct((8, length), F32),
        ],
        scratch_shapes=[
            pltpu.VMEM((Q + HALO, width), F32),
            pltpu.VMEM((Q + HALO, 2 * N), F32),
            pltpu.VMEM((N, width), F32),
        ],
        compiler_params=pltpu.CompilerParams(vmem_limit_bytes=VMEM_LIMIT),
        cost_estimate=cost(14),
        name="forward",
    )(window, seg_row, weights, kernel_x, kernel_bc, head, channel, z_proj, x_proj, bcdt)


def run_gradient(place, near, weights, scaled, window):
    features = near[0].shape[1]
    length, width = scaled.shape
    return pl.pallas_call(
        functools.partial(gradient_kernel, width, len(near)),
        grid=(length // Q,),
        in_specs=[
            scalar(),
            *[whole(block.shape) for block in near],
            whole((features, width)),
            pl.BlockSpec((Q, width), lambda i: (i, 0)),
            whole(window.shape),
        ],
        out_specs=[
            pl.BlockSpec((Q, features), lambda i: (i, 0)),
            pl.BlockSpec((Q, width), lambda i: (i, 0)),
            pl.BlockSpec((8, Q), lambda i: (0, i)),
        ],
        out_shape=[
            jax.ShapeDtypeStruct((length, features), BF16),
            jax.ShapeDtypeStruct((length, width), F32),
            jax.ShapeDtypeStruct((8, length), F32),
        ],
        compiler_params=pltpu.CompilerParams(vmem_limit_bytes=VMEM_LIMIT),
        cost_estimate=cost(5),
        name="out_gradient",
    )(place, *near, weights, scaled, window)


def weights_kernel(width, cot_ref, normed_ref, tokens_ref, grads_ref, first_ref, second_ref):
    tokens = tokens_ref[...]
    first_ref[:, :width] = dot_tn(cot_ref[...], normed_ref[...]).astype(BF16)
    first_ref[:, width:] = dot_tn(tokens, grads_ref[:, 2 * width :]).astype(BF16)
    second_ref[...] = dot_tn(tokens, grads_ref[:, : 2 * width]).astype(BF16)


def run_weights(cot, normed, tokens, grads):
    length, features = tokens.shape
    width = normed.shape[1]
    columns = [grads.shape[1] - width, 2 * width]
    return pl.pallas_call(
        functools.partial(weights_kernel, width),
        grid=(features // Q,),
        in_specs=[
            pl.BlockSpec((length, Q), lambda i: (0, i)),
            whole(normed.shape),
            pl.BlockSpec((length, Q), lambda i: (0, i)),
            whole(grads.shape),
        ],
        out_specs=[pl.BlockSpec((Q, count), lambda i: (i, 0)) for count in columns],
        out_shape=[jax.ShapeDtypeStruct((features, count), BF16) for count in columns],
        compiler_params=pltpu.CompilerParams(vmem_limit_bytes=VMEM_LIMIT),
        cost_estimate=cost(7),
        name="weight_gradients",
    )(cot, normed, tokens, grads)


def run_backward(
    heads, size, full_inner, stat, hidden, window, seg_row, weights, kernel_x, kernel_bc, head, channel,
    z_proj, mixed, x_proj, pre, bcdt, pre_bc, states, grad_out,
):
    length, features = hidden.shape
    width = heads * size
    blocks = length // Q
    rest = 2 * N + LANES
    total = 2 * width + rest

    def rows(columns):
        return pl.BlockSpec((Q, columns), lambda i: (blocks - 1 - i, 0))

    def made(columns, dtype):
        return jax.ShapeDtypeStruct((length, columns), dtype)

    across = pl.BlockSpec((8, Q), lambda i: (0, blocks - 1 - i))
    sums = [(8, width), (8, 2 * N), (8, LANES), (8, features)]
    return pl.pallas_call(
        functools.partial(backward_kernel, heads, size, full_inner),
        grid=(blocks,),
        in_specs=[
            across,
            rows(features),
            whole(window.shape),
            across,
            whole(weights.shape),
            whole(kernel_x.shape),
            whole(kernel_bc.shape),
            whole(head.shape),
            whole(channel.shape),
            rows(width),
            rows(width),
            rows(width),
            rows(width),
            rows(rest),
            rows(2 * N),
            pl.BlockSpec((1, N, width), lambda i: (blocks - 1 - i, 0, 0)),
            rows(width),
        ],
        out_specs=[rows(total), rows(features), rows(width)]
        + [whole(shape) for shape in sums],
        out_shape=[made(total, BF16), made(features, BF16), made(width, BF16)]
        + [jax.ShapeDtypeStruct(shape, F32) for shape in sums],
        scratch_shapes=[
            pltpu.VMEM((Q + HALO, width), F32),
            pltpu.VMEM((Q + HALO, 2 * N), F32),
            pltpu.VMEM((N, width), F32),
            pltpu.VMEM((8, LANES), F32),
        ],
        compiler_params=pltpu.CompilerParams(vmem_limit_bytes=VMEM_LIMIT),
        cost_estimate=cost(2),
        name="backward",
    )(
        stat, hidden, window, seg_row, weights, kernel_x, kernel_bc, head, channel,
        z_proj, mixed, x_proj, pre, bcdt, pre_bc, states, grad_out,
    )


def finish_kernel(sum_ref, hidden_ref, cot_ref, gain_ref, out_ref):
    grad = sum_ref[...].astype(F32) * gain_ref[0:1, :]
    hidden = hidden_ref[...].astype(F32)
    inverse = lax.rsqrt(jnp.mean(hidden * hidden, axis=1, keepdims=True) + EPS)
    unit = hidden * inverse
    along = jnp.mean(grad * unit, axis=1, keepdims=True)
    out_ref[...] = (cot_ref[...].astype(F32) + inverse * (grad - unit * along)).astype(BF16)


def run_finish(in_sum, hidden, cot, gain):
    length, features = hidden.shape
    rows = pl.BlockSpec((length // 2, features), lambda i: (i, 0))
    return pl.pallas_call(
        finish_kernel,
        grid=(2,),
        in_specs=[rows, rows, rows, whole(gain.shape)],
        out_specs=rows,
        out_shape=jax.ShapeDtypeStruct(hidden.shape, BF16),
        compiler_params=pltpu.CompilerParams(vmem_limit_bytes=VMEM_LIMIT),
        name="finish",
    )(in_sum, hidden, cot, gain)


def pad_lanes(values):
    return jnp.pad(values, ((0, 0), (0, LANES - values.shape[1])))


def after(value, *others):
    return lax.optimization_barrier((value, *others))[0]


def line_step(right, left, step, axis):
    n = lax.axis_size(axis)
    return (
        lax.ppermute(right, axis, [(i, i + 1) for i in range(step - 1, n - 1)]),
        lax.ppermute(left, axis, [(i, i - 1) for i in range(1, n - step + 1)]),
    )


def line_order(block, moved):
    return [pair[0] for pair in moved[::-1]] + [block] + [pair[1] for pair in moved]


def line_gather(block, axis):
    right = left = block
    moved = []
    for step in range(1, lax.axis_size(axis)):
        right, left = line_step(right, left, step, axis)
        moved.append((right, left))
    return line_order(block, moved)


def cube_scatter(first, second, small, axis):
    n = lax.axis_size(axis)
    if n & (n - 1):
        sums = [
            lax.psum_scatter(part, axis, scatter_dimension=0, tiled=True).astype(F32)
            for part in (first, second)
        ]
        return (*sums, lax.psum(small, axis), sums)
    place = lax.axis_index(axis)
    bits = list(range(n.bit_length() - 1))
    orders = [bits, bits[:1] + bits[:0:-1]]
    parts = [part.reshape((2,) * len(bits) + (-1, part.shape[1])) for part in (first, second)]
    left = [bits[::-1], bits[::-1]]
    came = [None, None]
    for step in range(len(bits)):
        for index in range(2):
            part = parts[index]
            bit = orders[index][step]
            dim = left[index].index(bit)
            mine = (place >> bit) & 1
            keep = lax.dynamic_index_in_dim(part, mine, dim, keepdims=False)
            send = lax.dynamic_index_in_dim(part, 1 - mine, dim, keepdims=False)
            pairs = [(i, i ^ (1 << bit)) for i in range(n)]
            if index == 0:
                columns = part.shape[-1]
                rows = send.size // columns
                extra = -(-small.size // (16 * columns)) * 16
                small = lax.reduce_precision(small, 8, 7)
                rider = jnp.pad(
                    small.astype(BF16).reshape(-1), (0, extra * columns - small.size)
                ).reshape(extra, columns)
                moved = lax.ppermute(
                    jnp.concatenate([send.reshape(rows, columns), rider]), axis, pairs
                )
                other = moved[:rows].reshape(send.shape)
                rider = moved[rows:].reshape(-1)[: small.size].reshape(small.shape)
                small = small + rider.astype(F32)
            else:
                moved = other = lax.ppermute(send, axis, pairs)
            came[index] = moved
            part = keep.astype(F32) + other.astype(F32)
            left[index] = [other_bit for other_bit in left[index] if other_bit != bit]
            parts[index] = part.astype(BF16) if left[index] else part
    return (*parts, small, came)


def around(values, axis):
    n = lax.axis_size(axis)
    return [values] + [
        lax.ppermute(values, axis, [(i, (i - k) % n) for i in range(n)]) for k in range(1, n)
    ]


def sum_around(values, axis):
    return functools.reduce(jnp.add, around(values, axis))


def shards(
    hidden,
    seg_ids,
    cotangent,
    norm_gain,
    w_in_z,
    w_in_x,
    w_in_bc,
    w_in_dt,
    conv_x,
    conv_x_bias,
    conv_bc,
    conv_bc_bias,
    dt_bias,
    a_log,
    d_skip,
    gate_gain,
    w_out,
):
    heads = dt_bias.shape[0]
    width = gate_gain.shape[0]
    size = width // heads
    full_inner = width * lax.axis_size("tensor")
    features = hidden.shape[2]
    hidden_local = hidden[0]

    steps = jnp.pad(
        jnp.concatenate([w_in_dt, norm_gain[:, None]], axis=1), ((0, 0), (0, LANES - heads - 1))
    )
    packed = jnp.concatenate([w_out, w_in_x, w_in_z, w_in_bc, steps], axis=1)
    n = lax.axis_size("tensor")
    axis_place = lax.axis_index("tensor")
    place = axis_place[None]
    near_hidden = line_gather(hidden_local, "tensor")
    weights = lax.all_gather(packed, "dp", axis=0, tiled=True)
    seg_stack = around(seg_ids[0], "tensor")
    count = seg_ids.shape[1]
    seg_full = lax.dynamic_slice_in_dim(
        jnp.concatenate(seg_stack + seg_stack), (n - axis_place) * count, n * count, 0
    )
    window = jnp.broadcast_to(
        jnp.pad(seg_full, (HALO, HALO), constant_values=-1)[:, None],
        (seg_full.shape[0] + 2 * HALO, LANES),
    )
    seg_row = jnp.broadcast_to(seg_full[None, :], (8, seg_full.shape[0]))
    kernel_x = jnp.concatenate([conv_x, conv_x_bias[None, :]], axis=0)
    kernel_bc = jnp.concatenate([conv_bc, conv_bc_bias[None, :]], axis=0)
    head = pad_lanes(jnp.stack([dt_bias, a_log]))
    channel = jnp.stack([gate_gain, jnp.repeat(d_skip, size)])

    hidden_full, tokens, z_proj, x_proj, bcdt, gain = run_project(
        heads, size, place, near_hidden, weights
    )
    right = left = after(cotangent[0], near_hidden[0], near_hidden[-1])
    moved = []
    right, left = line_step(right, left, 1, "tensor")
    moved.append((right, left))
    bcdt = after(bcdt, right, left)
    right, left = line_step(after(right, gain), after(left, gain), 2, "tensor")
    moved.append((right, left))
    mixed, pre, pre_bc, states, scaled, out_part, square = run_forward(
        heads, size, window, seg_row, weights, kernel_x, kernel_bc, head, channel, z_proj, x_proj,
        bcdt,
    )
    for step in range(3, n):
        right, left = line_step(after(right, square), after(left, square), step, "tensor")
        moved.append((right, left))
    near_cot = line_order(cotangent[0], moved)
    cot_full, grad_out, along = run_gradient(place, near_cot, weights, scaled, window)
    out_sum = lax.psum_scatter(
        out_part, "tensor", scatter_dimension=0, tiled=True
    )
    stat = sum_around(jnp.stack([square[0], along[0]]), "tensor")
    stat_full = jnp.pad(stat, ((0, 6), (0, 0)))
    out_scale = lax.rsqrt(stat[0] / full_inner + EPS) * (seg_full > 0).astype(F32)

    grads, in_part, normed_out, sum_x, sum_bc, sum_head, sum_gain = run_backward(
        heads, size, full_inner, stat_full, hidden_full, window, seg_row, weights, kernel_x,
        kernel_bc, head, channel, z_proj, mixed, x_proj, pre, bcdt, pre_bc, states, grad_out,
    )
    in_sum = lax.psum_scatter(in_part, "tensor", scatter_dimension=0, tiled=True)
    first, second = run_weights(cot_full, normed_out, tokens, after(grads, out_sum))
    own = jnp.concatenate([sum_x.reshape(-1, LANES), sum_head])
    both = jnp.concatenate([sum_gain[0].reshape(-1, LANES), sum_bc.reshape(-1, LANES)])
    first, second, small, came = cube_scatter(first, second, jnp.concatenate([own, both]), "dp")
    sum_x = small[: own.shape[0] - 8].reshape(8, width)
    sum_head = small[own.shape[0] - 8 : own.shape[0]]
    grad_bc = first[:, width : width + 2 * N]
    shared = jnp.concatenate([small[own.shape[0] :], grad_bc.reshape(-1, LANES)])
    shared = sum_around(shared, "tensor")
    gain_rows = features // LANES
    sum_gain = shared[:gain_rows].reshape(features)
    sum_bc = shared[gain_rows : both.shape[0]].reshape(8, 2 * N)
    grad_bc = shared[both.shape[0] :].reshape(grad_bc.shape)
    local_features = norm_gain.shape[0]
    grad_norm_gain = lax.dynamic_slice_in_dim(
        sum_gain, lax.axis_index("dp") * local_features, local_features, 0
    )

    local = hidden_local.shape[0]
    hidden_rows = hidden_local.astype(F32)
    scale_here = lax.dynamic_slice_in_dim(out_scale, axis_place * local, local, 0)[:, None]
    layer_out = (hidden_rows + out_sum.astype(F32) * scale_here).astype(BF16)

    grad_hidden = run_finish(in_sum, hidden_local, cotangent[0], after(gain, came[1]))

    return (
        layer_out[None],
        grad_hidden[None],
        grad_norm_gain,
        second[:, width:],
        second[:, :width],
        grad_bc,
        first[:, width + 2 * N : width + 2 * N + heads],
        sum_x[0:CONV],
        sum_x[CONV],
        sum_bc[0:CONV],
        sum_bc[CONV],
        sum_head[0, :heads],
        sum_head[1, :heads],
        jnp.sum(sum_x[CONV + 2].reshape(heads, size), axis=1),
        sum_x[CONV + 1],
        first[:, :width],
    )


def solution(mesh):
    in_specs = (
        P("dp", "tensor", None),
        P("dp", "tensor"),
        P("dp", "tensor", None),
        P("dp"),
        P("dp", "tensor"),
        P("dp", "tensor"),
        P("dp", None),
        P("dp", "tensor"),
        P(None, "tensor"),
        P("tensor"),
        P(),
        P(),
        P("tensor"),
        P("tensor"),
        P("tensor"),
        P("tensor"),
        P("dp", "tensor"),
    )
    out_specs = (
        P("dp", "tensor", None),
        P("dp", "tensor", None),
        P("dp"),
        P("dp", "tensor"),
        P("dp", "tensor"),
        P("dp", None),
        P("dp", "tensor"),
        P(None, "tensor"),
        P("tensor"),
        P(),
        P(),
        P("tensor"),
        P("tensor"),
        P("tensor"),
        P("tensor"),
        P("dp", "tensor"),
    )
    return jax.shard_map(shards, mesh=mesh, in_specs=in_specs, out_specs=out_specs, check_vma=False)
```

```python
import functools

import jax
import jax.numpy as jnp
from jax import lax
from jax.experimental import pallas as pl
from jax.experimental.pallas import tpu as pltpu
from jax.sharding import PartitionSpec as P

N = 128
CONV = 4
Q = 256
LANES = 128
HALO = 8
EPS = 1e-05
NEG = -1e30
F32 = jnp.float32
BF16 = jnp.bfloat16
VMEM_LIMIT = 52 * 1024 * 1024


def dot(a, b):
    return jnp.dot(a, b, preferred_element_type=F32)


def dot_nt(a, b):
    return lax.dot_general(a, b, (((1,), (1,)), ((), ())), preferred_element_type=F32)


def dot_tn(a, b):
    return lax.dot_general(a, b, (((0,), (0,)), ((), ())), preferred_element_type=F32)


def dot_exact(a, b):
    return jnp.dot(a, b, preferred_element_type=F32, precision=lax.Precision.HIGHEST)


def spread(cols, heads, size):
    rows = cols.shape[0]
    per = LANES // size
    lane = lax.broadcasted_iota(jnp.int32, (rows, LANES), 1)
    parts = []
    for first in range(0, heads, per):
        part = jnp.broadcast_to(cols[:, first : first + 1], (rows, LANES))
        for extra in range(1, per):
            part = jnp.where(lane < extra * size, part, cols[:, first + extra : first + extra + 1])
        parts.append(part)
    return jnp.concatenate(parts, axis=1)


def head_sums(values, heads, size):
    width = heads * size
    channel = lax.broadcasted_iota(jnp.int32, (width, LANES), 0)
    column = lax.broadcasted_iota(jnp.int32, (width, LANES), 1)
    first = column * size
    picks = jnp.where((channel >= first) & (channel < first + size), 1.0, 0.0).astype(BF16)
    high = values.astype(BF16)
    low = (values - high.astype(F32)).astype(BF16)
    return dot(high, picks) + dot(low, picks)


def widen(tile, width):
    return jnp.concatenate([tile] * (width // tile.shape[1]), axis=1)


def softplus(v):
    return jnp.maximum(v, 0.0) + jnp.log1p(jnp.exp(-jnp.abs(v)))


def sigmoid(v):
    return 1.0 / (1.0 + jnp.exp(-v))


def as_row(column):
    rows = column.shape[0]
    return jnp.broadcast_to(column, (rows, LANES)).T[:8]


def triangle(lower):
    row = lax.broadcasted_iota(jnp.int32, (Q, Q), 0)
    col = lax.broadcasted_iota(jnp.int32, (Q, Q), 1)
    return row >= col if lower else row <= col


def block_masks(window, seg_row):
    seg = window[HALO : HALO + Q]
    before = window[HALO - 1 : HALO]
    last = window[HALO + Q - 1 : HALO + Q]
    from_prev = (seg == before).astype(F32)
    same_last = (seg == last).astype(F32)
    passes = (last == before).astype(F32)
    keep = (widen(seg, Q) == seg_row) & triangle(True)
    bias = jnp.where(keep, 0.0, NEG)
    return seg, from_prev, same_last, passes, bias


def conv_forward(buffer, window, seg, kernel, conv_bias, width):
    total = conv_bias + kernel[CONV - 1 : CONV] * buffer[HALO : HALO + Q, :]
    for back in range(1, CONV):
        match = (window[HALO - back : HALO - back + Q] == seg).astype(F32)
        tap = kernel[CONV - 1 - back : CONV - back]
        total = total + tap * (buffer[HALO - back : HALO - back + Q, :] * widen(match, width))
    return total


def conv_backward(buffer, window, seg, kernel, values, width):
    here = buffer[0:Q, :]
    total = kernel[CONV - 1 : CONV] * here
    taps = [jnp.sum(values * here, axis=0, keepdims=True)]
    for ahead in range(1, CONV):
        match = (window[HALO + ahead : HALO + ahead + Q] == seg).astype(F32)
        moved = buffer[ahead : ahead + Q, :] * widen(match, width)
        total = total + kernel[CONV - 1 - ahead : CONV - ahead] * moved
        taps.append(jnp.sum(values * moved, axis=0, keepdims=True))
    return total, taps


def pick_block(place, near_refs, block):
    reach = len(near_refs) // 2
    away = pl.program_id(0) - place
    for index, ref in enumerate(near_refs):

        @pl.when(away == index - reach)
        def _():
            block[...] = ref[...]


def project_kernel(heads, size, near, place_ref, *refs):
    near_refs, refs = refs[:near], refs[near:]
    weights_ref, hidden_ref, tokens_ref, z_ref, x_ref, bcdt_ref, gain_ref = refs
    width = heads * size

    @pl.when(pl.program_id(0) == 0)
    def _():
        tail_columns = weights_ref[:, 3 * width + 2 * N :].astype(F32).T
        gain_ref[...] = jnp.broadcast_to(tail_columns[heads : heads + 1], gain_ref.shape)

    pick_block(place_ref[0], near_refs, hidden_ref)
    hidden = hidden_ref[...].astype(F32)
    inverse = lax.rsqrt(jnp.mean(hidden * hidden, axis=1, keepdims=True) + EPS)
    tokens = (hidden * inverse * gain_ref[0:1, :]).astype(BF16)
    tokens_ref[...] = tokens
    x_ref[...] = dot(tokens, weights_ref[:, width : 2 * width])
    z_ref[...] = dot(tokens, weights_ref[:, 2 * width : 3 * width])
    bcdt_ref[...] = dot(tokens, weights_ref[:, 3 * width :])


def forward_kernel(
    heads,
    size,
    window_ref,
    seg_row_ref,
    weights_ref,
    kernel_x_ref,
    kernel_bc_ref,
    head_ref,
    channel_ref,
    z_ref,
    x_ref,
    bcdt_ref,
    scaled_ref,
    part_ref,
    square_ref,
    state_ref,
    survive_ref,
    shape_ref,
    prob_ref,
    gated_ref,
    opened_ref,
    slope_z_ref,
    inner_ref,
    carried_ref,
    x_conv_ref,
    slope_x_ref,
    dt_ref,
    from_start_ref,
    to_end_ref,
    weighted_ref,
    weighted_end_ref,
    bc_ref,
    slope_bc_ref,
    decay_ref,
    slope_dt_ref,
    x_buffer,
    bc_buffer,
    carry,
):
    step = pl.program_id(0)
    width = heads * size

    @pl.when(step == 0)
    def _():
        x_buffer[0:HALO, :] = jnp.zeros((HALO, width), F32)
        bc_buffer[0:HALO, :] = jnp.zeros((HALO, 2 * N), F32)
        carry[...] = jnp.zeros((N, width), F32)

    window = window_ref[pl.ds(pl.multiple_of(step * Q, Q), Q + 2 * HALO), :]
    seg, from_prev, same_last, passes, bias = block_masks(window, seg_row_ref[0:1, :])
    bcdt = bcdt_ref[...]
    x_buffer[HALO : HALO + Q, :] = x_ref[...]
    bc_buffer[HALO : HALO + Q, :] = bcdt[:, : 2 * N]
    pre = conv_forward(
        x_buffer, window, seg, kernel_x_ref[...], kernel_x_ref[CONV : CONV + 1, :], width
    )
    pre_bc = conv_forward(
        bc_buffer, window, seg, kernel_bc_ref[...], kernel_bc_ref[CONV : CONV + 1, :], 2 * N
    )
    x_buffer[0:HALO, :] = x_buffer[Q : Q + HALO, :]
    bc_buffer[0:HALO, :] = bc_buffer[Q : Q + HALO, :]
    gate_x = sigmoid(pre)
    x_conv = pre * gate_x
    x_conv_ref[...] = x_conv
    slope_x_ref[...] = gate_x * (1.0 + pre * (1.0 - gate_x))
    gate_bc = sigmoid(pre_bc)
    bc_conv = (pre_bc * gate_bc).astype(BF16)
    bc_ref[...] = bc_conv
    slope_bc_ref[...] = gate_bc * (1.0 + pre_bc * (1.0 - gate_bc))
    b_in = bc_conv[:, :N]
    c_in = bc_conv[:, N:]

    raw = bcdt[:, 2 * N :] + head_ref[0:1, :]
    slope_dt_ref[...] = sigmoid(raw)
    dt = softplus(raw)
    decay = -dt * jnp.exp(head_ref[1:2, :])
    decay_ref[...] = decay
    total = dot_exact(triangle(True).astype(F32), decay)
    total_t = total.T
    dt_wide = spread(dt, heads, size)
    dt_ref[...] = dt_wide
    weighted = x_conv * dt_wide
    weighted_low = weighted.astype(BF16)
    weighted_ref[...] = weighted_low
    scores = dot_nt(c_in, b_in)
    before = carry[...]
    state_ref[0] = before

    per = LANES // size
    lane = lax.broadcasted_iota(jnp.int32, (Q, LANES), 1)
    none = jnp.zeros((Q, LANES), BF16)
    inner = []
    for first in range(0, heads, per):
        group = weighted_low[:, first * size : first * size + LANES]
        summed = jnp.zeros((Q, LANES), F32)
        for extra in range(per):
            h = first + extra
            shape = jnp.exp(total[:, h : h + 1] - total_t[h : h + 1, :] + bias)
            prob = (scores * shape).astype(BF16)
            shape_ref[:, h * Q : (h + 1) * Q] = shape.astype(BF16)
            prob_ref[:, h * Q : (h + 1) * Q] = prob
            mine = (lane >= extra * size) & (lane < (extra + 1) * size)
            summed = summed + dot(prob, jnp.where(mine, group, none))
        inner.append(summed)
    inner = jnp.concatenate(inner, axis=1)
    inner_ref[...] = inner
    carried = dot(c_in, before.astype(BF16))
    carried_ref[...] = carried
    from_start = spread(jnp.exp(total) * from_prev, heads, size)
    from_start_ref[...] = from_start
    last = total[Q - 1 : Q, :]
    to_end = spread(jnp.exp(last - total) * same_last, heads, size)
    to_end_ref[...] = to_end
    weighted_end = (weighted * to_end).astype(BF16)
    weighted_end_ref[...] = weighted_end
    survive = spread(jnp.exp(last) * passes, heads, size)
    survive_ref[0] = jnp.broadcast_to(survive, (8, width))
    carry[...] = dot_tn(b_in, weighted_end) + before * survive

    mixed = inner + carried * from_start + channel_ref[1:2, :] * x_conv
    z_proj = z_ref[...]
    gate = sigmoid(z_proj)
    opened = z_proj * gate
    opened_ref[...] = opened
    slope_z_ref[...] = mixed * (gate * (1.0 + z_proj * (1.0 - gate)))
    gated = mixed * opened
    gated_ref[...] = gated
    scaled = (gated * channel_ref[0:1, :]).astype(BF16)
    scaled_ref[...] = scaled
    part_ref[...] = dot_nt(scaled, weights_ref[...]).astype(BF16)
    square_ref[...] = as_row(jnp.sum(gated * gated, axis=1, keepdims=True))


def gradient_kernel(width, near, place_ref, *refs):
    near_refs, refs = refs[:near], refs[near:]
    weights_ref, scaled_ref, window_ref, cot_ref, grad_ref, along_ref = refs
    step = pl.program_id(0)
    pick_block(place_ref[0], near_refs, cot_ref)
    window = window_ref[pl.ds(pl.multiple_of(step * Q, Q), Q + 2 * HALO), :]
    live = (window[HALO : HALO + Q] > 0).astype(F32)
    grad = dot(cot_ref[...], weights_ref[...]) * widen(live, width)
    grad_ref[...] = grad
    along_ref[...] = as_row(jnp.sum(scaled_ref[...].astype(F32) * grad, axis=1, keepdims=True))


def backward_kernel(
    heads,
    size,
    full_inner,
    stat_ref,
    hidden_ref,
    window_ref,
    weights_ref,
    kernel_x_ref,
    kernel_bc_ref,
    head_ref,
    channel_ref,
    x_ref,
    bcdt_ref,
    grad_ref,
    state_ref,
    survive_ref,
    shape_ref,
    prob_ref,
    gated_ref,
    opened_ref,
    slope_z_ref,
    inner_ref,
    carried_ref,
    x_conv_ref,
    slope_x_ref,
    dt_ref,
    from_start_ref,
    to_end_ref,
    weighted_ref,
    weighted_end_ref,
    bc_ref,
    slope_bc_ref,
    decay_ref,
    slope_dt_ref,
    proj_ref,
    part_ref,
    out_ref,
    sum_x_ref,
    sum_bc_ref,
    sum_head_ref,
    sum_gain_ref,
    x_buffer,
    bc_buffer,
    carry,
    tail,
):
    turn = pl.program_id(0)
    step = pl.num_programs(0) - 1 - turn
    width = heads * size

    @pl.when(turn == 0)
    def _():
        x_buffer[...] = jnp.zeros((Q + HALO, width), F32)
        bc_buffer[...] = jnp.zeros((Q + HALO, 2 * N), F32)
        carry[...] = jnp.zeros((N, width), F32)
        tail[...] = jnp.zeros((8, LANES), F32)
        sum_x_ref[...] = jnp.zeros((8, width), F32)
        sum_bc_ref[...] = jnp.zeros((8, 2 * N), F32)
        sum_head_ref[...] = jnp.zeros((8, LANES), F32)
        sum_gain_ref[...] = jnp.zeros(sum_gain_ref.shape, F32)

    window = window_ref[pl.ds(pl.multiple_of(step * Q, Q), Q + 2 * HALO), :]
    seg = window[HALO : HALO + Q]
    live = (seg[:, 0:1] > 0).astype(F32)
    stat = stat_ref[...].T
    gate_inverse = lax.rsqrt(stat[:, 0:1] / full_inner + EPS)
    along = stat[:, 1:2] * (gate_inverse * gate_inverse * gate_inverse / full_inner)

    gain = channel_ref[0:1, :]
    skip = channel_ref[1:2, :]
    grad_out = grad_ref[...]
    gated = gated_ref[...]
    normal = gated * gate_inverse
    sum_gate = jnp.sum(grad_out * normal, axis=0, keepdims=True)
    out_ref[...] = (normal * gain * live).astype(BF16)
    grad_gated = grad_out * gain * gate_inverse - gated * along
    grad_z = (grad_gated * slope_z_ref[...]).astype(BF16)
    dy = grad_gated * opened_ref[...]
    dy_low = dy.astype(BF16)
    dy_start = (dy * from_start_ref[...]).astype(BF16)

    bc_conv = bc_ref[...]
    b_in = bc_conv[:, :N]
    c_in = bc_conv[:, N:]
    before = state_ref[0]
    before_low = before.astype(BF16)
    after_low = carry[...].astype(BF16)
    weighted_low = weighted_ref[...]
    weighted_end = weighted_end_ref[...]
    grad_c = dot_nt(dy_start, before_low)
    returned = dot(b_in, after_low)
    grad_b = dot_nt(weighted_end, after_low)
    new_after = dot_tn(c_in, dy_start) + carry[...] * survive_ref[0, 0:1, :]
    carry[...] = new_after

    per = LANES // size
    lane = lax.broadcasted_iota(jnp.int32, (Q, LANES), 1)
    grad_scores = jnp.zeros((Q, Q), F32)
    inner = []
    none = jnp.zeros((Q, LANES), BF16)
    for first in range(0, heads, per):
        at = first * size
        dy_group = dy_low[:, at : at + LANES]
        weighted_group = weighted_low[:, at : at + LANES]
        summed = jnp.zeros((Q, LANES), F32)
        for extra in range(per):
            h = first + extra
            mine = (lane >= extra * size) & (lane < (extra + 1) * size)
            dy_mine = jnp.where(mine, dy_group, none)
            shape = shape_ref[:, h * Q : (h + 1) * Q].astype(F32)
            grad_scores = grad_scores + dot_nt(dy_mine, weighted_group) * shape
            summed = summed + dot_tn(prob_ref[:, h * Q : (h + 1) * Q], dy_mine)
        inner.append(summed)
    grad_inner = jnp.concatenate(inner, axis=1)
    grad_weighted = to_end_ref[...] * returned + grad_inner
    grad_scores = grad_scores.astype(BF16)
    grad_c = grad_c + dot(grad_scores, b_in)
    grad_b = grad_b + dot_tn(grad_scores, c_in)

    x_conv = x_conv_ref[...]
    pairs = head_sums(
        dy_low.astype(F32) * inner_ref[...]
        + dy_start.astype(F32) * carried_ref[...]
        - weighted_low.astype(F32) * grad_inner
        - weighted_end.astype(F32) * returned,
        heads,
        size,
    )
    grad_decay = dot_exact(triangle(False).astype(F32), pairs) + tail[0:1, :]
    kept = jnp.sum(new_after.astype(BF16).astype(F32) * before, axis=0, keepdims=True)
    tail[...] = head_sums(jnp.broadcast_to(kept, (8, width)), heads, size)
    rate = jnp.exp(head_ref[1:2, :])
    grad_dt = head_sums(grad_weighted * x_conv, heads, size) - grad_decay * rate
    grad_raw = grad_dt * slope_dt_ref[...]
    sum_head_ref[0:1, :] += jnp.sum(grad_raw, axis=0, keepdims=True)
    sum_head_ref[1:2, :] += jnp.sum(grad_decay * decay_ref[...], axis=0, keepdims=True)

    sum_skip = jnp.sum(dy * x_conv, axis=0, keepdims=True)
    grad_pre = (grad_weighted * dt_ref[...] + skip * dy) * slope_x_ref[...]
    x_buffer[Q : Q + HALO, :] = x_buffer[0:HALO, :]
    x_buffer[0:Q, :] = grad_pre
    grad_proj, taps = conv_backward(
        x_buffer, window, seg, kernel_x_ref[...], x_ref[...], width
    )
    sum_bias = jnp.sum(grad_pre, axis=0, keepdims=True)
    blank = jnp.zeros((1, width), F32)
    sum_x_ref[...] += jnp.concatenate(
        [taps[3], taps[2], taps[1], taps[0], sum_bias, sum_gate, sum_skip, blank], axis=0
    )

    grad_pre_bc = jnp.concatenate([grad_b, grad_c], axis=1) * slope_bc_ref[...]
    bc_buffer[Q : Q + HALO, :] = bc_buffer[0:HALO, :]
    bc_buffer[0:Q, :] = grad_pre_bc
    grad_bc, taps_bc = conv_backward(
        bc_buffer, window, seg, kernel_bc_ref[...], bcdt_ref[:, : 2 * N], 2 * N
    )
    sum_bias_bc = jnp.sum(grad_pre_bc, axis=0, keepdims=True)
    blank_bc = jnp.zeros((3, 2 * N), F32)
    sum_bc_ref[...] += jnp.concatenate(
        [taps_bc[3], taps_bc[2], taps_bc[1], taps_bc[0], sum_bias_bc, blank_bc], axis=0
    )

    grads = jnp.concatenate(
        [grad_proj.astype(BF16), grad_z, grad_bc.astype(BF16), grad_raw.astype(BF16)], axis=1
    )
    proj_ref[...] = grads
    part = dot_nt(grads, weights_ref[:, width:])
    part_ref[...] = part.astype(BF16)
    hidden = hidden_ref[...].astype(F32)
    inverse = lax.rsqrt(jnp.mean(hidden * hidden, axis=1, keepdims=True) + EPS)
    sum_gain_ref[0:1, :] += jnp.sum(part * (hidden * inverse), axis=0, keepdims=True)


def pack_kernel(heads, out_ref_in, x_ref, z_ref, bc_ref, dt_ref, gain_ref, packed_ref):
    width = x_ref.shape[1]
    at = 0
    for ref in (out_ref_in, x_ref, z_ref, bc_ref):
        packed_ref[:, at : at + ref.shape[1]] = ref[...]
        at += ref.shape[1]
    rows = x_ref.shape[0]
    packed_ref[:, at:] = jnp.concatenate(
        [dt_ref[...], gain_ref[...], jnp.zeros((rows, LANES - heads - 1), BF16)], axis=1
    )


def run_pack(heads, *parts):
    rows = parts[0].shape[0]
    columns = sum(part.shape[1] for part in parts[:4]) + LANES
    return pl.pallas_call(
        functools.partial(pack_kernel, heads),
        out_shape=jax.ShapeDtypeStruct((rows, columns), BF16),
        compiler_params=pltpu.CompilerParams(vmem_limit_bytes=VMEM_LIMIT),
        name="pack",
    )(*parts)


def cost(micros):
    return pl.CostEstimate(flops=int(micros * 1e9), bytes_accessed=1 << 20, transcendentals=0)


def whole(shape):
    return pl.BlockSpec(shape, lambda i: (0,) * len(shape))


def scalar():
    return pl.BlockSpec(memory_space=pltpu.SMEM)


def run_project(heads, size, place, near, weights):
    features = near[0].shape[1]
    blocks = len(near) // 2 + 1
    length = blocks * Q
    width = heads * size
    rest = 2 * N + LANES

    def rows(columns):
        return pl.BlockSpec((Q, columns), lambda i: (i, 0))

    def made(columns, dtype):
        return jax.ShapeDtypeStruct((length, columns), dtype)

    return pl.pallas_call(
        functools.partial(project_kernel, heads, size, len(near)),
        grid=(blocks,),
        in_specs=[scalar(), *[whole(block.shape) for block in near], whole(weights.shape)],
        out_specs=[
            rows(features),
            rows(features),
            rows(width),
            rows(width),
            rows(rest),
            whole((8, features)),
        ],
        out_shape=[
            made(features, BF16),
            made(features, BF16),
            made(width, F32),
            made(width, F32),
            made(rest, F32),
            jax.ShapeDtypeStruct((8, features), F32),
        ],
        compiler_params=pltpu.CompilerParams(vmem_limit_bytes=VMEM_LIMIT),
        cost_estimate=cost(8),
        name="project",
    )(place, *near, weights)


def saved_rows(heads, size):
    width = heads * size
    return (
        [(heads * Q, BF16)] * 2
        + [(width, F32)] * 10
        + [(width, BF16)] * 2
        + [(2 * N, BF16), (2 * N, F32), (LANES, F32), (LANES, F32)]
    )


def saved_specs(heads, size, place):
    width = heads * size
    return [
        pl.BlockSpec((1, N, width), lambda i: (place(i), 0, 0)),
        pl.BlockSpec((1, 8, width), lambda i: (place(i), 0, 0)),
    ] + [
        pl.BlockSpec((Q, columns), lambda i: (place(i), 0))
        for columns, _ in saved_rows(heads, size)
    ]


def run_forward(
    heads, size, window, seg_row, weights, kernel_x, kernel_bc, head, channel, z_proj, x_proj, bcdt
):
    length, features = seg_row.shape[1], weights.shape[0]
    width = heads * size
    blocks = length // Q

    def rows(columns):
        return pl.BlockSpec((Q, columns), lambda i: (i, 0))

    def made(columns, dtype):
        return jax.ShapeDtypeStruct((length, columns), dtype)

    across = pl.BlockSpec((8, Q), lambda i: (0, i))
    return pl.pallas_call(
        functools.partial(forward_kernel, heads, size),
        grid=(blocks,),
        in_specs=[
            whole(window.shape),
            across,
            whole((features, width)),
            whole(kernel_x.shape),
            whole(kernel_bc.shape),
            whole(head.shape),
            whole(channel.shape),
            rows(width),
            rows(width),
            rows(bcdt.shape[1]),
        ],
        out_specs=[rows(width), rows(features), across, *saved_specs(heads, size, lambda i: i)],
        out_shape=[
            made(width, BF16),
            made(features, BF16),
            jax.ShapeDtypeStruct((8, length), F32),
            *[
                jax.ShapeDtypeStruct((blocks,) + shape, F32) for shape in ((N, width), (8, width))
            ],
            *[made(columns, dtype) for columns, dtype in saved_rows(heads, size)],
        ],
        scratch_shapes=[
            pltpu.VMEM((Q + HALO, width), F32),
            pltpu.VMEM((Q + HALO, 2 * N), F32),
            pltpu.VMEM((N, width), F32),
        ],
        compiler_params=pltpu.CompilerParams(vmem_limit_bytes=VMEM_LIMIT),
        cost_estimate=cost(14),
        name="forward",
    )(window, seg_row, weights, kernel_x, kernel_bc, head, channel, z_proj, x_proj, bcdt)


def run_gradient(place, near, weights, scaled, window):
    features = near[0].shape[1]
    length, width = scaled.shape
    return pl.pallas_call(
        functools.partial(gradient_kernel, width, len(near)),
        grid=(length // Q,),
        in_specs=[
            scalar(),
            *[whole(block.shape) for block in near],
            whole((features, width)),
            pl.BlockSpec((Q, width), lambda i: (i, 0)),
            whole(window.shape),
        ],
        out_specs=[
            pl.BlockSpec((Q, features), lambda i: (i, 0)),
            pl.BlockSpec((Q, width), lambda i: (i, 0)),
            pl.BlockSpec((8, Q), lambda i: (0, i)),
        ],
        out_shape=[
            jax.ShapeDtypeStruct((length, features), BF16),
            jax.ShapeDtypeStruct((length, width), F32),
            jax.ShapeDtypeStruct((8, length), F32),
        ],
        compiler_params=pltpu.CompilerParams(vmem_limit_bytes=VMEM_LIMIT),
        cost_estimate=cost(5),
        name="out_gradient",
    )(place, *near, weights, scaled, window)


def weights_kernel(width, cot_ref, normed_ref, tokens_ref, grads_ref, first_ref, second_ref):
    tokens = tokens_ref[...]
    first_ref[:, :width] = dot_tn(cot_ref[...], normed_ref[...]).astype(BF16)
    first_ref[:, width:] = dot_tn(tokens, grads_ref[:, 2 * width :]).astype(BF16)
    second_ref[...] = dot_tn(tokens, grads_ref[:, : 2 * width]).astype(BF16)


def run_weights(cot, normed, tokens, grads):
    length, features = tokens.shape
    width = normed.shape[1]
    columns = [grads.shape[1] - width, 2 * width]
    return pl.pallas_call(
        functools.partial(weights_kernel, width),
        grid=(features // Q,),
        in_specs=[
            pl.BlockSpec((length, Q), lambda i: (0, i)),
            whole(normed.shape),
            pl.BlockSpec((length, Q), lambda i: (0, i)),
            whole(grads.shape),
        ],
        out_specs=[pl.BlockSpec((Q, count), lambda i: (i, 0)) for count in columns],
        out_shape=[jax.ShapeDtypeStruct((features, count), BF16) for count in columns],
        compiler_params=pltpu.CompilerParams(vmem_limit_bytes=VMEM_LIMIT),
        cost_estimate=cost(7),
        name="weight_gradients",
    )(cot, normed, tokens, grads)


def run_backward(
    heads, size, full_inner, stat, hidden, window, weights, kernel_x, kernel_bc, head, channel,
    x_proj, bcdt, grad_out, saved,
):
    length, features = hidden.shape
    width = heads * size
    blocks = length // Q
    rest = 2 * N + LANES
    total = 2 * width + rest

    def rows(columns):
        return pl.BlockSpec((Q, columns), lambda i: (blocks - 1 - i, 0))

    def made(columns, dtype):
        return jax.ShapeDtypeStruct((length, columns), dtype)

    across = pl.BlockSpec((8, Q), lambda i: (0, blocks - 1 - i))
    sums = [(8, width), (8, 2 * N), (8, LANES), (8, features)]
    return pl.pallas_call(
        functools.partial(backward_kernel, heads, size, full_inner),
        grid=(blocks,),
        in_specs=[
            across,
            rows(features),
            whole(window.shape),
            whole(weights.shape),
            whole(kernel_x.shape),
            whole(kernel_bc.shape),
            whole(head.shape),
            whole(channel.shape),
            rows(width),
            rows(rest),
            rows(width),
            *saved_specs(heads, size, lambda i: blocks - 1 - i),
        ],
        out_specs=[rows(total), rows(features), rows(width)] + [whole(shape) for shape in sums],
        out_shape=[made(total, BF16), made(features, BF16), made(width, BF16)]
        + [jax.ShapeDtypeStruct(shape, F32) for shape in sums],
        scratch_shapes=[
            pltpu.VMEM((Q + HALO, width), F32),
            pltpu.VMEM((Q + HALO, 2 * N), F32),
            pltpu.VMEM((N, width), F32),
            pltpu.VMEM((8, LANES), F32),
        ],
        compiler_params=pltpu.CompilerParams(vmem_limit_bytes=VMEM_LIMIT),
        cost_estimate=cost(27),
        name="backward",
    )(
        stat, hidden, window, weights, kernel_x, kernel_bc, head, channel, x_proj, bcdt, grad_out,
        *saved,
    )


def finish_kernel(sum_ref, hidden_ref, cot_ref, gain_ref, out_ref):
    grad = sum_ref[...].astype(F32) * gain_ref[0:1, :]
    hidden = hidden_ref[...].astype(F32)
    inverse = lax.rsqrt(jnp.mean(hidden * hidden, axis=1, keepdims=True) + EPS)
    unit = hidden * inverse
    along = jnp.mean(grad * unit, axis=1, keepdims=True)
    out_ref[...] = (cot_ref[...].astype(F32) + inverse * (grad - unit * along)).astype(BF16)


def run_finish(in_sum, hidden, cot, gain):
    length, features = hidden.shape
    rows = pl.BlockSpec((length // 2, features), lambda i: (i, 0))
    return pl.pallas_call(
        finish_kernel,
        grid=(2,),
        in_specs=[rows, rows, rows, whole(gain.shape)],
        out_specs=rows,
        out_shape=jax.ShapeDtypeStruct(hidden.shape, BF16),
        compiler_params=pltpu.CompilerParams(vmem_limit_bytes=VMEM_LIMIT),
        name="finish",
    )(in_sum, hidden, cot, gain)


def pad_lanes(values):
    return jnp.pad(values, ((0, 0), (0, LANES - values.shape[1])))


def after(value, *others):
    return lax.optimization_barrier((value, *others))[0]


def line_step(right, left, step, axis):
    n = lax.axis_size(axis)
    return (
        lax.ppermute(right, axis, [(i, i + 1) for i in range(step - 1, n - 1)]),
        lax.ppermute(left, axis, [(i, i - 1) for i in range(1, n - step + 1)]),
    )


def line_order(block, moved):
    return [pair[0] for pair in moved[::-1]] + [block] + [pair[1] for pair in moved]


def line_gather(block, axis):
    right = left = block
    moved = []
    for step in range(1, lax.axis_size(axis)):
        right, left = line_step(right, left, step, axis)
        moved.append((right, left))
    return line_order(block, moved)


def cube_scatter(first, second, small, axis):
    n = lax.axis_size(axis)
    if n & (n - 1):
        sums = [
            lax.psum_scatter(part, axis, scatter_dimension=0, tiled=True).astype(F32)
            for part in (first, second)
        ]
        return (*sums, lax.psum(small, axis), sums)
    place = lax.axis_index(axis)
    bits = list(range(n.bit_length() - 1))
    orders = [bits, bits[:1] + bits[:0:-1]]
    parts = [part.reshape((2,) * len(bits) + (-1, part.shape[1])) for part in (first, second)]
    left = [bits[::-1], bits[::-1]]
    came = [None, None]
    for step in range(len(bits)):
        for index in range(2):
            part = parts[index]
            bit = orders[index][step]
            dim = left[index].index(bit)
            mine = (place >> bit) & 1
            keep = lax.dynamic_index_in_dim(part, mine, dim, keepdims=False)
            send = lax.dynamic_index_in_dim(part, 1 - mine, dim, keepdims=False)
            pairs = [(i, i ^ (1 << bit)) for i in range(n)]
            if index == 0:
                columns = part.shape[-1]
                rows = send.size // columns
                extra = -(-small.size // (16 * columns)) * 16
                small = lax.reduce_precision(small, 8, 7)
                rider = jnp.pad(
                    small.astype(BF16).reshape(-1), (0, extra * columns - small.size)
                ).reshape(extra, columns)
                moved = lax.ppermute(
                    jnp.concatenate([send.reshape(rows, columns), rider]), axis, pairs
                )
                other = moved[:rows].reshape(send.shape)
                rider = moved[rows:].reshape(-1)[: small.size].reshape(small.shape)
                small = small + rider.astype(F32)
            else:
                moved = other = lax.ppermute(send, axis, pairs)
            came[index] = moved
            part = keep.astype(F32) + other.astype(F32)
            left[index] = [other_bit for other_bit in left[index] if other_bit != bit]
            parts[index] = part.astype(BF16) if left[index] else part
    return (*parts, small, came)


def around(values, axis):
    n = lax.axis_size(axis)
    return [values] + [
        lax.ppermute(values, axis, [(i, (i - k) % n) for i in range(n)]) for k in range(1, n)
    ]


def sum_around(values, axis):
    return functools.reduce(jnp.add, around(values, axis))


def shards(
    hidden,
    seg_ids,
    cotangent,
    norm_gain,
    w_in_z,
    w_in_x,
    w_in_bc,
    w_in_dt,
    conv_x,
    conv_x_bias,
    conv_bc,
    conv_bc_bias,
    dt_bias,
    a_log,
    d_skip,
    gate_gain,
    w_out,
):
    heads = dt_bias.shape[0]
    width = gate_gain.shape[0]
    size = width // heads
    full_inner = width * lax.axis_size("tensor")
    features = hidden.shape[2]
    hidden_local = hidden[0]

    packed = run_pack(heads, w_out, w_in_x, w_in_z, w_in_bc, w_in_dt, norm_gain[:, None])
    n = lax.axis_size("tensor")
    axis_place = lax.axis_index("tensor")
    place = axis_place[None]
    near_hidden = line_gather(hidden_local, "tensor")
    weights = lax.all_gather(packed, "dp", axis=0, tiled=True)
    seg_stack = around(seg_ids[0], "tensor")
    count = seg_ids.shape[1]
    seg_full = lax.dynamic_slice_in_dim(
        jnp.concatenate(seg_stack + seg_stack), (n - axis_place) * count, n * count, 0
    )
    window = jnp.broadcast_to(
        jnp.pad(seg_full, (HALO, HALO), constant_values=-1)[:, None],
        (seg_full.shape[0] + 2 * HALO, LANES),
    )
    seg_row = jnp.broadcast_to(seg_full[None, :], (8, seg_full.shape[0]))
    kernel_x = jnp.concatenate([conv_x, conv_x_bias[None, :]], axis=0)
    kernel_bc = jnp.concatenate([conv_bc, conv_bc_bias[None, :]], axis=0)
    head = pad_lanes(jnp.stack([dt_bias, a_log]))
    channel = jnp.stack([gate_gain, jnp.repeat(d_skip, size)])

    hidden_full, tokens, z_proj, x_proj, bcdt, gain = run_project(
        heads, size, place, near_hidden, weights
    )
    right = left = after(cotangent[0], near_hidden[0], near_hidden[-1])
    moved = []
    right, left = line_step(right, left, 1, "tensor")
    moved.append((right, left))
    bcdt = after(bcdt, right, left)
    right, left = line_step(after(right, gain), after(left, gain), 2, "tensor")
    moved.append((right, left))
    scaled, out_part, square, *saved = run_forward(
        heads, size, window, seg_row, weights, kernel_x, kernel_bc, head, channel, z_proj, x_proj,
        bcdt,
    )
    for step in range(3, n):
        right, left = line_step(after(right, square), after(left, square), step, "tensor")
        moved.append((right, left))
    near_cot = line_order(cotangent[0], moved)
    cot_full, grad_out, along = run_gradient(place, near_cot, weights, scaled, window)
    out_sum = lax.psum_scatter(
        after(out_part, along), "tensor", scatter_dimension=0, tiled=True
    )
    stat = sum_around(jnp.stack([square[0], along[0]]), "tensor")
    stat_full = jnp.pad(stat, ((0, 6), (0, 0)))
    out_scale = lax.rsqrt(stat[0] / full_inner + EPS) * (seg_full > 0).astype(F32)

    grads, in_part, normed_out, sum_x, sum_bc, sum_head, sum_gain = run_backward(
        heads, size, full_inner, stat_full, hidden_full, window, weights, kernel_x, kernel_bc, head,
        channel, x_proj, bcdt, grad_out, saved,
    )
    in_sum = lax.psum_scatter(in_part, "tensor", scatter_dimension=0, tiled=True)
    first, second = run_weights(cot_full, normed_out, tokens, grads)
    own = jnp.concatenate([sum_x.reshape(-1, LANES), sum_head])
    both = jnp.concatenate([sum_gain[0].reshape(-1, LANES), sum_bc.reshape(-1, LANES)])
    first, second, small, came = cube_scatter(first, second, jnp.concatenate([own, both]), "dp")
    sum_x = small[: own.shape[0] - 8].reshape(8, width)
    sum_head = small[own.shape[0] - 8 : own.shape[0]]
    grad_bc = first[:, width : width + 2 * N]
    shared = jnp.concatenate([small[own.shape[0] :], grad_bc.reshape(-1, LANES)])
    shared = sum_around(shared, "tensor")
    gain_rows = features // LANES
    sum_gain = shared[:gain_rows].reshape(features)
    sum_bc = shared[gain_rows : both.shape[0]].reshape(8, 2 * N)
    grad_bc = shared[both.shape[0] :].reshape(grad_bc.shape)
    local_features = norm_gain.shape[0]
    grad_norm_gain = lax.dynamic_slice_in_dim(
        sum_gain, lax.axis_index("dp") * local_features, local_features, 0
    )

    local = hidden_local.shape[0]
    hidden_rows = hidden_local.astype(F32)
    scale_here = lax.dynamic_slice_in_dim(out_scale, axis_place * local, local, 0)[:, None]
    layer_out = (hidden_rows + out_sum.astype(F32) * scale_here).astype(BF16)

    grad_hidden = run_finish(in_sum, hidden_local, cotangent[0], after(gain, came[1]))

    return (
        layer_out[None],
        grad_hidden[None],
        grad_norm_gain,
        second[:, width:],
        second[:, :width],
        grad_bc,
        first[:, width + 2 * N : width + 2 * N + heads],
        sum_x[0:CONV],
        sum_x[CONV],
        sum_bc[0:CONV],
        sum_bc[CONV],
        sum_head[0, :heads],
        sum_head[1, :heads],
        jnp.sum(sum_x[CONV + 2].reshape(heads, size), axis=1),
        sum_x[CONV + 1],
        first[:, :width],
    )


def solution(mesh):
    in_specs = (
        P("dp", "tensor", None),
        P("dp", "tensor"),
        P("dp", "tensor", None),
        P("dp"),
        P("dp", "tensor"),
        P("dp", "tensor"),
        P("dp", None),
        P("dp", "tensor"),
        P(None, "tensor"),
        P("tensor"),
        P(),
        P(),
        P("tensor"),
        P("tensor"),
        P("tensor"),
        P("tensor"),
        P("dp", "tensor"),
    )
    out_specs = (
        P("dp", "tensor", None),
        P("dp", "tensor", None),
        P("dp"),
        P("dp", "tensor"),
        P("dp", "tensor"),
        P("dp", None),
        P("dp", "tensor"),
        P(None, "tensor"),
        P("tensor"),
        P(),
        P(),
        P("tensor"),
        P("tensor"),
        P("tensor"),
        P("tensor"),
        P("dp", "tensor"),
    )
    return jax.shard_map(shards, mesh=mesh, in_specs=in_specs, out_specs=out_specs, check_vma=False)
```

```python
import functools

import jax
import jax.numpy as jnp
from jax import lax
from jax.experimental import pallas as pl
from jax.experimental.pallas import tpu as pltpu
from jax.sharding import PartitionSpec as P

N = 128
CONV = 4
Q = 256
LANES = 128
HALO = 8
EPS = 1e-05
NEG = -1e30
F32 = jnp.float32
BF16 = jnp.bfloat16
VMEM_LIMIT = 52 * 1024 * 1024


def dot(a, b):
    return jnp.dot(a, b, preferred_element_type=F32)


def dot_nt(a, b):
    return lax.dot_general(a, b, (((1,), (1,)), ((), ())), preferred_element_type=F32)


def dot_tn(a, b):
    return lax.dot_general(a, b, (((0,), (0,)), ((), ())), preferred_element_type=F32)


def dot_exact(a, b):
    return jnp.dot(a, b, preferred_element_type=F32, precision=lax.Precision.HIGHEST)


def spread(cols, heads, size):
    rows = cols.shape[0]
    per = LANES // size
    lane = lax.broadcasted_iota(jnp.int32, (rows, LANES), 1)
    parts = []
    for first in range(0, heads, per):
        part = jnp.broadcast_to(cols[:, first : first + 1], (rows, LANES))
        for extra in range(1, per):
            part = jnp.where(lane < extra * size, part, cols[:, first + extra : first + extra + 1])
        parts.append(part)
    return jnp.concatenate(parts, axis=1)


def head_sums(values, heads, size):
    width = heads * size
    channel = lax.broadcasted_iota(jnp.int32, (width, LANES), 0)
    column = lax.broadcasted_iota(jnp.int32, (width, LANES), 1)
    first = column * size
    picks = jnp.where((channel >= first) & (channel < first + size), 1.0, 0.0).astype(BF16)
    high = values.astype(BF16)
    low = (values - high.astype(F32)).astype(BF16)
    return dot(high, picks) + dot(low, picks)


def widen(tile, width):
    return jnp.concatenate([tile] * (width // tile.shape[1]), axis=1)


def softplus(v):
    return jnp.maximum(v, 0.0) + jnp.log1p(jnp.exp(-jnp.abs(v)))


def sigmoid(v):
    return 1.0 / (1.0 + jnp.exp(-v))


def as_row(column):
    rows = column.shape[0]
    return jnp.broadcast_to(column, (rows, LANES)).T[:8]


def triangle(lower):
    row = lax.broadcasted_iota(jnp.int32, (Q, Q), 0)
    col = lax.broadcasted_iota(jnp.int32, (Q, Q), 1)
    return row >= col if lower else row <= col


def block_masks(window, seg_row):
    seg = window[HALO : HALO + Q]
    before = window[HALO - 1 : HALO]
    last = window[HALO + Q - 1 : HALO + Q]
    from_prev = (seg == before).astype(F32)
    same_last = (seg == last).astype(F32)
    passes = (last == before).astype(F32)
    keep = (widen(seg, Q) == seg_row) & triangle(True)
    bias = jnp.where(keep, 0.0, NEG)
    return seg, from_prev, same_last, passes, bias


def conv_forward(buffer, window, seg, kernel, conv_bias, width):
    total = conv_bias + kernel[CONV - 1 : CONV] * buffer[HALO : HALO + Q, :]
    for back in range(1, CONV):
        match = (window[HALO - back : HALO - back + Q] == seg).astype(F32)
        tap = kernel[CONV - 1 - back : CONV - back]
        total = total + tap * (buffer[HALO - back : HALO - back + Q, :] * widen(match, width))
    return total


def conv_backward(buffer, window, seg, kernel, values, width):
    here = buffer[0:Q, :]
    total = kernel[CONV - 1 : CONV] * here
    taps = [jnp.sum(values * here, axis=0, keepdims=True)]
    for ahead in range(1, CONV):
        match = (window[HALO + ahead : HALO + ahead + Q] == seg).astype(F32)
        moved = buffer[ahead : ahead + Q, :] * widen(match, width)
        total = total + kernel[CONV - 1 - ahead : CONV - ahead] * moved
        taps.append(jnp.sum(values * moved, axis=0, keepdims=True))
    return total, taps


def pick_block(place, near_refs, block):
    reach = len(near_refs) // 2
    away = pl.program_id(0) - place
    for index, ref in enumerate(near_refs):

        @pl.when(away == index - reach)
        def _():
            block[...] = ref[...]


def project_kernel(heads, size, near, place_ref, *refs):
    near_refs, refs = refs[:near], refs[near:]
    weights_ref, hidden_ref, tokens_ref, z_ref, x_ref, bcdt_ref, gain_ref = refs
    width = heads * size

    @pl.when(pl.program_id(0) == 0)
    def _():
        tail_columns = weights_ref[:, 3 * width + 2 * N :].astype(F32).T
        gain_ref[...] = jnp.broadcast_to(tail_columns[heads : heads + 1], gain_ref.shape)

    pick_block(place_ref[0], near_refs, hidden_ref)
    hidden = hidden_ref[...].astype(F32)
    inverse = lax.rsqrt(jnp.mean(hidden * hidden, axis=1, keepdims=True) + EPS)
    tokens = (hidden * inverse * gain_ref[0:1, :]).astype(BF16)
    tokens_ref[...] = tokens
    x_ref[...] = dot(tokens, weights_ref[:, width : 2 * width])
    z_ref[...] = dot(tokens, weights_ref[:, 2 * width : 3 * width])
    bcdt_ref[...] = dot(tokens, weights_ref[:, 3 * width :])


def forward_kernel(
    heads,
    size,
    window_ref,
    seg_row_ref,
    weights_ref,
    kernel_x_ref,
    kernel_bc_ref,
    head_ref,
    channel_ref,
    z_ref,
    x_ref,
    bcdt_ref,
    scaled_ref,
    part_ref,
    square_ref,
    state_ref,
    survive_ref,
    shape_ref,
    prob_ref,
    gated_ref,
    opened_ref,
    slope_z_ref,
    inner_ref,
    carried_ref,
    x_conv_ref,
    slope_x_ref,
    dt_ref,
    from_start_ref,
    to_end_ref,
    weighted_ref,
    weighted_end_ref,
    bc_ref,
    slope_bc_ref,
    decay_ref,
    slope_dt_ref,
    x_buffer,
    bc_buffer,
    carry,
):
    step = pl.program_id(0)
    width = heads * size

    @pl.when(step == 0)
    def _():
        x_buffer[0:HALO, :] = jnp.zeros((HALO, width), F32)
        bc_buffer[0:HALO, :] = jnp.zeros((HALO, 2 * N), F32)
        carry[...] = jnp.zeros((N, width), F32)

    window = window_ref[pl.ds(pl.multiple_of(step * Q, Q), Q + 2 * HALO), :]
    seg, from_prev, same_last, passes, bias = block_masks(window, seg_row_ref[0:1, :])
    bcdt = bcdt_ref[...]
    x_buffer[HALO : HALO + Q, :] = x_ref[...]
    bc_buffer[HALO : HALO + Q, :] = bcdt[:, : 2 * N]
    pre = conv_forward(
        x_buffer, window, seg, kernel_x_ref[...], kernel_x_ref[CONV : CONV + 1, :], width
    )
    pre_bc = conv_forward(
        bc_buffer, window, seg, kernel_bc_ref[...], kernel_bc_ref[CONV : CONV + 1, :], 2 * N
    )
    x_buffer[0:HALO, :] = x_buffer[Q : Q + HALO, :]
    bc_buffer[0:HALO, :] = bc_buffer[Q : Q + HALO, :]
    gate_x = sigmoid(pre)
    x_conv = pre * gate_x
    x_conv_ref[...] = x_conv
    slope_x_ref[...] = gate_x * (1.0 + pre * (1.0 - gate_x))
    gate_bc = sigmoid(pre_bc)
    bc_conv = (pre_bc * gate_bc).astype(BF16)
    bc_ref[...] = bc_conv
    slope_bc_ref[...] = gate_bc * (1.0 + pre_bc * (1.0 - gate_bc))
    b_in = bc_conv[:, :N]
    c_in = bc_conv[:, N:]

    raw = bcdt[:, 2 * N :] + head_ref[0:1, :]
    slope_dt_ref[...] = sigmoid(raw)
    dt = softplus(raw)
    decay = -dt * jnp.exp(head_ref[1:2, :])
    decay_ref[...] = decay
    total = dot_exact(triangle(True).astype(F32), decay)
    total_t = total.T
    dt_wide = spread(dt, heads, size)
    dt_ref[...] = dt_wide
    weighted = x_conv * dt_wide
    weighted_low = weighted.astype(BF16)
    weighted_ref[...] = weighted_low
    scores = dot_nt(c_in, b_in)
    before = carry[...]
    state_ref[0] = before

    per = LANES // size
    lane = lax.broadcasted_iota(jnp.int32, (Q, LANES), 1)
    none = jnp.zeros((Q, LANES), BF16)
    inner = []
    for first in range(0, heads, per):
        group = weighted_low[:, first * size : first * size + LANES]
        summed = jnp.zeros((Q, LANES), F32)
        for extra in range(per):
            h = first + extra
            shape = jnp.exp(total[:, h : h + 1] - total_t[h : h + 1, :] + bias)
            prob = (scores * shape).astype(BF16)
            shape_ref[:, h * Q : (h + 1) * Q] = shape.astype(BF16)
            prob_ref[:, h * Q : (h + 1) * Q] = prob
            mine = (lane >= extra * size) & (lane < (extra + 1) * size)
            summed = summed + dot(prob, jnp.where(mine, group, none))
        inner.append(summed)
    inner = jnp.concatenate(inner, axis=1)
    inner_ref[...] = inner
    carried = dot(c_in, before.astype(BF16))
    carried_ref[...] = carried
    from_start = spread(jnp.exp(total) * from_prev, heads, size)
    from_start_ref[...] = from_start
    last = total[Q - 1 : Q, :]
    to_end = spread(jnp.exp(last - total) * same_last, heads, size)
    to_end_ref[...] = to_end
    weighted_end = (weighted * to_end).astype(BF16)
    weighted_end_ref[...] = weighted_end
    survive = spread(jnp.exp(last) * passes, heads, size)
    survive_ref[0] = jnp.broadcast_to(survive, (8, width))
    carry[...] = dot_tn(b_in, weighted_end) + before * survive

    mixed = inner + carried * from_start + channel_ref[1:2, :] * x_conv
    z_proj = z_ref[...]
    gate = sigmoid(z_proj)
    opened = z_proj * gate
    opened_ref[...] = opened
    slope_z_ref[...] = mixed * (gate * (1.0 + z_proj * (1.0 - gate)))
    gated = mixed * opened
    gated_ref[...] = gated
    scaled = (gated * channel_ref[0:1, :]).astype(BF16)
    scaled_ref[...] = scaled
    part_ref[...] = dot_nt(scaled, weights_ref[...]).astype(BF16)
    square_ref[...] = as_row(jnp.sum(gated * gated, axis=1, keepdims=True))


def gradient_kernel(width, cot_ref, weights_ref, scaled_ref, window_ref, grad_ref, along_ref):
    step = pl.program_id(0)
    window = window_ref[pl.ds(pl.multiple_of(step * Q, Q), Q + 2 * HALO), :]
    live = (window[HALO : HALO + Q] > 0).astype(F32)
    grad = dot(cot_ref[...], weights_ref[...]) * widen(live, width)
    grad_ref[...] = grad
    along_ref[...] = as_row(jnp.sum(scaled_ref[...].astype(F32) * grad, axis=1, keepdims=True))


def backward_kernel(
    heads,
    size,
    full_inner,
    stat_ref,
    hidden_ref,
    window_ref,
    weights_ref,
    kernel_x_ref,
    kernel_bc_ref,
    head_ref,
    channel_ref,
    x_ref,
    bcdt_ref,
    grad_ref,
    state_ref,
    survive_ref,
    shape_ref,
    prob_ref,
    gated_ref,
    opened_ref,
    slope_z_ref,
    inner_ref,
    carried_ref,
    x_conv_ref,
    slope_x_ref,
    dt_ref,
    from_start_ref,
    to_end_ref,
    weighted_ref,
    weighted_end_ref,
    bc_ref,
    slope_bc_ref,
    decay_ref,
    slope_dt_ref,
    proj_ref,
    part_ref,
    out_ref,
    sum_x_ref,
    sum_bc_ref,
    sum_head_ref,
    sum_gain_ref,
    x_buffer,
    bc_buffer,
    carry,
    tail,
):
    turn = pl.program_id(0)
    step = pl.num_programs(0) - 1 - turn
    width = heads * size

    @pl.when(turn == 0)
    def _():
        x_buffer[...] = jnp.zeros((Q + HALO, width), F32)
        bc_buffer[...] = jnp.zeros((Q + HALO, 2 * N), F32)
        carry[...] = jnp.zeros((N, width), F32)
        tail[...] = jnp.zeros((8, LANES), F32)
        sum_x_ref[...] = jnp.zeros((8, width), F32)
        sum_bc_ref[...] = jnp.zeros((8, 2 * N), F32)
        sum_head_ref[...] = jnp.zeros((8, LANES), F32)
        sum_gain_ref[...] = jnp.zeros(sum_gain_ref.shape, F32)

    window = window_ref[pl.ds(pl.multiple_of(step * Q, Q), Q + 2 * HALO), :]
    seg = window[HALO : HALO + Q]
    live = (seg[:, 0:1] > 0).astype(F32)
    stat = stat_ref[...].T
    gate_inverse = lax.rsqrt(stat[:, 0:1] / full_inner + EPS)
    along = stat[:, 1:2] * (gate_inverse * gate_inverse * gate_inverse / full_inner)

    gain = channel_ref[0:1, :]
    skip = channel_ref[1:2, :]
    grad_out = grad_ref[...]
    gated = gated_ref[...]
    normal = gated * gate_inverse
    sum_gate = jnp.sum(grad_out * normal, axis=0, keepdims=True)
    out_ref[...] = (normal * gain * live).astype(BF16)
    grad_gated = grad_out * gain * gate_inverse - gated * along
    grad_z = (grad_gated * slope_z_ref[...]).astype(BF16)
    dy = grad_gated * opened_ref[...]
    dy_low = dy.astype(BF16)
    dy_start = (dy * from_start_ref[...]).astype(BF16)

    bc_conv = bc_ref[...]
    b_in = bc_conv[:, :N]
    c_in = bc_conv[:, N:]
    before = state_ref[0]
    before_low = before.astype(BF16)
    after_low = carry[...].astype(BF16)
    weighted_low = weighted_ref[...]
    weighted_end = weighted_end_ref[...]
    grad_c = dot_nt(dy_start, before_low)
    returned = dot(b_in, after_low)
    grad_b = dot_nt(weighted_end, after_low)
    new_after = dot_tn(c_in, dy_start) + carry[...] * survive_ref[0, 0:1, :]
    carry[...] = new_after

    per = LANES // size
    lane = lax.broadcasted_iota(jnp.int32, (Q, LANES), 1)
    grad_scores = jnp.zeros((Q, Q), F32)
    inner = []
    none = jnp.zeros((Q, LANES), BF16)
    for first in range(0, heads, per):
        at = first * size
        dy_group = dy_low[:, at : at + LANES]
        weighted_group = weighted_low[:, at : at + LANES]
        summed = jnp.zeros((Q, LANES), F32)
        for extra in range(per):
            h = first + extra
            mine = (lane >= extra * size) & (lane < (extra + 1) * size)
            dy_mine = jnp.where(mine, dy_group, none)
            shape = shape_ref[:, h * Q : (h + 1) * Q].astype(F32)
            grad_scores = grad_scores + dot_nt(dy_mine, weighted_group) * shape
            summed = summed + dot_tn(prob_ref[:, h * Q : (h + 1) * Q], dy_mine)
        inner.append(summed)
    grad_inner = jnp.concatenate(inner, axis=1)
    grad_weighted = to_end_ref[...] * returned + grad_inner
    grad_scores = grad_scores.astype(BF16)
    grad_c = grad_c + dot(grad_scores, b_in)
    grad_b = grad_b + dot_tn(grad_scores, c_in)

    x_conv = x_conv_ref[...]
    pairs = head_sums(
        dy_low.astype(F32) * inner_ref[...]
        + dy_start.astype(F32) * carried_ref[...]
        - weighted_low.astype(F32) * grad_inner
        - weighted_end.astype(F32) * returned,
        heads,
        size,
    )
    grad_decay = dot_exact(triangle(False).astype(F32), pairs) + tail[0:1, :]
    kept = jnp.sum(new_after.astype(BF16).astype(F32) * before, axis=0, keepdims=True)
    tail[...] = head_sums(jnp.broadcast_to(kept, (8, width)), heads, size)
    rate = jnp.exp(head_ref[1:2, :])
    grad_dt = head_sums(grad_weighted * x_conv, heads, size) - grad_decay * rate
    grad_raw = grad_dt * slope_dt_ref[...]
    sum_head_ref[0:1, :] += jnp.sum(grad_raw, axis=0, keepdims=True)
    sum_head_ref[1:2, :] += jnp.sum(grad_decay * decay_ref[...], axis=0, keepdims=True)

    sum_skip = jnp.sum(dy * x_conv, axis=0, keepdims=True)
    grad_pre = (grad_weighted * dt_ref[...] + skip * dy) * slope_x_ref[...]
    x_buffer[Q : Q + HALO, :] = x_buffer[0:HALO, :]
    x_buffer[0:Q, :] = grad_pre
    grad_proj, taps = conv_backward(
        x_buffer, window, seg, kernel_x_ref[...], x_ref[...], width
    )
    sum_bias = jnp.sum(grad_pre, axis=0, keepdims=True)
    blank = jnp.zeros((1, width), F32)
    sum_x_ref[...] += jnp.concatenate(
        [taps[3], taps[2], taps[1], taps[0], sum_bias, sum_gate, sum_skip, blank], axis=0
    )

    grad_pre_bc = jnp.concatenate([grad_b, grad_c], axis=1) * slope_bc_ref[...]
    bc_buffer[Q : Q + HALO, :] = bc_buffer[0:HALO, :]
    bc_buffer[0:Q, :] = grad_pre_bc
    grad_bc, taps_bc = conv_backward(
        bc_buffer, window, seg, kernel_bc_ref[...], bcdt_ref[:, : 2 * N], 2 * N
    )
    sum_bias_bc = jnp.sum(grad_pre_bc, axis=0, keepdims=True)
    blank_bc = jnp.zeros((3, 2 * N), F32)
    sum_bc_ref[...] += jnp.concatenate(
        [taps_bc[3], taps_bc[2], taps_bc[1], taps_bc[0], sum_bias_bc, blank_bc], axis=0
    )

    grads = jnp.concatenate(
        [grad_proj.astype(BF16), grad_z, grad_bc.astype(BF16), grad_raw.astype(BF16)], axis=1
    )
    proj_ref[...] = grads
    part = dot_nt(grads, weights_ref[:, width:])
    part_ref[...] = part.astype(BF16)
    hidden = hidden_ref[...].astype(F32)
    inverse = lax.rsqrt(jnp.mean(hidden * hidden, axis=1, keepdims=True) + EPS)
    sum_gain_ref[0:1, :] += jnp.sum(part * (hidden * inverse), axis=0, keepdims=True)


def pack_kernel(*refs):
    *parts, packed, sems = refs
    at = 0
    copies = []
    for index, part in enumerate(parts):
        columns = part.shape[1]
        copies.append(
            pltpu.make_async_copy(part, packed.at[:, pl.ds(at, columns)], sems.at[index])
        )
        at += columns
    for copy in copies:
        copy.start()
    for copy in copies:
        copy.wait()


def run_pack(*parts):
    rows = parts[0].shape[0]
    columns = sum(part.shape[1] for part in parts)
    return pl.pallas_call(
        pack_kernel,
        in_specs=[pl.BlockSpec(memory_space=pl.ANY)] * len(parts),
        out_specs=pl.BlockSpec(memory_space=pl.ANY),
        out_shape=jax.ShapeDtypeStruct((rows, columns), BF16),
        scratch_shapes=[pltpu.SemaphoreType.DMA((len(parts),))],
        compiler_params=pltpu.CompilerParams(vmem_limit_bytes=VMEM_LIMIT),
        name="pack",
    )(*parts)


def cost(micros):
    return pl.CostEstimate(flops=int(micros * 1e9), bytes_accessed=1 << 20, transcendentals=0)


def whole(shape):
    return pl.BlockSpec(shape, lambda i: (0,) * len(shape))


def scalar():
    return pl.BlockSpec(memory_space=pltpu.SMEM)


def run_project(heads, size, place, near, weights):
    features = near[0].shape[1]
    blocks = len(near) // 2 + 1
    length = blocks * Q
    width = heads * size
    rest = 2 * N + LANES

    def rows(columns):
        return pl.BlockSpec((Q, columns), lambda i: (i, 0))

    def made(columns, dtype):
        return jax.ShapeDtypeStruct((length, columns), dtype)

    return pl.pallas_call(
        functools.partial(project_kernel, heads, size, len(near)),
        grid=(blocks,),
        in_specs=[scalar(), *[whole(block.shape) for block in near], whole(weights.shape)],
        out_specs=[
            rows(features),
            rows(features),
            rows(width),
            rows(width),
            rows(rest),
            whole((8, features)),
        ],
        out_shape=[
            made(features, BF16),
            made(features, BF16),
            made(width, F32),
            made(width, F32),
            made(rest, F32),
            jax.ShapeDtypeStruct((8, features), F32),
        ],
        compiler_params=pltpu.CompilerParams(vmem_limit_bytes=VMEM_LIMIT),
        cost_estimate=cost(8),
        name="project",
    )(place, *near, weights)


def saved_rows(heads, size):
    width = heads * size
    return (
        [(heads * Q, BF16)] * 2
        + [(width, F32)] * 10
        + [(width, BF16)] * 2
        + [(2 * N, BF16), (2 * N, F32), (LANES, F32), (LANES, F32)]
    )


def saved_specs(heads, size, place):
    width = heads * size
    return [
        pl.BlockSpec((1, N, width), lambda i: (place(i), 0, 0)),
        pl.BlockSpec((1, 8, width), lambda i: (place(i), 0, 0)),
    ] + [
        pl.BlockSpec((Q, columns), lambda i: (place(i), 0))
        for columns, _ in saved_rows(heads, size)
    ]


def run_forward(
    heads, size, window, seg_row, weights, kernel_x, kernel_bc, head, channel, z_proj, x_proj, bcdt
):
    length, features = seg_row.shape[1], weights.shape[0]
    width = heads * size
    blocks = length // Q

    def rows(columns):
        return pl.BlockSpec((Q, columns), lambda i: (i, 0))

    def made(columns, dtype):
        return jax.ShapeDtypeStruct((length, columns), dtype)

    across = pl.BlockSpec((8, Q), lambda i: (0, i))
    return pl.pallas_call(
        functools.partial(forward_kernel, heads, size),
        grid=(blocks,),
        in_specs=[
            whole(window.shape),
            across,
            whole((features, width)),
            whole(kernel_x.shape),
            whole(kernel_bc.shape),
            whole(head.shape),
            whole(channel.shape),
            rows(width),
            rows(width),
            rows(bcdt.shape[1]),
        ],
        out_specs=[rows(width), rows(features), across, *saved_specs(heads, size, lambda i: i)],
        out_shape=[
            made(width, BF16),
            made(features, BF16),
            jax.ShapeDtypeStruct((8, length), F32),
            *[
                jax.ShapeDtypeStruct((blocks,) + shape, F32) for shape in ((N, width), (8, width))
            ],
            *[made(columns, dtype) for columns, dtype in saved_rows(heads, size)],
        ],
        scratch_shapes=[
            pltpu.VMEM((Q + HALO, width), F32),
            pltpu.VMEM((Q + HALO, 2 * N), F32),
            pltpu.VMEM((N, width), F32),
        ],
        compiler_params=pltpu.CompilerParams(vmem_limit_bytes=VMEM_LIMIT),
        cost_estimate=cost(14),
        name="forward",
    )(window, seg_row, weights, kernel_x, kernel_bc, head, channel, z_proj, x_proj, bcdt)


def run_gradient(cot, weights, scaled, window):
    length, features = cot.shape
    width = scaled.shape[1]
    return pl.pallas_call(
        functools.partial(gradient_kernel, width),
        grid=(length // Q,),
        in_specs=[
            pl.BlockSpec((Q, features), lambda i: (i, 0)),
            whole((features, width)),
            pl.BlockSpec((Q, width), lambda i: (i, 0)),
            whole(window.shape),
        ],
        out_specs=[
            pl.BlockSpec((Q, width), lambda i: (i, 0)),
            pl.BlockSpec((8, Q), lambda i: (0, i)),
        ],
        out_shape=[
            jax.ShapeDtypeStruct((length, width), F32),
            jax.ShapeDtypeStruct((8, length), F32),
        ],
        compiler_params=pltpu.CompilerParams(vmem_limit_bytes=VMEM_LIMIT),
        cost_estimate=cost(5),
        name="out_gradient",
    )(cot, weights, scaled, window)


def first_kernel(width, cot_ref, normed_ref, tokens_ref, grads_ref, sum_ref):
    sum_ref[:, :width] = dot_tn(cot_ref[...], normed_ref[...]).astype(BF16)
    sum_ref[:, width:] = dot_tn(tokens_ref[...], grads_ref[...]).astype(BF16)


def second_kernel(tokens_ref, grads_ref, sum_ref):
    sum_ref[...] = dot_tn(tokens_ref[...], grads_ref[...]).astype(BF16)


def run_weights(cot, normed, tokens, grads):
    length, features = tokens.shape
    width = normed.shape[1]
    rest = grads.shape[1] - 2 * width
    params = pltpu.CompilerParams(vmem_limit_bytes=VMEM_LIMIT)
    strip = pl.BlockSpec((length, Q), lambda i: (0, i))
    second = pl.pallas_call(
        second_kernel,
        grid=(features // Q,),
        in_specs=[strip, pl.BlockSpec((length, 2 * width), lambda i: (0, 0))],
        out_specs=pl.BlockSpec((Q, 2 * width), lambda i: (i, 0)),
        out_shape=jax.ShapeDtypeStruct((features, 2 * width), BF16),
        compiler_params=params,
        cost_estimate=cost(4),
        name="weight_gradients_xz",
    )(tokens, grads)
    first = pl.pallas_call(
        functools.partial(first_kernel, width),
        grid=(features // Q,),
        in_specs=[strip, whole(normed.shape), strip, whole((length, rest))],
        out_specs=pl.BlockSpec((Q, width + rest), lambda i: (i, 0)),
        out_shape=jax.ShapeDtypeStruct((features, width + rest), BF16),
        compiler_params=params,
        cost_estimate=cost(4),
        name="weight_gradients_out",
    )(cot, normed, tokens, grads[:, 2 * width :])
    return first, second


def run_backward(
    heads, size, full_inner, stat, hidden, window, weights, kernel_x, kernel_bc, head, channel,
    x_proj, bcdt, grad_out, saved,
):
    length, features = hidden.shape
    width = heads * size
    blocks = length // Q
    rest = 2 * N + LANES
    total = 2 * width + rest

    def rows(columns):
        return pl.BlockSpec((Q, columns), lambda i: (blocks - 1 - i, 0))

    def made(columns, dtype):
        return jax.ShapeDtypeStruct((length, columns), dtype)

    across = pl.BlockSpec((8, Q), lambda i: (0, blocks - 1 - i))
    sums = [(8, width), (8, 2 * N), (8, LANES), (8, features)]
    return pl.pallas_call(
        functools.partial(backward_kernel, heads, size, full_inner),
        grid=(blocks,),
        in_specs=[
            across,
            rows(features),
            whole(window.shape),
            whole(weights.shape),
            whole(kernel_x.shape),
            whole(kernel_bc.shape),
            whole(head.shape),
            whole(channel.shape),
            rows(width),
            rows(rest),
            rows(width),
            *saved_specs(heads, size, lambda i: blocks - 1 - i),
        ],
        out_specs=[rows(total), rows(features), rows(width)] + [whole(shape) for shape in sums],
        out_shape=[made(total, BF16), made(features, BF16), made(width, BF16)]
        + [jax.ShapeDtypeStruct(shape, F32) for shape in sums],
        scratch_shapes=[
            pltpu.VMEM((Q + HALO, width), F32),
            pltpu.VMEM((Q + HALO, 2 * N), F32),
            pltpu.VMEM((N, width), F32),
            pltpu.VMEM((8, LANES), F32),
        ],
        compiler_params=pltpu.CompilerParams(vmem_limit_bytes=VMEM_LIMIT),
        cost_estimate=cost(2),
        name="backward",
    )(
        stat, hidden, window, weights, kernel_x, kernel_bc, head, channel, x_proj, bcdt, grad_out,
        *saved,
    )


def finish_kernel(sum_ref, hidden_ref, cot_ref, gain_ref, out_ref):
    grad = sum_ref[...].astype(F32) * gain_ref[0:1, :]
    hidden = hidden_ref[...].astype(F32)
    inverse = lax.rsqrt(jnp.mean(hidden * hidden, axis=1, keepdims=True) + EPS)
    unit = hidden * inverse
    along = jnp.mean(grad * unit, axis=1, keepdims=True)
    out_ref[...] = (cot_ref[...].astype(F32) + inverse * (grad - unit * along)).astype(BF16)


def run_finish(in_sum, hidden, cot, gain):
    length, features = hidden.shape
    rows = pl.BlockSpec((length // 2, features), lambda i: (i, 0))
    return pl.pallas_call(
        finish_kernel,
        grid=(2,),
        in_specs=[rows, rows, rows, whole(gain.shape)],
        out_specs=rows,
        out_shape=jax.ShapeDtypeStruct(hidden.shape, BF16),
        compiler_params=pltpu.CompilerParams(vmem_limit_bytes=VMEM_LIMIT),
        name="finish",
    )(in_sum, hidden, cot, gain)


def pad_lanes(values):
    return jnp.pad(values, ((0, 0), (0, LANES - values.shape[1])))


def after(value, *others):
    return lax.optimization_barrier((value, *others))[0]


def line_step(right, left, step, axis):
    n = lax.axis_size(axis)
    return (
        lax.ppermute(right, axis, [(i, i + 1) for i in range(step - 1, n - 1)]),
        lax.ppermute(left, axis, [(i, i - 1) for i in range(1, n - step + 1)]),
    )


def line_order(block, moved):
    return [pair[0] for pair in moved[::-1]] + [block] + [pair[1] for pair in moved]


def line_gather(block, axis):
    right = left = block
    moved = []
    for step in range(1, lax.axis_size(axis)):
        right, left = line_step(right, left, step, axis)
        moved.append((right, left))
    return line_order(block, moved)


def cube_scatter(first, second, small, axis):
    n = lax.axis_size(axis)
    if n & (n - 1):
        sums = [
            lax.psum_scatter(part, axis, scatter_dimension=0, tiled=True).astype(F32)
            for part in (first, second)
        ]
        return (*sums, lax.psum(small, axis), sums)
    place = lax.axis_index(axis)
    bits = list(range(n.bit_length() - 1))
    orders = [bits, bits[:1] + bits[:0:-1]]
    parts = [part.reshape((2,) * len(bits) + (-1, part.shape[1])) for part in (first, second)]
    left = [bits[::-1], bits[::-1]]
    came = [None, None]
    for step in range(len(bits)):
        for index in range(2):
            part = parts[index]
            bit = orders[index][step]
            dim = left[index].index(bit)
            mine = (place >> bit) & 1
            keep = lax.dynamic_index_in_dim(part, mine, dim, keepdims=False)
            send = lax.dynamic_index_in_dim(part, 1 - mine, dim, keepdims=False)
            pairs = [(i, i ^ (1 << bit)) for i in range(n)]
            if index == 0:
                columns = part.shape[-1]
                rows = send.size // columns
                extra = -(-small.size // (16 * columns)) * 16
                small = lax.reduce_precision(small, 8, 7)
                rider = jnp.pad(
                    small.astype(BF16).reshape(-1), (0, extra * columns - small.size)
                ).reshape(extra, columns)
                moved = lax.ppermute(
                    jnp.concatenate([send.reshape(rows, columns), rider]), axis, pairs
                )
                other = moved[:rows].reshape(send.shape)
                rider = moved[rows:].reshape(-1)[: small.size].reshape(small.shape)
                small = small + rider.astype(F32)
            else:
                moved = other = lax.ppermute(send, axis, pairs)
            came[index] = moved
            part = keep.astype(F32) + other.astype(F32)
            left[index] = [other_bit for other_bit in left[index] if other_bit != bit]
            parts[index] = part.astype(BF16) if left[index] else part
    return (*parts, small, came)


def around(values, axis):
    n = lax.axis_size(axis)
    return [values] + [
        lax.ppermute(values, axis, [(i, (i - k) % n) for i in range(n)]) for k in range(1, n)
    ]


def sum_around(values, axis):
    return functools.reduce(jnp.add, around(values, axis))


def sum_around_low(values, axis):
    low = around(lax.reduce_precision(values, 8, 7).astype(BF16), axis)
    return functools.reduce(jnp.add, [share.astype(F32) for share in low])


def shards(
    hidden,
    seg_ids,
    cotangent,
    norm_gain,
    w_in_z,
    w_in_x,
    w_in_bc,
    w_in_dt,
    conv_x,
    conv_x_bias,
    conv_bc,
    conv_bc_bias,
    dt_bias,
    a_log,
    d_skip,
    gate_gain,
    w_out,
):
    heads = dt_bias.shape[0]
    width = gate_gain.shape[0]
    size = width // heads
    full_inner = width * lax.axis_size("tensor")
    features = hidden.shape[2]
    hidden_local = hidden[0]

    steps = jnp.pad(
        jnp.concatenate([w_in_dt, norm_gain[:, None]], axis=1), ((0, 0), (0, LANES - heads - 1))
    )
    packed = run_pack(w_out, w_in_x, w_in_z, w_in_bc, steps)
    n = lax.axis_size("tensor")
    axis_place = lax.axis_index("tensor")
    place = axis_place[None]
    near_hidden = line_gather(hidden_local, "tensor")
    weights = lax.all_gather(packed, "dp", axis=0, tiled=True)
    seg_stack = around(seg_ids[0], "tensor")
    count = seg_ids.shape[1]
    seg_full = lax.dynamic_slice_in_dim(
        jnp.concatenate(seg_stack + seg_stack), (n - axis_place) * count, n * count, 0
    )
    window = jnp.broadcast_to(
        jnp.pad(seg_full, (HALO, HALO), constant_values=-1)[:, None],
        (seg_full.shape[0] + 2 * HALO, LANES),
    )
    seg_row = jnp.broadcast_to(seg_full[None, :], (8, seg_full.shape[0]))
    kernel_x = jnp.concatenate([conv_x, conv_x_bias[None, :]], axis=0)
    kernel_bc = jnp.concatenate([conv_bc, conv_bc_bias[None, :]], axis=0)
    head = pad_lanes(jnp.stack([dt_bias, a_log]))
    channel = jnp.stack([gate_gain, jnp.repeat(d_skip, size)])

    hidden_full, tokens, z_proj, x_proj, bcdt, gain = run_project(
        heads, size, place, near_hidden, weights
    )
    cot_full = lax.all_gather(
        after(cotangent[0], near_hidden[0], near_hidden[-1]), "tensor", axis=0, tiled=True
    )
    scaled, out_part, square, *saved = run_forward(
        heads, size, window, seg_row, weights, kernel_x, kernel_bc, head, channel, z_proj, x_proj,
        bcdt,
    )
    grad_out, along = run_gradient(cot_full, weights, scaled, window)
    out_sum = lax.psum_scatter(
        out_part, "tensor", scatter_dimension=0, tiled=True
    )
    stat = sum_around(jnp.stack([square[0], along[0]]), "tensor")
    stat_full = jnp.pad(stat, ((0, 6), (0, 0)))
    out_scale = lax.rsqrt(stat[0] / full_inner + EPS) * (seg_full > 0).astype(F32)

    grads, in_part, normed_out, sum_x, sum_bc, sum_head, sum_gain = run_backward(
        heads, size, full_inner, stat_full, hidden_full, window, weights, kernel_x, kernel_bc, head,
        channel, x_proj, bcdt, grad_out, saved,
    )
    in_sum = lax.psum_scatter(in_part, "tensor", scatter_dimension=0, tiled=True)
    first, second = run_weights(cot_full, normed_out, tokens, after(grads, out_sum))
    own = jnp.concatenate([sum_x.reshape(-1, LANES), sum_head])
    both = jnp.concatenate([sum_gain[0].reshape(-1, LANES), sum_bc.reshape(-1, LANES)])
    first, second, small, came = cube_scatter(first, second, jnp.concatenate([own, both]), "dp")
    sum_x = small[: own.shape[0] - 8].reshape(8, width)
    sum_head = small[own.shape[0] - 8 : own.shape[0]]
    grad_bc = first[:, width : width + 2 * N]
    shared = jnp.concatenate([small[own.shape[0] :], grad_bc.reshape(-1, LANES)])
    shared = sum_around_low(shared, "tensor")
    gain_rows = features // LANES
    sum_gain = shared[:gain_rows].reshape(features)
    sum_bc = shared[gain_rows : both.shape[0]].reshape(8, 2 * N)
    grad_bc = shared[both.shape[0] :].reshape(grad_bc.shape)
    local_features = norm_gain.shape[0]
    grad_norm_gain = lax.dynamic_slice_in_dim(
        sum_gain, lax.axis_index("dp") * local_features, local_features, 0
    )

    local = hidden_local.shape[0]
    hidden_rows = hidden_local.astype(F32)
    scale_here = lax.dynamic_slice_in_dim(out_scale, axis_place * local, local, 0)[:, None]
    layer_out = (hidden_rows + out_sum.astype(F32) * scale_here).astype(BF16)

    grad_hidden = run_finish(in_sum, hidden_local, cotangent[0], after(gain, came[1]))

    return (
        layer_out[None],
        grad_hidden[None],
        grad_norm_gain,
        second[:, width:],
        second[:, :width],
        grad_bc,
        first[:, width + 2 * N : width + 2 * N + heads],
        sum_x[0:CONV],
        sum_x[CONV],
        sum_bc[0:CONV],
        sum_bc[CONV],
        sum_head[0, :heads],
        sum_head[1, :heads],
        jnp.sum(sum_x[CONV + 2].reshape(heads, size), axis=1),
        sum_x[CONV + 1],
        first[:, :width],
    )


def solution(mesh):
    in_specs = (
        P("dp", "tensor", None),
        P("dp", "tensor"),
        P("dp", "tensor", None),
        P("dp"),
        P("dp", "tensor"),
        P("dp", "tensor"),
        P("dp", None),
        P("dp", "tensor"),
        P(None, "tensor"),
        P("tensor"),
        P(),
        P(),
        P("tensor"),
        P("tensor"),
        P("tensor"),
        P("tensor"),
        P("dp", "tensor"),
    )
    out_specs = (
        P("dp", "tensor", None),
        P("dp", "tensor", None),
        P("dp"),
        P("dp", "tensor"),
        P("dp", "tensor"),
        P("dp", None),
        P("dp", "tensor"),
        P(None, "tensor"),
        P("tensor"),
        P(),
        P(),
        P("tensor"),
        P("tensor"),
        P("tensor"),
        P("tensor"),
        P("dp", "tensor"),
    )
    return jax.shard_map(shards, mesh=mesh, in_specs=in_specs, out_specs=out_specs, check_vma=False)
```

```python
import functools

import jax
import jax.numpy as jnp
from jax import lax
from jax.experimental import pallas as pl
from jax.experimental.pallas import tpu as pltpu
from jax.sharding import PartitionSpec as P

N = 128
CONV = 4
Q = 256
LANES = 128
HALO = 8
EPS = 1e-05
NEG = -1e30
F32 = jnp.float32
BF16 = jnp.bfloat16
VMEM_LIMIT = 52 * 1024 * 1024


def dot(a, b):
    return jnp.dot(a, b, preferred_element_type=F32)


def dot_nt(a, b):
    return lax.dot_general(a, b, (((1,), (1,)), ((), ())), preferred_element_type=F32)


def dot_tn(a, b):
    return lax.dot_general(a, b, (((0,), (0,)), ((), ())), preferred_element_type=F32)


def dot_exact(a, b):
    return jnp.dot(a, b, preferred_element_type=F32, precision=lax.Precision.HIGHEST)


def spread(cols, heads, size):
    rows = cols.shape[0]
    per = LANES // size
    lane = lax.broadcasted_iota(jnp.int32, (rows, LANES), 1)
    parts = []
    for first in range(0, heads, per):
        part = jnp.broadcast_to(cols[:, first : first + 1], (rows, LANES))
        for extra in range(1, per):
            part = jnp.where(lane < extra * size, part, cols[:, first + extra : first + extra + 1])
        parts.append(part)
    return jnp.concatenate(parts, axis=1)


def head_sums(values, heads, size):
    width = heads * size
    channel = lax.broadcasted_iota(jnp.int32, (width, LANES), 0)
    column = lax.broadcasted_iota(jnp.int32, (width, LANES), 1)
    first = column * size
    picks = jnp.where((channel >= first) & (channel < first + size), 1.0, 0.0).astype(BF16)
    high = values.astype(BF16)
    low = (values - high.astype(F32)).astype(BF16)
    return dot(high, picks) + dot(low, picks)


def widen(tile, width):
    return jnp.concatenate([tile] * (width // tile.shape[1]), axis=1)


def softplus(v):
    return jnp.maximum(v, 0.0) + jnp.log1p(jnp.exp(-jnp.abs(v)))


def sigmoid(v):
    return 1.0 / (1.0 + jnp.exp(-v))


def as_row(column):
    rows = column.shape[0]
    return jnp.broadcast_to(column, (rows, LANES)).T[:8]


def triangle(lower):
    row = lax.broadcasted_iota(jnp.int32, (Q, Q), 0)
    col = lax.broadcasted_iota(jnp.int32, (Q, Q), 1)
    return row >= col if lower else row <= col


def block_masks(window, seg_row):
    seg = window[HALO : HALO + Q]
    before = window[HALO - 1 : HALO]
    last = window[HALO + Q - 1 : HALO + Q]
    from_prev = (seg == before).astype(F32)
    same_last = (seg == last).astype(F32)
    passes = (last == before).astype(F32)
    keep = (widen(seg, Q) == seg_row) & triangle(True)
    bias = jnp.where(keep, 0.0, NEG)
    return seg, from_prev, same_last, passes, bias


def conv_forward(buffer, window, seg, kernel, conv_bias, width):
    total = conv_bias + kernel[CONV - 1 : CONV] * buffer[HALO : HALO + Q, :]
    for back in range(1, CONV):
        match = (window[HALO - back : HALO - back + Q] == seg).astype(F32)
        tap = kernel[CONV - 1 - back : CONV - back]
        total = total + tap * (buffer[HALO - back : HALO - back + Q, :] * widen(match, width))
    return total


def conv_backward(buffer, window, seg, kernel, values, width):
    here = buffer[0:Q, :]
    total = kernel[CONV - 1 : CONV] * here
    taps = [jnp.sum(values * here, axis=0, keepdims=True)]
    for ahead in range(1, CONV):
        match = (window[HALO + ahead : HALO + ahead + Q] == seg).astype(F32)
        moved = buffer[ahead : ahead + Q, :] * widen(match, width)
        total = total + kernel[CONV - 1 - ahead : CONV - ahead] * moved
        taps.append(jnp.sum(values * moved, axis=0, keepdims=True))
    return total, taps


def pick_block(place, near_refs, block):
    reach = len(near_refs) // 2
    away = pl.program_id(0) - place
    for index, ref in enumerate(near_refs):

        @pl.when(away == index - reach)
        def _():
            block[...] = ref[...]


def project_kernel(heads, size, near, place_ref, *refs):
    near_refs, refs = refs[:near], refs[near:]
    weights_ref, hidden_ref, tokens_ref, z_ref, x_ref, bcdt_ref, gain_ref = refs
    width = heads * size

    @pl.when(pl.program_id(0) == 0)
    def _():
        tail_columns = weights_ref[:, 3 * width + 2 * N :].astype(F32).T
        gain_ref[...] = jnp.broadcast_to(tail_columns[heads : heads + 1], gain_ref.shape)

    pick_block(place_ref[0], near_refs, hidden_ref)
    hidden = hidden_ref[...].astype(F32)
    inverse = lax.rsqrt(jnp.mean(hidden * hidden, axis=1, keepdims=True) + EPS)
    tokens = (hidden * inverse * gain_ref[0:1, :]).astype(BF16)
    tokens_ref[...] = tokens
    x_ref[...] = dot(tokens, weights_ref[:, width : 2 * width])
    z_ref[...] = dot(tokens, weights_ref[:, 2 * width : 3 * width])
    bcdt_ref[...] = dot(tokens, weights_ref[:, 3 * width :])


def forward_kernel(
    heads,
    size,
    window_ref,
    seg_row_ref,
    weights_ref,
    kernel_x_ref,
    kernel_bc_ref,
    head_ref,
    channel_ref,
    z_ref,
    x_ref,
    bcdt_ref,
    scaled_ref,
    part_ref,
    square_ref,
    state_ref,
    survive_ref,
    shape_ref,
    prob_ref,
    gated_ref,
    opened_ref,
    slope_z_ref,
    inner_ref,
    carried_ref,
    x_conv_ref,
    slope_x_ref,
    dt_ref,
    from_start_ref,
    to_end_ref,
    weighted_ref,
    weighted_end_ref,
    bc_ref,
    slope_bc_ref,
    decay_ref,
    slope_dt_ref,
    x_buffer,
    bc_buffer,
    carry,
):
    step = pl.program_id(0)
    width = heads * size

    @pl.when(step == 0)
    def _():
        x_buffer[0:HALO, :] = jnp.zeros((HALO, width), F32)
        bc_buffer[0:HALO, :] = jnp.zeros((HALO, 2 * N), F32)
        carry[...] = jnp.zeros((N, width), F32)

    window = window_ref[pl.ds(pl.multiple_of(step * Q, Q), Q + 2 * HALO), :]
    seg, from_prev, same_last, passes, bias = block_masks(window, seg_row_ref[0:1, :])
    bcdt = bcdt_ref[...]
    x_buffer[HALO : HALO + Q, :] = x_ref[...]
    bc_buffer[HALO : HALO + Q, :] = bcdt[:, : 2 * N]
    pre = conv_forward(
        x_buffer, window, seg, kernel_x_ref[...], kernel_x_ref[CONV : CONV + 1, :], width
    )
    pre_bc = conv_forward(
        bc_buffer, window, seg, kernel_bc_ref[...], kernel_bc_ref[CONV : CONV + 1, :], 2 * N
    )
    x_buffer[0:HALO, :] = x_buffer[Q : Q + HALO, :]
    bc_buffer[0:HALO, :] = bc_buffer[Q : Q + HALO, :]
    gate_x = sigmoid(pre)
    x_conv = pre * gate_x
    x_conv_ref[...] = x_conv
    slope_x_ref[...] = gate_x * (1.0 + pre * (1.0 - gate_x))
    gate_bc = sigmoid(pre_bc)
    bc_conv = (pre_bc * gate_bc).astype(BF16)
    bc_ref[...] = bc_conv
    slope_bc_ref[...] = gate_bc * (1.0 + pre_bc * (1.0 - gate_bc))
    b_in = bc_conv[:, :N]
    c_in = bc_conv[:, N:]

    raw = bcdt[:, 2 * N :] + head_ref[0:1, :]
    slope_dt_ref[...] = sigmoid(raw)
    dt = softplus(raw)
    decay = -dt * jnp.exp(head_ref[1:2, :])
    decay_ref[...] = decay
    total = dot_exact(triangle(True).astype(F32), decay)
    total_t = total.T
    dt_wide = spread(dt, heads, size)
    dt_ref[...] = dt_wide
    weighted = x_conv * dt_wide
    weighted_low = weighted.astype(BF16)
    weighted_ref[...] = weighted_low
    scores = dot_nt(c_in, b_in)
    before = carry[...]
    state_ref[0] = before

    per = LANES // size
    lane = lax.broadcasted_iota(jnp.int32, (Q, LANES), 1)
    none = jnp.zeros((Q, LANES), BF16)
    inner = []
    for first in range(0, heads, per):
        group = weighted_low[:, first * size : first * size + LANES]
        summed = jnp.zeros((Q, LANES), F32)
        for extra in range(per):
            h = first + extra
            shape = jnp.exp(total[:, h : h + 1] - total_t[h : h + 1, :] + bias)
            prob = (scores * shape).astype(BF16)
            shape_ref[:, h * Q : (h + 1) * Q] = shape.astype(BF16)
            prob_ref[:, h * Q : (h + 1) * Q] = prob
            mine = (lane >= extra * size) & (lane < (extra + 1) * size)
            summed = summed + dot(prob, jnp.where(mine, group, none))
        inner.append(summed)
    inner = jnp.concatenate(inner, axis=1)
    inner_ref[...] = inner
    carried = dot(c_in, before.astype(BF16))
    carried_ref[...] = carried
    from_start = spread(jnp.exp(total) * from_prev, heads, size)
    from_start_ref[...] = from_start
    last = total[Q - 1 : Q, :]
    to_end = spread(jnp.exp(last - total) * same_last, heads, size)
    to_end_ref[...] = to_end
    weighted_end = (weighted * to_end).astype(BF16)
    weighted_end_ref[...] = weighted_end
    survive = spread(jnp.exp(last) * passes, heads, size)
    survive_ref[0] = jnp.broadcast_to(survive, (8, width))
    carry[...] = dot_tn(b_in, weighted_end) + before * survive

    mixed = inner + carried * from_start + channel_ref[1:2, :] * x_conv
    z_proj = z_ref[...]
    gate = sigmoid(z_proj)
    opened = z_proj * gate
    opened_ref[...] = opened
    slope_z_ref[...] = mixed * (gate * (1.0 + z_proj * (1.0 - gate)))
    gated = mixed * opened
    gated_ref[...] = gated
    scaled = (gated * channel_ref[0:1, :]).astype(BF16)
    scaled_ref[...] = scaled
    part_ref[...] = dot_nt(scaled, weights_ref[...]).astype(BF16)
    square_ref[...] = as_row(jnp.sum(gated * gated, axis=1, keepdims=True))


def gradient_kernel(width, cot_ref, weights_ref, scaled_ref, window_ref, grad_ref, along_ref):
    step = pl.program_id(0)
    window = window_ref[pl.ds(pl.multiple_of(step * Q, Q), Q + 2 * HALO), :]
    live = (window[HALO : HALO + Q] > 0).astype(F32)
    grad = dot(cot_ref[...], weights_ref[...]) * widen(live, width)
    grad_ref[...] = grad
    along_ref[...] = as_row(jnp.sum(scaled_ref[...].astype(F32) * grad, axis=1, keepdims=True))


def backward_kernel(
    heads,
    size,
    full_inner,
    stat_ref,
    hidden_ref,
    window_ref,
    weights_ref,
    kernel_x_ref,
    kernel_bc_ref,
    head_ref,
    channel_ref,
    x_ref,
    bcdt_ref,
    grad_ref,
    state_ref,
    survive_ref,
    shape_ref,
    prob_ref,
    gated_ref,
    opened_ref,
    slope_z_ref,
    inner_ref,
    carried_ref,
    x_conv_ref,
    slope_x_ref,
    dt_ref,
    from_start_ref,
    to_end_ref,
    weighted_ref,
    weighted_end_ref,
    bc_ref,
    slope_bc_ref,
    decay_ref,
    slope_dt_ref,
    proj_ref,
    rest_ref,
    part_ref,
    out_ref,
    sum_x_ref,
    sum_bc_ref,
    sum_head_ref,
    sum_gain_ref,
    x_buffer,
    bc_buffer,
    carry,
    tail,
):
    turn = pl.program_id(0)
    step = pl.num_programs(0) - 1 - turn
    width = heads * size

    @pl.when(turn == 0)
    def _():
        x_buffer[...] = jnp.zeros((Q + HALO, width), F32)
        bc_buffer[...] = jnp.zeros((Q + HALO, 2 * N), F32)
        carry[...] = jnp.zeros((N, width), F32)
        tail[...] = jnp.zeros((8, LANES), F32)
        sum_x_ref[...] = jnp.zeros((8, width), F32)
        sum_bc_ref[...] = jnp.zeros((8, 2 * N), F32)
        sum_head_ref[...] = jnp.zeros((8, LANES), F32)
        sum_gain_ref[...] = jnp.zeros(sum_gain_ref.shape, F32)

    window = window_ref[pl.ds(pl.multiple_of(step * Q, Q), Q + 2 * HALO), :]
    seg = window[HALO : HALO + Q]
    live = (seg[:, 0:1] > 0).astype(F32)
    stat = stat_ref[...].T
    gate_inverse = lax.rsqrt(stat[:, 0:1] / full_inner + EPS)
    along = stat[:, 1:2] * (gate_inverse * gate_inverse * gate_inverse / full_inner)

    gain = channel_ref[0:1, :]
    skip = channel_ref[1:2, :]
    grad_out = grad_ref[...]
    gated = gated_ref[...]
    normal = gated * gate_inverse
    sum_gate = jnp.sum(grad_out * normal, axis=0, keepdims=True)
    out_ref[...] = (normal * gain * live).astype(BF16)
    grad_gated = grad_out * gain * gate_inverse - gated * along
    grad_z = (grad_gated * slope_z_ref[...]).astype(BF16)
    dy = grad_gated * opened_ref[...]
    dy_low = dy.astype(BF16)
    dy_start = (dy * from_start_ref[...]).astype(BF16)

    bc_conv = bc_ref[...]
    b_in = bc_conv[:, :N]
    c_in = bc_conv[:, N:]
    before = state_ref[0]
    before_low = before.astype(BF16)
    after_low = carry[...].astype(BF16)
    weighted_low = weighted_ref[...]
    weighted_end = weighted_end_ref[...]
    grad_c = dot_nt(dy_start, before_low)
    returned = dot(b_in, after_low)
    grad_b = dot_nt(weighted_end, after_low)
    new_after = dot_tn(c_in, dy_start) + carry[...] * survive_ref[0, 0:1, :]
    carry[...] = new_after

    per = LANES // size
    lane = lax.broadcasted_iota(jnp.int32, (Q, LANES), 1)
    grad_scores = jnp.zeros((Q, Q), F32)
    inner = []
    none = jnp.zeros((Q, LANES), BF16)
    for first in range(0, heads, per):
        at = first * size
        dy_group = dy_low[:, at : at + LANES]
        weighted_group = weighted_low[:, at : at + LANES]
        summed = jnp.zeros((Q, LANES), F32)
        for extra in range(per):
            h = first + extra
            mine = (lane >= extra * size) & (lane < (extra + 1) * size)
            dy_mine = jnp.where(mine, dy_group, none)
            shape = shape_ref[:, h * Q : (h + 1) * Q].astype(F32)
            grad_scores = grad_scores + dot_nt(dy_mine, weighted_group) * shape
            summed = summed + dot_tn(prob_ref[:, h * Q : (h + 1) * Q], dy_mine)
        inner.append(summed)
    grad_inner = jnp.concatenate(inner, axis=1)
    grad_weighted = to_end_ref[...] * returned + grad_inner
    grad_scores = grad_scores.astype(BF16)
    grad_c = grad_c + dot(grad_scores, b_in)
    grad_b = grad_b + dot_tn(grad_scores, c_in)

    x_conv = x_conv_ref[...]
    pairs = head_sums(
        dy_low.astype(F32) * inner_ref[...]
        + dy_start.astype(F32) * carried_ref[...]
        - weighted_low.astype(F32) * grad_inner
        - weighted_end.astype(F32) * returned,
        heads,
        size,
    )
    grad_decay = dot_exact(triangle(False).astype(F32), pairs) + tail[0:1, :]
    kept = jnp.sum(new_after.astype(BF16).astype(F32) * before, axis=0, keepdims=True)
    tail[...] = head_sums(jnp.broadcast_to(kept, (8, width)), heads, size)
    rate = jnp.exp(head_ref[1:2, :])
    grad_dt = head_sums(grad_weighted * x_conv, heads, size) - grad_decay * rate
    grad_raw = grad_dt * slope_dt_ref[...]
    sum_head_ref[0:1, :] += jnp.sum(grad_raw, axis=0, keepdims=True)
    sum_head_ref[1:2, :] += jnp.sum(grad_decay * decay_ref[...], axis=0, keepdims=True)

    sum_skip = jnp.sum(dy * x_conv, axis=0, keepdims=True)
    grad_pre = (grad_weighted * dt_ref[...] + skip * dy) * slope_x_ref[...]
    x_buffer[Q : Q + HALO, :] = x_buffer[0:HALO, :]
    x_buffer[0:Q, :] = grad_pre
    grad_proj, taps = conv_backward(
        x_buffer, window, seg, kernel_x_ref[...], x_ref[...], width
    )
    sum_bias = jnp.sum(grad_pre, axis=0, keepdims=True)
    blank = jnp.zeros((1, width), F32)
    sum_x_ref[...] += jnp.concatenate(
        [taps[3], taps[2], taps[1], taps[0], sum_bias, sum_gate, sum_skip, blank], axis=0
    )

    grad_pre_bc = jnp.concatenate([grad_b, grad_c], axis=1) * slope_bc_ref[...]
    bc_buffer[Q : Q + HALO, :] = bc_buffer[0:HALO, :]
    bc_buffer[0:Q, :] = grad_pre_bc
    grad_bc, taps_bc = conv_backward(
        bc_buffer, window, seg, kernel_bc_ref[...], bcdt_ref[:, : 2 * N], 2 * N
    )
    sum_bias_bc = jnp.sum(grad_pre_bc, axis=0, keepdims=True)
    blank_bc = jnp.zeros((3, 2 * N), F32)
    sum_bc_ref[...] += jnp.concatenate(
        [taps_bc[3], taps_bc[2], taps_bc[1], taps_bc[0], sum_bias_bc, blank_bc], axis=0
    )

    grads = jnp.concatenate(
        [grad_proj.astype(BF16), grad_z, grad_bc.astype(BF16), grad_raw.astype(BF16)], axis=1
    )
    proj_ref[...] = grads[:, : 2 * width]
    rest_ref[...] = grads[:, 2 * width :]
    part = dot_nt(grads, weights_ref[:, width:])
    part_ref[...] = part.astype(BF16)
    hidden = hidden_ref[...].astype(F32)
    inverse = lax.rsqrt(jnp.mean(hidden * hidden, axis=1, keepdims=True) + EPS)
    sum_gain_ref[0:1, :] += jnp.sum(part * (hidden * inverse), axis=0, keepdims=True)


def pack_kernel(*refs):
    *parts, packed, sems = refs
    at = 0
    copies = []
    for index, part in enumerate(parts):
        columns = part.shape[1]
        copies.append(
            pltpu.make_async_copy(part, packed.at[:, pl.ds(at, columns)], sems.at[index])
        )
        at += columns
    for copy in copies:
        copy.start()
    for copy in copies:
        copy.wait()


def run_pack(*parts):
    rows = parts[0].shape[0]
    columns = sum(part.shape[1] for part in parts)
    return pl.pallas_call(
        pack_kernel,
        in_specs=[pl.BlockSpec(memory_space=pl.ANY)] * len(parts),
        out_specs=pl.BlockSpec(memory_space=pl.ANY),
        out_shape=jax.ShapeDtypeStruct((rows, columns), BF16),
        scratch_shapes=[pltpu.SemaphoreType.DMA((len(parts),))],
        compiler_params=pltpu.CompilerParams(vmem_limit_bytes=VMEM_LIMIT),
        name="pack",
    )(*parts)


def cost(micros):
    return pl.CostEstimate(flops=int(micros * 1e9), bytes_accessed=1 << 20, transcendentals=0)


def whole(shape):
    return pl.BlockSpec(shape, lambda i: (0,) * len(shape))


def scalar():
    return pl.BlockSpec(memory_space=pltpu.SMEM)


def run_project(heads, size, place, near, weights):
    features = near[0].shape[1]
    blocks = len(near) // 2 + 1
    length = blocks * Q
    width = heads * size
    rest = 2 * N + LANES

    def rows(columns):
        return pl.BlockSpec((Q, columns), lambda i: (i, 0))

    def made(columns, dtype):
        return jax.ShapeDtypeStruct((length, columns), dtype)

    return pl.pallas_call(
        functools.partial(project_kernel, heads, size, len(near)),
        grid=(blocks,),
        in_specs=[scalar(), *[whole(block.shape) for block in near], whole(weights.shape)],
        out_specs=[
            rows(features),
            rows(features),
            rows(width),
            rows(width),
            rows(rest),
            whole((8, features)),
        ],
        out_shape=[
            made(features, BF16),
            made(features, BF16),
            made(width, F32),
            made(width, F32),
            made(rest, F32),
            jax.ShapeDtypeStruct((8, features), F32),
        ],
        compiler_params=pltpu.CompilerParams(vmem_limit_bytes=VMEM_LIMIT),
        cost_estimate=cost(8),
        name="project",
    )(place, *near, weights)


def saved_rows(heads, size):
    width = heads * size
    return (
        [(heads * Q, BF16)] * 2
        + [(width, F32)] * 10
        + [(width, BF16)] * 2
        + [(2 * N, BF16), (2 * N, F32), (LANES, F32), (LANES, F32)]
    )


def saved_specs(heads, size, place):
    width = heads * size
    return [
        pl.BlockSpec((1, N, width), lambda i: (place(i), 0, 0)),
        pl.BlockSpec((1, 8, width), lambda i: (place(i), 0, 0)),
    ] + [
        pl.BlockSpec((Q, columns), lambda i: (place(i), 0))
        for columns, _ in saved_rows(heads, size)
    ]


def run_forward(
    heads, size, window, seg_row, weights, kernel_x, kernel_bc, head, channel, z_proj, x_proj, bcdt
):
    length, features = seg_row.shape[1], weights.shape[0]
    width = heads * size
    blocks = length // Q

    def rows(columns):
        return pl.BlockSpec((Q, columns), lambda i: (i, 0))

    def made(columns, dtype):
        return jax.ShapeDtypeStruct((length, columns), dtype)

    across = pl.BlockSpec((8, Q), lambda i: (0, i))
    return pl.pallas_call(
        functools.partial(forward_kernel, heads, size),
        grid=(blocks,),
        in_specs=[
            whole(window.shape),
            across,
            whole((features, width)),
            whole(kernel_x.shape),
            whole(kernel_bc.shape),
            whole(head.shape),
            whole(channel.shape),
            rows(width),
            rows(width),
            rows(bcdt.shape[1]),
        ],
        out_specs=[rows(width), rows(features), across, *saved_specs(heads, size, lambda i: i)],
        out_shape=[
            made(width, BF16),
            made(features, BF16),
            jax.ShapeDtypeStruct((8, length), F32),
            *[
                jax.ShapeDtypeStruct((blocks,) + shape, F32) for shape in ((N, width), (8, width))
            ],
            *[made(columns, dtype) for columns, dtype in saved_rows(heads, size)],
        ],
        scratch_shapes=[
            pltpu.VMEM((Q + HALO, width), F32),
            pltpu.VMEM((Q + HALO, 2 * N), F32),
            pltpu.VMEM((N, width), F32),
        ],
        compiler_params=pltpu.CompilerParams(vmem_limit_bytes=VMEM_LIMIT),
        cost_estimate=cost(14),
        name="forward",
    )(window, seg_row, weights, kernel_x, kernel_bc, head, channel, z_proj, x_proj, bcdt)


def run_gradient(cot, weights, scaled, window):
    length, features = cot.shape
    width = scaled.shape[1]
    return pl.pallas_call(
        functools.partial(gradient_kernel, width),
        grid=(length // Q,),
        in_specs=[
            pl.BlockSpec((Q, features), lambda i: (i, 0)),
            whole((features, width)),
            pl.BlockSpec((Q, width), lambda i: (i, 0)),
            whole(window.shape),
        ],
        out_specs=[
            pl.BlockSpec((Q, width), lambda i: (i, 0)),
            pl.BlockSpec((8, Q), lambda i: (0, i)),
        ],
        out_shape=[
            jax.ShapeDtypeStruct((length, width), F32),
            jax.ShapeDtypeStruct((8, length), F32),
        ],
        compiler_params=pltpu.CompilerParams(vmem_limit_bytes=VMEM_LIMIT),
        cost_estimate=cost(0),
        name="out_gradient",
    )(cot, weights, scaled, window)


def first_kernel(width, cot_ref, normed_ref, tokens_ref, grads_ref, sum_ref):
    sum_ref[:, :width] = dot_tn(cot_ref[...], normed_ref[...]).astype(BF16)
    sum_ref[:, width:] = dot_tn(tokens_ref[...], grads_ref[...]).astype(BF16)


def second_kernel(tokens_ref, grads_ref, sum_ref):
    sum_ref[...] = dot_tn(tokens_ref[...], grads_ref[...]).astype(BF16)


def run_weights(cot, normed, tokens, grads, rest_grads):
    length, features = tokens.shape
    width = normed.shape[1]
    rest = rest_grads.shape[1]
    params = pltpu.CompilerParams(vmem_limit_bytes=VMEM_LIMIT)
    strip = pl.BlockSpec((length, Q), lambda i: (0, i))
    second = pl.pallas_call(
        second_kernel,
        grid=(features // Q,),
        in_specs=[strip, pl.BlockSpec((length, 2 * width), lambda i: (0, 0))],
        out_specs=pl.BlockSpec((Q, 2 * width), lambda i: (i, 0)),
        out_shape=jax.ShapeDtypeStruct((features, 2 * width), BF16),
        compiler_params=params,
        cost_estimate=cost(0),
        name="weight_gradients_xz",
    )(tokens, grads)
    first = pl.pallas_call(
        functools.partial(first_kernel, width),
        grid=(features // Q,),
        in_specs=[strip, whole(normed.shape), strip, whole((length, rest))],
        out_specs=pl.BlockSpec((Q, width + rest), lambda i: (i, 0)),
        out_shape=jax.ShapeDtypeStruct((features, width + rest), BF16),
        compiler_params=params,
        cost_estimate=cost(0),
        name="weight_gradients_out",
    )(cot, normed, tokens, rest_grads)
    return first, second


def run_backward(
    heads, size, full_inner, stat, hidden, window, weights, kernel_x, kernel_bc, head, channel,
    x_proj, bcdt, grad_out, saved,
):
    length, features = hidden.shape
    width = heads * size
    blocks = length // Q
    rest = 2 * N + LANES

    def rows(columns):
        return pl.BlockSpec((Q, columns), lambda i: (blocks - 1 - i, 0))

    def made(columns, dtype):
        return jax.ShapeDtypeStruct((length, columns), dtype)

    across = pl.BlockSpec((8, Q), lambda i: (0, blocks - 1 - i))
    sums = [(8, width), (8, 2 * N), (8, LANES), (8, features)]
    return pl.pallas_call(
        functools.partial(backward_kernel, heads, size, full_inner),
        grid=(blocks,),
        in_specs=[
            across,
            rows(features),
            whole(window.shape),
            whole(weights.shape),
            whole(kernel_x.shape),
            whole(kernel_bc.shape),
            whole(head.shape),
            whole(channel.shape),
            rows(width),
            rows(rest),
            rows(width),
            *saved_specs(heads, size, lambda i: blocks - 1 - i),
        ],
        out_specs=[rows(2 * width), rows(rest), rows(features), rows(width)] + [whole(shape) for shape in sums],
        out_shape=[
            made(2 * width, BF16), made(rest, BF16), made(features, BF16), made(width, BF16)
        ]
        + [jax.ShapeDtypeStruct(shape, F32) for shape in sums],
        scratch_shapes=[
            pltpu.VMEM((Q + HALO, width), F32),
            pltpu.VMEM((Q + HALO, 2 * N), F32),
            pltpu.VMEM((N, width), F32),
            pltpu.VMEM((8, LANES), F32),
        ],
        compiler_params=pltpu.CompilerParams(vmem_limit_bytes=VMEM_LIMIT),
        cost_estimate=cost(0),
        name="backward",
    )(
        stat, hidden, window, weights, kernel_x, kernel_bc, head, channel, x_proj, bcdt, grad_out,
        *saved,
    )


def finish_kernel(sum_ref, hidden_ref, cot_ref, gain_ref, out_ref):
    grad = sum_ref[...].astype(F32) * gain_ref[0:1, :]
    hidden = hidden_ref[...].astype(F32)
    inverse = lax.rsqrt(jnp.mean(hidden * hidden, axis=1, keepdims=True) + EPS)
    unit = hidden * inverse
    along = jnp.mean(grad * unit, axis=1, keepdims=True)
    out_ref[...] = (cot_ref[...].astype(F32) + inverse * (grad - unit * along)).astype(BF16)


def run_finish(in_sum, hidden, cot, gain):
    length, features = hidden.shape
    rows = pl.BlockSpec((length // 2, features), lambda i: (i, 0))
    return pl.pallas_call(
        finish_kernel,
        grid=(2,),
        in_specs=[rows, rows, rows, whole(gain.shape)],
        out_specs=rows,
        out_shape=jax.ShapeDtypeStruct(hidden.shape, BF16),
        compiler_params=pltpu.CompilerParams(vmem_limit_bytes=VMEM_LIMIT),
        name="finish",
    )(in_sum, hidden, cot, gain)


def pad_lanes(values):
    return jnp.pad(values, ((0, 0), (0, LANES - values.shape[1])))


def after(value, *others):
    return lax.optimization_barrier((value, *others))[0]


def line_step(right, left, step, axis):
    n = lax.axis_size(axis)
    return (
        lax.ppermute(right, axis, [(i, i + 1) for i in range(step - 1, n - 1)]),
        lax.ppermute(left, axis, [(i, i - 1) for i in range(1, n - step + 1)]),
    )


def line_order(block, moved):
    return [pair[0] for pair in moved[::-1]] + [block] + [pair[1] for pair in moved]


def line_gather(block, axis):
    right = left = block
    moved = []
    for step in range(1, lax.axis_size(axis)):
        right, left = line_step(right, left, step, axis)
        moved.append((right, left))
    return line_order(block, moved)


def cube_scatter(first, second, small, axis):
    n = lax.axis_size(axis)
    if n & (n - 1):
        sums = [
            lax.psum_scatter(part, axis, scatter_dimension=0, tiled=True).astype(F32)
            for part in (first, second)
        ]
        return (*sums, lax.psum(small, axis), sums)
    place = lax.axis_index(axis)
    bits = list(range(n.bit_length() - 1))
    orders = [bits, bits[:1] + bits[:0:-1]]
    parts = [part.reshape((2,) * len(bits) + (-1, part.shape[1])) for part in (first, second)]
    left = [bits[::-1], bits[::-1]]
    came = []
    for step in range(len(bits)):
        for index in range(2):
            part = parts[index]
            bit = orders[index][step]
            dim = left[index].index(bit)
            mine = (place >> bit) & 1
            keep = lax.dynamic_index_in_dim(part, mine, dim, keepdims=False)
            send = lax.dynamic_index_in_dim(part, 1 - mine, dim, keepdims=False)
            pairs = [(i, i ^ (1 << bit)) for i in range(n)]
            if index == 0:
                columns = part.shape[-1]
                rows = send.size // columns
                extra = -(-small.size // (16 * columns)) * 16
                small = lax.reduce_precision(small, 8, 7)
                rider = jnp.pad(
                    small.astype(BF16).reshape(-1), (0, extra * columns - small.size)
                ).reshape(extra, columns)
                moved = lax.ppermute(
                    jnp.concatenate([send.reshape(rows, columns), rider]), axis, pairs
                )
                other = moved[:rows].reshape(send.shape)
                rider = moved[rows:].reshape(-1)[: small.size].reshape(small.shape)
                small = small + rider.astype(F32)
            else:
                moved = other = lax.ppermute(send, axis, pairs)
            came.append(moved)
            part = keep.astype(F32) + other.astype(F32)
            left[index] = [other_bit for other_bit in left[index] if other_bit != bit]
            parts[index] = part.astype(BF16) if left[index] else part
    return (*parts, small, came)


def around(values, axis):
    n = lax.axis_size(axis)
    return [values] + [
        lax.ppermute(values, axis, [(i, (i - k) % n) for i in range(n)]) for k in range(1, n)
    ]


def sum_around(values, axis):
    return functools.reduce(jnp.add, around(values, axis))


def sum_around_low(values, axis):
    low = around(lax.reduce_precision(values, 8, 7).astype(BF16), axis)
    return functools.reduce(jnp.add, [share.astype(F32) for share in low])


def shards(
    hidden,
    seg_ids,
    cotangent,
    norm_gain,
    w_in_z,
    w_in_x,
    w_in_bc,
    w_in_dt,
    conv_x,
    conv_x_bias,
    conv_bc,
    conv_bc_bias,
    dt_bias,
    a_log,
    d_skip,
    gate_gain,
    w_out,
):
    heads = dt_bias.shape[0]
    width = gate_gain.shape[0]
    size = width // heads
    full_inner = width * lax.axis_size("tensor")
    features = hidden.shape[2]
    hidden_local = hidden[0]

    steps = jnp.pad(
        jnp.concatenate([w_in_dt, norm_gain[:, None]], axis=1), ((0, 0), (0, LANES - heads - 1))
    )
    packed = run_pack(w_out, w_in_x, w_in_z, w_in_bc, steps)
    n = lax.axis_size("tensor")
    axis_place = lax.axis_index("tensor")
    place = axis_place[None]
    near_hidden = line_gather(hidden_local, "tensor")
    weights = lax.all_gather(packed, "dp", axis=0, tiled=True)
    seg_stack = around(seg_ids[0], "tensor")
    count = seg_ids.shape[1]
    seg_full = lax.dynamic_slice_in_dim(
        jnp.concatenate(seg_stack + seg_stack), (n - axis_place) * count, n * count, 0
    )
    window = jnp.broadcast_to(
        jnp.pad(seg_full, (HALO, HALO), constant_values=-1)[:, None],
        (seg_full.shape[0] + 2 * HALO, LANES),
    )
    seg_row = jnp.broadcast_to(seg_full[None, :], (8, seg_full.shape[0]))
    kernel_x = jnp.concatenate([conv_x, conv_x_bias[None, :]], axis=0)
    kernel_bc = jnp.concatenate([conv_bc, conv_bc_bias[None, :]], axis=0)
    head = pad_lanes(jnp.stack([dt_bias, a_log]))
    channel = jnp.stack([gate_gain, jnp.repeat(d_skip, size)])

    hidden_full, tokens, z_proj, x_proj, bcdt, gain = run_project(
        heads, size, place, near_hidden, weights
    )
    cot_full = lax.all_gather(
        after(cotangent[0], near_hidden[0], near_hidden[-1]), "tensor", axis=0, tiled=True
    )
    scaled, out_part, square, *saved = run_forward(
        heads, size, window, seg_row, weights, kernel_x, kernel_bc, head, channel, z_proj, x_proj,
        bcdt,
    )
    grad_out, along = run_gradient(cot_full, weights, scaled, window)
    out_sum = lax.psum_scatter(
        out_part, "tensor", scatter_dimension=0, tiled=True
    )
    stat = sum_around(jnp.stack([square[0], along[0]]), "tensor")
    stat_full = jnp.pad(stat, ((0, 6), (0, 0)))
    out_scale = lax.rsqrt(stat[0] / full_inner + EPS) * (seg_full > 0).astype(F32)

    grads, rest_grads, in_part, normed_out, sum_x, sum_bc, sum_head, sum_gain = run_backward(
        heads, size, full_inner, stat_full, hidden_full, window, weights, kernel_x, kernel_bc, head,
        channel, x_proj, bcdt, grad_out, saved,
    )
    in_sum = lax.psum_scatter(in_part, "tensor", scatter_dimension=0, tiled=True)
    first, second = run_weights(cot_full, after(normed_out, out_sum), tokens, grads, rest_grads)
    own = jnp.concatenate([sum_x.reshape(-1, LANES), sum_head])
    both = jnp.concatenate([sum_gain[0].reshape(-1, LANES), sum_bc.reshape(-1, LANES)])
    first, second, small, came = cube_scatter(first, second, jnp.concatenate([own, both]), "dp")
    sum_x = small[: own.shape[0] - 8].reshape(8, width)
    sum_head = small[own.shape[0] - 8 : own.shape[0]]
    grad_bc = first[:, width : width + 2 * N]
    shared = jnp.concatenate([small[own.shape[0] :], grad_bc.reshape(-1, LANES)])
    shared = sum_around_low(shared, "tensor")
    gain_rows = features // LANES
    sum_gain = shared[:gain_rows].reshape(features)
    sum_bc = shared[gain_rows : both.shape[0]].reshape(8, 2 * N)
    grad_bc = shared[both.shape[0] :].reshape(grad_bc.shape)
    local_features = norm_gain.shape[0]
    grad_norm_gain = lax.dynamic_slice_in_dim(
        sum_gain, lax.axis_index("dp") * local_features, local_features, 0
    )

    local = hidden_local.shape[0]
    hidden_rows = hidden_local.astype(F32)
    scale_here = lax.dynamic_slice_in_dim(out_scale, axis_place * local, local, 0)[:, None]
    layer_out = (hidden_rows + out_sum.astype(F32) * scale_here).astype(BF16)

    grad_hidden = run_finish(in_sum, hidden_local, cotangent[0], after(gain, shared))

    return (
        layer_out[None],
        grad_hidden[None],
        grad_norm_gain,
        second[:, width:],
        second[:, :width],
        grad_bc,
        first[:, width + 2 * N : width + 2 * N + heads],
        sum_x[0:CONV],
        sum_x[CONV],
        sum_bc[0:CONV],
        sum_bc[CONV],
        sum_head[0, :heads],
        sum_head[1, :heads],
        jnp.sum(sum_x[CONV + 2].reshape(heads, size), axis=1),
        sum_x[CONV + 1],
        first[:, :width],
    )


def solution(mesh):
    in_specs = (
        P("dp", "tensor", None),
        P("dp", "tensor"),
        P("dp", "tensor", None),
        P("dp"),
        P("dp", "tensor"),
        P("dp", "tensor"),
        P("dp", None),
        P("dp", "tensor"),
        P(None, "tensor"),
        P("tensor"),
        P(),
        P(),
        P("tensor"),
        P("tensor"),
        P("tensor"),
        P("tensor"),
        P("dp", "tensor"),
    )
    out_specs = (
        P("dp", "tensor", None),
        P("dp", "tensor", None),
        P("dp"),
        P("dp", "tensor"),
        P("dp", "tensor"),
        P("dp", None),
        P("dp", "tensor"),
        P(None, "tensor"),
        P("tensor"),
        P(),
        P(),
        P("tensor"),
        P("tensor"),
        P("tensor"),
        P("tensor"),
        P("dp", "tensor"),
    )
    return jax.shard_map(shards, mesh=mesh, in_specs=in_specs, out_specs=out_specs, check_vma=False)
```

```python
import functools

import jax
import jax.numpy as jnp
from jax import lax
from jax.experimental import pallas as pl
from jax.experimental.pallas import tpu as pltpu
from jax.sharding import PartitionSpec as P

N = 128
CONV = 4
Q = 256
LANES = 128
HALO = 8
EPS = 1e-05
NEG = -1e30
F32 = jnp.float32
BF16 = jnp.bfloat16
VMEM_LIMIT = 52 * 1024 * 1024


def dot(a, b):
    return jnp.dot(a, b, preferred_element_type=F32)


def dot_nt(a, b):
    return lax.dot_general(a, b, (((1,), (1,)), ((), ())), preferred_element_type=F32)


def dot_tn(a, b):
    return lax.dot_general(a, b, (((0,), (0,)), ((), ())), preferred_element_type=F32)


def dot_exact(a, b):
    return jnp.dot(a, b, preferred_element_type=F32, precision=lax.Precision.HIGHEST)


def spread(cols, heads, size):
    rows = cols.shape[0]
    per = LANES // size
    lane = lax.broadcasted_iota(jnp.int32, (rows, LANES), 1)
    parts = []
    for first in range(0, heads, per):
        part = jnp.broadcast_to(cols[:, first : first + 1], (rows, LANES))
        for extra in range(1, per):
            part = jnp.where(lane < extra * size, part, cols[:, first + extra : first + extra + 1])
        parts.append(part)
    return jnp.concatenate(parts, axis=1)


def head_sums(values, heads, size):
    width = heads * size
    channel = lax.broadcasted_iota(jnp.int32, (width, LANES), 0)
    column = lax.broadcasted_iota(jnp.int32, (width, LANES), 1)
    first = column * size
    picks = jnp.where((channel >= first) & (channel < first + size), 1.0, 0.0).astype(BF16)
    high = values.astype(BF16)
    low = (values - high.astype(F32)).astype(BF16)
    return dot(high, picks) + dot(low, picks)


def widen(tile, width):
    return jnp.concatenate([tile] * (width // tile.shape[1]), axis=1)


def softplus(v):
    return jnp.maximum(v, 0.0) + jnp.log1p(jnp.exp(-jnp.abs(v)))


def sigmoid(v):
    return 1.0 / (1.0 + jnp.exp(-v))


def as_row(column):
    rows = column.shape[0]
    return jnp.broadcast_to(column, (rows, LANES)).T[:8]


def triangle(lower):
    row = lax.broadcasted_iota(jnp.int32, (Q, Q), 0)
    col = lax.broadcasted_iota(jnp.int32, (Q, Q), 1)
    return row >= col if lower else row <= col


def block_masks(window, seg_row):
    seg = window[HALO : HALO + Q]
    before = window[HALO - 1 : HALO]
    last = window[HALO + Q - 1 : HALO + Q]
    from_prev = (seg == before).astype(F32)
    same_last = (seg == last).astype(F32)
    passes = (last == before).astype(F32)
    keep = (widen(seg, Q) == seg_row) & triangle(True)
    bias = jnp.where(keep, 0.0, NEG)
    return seg, from_prev, same_last, passes, bias


def conv_forward(buffer, window, seg, kernel, conv_bias, width):
    total = conv_bias + kernel[CONV - 1 : CONV] * buffer[HALO : HALO + Q, :]
    for back in range(1, CONV):
        match = (window[HALO - back : HALO - back + Q] == seg).astype(F32)
        tap = kernel[CONV - 1 - back : CONV - back]
        total = total + tap * (buffer[HALO - back : HALO - back + Q, :] * widen(match, width))
    return total


def conv_backward(buffer, window, seg, kernel, values, width):
    here = buffer[0:Q, :]
    total = kernel[CONV - 1 : CONV] * here
    taps = [jnp.sum(values * here, axis=0, keepdims=True)]
    for ahead in range(1, CONV):
        match = (window[HALO + ahead : HALO + ahead + Q] == seg).astype(F32)
        moved = buffer[ahead : ahead + Q, :] * widen(match, width)
        total = total + kernel[CONV - 1 - ahead : CONV - ahead] * moved
        taps.append(jnp.sum(values * moved, axis=0, keepdims=True))
    return total, taps


def pick_block(place, near_refs, block):
    reach = len(near_refs) // 2
    away = pl.program_id(0) - place
    for index, ref in enumerate(near_refs):

        @pl.when(away == index - reach)
        def _():
            block[...] = ref[...]


def project_kernel(heads, size, near, place_ref, *refs):
    near_refs, refs = refs[:near], refs[near:]
    weights_ref, hidden_ref, tokens_ref, z_ref, x_ref, bcdt_ref, gain_ref = refs
    width = heads * size

    @pl.when(pl.program_id(0) == 0)
    def _():
        tail_columns = weights_ref[:, 3 * width + 2 * N :].astype(F32).T
        gain_ref[...] = jnp.broadcast_to(tail_columns[heads : heads + 1], gain_ref.shape)

    pick_block(place_ref[0], near_refs, hidden_ref)
    hidden = hidden_ref[...].astype(F32)
    inverse = lax.rsqrt(jnp.mean(hidden * hidden, axis=1, keepdims=True) + EPS)
    tokens = (hidden * inverse * gain_ref[0:1, :]).astype(BF16)
    tokens_ref[...] = tokens
    x_ref[...] = dot(tokens, weights_ref[:, width : 2 * width])
    z_ref[...] = dot(tokens, weights_ref[:, 2 * width : 3 * width])
    bcdt_ref[...] = dot(tokens, weights_ref[:, 3 * width :])


def forward_kernel(
    heads,
    size,
    window_ref,
    seg_row_ref,
    weights_ref,
    kernel_x_ref,
    kernel_bc_ref,
    head_ref,
    channel_ref,
    z_ref,
    x_ref,
    bcdt_ref,
    scaled_ref,
    part_ref,
    square_ref,
    state_ref,
    survive_ref,
    shape_ref,
    prob_ref,
    gated_ref,
    opened_ref,
    slope_z_ref,
    inner_ref,
    carried_ref,
    x_conv_ref,
    slope_x_ref,
    dt_ref,
    from_start_ref,
    to_end_ref,
    weighted_ref,
    weighted_end_ref,
    bc_ref,
    slope_bc_ref,
    decay_ref,
    slope_dt_ref,
    x_buffer,
    bc_buffer,
    carry,
):
    step = pl.program_id(0)
    width = heads * size

    @pl.when(step == 0)
    def _():
        x_buffer[0:HALO, :] = jnp.zeros((HALO, width), F32)
        bc_buffer[0:HALO, :] = jnp.zeros((HALO, 2 * N), F32)
        carry[...] = jnp.zeros((N, width), F32)

    window = window_ref[pl.ds(pl.multiple_of(step * Q, Q), Q + 2 * HALO), :]
    seg, from_prev, same_last, passes, bias = block_masks(window, seg_row_ref[0:1, :])
    bcdt = bcdt_ref[...]
    x_buffer[HALO : HALO + Q, :] = x_ref[...]
    bc_buffer[HALO : HALO + Q, :] = bcdt[:, : 2 * N]
    pre = conv_forward(
        x_buffer, window, seg, kernel_x_ref[...], kernel_x_ref[CONV : CONV + 1, :], width
    )
    pre_bc = conv_forward(
        bc_buffer, window, seg, kernel_bc_ref[...], kernel_bc_ref[CONV : CONV + 1, :], 2 * N
    )
    x_buffer[0:HALO, :] = x_buffer[Q : Q + HALO, :]
    bc_buffer[0:HALO, :] = bc_buffer[Q : Q + HALO, :]
    gate_x = sigmoid(pre)
    x_conv = pre * gate_x
    x_conv_ref[...] = x_conv
    slope_x_ref[...] = gate_x * (1.0 + pre * (1.0 - gate_x))
    gate_bc = sigmoid(pre_bc)
    bc_conv = (pre_bc * gate_bc).astype(BF16)
    bc_ref[...] = bc_conv
    slope_bc_ref[...] = gate_bc * (1.0 + pre_bc * (1.0 - gate_bc))
    b_in = bc_conv[:, :N]
    c_in = bc_conv[:, N:]

    raw = bcdt[:, 2 * N :] + head_ref[0:1, :]
    slope_dt_ref[...] = sigmoid(raw)
    dt = softplus(raw)
    decay = -dt * jnp.exp(head_ref[1:2, :])
    decay_ref[...] = decay
    total = dot_exact(triangle(True).astype(F32), decay)
    total_t = total.T
    dt_wide = spread(dt, heads, size)
    dt_ref[...] = dt_wide
    weighted = x_conv * dt_wide
    weighted_low = weighted.astype(BF16)
    weighted_ref[...] = weighted_low
    scores = dot_nt(c_in, b_in)
    before = carry[...]
    state_ref[0] = before

    per = LANES // size
    lane = lax.broadcasted_iota(jnp.int32, (Q, LANES), 1)
    none = jnp.zeros((Q, LANES), BF16)
    inner = []
    for first in range(0, heads, per):
        group = weighted_low[:, first * size : first * size + LANES]
        summed = jnp.zeros((Q, LANES), F32)
        for extra in range(per):
            h = first + extra
            shape = jnp.exp(total[:, h : h + 1] - total_t[h : h + 1, :] + bias)
            prob = (scores * shape).astype(BF16)
            shape_ref[:, h * Q : (h + 1) * Q] = shape.astype(BF16)
            prob_ref[:, h * Q : (h + 1) * Q] = prob
            mine = (lane >= extra * size) & (lane < (extra + 1) * size)
            summed = summed + dot(prob, jnp.where(mine, group, none))
        inner.append(summed)
    inner = jnp.concatenate(inner, axis=1)
    inner_ref[...] = inner
    carried = dot(c_in, before.astype(BF16))
    carried_ref[...] = carried
    from_start = spread(jnp.exp(total) * from_prev, heads, size)
    from_start_ref[...] = from_start
    last = total[Q - 1 : Q, :]
    to_end = spread(jnp.exp(last - total) * same_last, heads, size)
    to_end_ref[...] = to_end
    weighted_end = (weighted * to_end).astype(BF16)
    weighted_end_ref[...] = weighted_end
    survive = spread(jnp.exp(last) * passes, heads, size)
    survive_ref[0] = jnp.broadcast_to(survive, (8, width))
    carry[...] = dot_tn(b_in, weighted_end) + before * survive

    mixed = inner + carried * from_start + channel_ref[1:2, :] * x_conv
    z_proj = z_ref[...]
    gate = sigmoid(z_proj)
    opened = z_proj * gate
    opened_ref[...] = opened
    slope_z_ref[...] = mixed * (gate * (1.0 + z_proj * (1.0 - gate)))
    gated = mixed * opened
    gated_ref[...] = gated
    scaled = (gated * channel_ref[0:1, :]).astype(BF16)
    scaled_ref[...] = scaled
    part_ref[...] = dot_nt(scaled, weights_ref[...]).astype(BF16)
    square_ref[...] = as_row(jnp.sum(gated * gated, axis=1, keepdims=True))


def gradient_kernel(width, cot_ref, weights_ref, scaled_ref, window_ref, grad_ref, along_ref):
    step = pl.program_id(0)
    window = window_ref[pl.ds(pl.multiple_of(step * Q, Q), Q + 2 * HALO), :]
    live = (window[HALO : HALO + Q] > 0).astype(F32)
    grad = dot(cot_ref[...], weights_ref[...]) * widen(live, width)
    grad_ref[...] = grad
    along_ref[...] = as_row(jnp.sum(scaled_ref[...].astype(F32) * grad, axis=1, keepdims=True))


def backward_kernel(
    heads,
    size,
    full_inner,
    stat_ref,
    hidden_ref,
    window_ref,
    weights_ref,
    kernel_x_ref,
    kernel_bc_ref,
    head_ref,
    channel_ref,
    x_ref,
    bcdt_ref,
    grad_ref,
    state_ref,
    survive_ref,
    shape_ref,
    prob_ref,
    gated_ref,
    opened_ref,
    slope_z_ref,
    inner_ref,
    carried_ref,
    x_conv_ref,
    slope_x_ref,
    dt_ref,
    from_start_ref,
    to_end_ref,
    weighted_ref,
    weighted_end_ref,
    bc_ref,
    slope_bc_ref,
    decay_ref,
    slope_dt_ref,
    proj_ref,
    part_ref,
    out_ref,
    sum_x_ref,
    sum_bc_ref,
    sum_head_ref,
    sum_gain_ref,
    x_buffer,
    bc_buffer,
    carry,
    tail,
):
    turn = pl.program_id(0)
    step = pl.num_programs(0) - 1 - turn
    width = heads * size

    @pl.when(turn == 0)
    def _():
        x_buffer[...] = jnp.zeros((Q + HALO, width), F32)
        bc_buffer[...] = jnp.zeros((Q + HALO, 2 * N), F32)
        carry[...] = jnp.zeros((N, width), F32)
        tail[...] = jnp.zeros((8, LANES), F32)
        sum_x_ref[...] = jnp.zeros((8, width), F32)
        sum_bc_ref[...] = jnp.zeros((8, 2 * N), F32)
        sum_head_ref[...] = jnp.zeros((8, LANES), F32)
        sum_gain_ref[...] = jnp.zeros(sum_gain_ref.shape, F32)

    window = window_ref[pl.ds(pl.multiple_of(step * Q, Q), Q + 2 * HALO), :]
    seg = window[HALO : HALO + Q]
    live = (seg[:, 0:1] > 0).astype(F32)
    stat = stat_ref[...].T
    gate_inverse = lax.rsqrt(stat[:, 0:1] / full_inner + EPS)
    along = stat[:, 1:2] * (gate_inverse * gate_inverse * gate_inverse / full_inner)

    gain = channel_ref[0:1, :]
    skip = channel_ref[1:2, :]
    grad_out = grad_ref[...]
    gated = gated_ref[...]
    normal = gated * gate_inverse
    sum_gate = jnp.sum(grad_out * normal, axis=0, keepdims=True)
    out_ref[...] = (normal * gain * live).astype(BF16)
    grad_gated = grad_out * gain * gate_inverse - gated * along
    grad_z = (grad_gated * slope_z_ref[...]).astype(BF16)
    dy = grad_gated * opened_ref[...]
    dy_low = dy.astype(BF16)
    dy_start = (dy * from_start_ref[...]).astype(BF16)

    bc_conv = bc_ref[...]
    b_in = bc_conv[:, :N]
    c_in = bc_conv[:, N:]
    before = state_ref[0]
    before_low = before.astype(BF16)
    after_low = carry[...].astype(BF16)
    weighted_low = weighted_ref[...]
    weighted_end = weighted_end_ref[...]
    grad_c = dot_nt(dy_start, before_low)
    returned = dot(b_in, after_low)
    grad_b = dot_nt(weighted_end, after_low)
    new_after = dot_tn(c_in, dy_start) + carry[...] * survive_ref[0, 0:1, :]
    carry[...] = new_after

    per = LANES // size
    lane = lax.broadcasted_iota(jnp.int32, (Q, LANES), 1)
    grad_scores = jnp.zeros((Q, Q), F32)
    inner = []
    none = jnp.zeros((Q, LANES), BF16)
    for first in range(0, heads, per):
        at = first * size
        dy_group = dy_low[:, at : at + LANES]
        weighted_group = weighted_low[:, at : at + LANES]
        summed = jnp.zeros((Q, LANES), F32)
        for extra in range(per):
            h = first + extra
            mine = (lane >= extra * size) & (lane < (extra + 1) * size)
            dy_mine = jnp.where(mine, dy_group, none)
            shape = shape_ref[:, h * Q : (h + 1) * Q].astype(F32)
            grad_scores = grad_scores + dot_nt(dy_mine, weighted_group) * shape
            summed = summed + dot_tn(prob_ref[:, h * Q : (h + 1) * Q], dy_mine)
        inner.append(summed)
    grad_inner = jnp.concatenate(inner, axis=1)
    grad_weighted = to_end_ref[...] * returned + grad_inner
    grad_scores = grad_scores.astype(BF16)
    grad_c = grad_c + dot(grad_scores, b_in)
    grad_b = grad_b + dot_tn(grad_scores, c_in)

    x_conv = x_conv_ref[...]
    pairs = head_sums(
        dy_low.astype(F32) * inner_ref[...]
        + dy_start.astype(F32) * carried_ref[...]
        - weighted_low.astype(F32) * grad_inner
        - weighted_end.astype(F32) * returned,
        heads,
        size,
    )
    grad_decay = dot_exact(triangle(False).astype(F32), pairs) + tail[0:1, :]
    kept = jnp.sum(new_after.astype(BF16).astype(F32) * before, axis=0, keepdims=True)
    tail[...] = head_sums(jnp.broadcast_to(kept, (8, width)), heads, size)
    rate = jnp.exp(head_ref[1:2, :])
    grad_dt = head_sums(grad_weighted * x_conv, heads, size) - grad_decay * rate
    grad_raw = grad_dt * slope_dt_ref[...]
    sum_head_ref[0:1, :] += jnp.sum(grad_raw, axis=0, keepdims=True)
    sum_head_ref[1:2, :] += jnp.sum(grad_decay * decay_ref[...], axis=0, keepdims=True)

    sum_skip = jnp.sum(dy * x_conv, axis=0, keepdims=True)
    grad_pre = (grad_weighted * dt_ref[...] + skip * dy) * slope_x_ref[...]
    x_buffer[Q : Q + HALO, :] = x_buffer[0:HALO, :]
    x_buffer[0:Q, :] = grad_pre
    grad_proj, taps = conv_backward(
        x_buffer, window, seg, kernel_x_ref[...], x_ref[...], width
    )
    sum_bias = jnp.sum(grad_pre, axis=0, keepdims=True)
    blank = jnp.zeros((1, width), F32)
    sum_x_ref[...] += jnp.concatenate(
        [taps[3], taps[2], taps[1], taps[0], sum_bias, sum_gate, sum_skip, blank], axis=0
    )

    grad_pre_bc = jnp.concatenate([grad_b, grad_c], axis=1) * slope_bc_ref[...]
    bc_buffer[Q : Q + HALO, :] = bc_buffer[0:HALO, :]
    bc_buffer[0:Q, :] = grad_pre_bc
    grad_bc, taps_bc = conv_backward(
        bc_buffer, window, seg, kernel_bc_ref[...], bcdt_ref[:, : 2 * N], 2 * N
    )
    sum_bias_bc = jnp.sum(grad_pre_bc, axis=0, keepdims=True)
    blank_bc = jnp.zeros((3, 2 * N), F32)
    sum_bc_ref[...] += jnp.concatenate(
        [taps_bc[3], taps_bc[2], taps_bc[1], taps_bc[0], sum_bias_bc, blank_bc], axis=0
    )

    grads = jnp.concatenate(
        [grad_proj.astype(BF16), grad_z, grad_bc.astype(BF16), grad_raw.astype(BF16)], axis=1
    )
    proj_ref[...] = grads
    part = dot_nt(grads, weights_ref[:, width:])
    part_ref[...] = part.astype(BF16)
    hidden = hidden_ref[...].astype(F32)
    inverse = lax.rsqrt(jnp.mean(hidden * hidden, axis=1, keepdims=True) + EPS)
    sum_gain_ref[0:1, :] += jnp.sum(part * (hidden * inverse), axis=0, keepdims=True)


def pack_kernel(*refs):
    *parts, packed, sems = refs
    at = 0
    copies = []
    for index, part in enumerate(parts):
        columns = part.shape[1]
        copies.append(
            pltpu.make_async_copy(part, packed.at[:, pl.ds(at, columns)], sems.at[index])
        )
        at += columns
    for copy in copies:
        copy.start()
    for copy in copies:
        copy.wait()


def run_pack(*parts):
    rows = parts[0].shape[0]
    columns = sum(part.shape[1] for part in parts)
    return pl.pallas_call(
        pack_kernel,
        in_specs=[pl.BlockSpec(memory_space=pl.ANY)] * len(parts),
        out_specs=pl.BlockSpec(memory_space=pl.ANY),
        out_shape=jax.ShapeDtypeStruct((rows, columns), BF16),
        scratch_shapes=[pltpu.SemaphoreType.DMA((len(parts),))],
        compiler_params=pltpu.CompilerParams(vmem_limit_bytes=VMEM_LIMIT),
        name="pack",
    )(*parts)


def cost(micros):
    return pl.CostEstimate(flops=int(micros * 1e9), bytes_accessed=1 << 20, transcendentals=0)


def whole(shape):
    return pl.BlockSpec(shape, lambda i: (0,) * len(shape))


def scalar():
    return pl.BlockSpec(memory_space=pltpu.SMEM)


def run_project(heads, size, place, near, weights):
    features = near[0].shape[1]
    blocks = len(near) // 2 + 1
    length = blocks * Q
    width = heads * size
    rest = 2 * N + LANES

    def rows(columns):
        return pl.BlockSpec((Q, columns), lambda i: (i, 0))

    def made(columns, dtype):
        return jax.ShapeDtypeStruct((length, columns), dtype)

    return pl.pallas_call(
        functools.partial(project_kernel, heads, size, len(near)),
        grid=(blocks,),
        in_specs=[scalar(), *[whole(block.shape) for block in near], whole(weights.shape)],
        out_specs=[
            rows(features),
            rows(features),
            rows(width),
            rows(width),
            rows(rest),
            whole((8, features)),
        ],
        out_shape=[
            made(features, BF16),
            made(features, BF16),
            made(width, F32),
            made(width, F32),
            made(rest, F32),
            jax.ShapeDtypeStruct((8, features), F32),
        ],
        compiler_params=pltpu.CompilerParams(vmem_limit_bytes=VMEM_LIMIT),
        cost_estimate=cost(8),
        name="project",
    )(place, *near, weights)


def saved_rows(heads, size):
    width = heads * size
    return (
        [(heads * Q, BF16)] * 2
        + [(width, F32)] * 10
        + [(width, BF16)] * 2
        + [(2 * N, BF16), (2 * N, F32), (LANES, F32), (LANES, F32)]
    )


def saved_specs(heads, size, place):
    width = heads * size
    return [
        pl.BlockSpec((1, N, width), lambda i: (place(i), 0, 0)),
        pl.BlockSpec((1, 8, width), lambda i: (place(i), 0, 0)),
    ] + [
        pl.BlockSpec((Q, columns), lambda i: (place(i), 0))
        for columns, _ in saved_rows(heads, size)
    ]


def run_forward(
    heads, size, window, seg_row, weights, kernel_x, kernel_bc, head, channel, z_proj, x_proj, bcdt
):
    length, features = seg_row.shape[1], weights.shape[0]
    width = heads * size
    blocks = length // Q

    def rows(columns):
        return pl.BlockSpec((Q, columns), lambda i: (i, 0))

    def made(columns, dtype):
        return jax.ShapeDtypeStruct((length, columns), dtype)

    across = pl.BlockSpec((8, Q), lambda i: (0, i))
    return pl.pallas_call(
        functools.partial(forward_kernel, heads, size),
        grid=(blocks,),
        in_specs=[
            whole(window.shape),
            across,
            whole((features, width)),
            whole(kernel_x.shape),
            whole(kernel_bc.shape),
            whole(head.shape),
            whole(channel.shape),
            rows(width),
            rows(width),
            rows(bcdt.shape[1]),
        ],
        out_specs=[rows(width), rows(features), across, *saved_specs(heads, size, lambda i: i)],
        out_shape=[
            made(width, BF16),
            made(features, BF16),
            jax.ShapeDtypeStruct((8, length), F32),
            *[
                jax.ShapeDtypeStruct((blocks,) + shape, F32) for shape in ((N, width), (8, width))
            ],
            *[made(columns, dtype) for columns, dtype in saved_rows(heads, size)],
        ],
        scratch_shapes=[
            pltpu.VMEM((Q + HALO, width), F32),
            pltpu.VMEM((Q + HALO, 2 * N), F32),
            pltpu.VMEM((N, width), F32),
        ],
        compiler_params=pltpu.CompilerParams(vmem_limit_bytes=VMEM_LIMIT),
        cost_estimate=cost(14),
        name="forward",
    )(window, seg_row, weights, kernel_x, kernel_bc, head, channel, z_proj, x_proj, bcdt)


def run_gradient(cot, weights, scaled, window):
    length, features = cot.shape
    width = scaled.shape[1]
    return pl.pallas_call(
        functools.partial(gradient_kernel, width),
        grid=(length // Q,),
        in_specs=[
            pl.BlockSpec((Q, features), lambda i: (i, 0)),
            whole((features, width)),
            pl.BlockSpec((Q, width), lambda i: (i, 0)),
            whole(window.shape),
        ],
        out_specs=[
            pl.BlockSpec((Q, width), lambda i: (i, 0)),
            pl.BlockSpec((8, Q), lambda i: (0, i)),
        ],
        out_shape=[
            jax.ShapeDtypeStruct((length, width), F32),
            jax.ShapeDtypeStruct((8, length), F32),
        ],
        compiler_params=pltpu.CompilerParams(vmem_limit_bytes=VMEM_LIMIT),
        cost_estimate=cost(5),
        name="out_gradient",
    )(cot, weights, scaled, window)


def weights_kernel(width, cot_ref, normed_ref, tokens_ref, grads_ref, first_ref, second_ref):
    tokens = tokens_ref[...]
    first_ref[:, :width] = dot_tn(cot_ref[...], normed_ref[...]).astype(BF16)
    first_ref[:, width:] = dot_tn(tokens, grads_ref[:, 2 * width :]).astype(BF16)
    second_ref[...] = dot_tn(tokens, grads_ref[:, : 2 * width]).astype(BF16)


def run_weights(cot, normed, tokens, grads):
    length, features = tokens.shape
    width = normed.shape[1]
    columns = [grads.shape[1] - width, 2 * width]
    return pl.pallas_call(
        functools.partial(weights_kernel, width),
        grid=(features // Q,),
        in_specs=[
            pl.BlockSpec((length, Q), lambda i: (0, i)),
            whole(normed.shape),
            pl.BlockSpec((length, Q), lambda i: (0, i)),
            whole(grads.shape),
        ],
        out_specs=[pl.BlockSpec((Q, count), lambda i: (i, 0)) for count in columns],
        out_shape=[jax.ShapeDtypeStruct((features, count), BF16) for count in columns],
        compiler_params=pltpu.CompilerParams(vmem_limit_bytes=VMEM_LIMIT),
        cost_estimate=cost(7),
        name="weight_gradients",
    )(cot, normed, tokens, grads)


def run_backward(
    heads, size, full_inner, stat, hidden, window, weights, kernel_x, kernel_bc, head, channel,
    x_proj, bcdt, grad_out, saved,
):
    length, features = hidden.shape
    width = heads * size
    blocks = length // Q
    rest = 2 * N + LANES
    total = 2 * width + rest

    def rows(columns):
        return pl.BlockSpec((Q, columns), lambda i: (blocks - 1 - i, 0))

    def made(columns, dtype):
        return jax.ShapeDtypeStruct((length, columns), dtype)

    across = pl.BlockSpec((8, Q), lambda i: (0, blocks - 1 - i))
    sums = [(8, width), (8, 2 * N), (8, LANES), (8, features)]
    return pl.pallas_call(
        functools.partial(backward_kernel, heads, size, full_inner),
        grid=(blocks,),
        in_specs=[
            across,
            rows(features),
            whole(window.shape),
            whole(weights.shape),
            whole(kernel_x.shape),
            whole(kernel_bc.shape),
            whole(head.shape),
            whole(channel.shape),
            rows(width),
            rows(rest),
            rows(width),
            *saved_specs(heads, size, lambda i: blocks - 1 - i),
        ],
        out_specs=[rows(total), rows(features), rows(width)] + [whole(shape) for shape in sums],
        out_shape=[made(total, BF16), made(features, BF16), made(width, BF16)]
        + [jax.ShapeDtypeStruct(shape, F32) for shape in sums],
        scratch_shapes=[
            pltpu.VMEM((Q + HALO, width), F32),
            pltpu.VMEM((Q + HALO, 2 * N), F32),
            pltpu.VMEM((N, width), F32),
            pltpu.VMEM((8, LANES), F32),
        ],
        compiler_params=pltpu.CompilerParams(vmem_limit_bytes=VMEM_LIMIT),
        cost_estimate=cost(2),
        name="backward",
    )(
        stat, hidden, window, weights, kernel_x, kernel_bc, head, channel, x_proj, bcdt, grad_out,
        *saved,
    )


def finish_kernel(sum_ref, hidden_ref, cot_ref, gain_ref, out_ref):
    grad = sum_ref[...].astype(F32) * gain_ref[0:1, :]
    hidden = hidden_ref[...].astype(F32)
    inverse = lax.rsqrt(jnp.mean(hidden * hidden, axis=1, keepdims=True) + EPS)
    unit = hidden * inverse
    along = jnp.mean(grad * unit, axis=1, keepdims=True)
    out_ref[...] = (cot_ref[...].astype(F32) + inverse * (grad - unit * along)).astype(BF16)


def run_finish(in_sum, hidden, cot, gain):
    length, features = hidden.shape
    rows = pl.BlockSpec((length // 2, features), lambda i: (i, 0))
    return pl.pallas_call(
        finish_kernel,
        grid=(2,),
        in_specs=[rows, rows, rows, whole(gain.shape)],
        out_specs=rows,
        out_shape=jax.ShapeDtypeStruct(hidden.shape, BF16),
        compiler_params=pltpu.CompilerParams(vmem_limit_bytes=VMEM_LIMIT),
        name="finish",
    )(in_sum, hidden, cot, gain)


def pad_lanes(values):
    return jnp.pad(values, ((0, 0), (0, LANES - values.shape[1])))


def after(value, *others):
    return lax.optimization_barrier((value, *others))[0]


def line_step(right, left, step, axis):
    n = lax.axis_size(axis)
    return (
        lax.ppermute(right, axis, [(i, i + 1) for i in range(step - 1, n - 1)]),
        lax.ppermute(left, axis, [(i, i - 1) for i in range(1, n - step + 1)]),
    )


def line_order(block, moved):
    return [pair[0] for pair in moved[::-1]] + [block] + [pair[1] for pair in moved]


def line_gather(block, axis):
    right = left = block
    moved = []
    for step in range(1, lax.axis_size(axis)):
        right, left = line_step(right, left, step, axis)
        moved.append((right, left))
    return line_order(block, moved)


def cube_scatter(first, second, small, axis):
    n = lax.axis_size(axis)
    if n & (n - 1):
        sums = [
            lax.psum_scatter(part, axis, scatter_dimension=0, tiled=True).astype(F32)
            for part in (first, second)
        ]
        return (*sums, lax.psum(small, axis), sums)
    place = lax.axis_index(axis)
    bits = list(range(n.bit_length() - 1))
    orders = [bits, bits[:1] + bits[:0:-1]]
    parts = [part.reshape((2,) * len(bits) + (-1, part.shape[1])) for part in (first, second)]
    left = [bits[::-1], bits[::-1]]
    came = []
    for step in range(len(bits)):
        for index in range(2):
            part = parts[index]
            bit = orders[index][step]
            dim = left[index].index(bit)
            mine = (place >> bit) & 1
            keep = lax.dynamic_index_in_dim(part, mine, dim, keepdims=False)
            send = lax.dynamic_index_in_dim(part, 1 - mine, dim, keepdims=False)
            pairs = [(i, i ^ (1 << bit)) for i in range(n)]
            if index == 0:
                columns = part.shape[-1]
                rows = send.size // columns
                extra = -(-small.size // (16 * columns)) * 16
                small = lax.reduce_precision(small, 8, 7)
                rider = jnp.pad(
                    small.astype(BF16).reshape(-1), (0, extra * columns - small.size)
                ).reshape(extra, columns)
                moved = lax.ppermute(
                    jnp.concatenate([send.reshape(rows, columns), rider]), axis, pairs
                )
                other = moved[:rows].reshape(send.shape)
                rider = moved[rows:].reshape(-1)[: small.size].reshape(small.shape)
                small = small + rider.astype(F32)
            else:
                moved = other = lax.ppermute(send, axis, pairs)
            came.append(moved)
            part = keep.astype(F32) + other.astype(F32)
            left[index] = [other_bit for other_bit in left[index] if other_bit != bit]
            parts[index] = part.astype(BF16) if left[index] else part
    return (*parts, small, came)


def around(values, axis):
    n = lax.axis_size(axis)
    return [values] + [
        lax.ppermute(values, axis, [(i, (i - k) % n) for i in range(n)]) for k in range(1, n)
    ]


def sum_around(values, axis):
    return functools.reduce(jnp.add, around(values, axis))


def sum_around_low(values, axis):
    low = around(lax.reduce_precision(values, 8, 7).astype(BF16), axis)
    return functools.reduce(jnp.add, [share.astype(F32) for share in low])


def shards(
    hidden,
    seg_ids,
    cotangent,
    norm_gain,
    w_in_z,
    w_in_x,
    w_in_bc,
    w_in_dt,
    conv_x,
    conv_x_bias,
    conv_bc,
    conv_bc_bias,
    dt_bias,
    a_log,
    d_skip,
    gate_gain,
    w_out,
):
    heads = dt_bias.shape[0]
    width = gate_gain.shape[0]
    size = width // heads
    full_inner = width * lax.axis_size("tensor")
    features = hidden.shape[2]
    hidden_local = hidden[0]

    steps = jnp.pad(
        jnp.concatenate([w_in_dt, norm_gain[:, None]], axis=1), ((0, 0), (0, LANES - heads - 1))
    )
    packed = run_pack(w_out, w_in_x, w_in_z, w_in_bc, steps)
    n = lax.axis_size("tensor")
    axis_place = lax.axis_index("tensor")
    place = axis_place[None]
    near_hidden = line_gather(hidden_local, "tensor")
    weights = lax.all_gather(packed, "dp", axis=0, tiled=True)
    seg_stack = around(seg_ids[0], "tensor")
    count = seg_ids.shape[1]
    seg_full = lax.dynamic_slice_in_dim(
        jnp.concatenate(seg_stack + seg_stack), (n - axis_place) * count, n * count, 0
    )
    window = jnp.broadcast_to(
        jnp.pad(seg_full, (HALO, HALO), constant_values=-1)[:, None],
        (seg_full.shape[0] + 2 * HALO, LANES),
    )
    seg_row = jnp.broadcast_to(seg_full[None, :], (8, seg_full.shape[0]))
    kernel_x = jnp.concatenate([conv_x, conv_x_bias[None, :]], axis=0)
    kernel_bc = jnp.concatenate([conv_bc, conv_bc_bias[None, :]], axis=0)
    head = pad_lanes(jnp.stack([dt_bias, a_log]))
    channel = jnp.stack([gate_gain, jnp.repeat(d_skip, size)])

    hidden_full, tokens, z_proj, x_proj, bcdt, gain = run_project(
        heads, size, place, near_hidden, weights
    )
    cot_full = lax.all_gather(
        after(cotangent[0], near_hidden[0], near_hidden[-1]), "tensor", axis=0, tiled=True
    )
    scaled, out_part, square, *saved = run_forward(
        heads, size, window, seg_row, weights, kernel_x, kernel_bc, head, channel, z_proj, x_proj,
        bcdt,
    )
    grad_out, along = run_gradient(cot_full, weights, scaled, window)
    out_sum = lax.psum_scatter(
        out_part, "tensor", scatter_dimension=0, tiled=True
    )
    stat = sum_around(jnp.stack([square[0], along[0]]), "tensor")
    stat_full = jnp.pad(stat, ((0, 6), (0, 0)))
    out_scale = lax.rsqrt(stat[0] / full_inner + EPS) * (seg_full > 0).astype(F32)

    grads, in_part, normed_out, sum_x, sum_bc, sum_head, sum_gain = run_backward(
        heads, size, full_inner, stat_full, hidden_full, window, weights, kernel_x, kernel_bc, head,
        channel, x_proj, bcdt, grad_out, saved,
    )
    in_sum = lax.psum_scatter(in_part, "tensor", scatter_dimension=0, tiled=True)
    first, second = run_weights(cot_full, normed_out, tokens, after(grads, out_sum))
    own = jnp.concatenate([sum_x.reshape(-1, LANES), sum_head])
    both = jnp.concatenate([sum_gain[0].reshape(-1, LANES), sum_bc.reshape(-1, LANES)])
    first, second, small, came = cube_scatter(first, second, jnp.concatenate([own, both]), "dp")
    sum_x = small[: own.shape[0] - 8].reshape(8, width)
    sum_head = small[own.shape[0] - 8 : own.shape[0]]
    grad_bc = first[:, width : width + 2 * N]
    shared = jnp.concatenate([small[own.shape[0] :], grad_bc.reshape(-1, LANES)])
    shared = sum_around_low(shared, "tensor")
    gain_rows = features // LANES
    sum_gain = shared[:gain_rows].reshape(features)
    sum_bc = shared[gain_rows : both.shape[0]].reshape(8, 2 * N)
    grad_bc = shared[both.shape[0] :].reshape(grad_bc.shape)
    local_features = norm_gain.shape[0]
    grad_norm_gain = lax.dynamic_slice_in_dim(
        sum_gain, lax.axis_index("dp") * local_features, local_features, 0
    )

    local = hidden_local.shape[0]
    hidden_rows = hidden_local.astype(F32)
    scale_here = lax.dynamic_slice_in_dim(out_scale, axis_place * local, local, 0)[:, None]
    layer_out = (hidden_rows + out_sum.astype(F32) * scale_here).astype(BF16)

    grad_hidden = run_finish(in_sum, hidden_local, cotangent[0], after(gain, shared))

    return (
        layer_out[None],
        grad_hidden[None],
        grad_norm_gain,
        second[:, width:],
        second[:, :width],
        grad_bc,
        first[:, width + 2 * N : width + 2 * N + heads],
        sum_x[0:CONV],
        sum_x[CONV],
        sum_bc[0:CONV],
        sum_bc[CONV],
        sum_head[0, :heads],
        sum_head[1, :heads],
        jnp.sum(sum_x[CONV + 2].reshape(heads, size), axis=1),
        sum_x[CONV + 1],
        first[:, :width],
    )


def solution(mesh):
    in_specs = (
        P("dp", "tensor", None),
        P("dp", "tensor"),
        P("dp", "tensor", None),
        P("dp"),
        P("dp", "tensor"),
        P("dp", "tensor"),
        P("dp", None),
        P("dp", "tensor"),
        P(None, "tensor"),
        P("tensor"),
        P(),
        P(),
        P("tensor"),
        P("tensor"),
        P("tensor"),
        P("tensor"),
        P("dp", "tensor"),
    )
    out_specs = (
        P("dp", "tensor", None),
        P("dp", "tensor", None),
        P("dp"),
        P("dp", "tensor"),
        P("dp", "tensor"),
        P("dp", None),
        P("dp", "tensor"),
        P(None, "tensor"),
        P("tensor"),
        P(),
        P(),
        P("tensor"),
        P("tensor"),
        P("tensor"),
        P("tensor"),
        P("dp", "tensor"),
    )
    return jax.shard_map(shards, mesh=mesh, in_specs=in_specs, out_specs=out_specs, check_vma=False)
```

```python
import functools

import jax
import jax.numpy as jnp
from jax import lax
from jax.experimental import pallas as pl
from jax.experimental.pallas import tpu as pltpu
from jax.sharding import PartitionSpec as P

N = 128
CONV = 4
Q = 256
LANES = 128
HALO = 8
EPS = 1e-05
NEG = -1e30
F32 = jnp.float32
BF16 = jnp.bfloat16
VMEM_LIMIT = 52 * 1024 * 1024


def dot(a, b):
    return jnp.dot(a, b, preferred_element_type=F32)


def dot_nt(a, b):
    return lax.dot_general(a, b, (((1,), (1,)), ((), ())), preferred_element_type=F32)


def dot_tn(a, b):
    return lax.dot_general(a, b, (((0,), (0,)), ((), ())), preferred_element_type=F32)


def dot_exact(a, b):
    return jnp.dot(a, b, preferred_element_type=F32, precision=lax.Precision.HIGHEST)


def spread(cols, heads, size):
    rows = cols.shape[0]
    per = LANES // size
    lane = lax.broadcasted_iota(jnp.int32, (rows, LANES), 1)
    parts = []
    for first in range(0, heads, per):
        part = jnp.broadcast_to(cols[:, first : first + 1], (rows, LANES))
        for extra in range(1, per):
            part = jnp.where(lane < extra * size, part, cols[:, first + extra : first + extra + 1])
        parts.append(part)
    return jnp.concatenate(parts, axis=1)


def head_sums(values, heads, size):
    width = heads * size
    channel = lax.broadcasted_iota(jnp.int32, (width, LANES), 0)
    column = lax.broadcasted_iota(jnp.int32, (width, LANES), 1)
    first = column * size
    picks = jnp.where((channel >= first) & (channel < first + size), 1.0, 0.0).astype(BF16)
    high = values.astype(BF16)
    low = (values - high.astype(F32)).astype(BF16)
    return dot(high, picks) + dot(low, picks)


def widen(tile, width):
    return jnp.concatenate([tile] * (width // tile.shape[1]), axis=1)


def softplus(v):
    return jnp.maximum(v, 0.0) + jnp.log1p(jnp.exp(-jnp.abs(v)))


def sigmoid(v):
    return 1.0 / (1.0 + jnp.exp(-v))


def as_row(column):
    rows = column.shape[0]
    return jnp.broadcast_to(column, (rows, LANES)).T[:8]


def triangle(lower):
    row = lax.broadcasted_iota(jnp.int32, (Q, Q), 0)
    col = lax.broadcasted_iota(jnp.int32, (Q, Q), 1)
    return row >= col if lower else row <= col


def block_masks(window, seg_row):
    seg = window[HALO : HALO + Q]
    before = window[HALO - 1 : HALO]
    last = window[HALO + Q - 1 : HALO + Q]
    from_prev = (seg == before).astype(F32)
    same_last = (seg == last).astype(F32)
    passes = (last == before).astype(F32)
    keep = (widen(seg, Q) == seg_row) & triangle(True)
    bias = jnp.where(keep, 0.0, NEG)
    return seg, from_prev, same_last, passes, bias


def conv_forward(buffer, window, seg, kernel, conv_bias, width):
    total = conv_bias + kernel[CONV - 1 : CONV] * buffer[HALO : HALO + Q, :]
    for back in range(1, CONV):
        match = (window[HALO - back : HALO - back + Q] == seg).astype(F32)
        tap = kernel[CONV - 1 - back : CONV - back]
        total = total + tap * (buffer[HALO - back : HALO - back + Q, :] * widen(match, width))
    return total


def conv_backward(buffer, window, seg, kernel, values, width):
    here = buffer[0:Q, :]
    total = kernel[CONV - 1 : CONV] * here
    taps = [jnp.sum(values * here, axis=0, keepdims=True)]
    for ahead in range(1, CONV):
        match = (window[HALO + ahead : HALO + ahead + Q] == seg).astype(F32)
        moved = buffer[ahead : ahead + Q, :] * widen(match, width)
        total = total + kernel[CONV - 1 - ahead : CONV - ahead] * moved
        taps.append(jnp.sum(values * moved, axis=0, keepdims=True))
    return total, taps


def pick_block(place, near_refs, block):
    reach = len(near_refs) // 2
    away = pl.program_id(0) - place
    for index, ref in enumerate(near_refs):

        @pl.when(away == index - reach)
        def _():
            block[...] = ref[...]


def project_kernel(heads, size, near, place_ref, *refs):
    near_refs, refs = refs[:near], refs[near:]
    weights_ref, hidden_ref, tokens_ref, z_ref, x_ref, bcdt_ref, gain_ref = refs
    width = heads * size

    @pl.when(pl.program_id(0) == 0)
    def _():
        tail_columns = weights_ref[:, 3 * width + 2 * N :].astype(F32).T
        gain_ref[...] = jnp.broadcast_to(tail_columns[heads : heads + 1], gain_ref.shape)

    pick_block(place_ref[0], near_refs, hidden_ref)
    hidden = hidden_ref[...].astype(F32)
    inverse = lax.rsqrt(jnp.mean(hidden * hidden, axis=1, keepdims=True) + EPS)
    tokens = (hidden * inverse * gain_ref[0:1, :]).astype(BF16)
    tokens_ref[...] = tokens
    x_ref[...] = dot(tokens, weights_ref[:, width : 2 * width])
    z_ref[...] = dot(tokens, weights_ref[:, 2 * width : 3 * width])
    bcdt_ref[...] = dot(tokens, weights_ref[:, 3 * width :])


def forward_kernel(
    heads,
    size,
    window_ref,
    seg_row_ref,
    weights_ref,
    kernel_x_ref,
    kernel_bc_ref,
    head_ref,
    channel_ref,
    z_ref,
    x_ref,
    bcdt_ref,
    scaled_ref,
    part_ref,
    square_ref,
    state_ref,
    survive_ref,
    shape_ref,
    prob_ref,
    gated_ref,
    opened_ref,
    slope_z_ref,
    inner_ref,
    carried_ref,
    x_conv_ref,
    slope_x_ref,
    dt_ref,
    from_start_ref,
    to_end_ref,
    weighted_ref,
    weighted_end_ref,
    bc_ref,
    slope_bc_ref,
    decay_ref,
    slope_dt_ref,
    x_buffer,
    bc_buffer,
    carry,
):
    step = pl.program_id(0)
    width = heads * size

    @pl.when(step == 0)
    def _():
        x_buffer[0:HALO, :] = jnp.zeros((HALO, width), F32)
        bc_buffer[0:HALO, :] = jnp.zeros((HALO, 2 * N), F32)
        carry[...] = jnp.zeros((N, width), F32)

    window = window_ref[pl.ds(pl.multiple_of(step * Q, Q), Q + 2 * HALO), :]
    seg, from_prev, same_last, passes, bias = block_masks(window, seg_row_ref[0:1, :])
    bcdt = bcdt_ref[...]
    x_buffer[HALO : HALO + Q, :] = x_ref[...]
    bc_buffer[HALO : HALO + Q, :] = bcdt[:, : 2 * N]
    pre = conv_forward(
        x_buffer, window, seg, kernel_x_ref[...], kernel_x_ref[CONV : CONV + 1, :], width
    )
    pre_bc = conv_forward(
        bc_buffer, window, seg, kernel_bc_ref[...], kernel_bc_ref[CONV : CONV + 1, :], 2 * N
    )
    x_buffer[0:HALO, :] = x_buffer[Q : Q + HALO, :]
    bc_buffer[0:HALO, :] = bc_buffer[Q : Q + HALO, :]
    gate_x = sigmoid(pre)
    x_conv = pre * gate_x
    x_conv_ref[...] = x_conv
    slope_x_ref[...] = gate_x * (1.0 + pre * (1.0 - gate_x))
    gate_bc = sigmoid(pre_bc)
    bc_conv = (pre_bc * gate_bc).astype(BF16)
    bc_ref[...] = bc_conv
    slope_bc_ref[...] = gate_bc * (1.0 + pre_bc * (1.0 - gate_bc))
    b_in = bc_conv[:, :N]
    c_in = bc_conv[:, N:]

    raw = bcdt[:, 2 * N :] + head_ref[0:1, :]
    slope_dt_ref[...] = sigmoid(raw)
    dt = softplus(raw)
    decay = -dt * jnp.exp(head_ref[1:2, :])
    decay_ref[...] = decay
    total = dot_exact(triangle(True).astype(F32), decay)
    total_t = total.T
    dt_wide = spread(dt, heads, size)
    dt_ref[...] = dt_wide
    weighted = x_conv * dt_wide
    weighted_low = weighted.astype(BF16)
    weighted_ref[...] = weighted_low
    scores = dot_nt(c_in, b_in)
    before = carry[...]
    state_ref[0] = before

    per = LANES // size
    lane = lax.broadcasted_iota(jnp.int32, (Q, LANES), 1)
    none = jnp.zeros((Q, LANES), BF16)
    inner = []
    for first in range(0, heads, per):
        group = weighted_low[:, first * size : first * size + LANES]
        summed = jnp.zeros((Q, LANES), F32)
        for extra in range(per):
            h = first + extra
            shape = jnp.exp(total[:, h : h + 1] - total_t[h : h + 1, :] + bias)
            prob = (scores * shape).astype(BF16)
            shape_ref[:, h * Q : (h + 1) * Q] = shape.astype(BF16)
            prob_ref[:, h * Q : (h + 1) * Q] = prob
            mine = (lane >= extra * size) & (lane < (extra + 1) * size)
            summed = summed + dot(prob, jnp.where(mine, group, none))
        inner.append(summed)
    inner = jnp.concatenate(inner, axis=1)
    inner_ref[...] = inner
    carried = dot(c_in, before.astype(BF16))
    carried_ref[...] = carried
    from_start = spread(jnp.exp(total) * from_prev, heads, size)
    from_start_ref[...] = from_start
    last = total[Q - 1 : Q, :]
    to_end = spread(jnp.exp(last - total) * same_last, heads, size)
    to_end_ref[...] = to_end
    weighted_end = (weighted * to_end).astype(BF16)
    weighted_end_ref[...] = weighted_end
    survive = spread(jnp.exp(last) * passes, heads, size)
    survive_ref[0] = jnp.broadcast_to(survive, (8, width))
    carry[...] = dot_tn(b_in, weighted_end) + before * survive

    mixed = inner + carried * from_start + channel_ref[1:2, :] * x_conv
    z_proj = z_ref[...]
    gate = sigmoid(z_proj)
    opened = z_proj * gate
    opened_ref[...] = opened
    slope_z_ref[...] = mixed * (gate * (1.0 + z_proj * (1.0 - gate)))
    gated = mixed * opened
    gated_ref[...] = gated
    scaled = (gated * channel_ref[0:1, :]).astype(BF16)
    scaled_ref[...] = scaled
    part_ref[...] = dot_nt(scaled, weights_ref[...]).astype(BF16)
    square_ref[...] = as_row(jnp.sum(gated * gated, axis=1, keepdims=True))


def gradient_kernel(width, cot_ref, weights_ref, scaled_ref, window_ref, grad_ref, along_ref):
    step = pl.program_id(0)
    window = window_ref[pl.ds(pl.multiple_of(step * Q, Q), Q + 2 * HALO), :]
    live = (window[HALO : HALO + Q] > 0).astype(F32)
    grad = dot(cot_ref[...], weights_ref[...]) * widen(live, width)
    grad_ref[...] = grad
    along_ref[...] = as_row(jnp.sum(scaled_ref[...].astype(F32) * grad, axis=1, keepdims=True))


def backward_kernel(
    heads,
    size,
    full_inner,
    stat_ref,
    hidden_ref,
    window_ref,
    weights_ref,
    kernel_x_ref,
    kernel_bc_ref,
    head_ref,
    channel_ref,
    x_ref,
    bcdt_ref,
    grad_ref,
    state_ref,
    survive_ref,
    shape_ref,
    prob_ref,
    gated_ref,
    opened_ref,
    slope_z_ref,
    inner_ref,
    carried_ref,
    x_conv_ref,
    slope_x_ref,
    dt_ref,
    from_start_ref,
    to_end_ref,
    weighted_ref,
    weighted_end_ref,
    bc_ref,
    slope_bc_ref,
    decay_ref,
    slope_dt_ref,
    proj_ref,
    part_ref,
    out_ref,
    sum_x_ref,
    sum_bc_ref,
    sum_head_ref,
    sum_gain_ref,
    x_buffer,
    bc_buffer,
    carry,
    tail,
):
    turn = pl.program_id(0)
    step = pl.num_programs(0) - 1 - turn
    width = heads * size

    @pl.when(turn == 0)
    def _():
        x_buffer[...] = jnp.zeros((Q + HALO, width), F32)
        bc_buffer[...] = jnp.zeros((Q + HALO, 2 * N), F32)
        carry[...] = jnp.zeros((N, width), F32)
        tail[...] = jnp.zeros((8, LANES), F32)
        sum_x_ref[...] = jnp.zeros((8, width), F32)
        sum_bc_ref[...] = jnp.zeros((8, 2 * N), F32)
        sum_head_ref[...] = jnp.zeros((8, LANES), F32)
        sum_gain_ref[...] = jnp.zeros(sum_gain_ref.shape, F32)

    window = window_ref[pl.ds(pl.multiple_of(step * Q, Q), Q + 2 * HALO), :]
    seg = window[HALO : HALO + Q]
    live = (seg[:, 0:1] > 0).astype(F32)
    stat = stat_ref[...].T
    gate_inverse = lax.rsqrt(stat[:, 0:1] / full_inner + EPS)
    along = stat[:, 1:2] * (gate_inverse * gate_inverse * gate_inverse / full_inner)

    gain = channel_ref[0:1, :]
    skip = channel_ref[1:2, :]
    grad_out = grad_ref[...]
    gated = gated_ref[...]
    normal = gated * gate_inverse
    sum_gate = jnp.sum(grad_out * normal, axis=0, keepdims=True)
    out_ref[...] = (normal * gain * live).astype(BF16)
    grad_gated = grad_out * gain * gate_inverse - gated * along
    grad_z = (grad_gated * slope_z_ref[...]).astype(BF16)
    dy = grad_gated * opened_ref[...]
    dy_low = dy.astype(BF16)
    dy_start = (dy * from_start_ref[...]).astype(BF16)

    bc_conv = bc_ref[...]
    b_in = bc_conv[:, :N]
    c_in = bc_conv[:, N:]
    before = state_ref[0]
    before_low = before.astype(BF16)
    after_low = carry[...].astype(BF16)
    weighted_low = weighted_ref[...]
    weighted_end = weighted_end_ref[...]
    grad_c = dot_nt(dy_start, before_low)
    returned = dot(b_in, after_low)
    grad_b = dot_nt(weighted_end, after_low)
    new_after = dot_tn(c_in, dy_start) + carry[...] * survive_ref[0, 0:1, :]
    carry[...] = new_after

    per = LANES // size
    lane = lax.broadcasted_iota(jnp.int32, (Q, LANES), 1)
    grad_scores = jnp.zeros((Q, Q), F32)
    inner = []
    none = jnp.zeros((Q, LANES), BF16)
    for first in range(0, heads, per):
        at = first * size
        dy_group = dy_low[:, at : at + LANES]
        weighted_group = weighted_low[:, at : at + LANES]
        summed = jnp.zeros((Q, LANES), F32)
        for extra in range(per):
            h = first + extra
            mine = (lane >= extra * size) & (lane < (extra + 1) * size)
            dy_mine = jnp.where(mine, dy_group, none)
            shape = shape_ref[:, h * Q : (h + 1) * Q].astype(F32)
            grad_scores = grad_scores + dot_nt(dy_mine, weighted_group) * shape
            summed = summed + dot_tn(prob_ref[:, h * Q : (h + 1) * Q], dy_mine)
        inner.append(summed)
    grad_inner = jnp.concatenate(inner, axis=1)
    grad_weighted = to_end_ref[...] * returned + grad_inner
    grad_scores = grad_scores.astype(BF16)
    grad_c = grad_c + dot(grad_scores, b_in)
    grad_b = grad_b + dot_tn(grad_scores, c_in)

    x_conv = x_conv_ref[...]
    pairs = head_sums(
        dy_low.astype(F32) * inner_ref[...]
        + dy_start.astype(F32) * carried_ref[...]
        - weighted_low.astype(F32) * grad_inner
        - weighted_end.astype(F32) * returned,
        heads,
        size,
    )
    grad_decay = dot_exact(triangle(False).astype(F32), pairs) + tail[0:1, :]
    kept = jnp.sum(new_after.astype(BF16).astype(F32) * before, axis=0, keepdims=True)
    tail[...] = head_sums(jnp.broadcast_to(kept, (8, width)), heads, size)
    rate = jnp.exp(head_ref[1:2, :])
    grad_dt = head_sums(grad_weighted * x_conv, heads, size) - grad_decay * rate
    grad_raw = grad_dt * slope_dt_ref[...]
    sum_head_ref[0:1, :] += jnp.sum(grad_raw, axis=0, keepdims=True)
    sum_head_ref[1:2, :] += jnp.sum(grad_decay * decay_ref[...], axis=0, keepdims=True)

    sum_skip = jnp.sum(dy * x_conv, axis=0, keepdims=True)
    grad_pre = (grad_weighted * dt_ref[...] + skip * dy) * slope_x_ref[...]
    x_buffer[Q : Q + HALO, :] = x_buffer[0:HALO, :]
    x_buffer[0:Q, :] = grad_pre
    grad_proj, taps = conv_backward(
        x_buffer, window, seg, kernel_x_ref[...], x_ref[...], width
    )
    sum_bias = jnp.sum(grad_pre, axis=0, keepdims=True)
    blank = jnp.zeros((1, width), F32)
    sum_x_ref[...] += jnp.concatenate(
        [taps[3], taps[2], taps[1], taps[0], sum_bias, sum_gate, sum_skip, blank], axis=0
    )

    grad_pre_bc = jnp.concatenate([grad_b, grad_c], axis=1) * slope_bc_ref[...]
    bc_buffer[Q : Q + HALO, :] = bc_buffer[0:HALO, :]
    bc_buffer[0:Q, :] = grad_pre_bc
    grad_bc, taps_bc = conv_backward(
        bc_buffer, window, seg, kernel_bc_ref[...], bcdt_ref[:, : 2 * N], 2 * N
    )
    sum_bias_bc = jnp.sum(grad_pre_bc, axis=0, keepdims=True)
    blank_bc = jnp.zeros((3, 2 * N), F32)
    sum_bc_ref[...] += jnp.concatenate(
        [taps_bc[3], taps_bc[2], taps_bc[1], taps_bc[0], sum_bias_bc, blank_bc], axis=0
    )

    grads = jnp.concatenate(
        [grad_proj.astype(BF16), grad_z, grad_bc.astype(BF16), grad_raw.astype(BF16)], axis=1
    )
    proj_ref[...] = grads
    part = dot_nt(grads, weights_ref[:, width:])
    part_ref[...] = part.astype(BF16)
    hidden = hidden_ref[...].astype(F32)
    inverse = lax.rsqrt(jnp.mean(hidden * hidden, axis=1, keepdims=True) + EPS)
    sum_gain_ref[0:1, :] += jnp.sum(part * (hidden * inverse), axis=0, keepdims=True)


def pack_kernel(*refs):
    *parts, packed, sems = refs
    at = 0
    copies = []
    for index, part in enumerate(parts):
        columns = part.shape[1]
        copies.append(
            pltpu.make_async_copy(part, packed.at[:, pl.ds(at, columns)], sems.at[index])
        )
        at += columns
    for copy in copies:
        copy.start()
    for copy in copies:
        copy.wait()


def run_pack(*parts):
    rows = parts[0].shape[0]
    columns = sum(part.shape[1] for part in parts)
    return pl.pallas_call(
        pack_kernel,
        in_specs=[pl.BlockSpec(memory_space=pl.ANY)] * len(parts),
        out_specs=pl.BlockSpec(memory_space=pl.ANY),
        out_shape=jax.ShapeDtypeStruct((rows, columns), BF16),
        scratch_shapes=[pltpu.SemaphoreType.DMA((len(parts),))],
        compiler_params=pltpu.CompilerParams(vmem_limit_bytes=VMEM_LIMIT),
        name="pack",
    )(*parts)


def cost(micros):
    return pl.CostEstimate(flops=int(micros * 1e9), bytes_accessed=1 << 20, transcendentals=0)


def whole(shape):
    return pl.BlockSpec(shape, lambda i: (0,) * len(shape))


def scalar():
    return pl.BlockSpec(memory_space=pltpu.SMEM)


def run_project(heads, size, place, near, weights):
    features = near[0].shape[1]
    blocks = len(near) // 2 + 1
    length = blocks * Q
    width = heads * size
    rest = 2 * N + LANES

    def rows(columns):
        return pl.BlockSpec((Q, columns), lambda i: (i, 0))

    def made(columns, dtype):
        return jax.ShapeDtypeStruct((length, columns), dtype)

    return pl.pallas_call(
        functools.partial(project_kernel, heads, size, len(near)),
        grid=(blocks,),
        in_specs=[scalar(), *[whole(block.shape) for block in near], whole(weights.shape)],
        out_specs=[
            rows(features),
            rows(features),
            rows(width),
            rows(width),
            rows(rest),
            whole((8, features)),
        ],
        out_shape=[
            made(features, BF16),
            made(features, BF16),
            made(width, F32),
            made(width, F32),
            made(rest, F32),
            jax.ShapeDtypeStruct((8, features), F32),
        ],
        compiler_params=pltpu.CompilerParams(vmem_limit_bytes=VMEM_LIMIT),
        cost_estimate=cost(8),
        name="project",
    )(place, *near, weights)


def saved_rows(heads, size):
    width = heads * size
    return (
        [(heads * Q, BF16)] * 2
        + [(width, F32)] * 10
        + [(width, BF16)] * 2
        + [(2 * N, BF16), (2 * N, F32), (LANES, F32), (LANES, F32)]
    )


def saved_specs(heads, size, place):
    width = heads * size
    return [
        pl.BlockSpec((1, N, width), lambda i: (place(i), 0, 0)),
        pl.BlockSpec((1, 8, width), lambda i: (place(i), 0, 0)),
    ] + [
        pl.BlockSpec((Q, columns), lambda i: (place(i), 0))
        for columns, _ in saved_rows(heads, size)
    ]


def run_forward(
    heads, size, window, seg_row, weights, kernel_x, kernel_bc, head, channel, z_proj, x_proj, bcdt
):
    length, features = seg_row.shape[1], weights.shape[0]
    width = heads * size
    blocks = length // Q

    def rows(columns):
        return pl.BlockSpec((Q, columns), lambda i: (i, 0))

    def made(columns, dtype):
        return jax.ShapeDtypeStruct((length, columns), dtype)

    across = pl.BlockSpec((8, Q), lambda i: (0, i))
    return pl.pallas_call(
        functools.partial(forward_kernel, heads, size),
        grid=(blocks,),
        in_specs=[
            whole(window.shape),
            across,
            whole((features, width)),
            whole(kernel_x.shape),
            whole(kernel_bc.shape),
            whole(head.shape),
            whole(channel.shape),
            rows(width),
            rows(width),
            rows(bcdt.shape[1]),
        ],
        out_specs=[rows(width), rows(features), across, *saved_specs(heads, size, lambda i: i)],
        out_shape=[
            made(width, BF16),
            made(features, BF16),
            jax.ShapeDtypeStruct((8, length), F32),
            *[
                jax.ShapeDtypeStruct((blocks,) + shape, F32) for shape in ((N, width), (8, width))
            ],
            *[made(columns, dtype) for columns, dtype in saved_rows(heads, size)],
        ],
        scratch_shapes=[
            pltpu.VMEM((Q + HALO, width), F32),
            pltpu.VMEM((Q + HALO, 2 * N), F32),
            pltpu.VMEM((N, width), F32),
        ],
        compiler_params=pltpu.CompilerParams(vmem_limit_bytes=VMEM_LIMIT),
        cost_estimate=cost(14),
        name="forward",
    )(window, seg_row, weights, kernel_x, kernel_bc, head, channel, z_proj, x_proj, bcdt)


def run_gradient(cot, weights, scaled, window):
    length, features = cot.shape
    width = scaled.shape[1]
    return pl.pallas_call(
        functools.partial(gradient_kernel, width),
        grid=(length // Q,),
        in_specs=[
            pl.BlockSpec((Q, features), lambda i: (i, 0)),
            whole((features, width)),
            pl.BlockSpec((Q, width), lambda i: (i, 0)),
            whole(window.shape),
        ],
        out_specs=[
            pl.BlockSpec((Q, width), lambda i: (i, 0)),
            pl.BlockSpec((8, Q), lambda i: (0, i)),
        ],
        out_shape=[
            jax.ShapeDtypeStruct((length, width), F32),
            jax.ShapeDtypeStruct((8, length), F32),
        ],
        compiler_params=pltpu.CompilerParams(vmem_limit_bytes=VMEM_LIMIT),
        cost_estimate=cost(5),
        name="out_gradient",
    )(cot, weights, scaled, window)


def weights_kernel(width, cot_ref, normed_ref, tokens_ref, grads_ref, first_ref, second_ref):
    tokens = tokens_ref[...]
    first_ref[:, :width] = dot_tn(cot_ref[...], normed_ref[...]).astype(BF16)
    first_ref[:, width:] = dot_tn(tokens, grads_ref[:, 2 * width :]).astype(BF16)
    second_ref[...] = dot_tn(tokens, grads_ref[:, : 2 * width]).astype(BF16)


def run_weights(cot, normed, tokens, grads):
    length, features = tokens.shape
    width = normed.shape[1]
    columns = [grads.shape[1] - width, 2 * width]
    return pl.pallas_call(
        functools.partial(weights_kernel, width),
        grid=(features // Q,),
        in_specs=[
            pl.BlockSpec((length, Q), lambda i: (0, i)),
            whole(normed.shape),
            pl.BlockSpec((length, Q), lambda i: (0, i)),
            whole(grads.shape),
        ],
        out_specs=[pl.BlockSpec((Q, count), lambda i: (i, 0)) for count in columns],
        out_shape=[jax.ShapeDtypeStruct((features, count), BF16) for count in columns],
        compiler_params=pltpu.CompilerParams(vmem_limit_bytes=VMEM_LIMIT),
        cost_estimate=cost(7),
        name="weight_gradients",
    )(cot, normed, tokens, grads)


def run_backward(
    heads, size, full_inner, stat, hidden, window, weights, kernel_x, kernel_bc, head, channel,
    x_proj, bcdt, grad_out, saved,
):
    length, features = hidden.shape
    width = heads * size
    blocks = length // Q
    rest = 2 * N + LANES
    total = 2 * width + rest

    def rows(columns):
        return pl.BlockSpec((Q, columns), lambda i: (blocks - 1 - i, 0))

    def made(columns, dtype):
        return jax.ShapeDtypeStruct((length, columns), dtype)

    across = pl.BlockSpec((8, Q), lambda i: (0, blocks - 1 - i))
    sums = [(8, width), (8, 2 * N), (8, LANES), (8, features)]
    return pl.pallas_call(
        functools.partial(backward_kernel, heads, size, full_inner),
        grid=(blocks,),
        in_specs=[
            across,
            rows(features),
            whole(window.shape),
            whole(weights.shape),
            whole(kernel_x.shape),
            whole(kernel_bc.shape),
            whole(head.shape),
            whole(channel.shape),
            rows(width),
            rows(rest),
            rows(width),
            *saved_specs(heads, size, lambda i: blocks - 1 - i),
        ],
        out_specs=[rows(total), rows(features), rows(width)] + [whole(shape) for shape in sums],
        out_shape=[made(total, BF16), made(features, BF16), made(width, BF16)]
        + [jax.ShapeDtypeStruct(shape, F32) for shape in sums],
        scratch_shapes=[
            pltpu.VMEM((Q + HALO, width), F32),
            pltpu.VMEM((Q + HALO, 2 * N), F32),
            pltpu.VMEM((N, width), F32),
            pltpu.VMEM((8, LANES), F32),
        ],
        compiler_params=pltpu.CompilerParams(vmem_limit_bytes=VMEM_LIMIT),
        cost_estimate=cost(2),
        name="backward",
    )(
        stat, hidden, window, weights, kernel_x, kernel_bc, head, channel, x_proj, bcdt, grad_out,
        *saved,
    )


def finish_kernel(sum_ref, hidden_ref, cot_ref, gain_ref, out_ref):
    grad = sum_ref[...].astype(F32) * gain_ref[0:1, :]
    hidden = hidden_ref[...].astype(F32)
    inverse = lax.rsqrt(jnp.mean(hidden * hidden, axis=1, keepdims=True) + EPS)
    unit = hidden * inverse
    along = jnp.mean(grad * unit, axis=1, keepdims=True)
    out_ref[...] = (cot_ref[...].astype(F32) + inverse * (grad - unit * along)).astype(BF16)


def run_finish(in_sum, hidden, cot, gain):
    length, features = hidden.shape
    rows = pl.BlockSpec((length // 2, features), lambda i: (i, 0))
    return pl.pallas_call(
        finish_kernel,
        grid=(2,),
        in_specs=[rows, rows, rows, whole(gain.shape)],
        out_specs=rows,
        out_shape=jax.ShapeDtypeStruct(hidden.shape, BF16),
        compiler_params=pltpu.CompilerParams(vmem_limit_bytes=VMEM_LIMIT),
        name="finish",
    )(in_sum, hidden, cot, gain)


def pad_lanes(values):
    return jnp.pad(values, ((0, 0), (0, LANES - values.shape[1])))


def after(value, *others):
    return lax.optimization_barrier((value, *others))[0]


def line_step(right, left, step, axis):
    n = lax.axis_size(axis)
    return (
        lax.ppermute(right, axis, [(i, i + 1) for i in range(step - 1, n - 1)]),
        lax.ppermute(left, axis, [(i, i - 1) for i in range(1, n - step + 1)]),
    )


def line_order(block, moved):
    return [pair[0] for pair in moved[::-1]] + [block] + [pair[1] for pair in moved]


def line_gather(block, axis):
    right = left = block
    moved = []
    for step in range(1, lax.axis_size(axis)):
        right, left = line_step(right, left, step, axis)
        moved.append((right, left))
    return line_order(block, moved)


def cube_scatter(first, second, small, axis):
    n = lax.axis_size(axis)
    if n & (n - 1):
        sums = [
            lax.psum_scatter(part, axis, scatter_dimension=0, tiled=True).astype(F32)
            for part in (first, second)
        ]
        return (*sums, lax.psum(small, axis), sums)
    place = lax.axis_index(axis)
    bits = list(range(n.bit_length() - 1))
    orders = [bits, bits[:1] + bits[:0:-1]]
    parts = [part.reshape((2,) * len(bits) + (-1, part.shape[1])) for part in (first, second)]
    left = [bits[::-1], bits[::-1]]
    came = []
    for step in range(len(bits)):
        for index in range(2):
            part = parts[index]
            bit = orders[index][step]
            dim = left[index].index(bit)
            mine = (place >> bit) & 1
            keep = lax.dynamic_index_in_dim(part, mine, dim, keepdims=False)
            send = lax.dynamic_index_in_dim(part, 1 - mine, dim, keepdims=False)
            pairs = [(i, i ^ (1 << bit)) for i in range(n)]
            if index == 0:
                columns = part.shape[-1]
                rows = send.size // columns
                extra = -(-small.size // (16 * columns)) * 16
                small = lax.reduce_precision(small, 8, 7)
                rider = jnp.pad(
                    small.astype(BF16).reshape(-1), (0, extra * columns - small.size)
                ).reshape(extra, columns)
                moved = lax.ppermute(
                    jnp.concatenate([send.reshape(rows, columns), rider]), axis, pairs
                )
                other = moved[:rows].reshape(send.shape)
                rider = moved[rows:].reshape(-1)[: small.size].reshape(small.shape)
                small = small + rider.astype(F32)
            else:
                moved = other = lax.ppermute(send, axis, pairs)
            came.append(moved)
            part = keep.astype(F32) + other.astype(F32)
            left[index] = [other_bit for other_bit in left[index] if other_bit != bit]
            parts[index] = part.astype(BF16) if left[index] else part
    return (*parts, small, came)


def around(values, axis):
    n = lax.axis_size(axis)
    return [values] + [
        lax.ppermute(values, axis, [(i, (i - k) % n) for i in range(n)]) for k in range(1, n)
    ]


def sum_around(values, axis):
    return functools.reduce(jnp.add, around(values, axis))


def sum_around_low(values, axis):
    low = around(lax.reduce_precision(values, 8, 7).astype(BF16), axis)
    return functools.reduce(jnp.add, [share.astype(F32) for share in low])


def shards(
    hidden,
    seg_ids,
    cotangent,
    norm_gain,
    w_in_z,
    w_in_x,
    w_in_bc,
    w_in_dt,
    conv_x,
    conv_x_bias,
    conv_bc,
    conv_bc_bias,
    dt_bias,
    a_log,
    d_skip,
    gate_gain,
    w_out,
):
    heads = dt_bias.shape[0]
    width = gate_gain.shape[0]
    size = width // heads
    full_inner = width * lax.axis_size("tensor")
    features = hidden.shape[2]
    hidden_local = hidden[0]

    steps = jnp.pad(
        jnp.concatenate([w_in_dt, norm_gain[:, None]], axis=1), ((0, 0), (0, LANES - heads - 1))
    )
    packed = run_pack(w_out, w_in_x, w_in_z, w_in_bc, steps)
    n = lax.axis_size("tensor")
    axis_place = lax.axis_index("tensor")
    place = axis_place[None]
    near_hidden = line_gather(hidden_local, "tensor")
    weights = lax.all_gather(packed, "dp", axis=0, tiled=True)
    seg_stack = around(seg_ids[0], "tensor")
    count = seg_ids.shape[1]
    seg_full = lax.dynamic_slice_in_dim(
        jnp.concatenate(seg_stack + seg_stack), (n - axis_place) * count, n * count, 0
    )
    window = jnp.broadcast_to(
        jnp.pad(seg_full, (HALO, HALO), constant_values=-1)[:, None],
        (seg_full.shape[0] + 2 * HALO, LANES),
    )
    seg_row = jnp.broadcast_to(seg_full[None, :], (8, seg_full.shape[0]))
    kernel_x = jnp.concatenate([conv_x, conv_x_bias[None, :]], axis=0)
    kernel_bc = jnp.concatenate([conv_bc, conv_bc_bias[None, :]], axis=0)
    head = pad_lanes(jnp.stack([dt_bias, a_log]))
    channel = jnp.stack([gate_gain, jnp.repeat(d_skip, size)])

    hidden_full, tokens, z_proj, x_proj, bcdt, gain = run_project(
        heads, size, place, near_hidden, weights
    )
    cot_full = lax.all_gather(
        after(cotangent[0], near_hidden[0], near_hidden[-1]), "tensor", axis=0, tiled=True
    )
    scaled, out_part, square, *saved = run_forward(
        heads, size, window, seg_row, weights, kernel_x, kernel_bc, head, channel, z_proj, x_proj,
        bcdt,
    )
    grad_out, along = run_gradient(cot_full, weights, scaled, window)
    out_sum = lax.psum_scatter(
        out_part, "tensor", scatter_dimension=0, tiled=True
    )
    stat = sum_around(jnp.stack([square[0], along[0]]), "tensor")
    stat_full = jnp.pad(stat, ((0, 6), (0, 0)))
    out_scale = lax.rsqrt(stat[0] / full_inner + EPS) * (seg_full > 0).astype(F32)

    grads, in_part, normed_out, sum_x, sum_bc, sum_head, sum_gain = run_backward(
        heads, size, full_inner, stat_full, hidden_full, window, weights, kernel_x, kernel_bc, head,
        channel, x_proj, bcdt, grad_out, saved,
    )
    in_sum = lax.psum_scatter(in_part, "tensor", scatter_dimension=0, tiled=True)
    first, second = run_weights(cot_full, normed_out, tokens, grads)
    own = jnp.concatenate([sum_x.reshape(-1, LANES), sum_head])
    both = jnp.concatenate([sum_gain[0].reshape(-1, LANES), sum_bc.reshape(-1, LANES)])
    first, second, small, came = cube_scatter(first, second, jnp.concatenate([own, both]), "dp")
    sum_x = small[: own.shape[0] - 8].reshape(8, width)
    sum_head = small[own.shape[0] - 8 : own.shape[0]]
    grad_bc = first[:, width : width + 2 * N]
    shared = jnp.concatenate([small[own.shape[0] :], grad_bc.reshape(-1, LANES)])
    shared = sum_around_low(shared, "tensor")
    gain_rows = features // LANES
    sum_gain = shared[:gain_rows].reshape(features)
    sum_bc = shared[gain_rows : both.shape[0]].reshape(8, 2 * N)
    grad_bc = shared[both.shape[0] :].reshape(grad_bc.shape)
    local_features = norm_gain.shape[0]
    grad_norm_gain = lax.dynamic_slice_in_dim(
        sum_gain, lax.axis_index("dp") * local_features, local_features, 0
    )

    local = hidden_local.shape[0]
    hidden_rows = hidden_local.astype(F32)
    scale_here = lax.dynamic_slice_in_dim(out_scale, axis_place * local, local, 0)[:, None]
    layer_out = (hidden_rows + out_sum.astype(F32) * scale_here).astype(BF16)

    grad_hidden = run_finish(in_sum, hidden_local, cotangent[0], after(gain, shared))

    return (
        layer_out[None],
        grad_hidden[None],
        grad_norm_gain,
        second[:, width:],
        second[:, :width],
        grad_bc,
        first[:, width + 2 * N : width + 2 * N + heads],
        sum_x[0:CONV],
        sum_x[CONV],
        sum_bc[0:CONV],
        sum_bc[CONV],
        sum_head[0, :heads],
        sum_head[1, :heads],
        jnp.sum(sum_x[CONV + 2].reshape(heads, size), axis=1),
        sum_x[CONV + 1],
        first[:, :width],
    )


def solution(mesh):
    in_specs = (
        P("dp", "tensor", None),
        P("dp", "tensor"),
        P("dp", "tensor", None),
        P("dp"),
        P("dp", "tensor"),
        P("dp", "tensor"),
        P("dp", None),
        P("dp", "tensor"),
        P(None, "tensor"),
        P("tensor"),
        P(),
        P(),
        P("tensor"),
        P("tensor"),
        P("tensor"),
        P("tensor"),
        P("dp", "tensor"),
    )
    out_specs = (
        P("dp", "tensor", None),
        P("dp", "tensor", None),
        P("dp"),
        P("dp", "tensor"),
        P("dp", "tensor"),
        P("dp", None),
        P("dp", "tensor"),
        P(None, "tensor"),
        P("tensor"),
        P(),
        P(),
        P("tensor"),
        P("tensor"),
        P("tensor"),
        P("tensor"),
        P("dp", "tensor"),
    )
    return jax.shard_map(shards, mesh=mesh, in_specs=in_specs, out_specs=out_specs, check_vma=False)
```

```python
import functools

import jax
import jax.numpy as jnp
from jax import lax
from jax.experimental import pallas as pl
from jax.experimental.pallas import tpu as pltpu
from jax.sharding import PartitionSpec as P

N = 128
CONV = 4
Q = 256
LANES = 128
HALO = 8
EPS = 1e-05
NEG = -1e30
F32 = jnp.float32
BF16 = jnp.bfloat16
VMEM_LIMIT = 52 * 1024 * 1024


def dot(a, b):
    return jnp.dot(a, b, preferred_element_type=F32)


def dot_nt(a, b):
    return lax.dot_general(a, b, (((1,), (1,)), ((), ())), preferred_element_type=F32)


def dot_tn(a, b):
    return lax.dot_general(a, b, (((0,), (0,)), ((), ())), preferred_element_type=F32)


def dot_exact(a, b):
    return jnp.dot(a, b, preferred_element_type=F32, precision=lax.Precision.HIGHEST)


def spread(cols, heads, size):
    rows = cols.shape[0]
    per = LANES // size
    lane = lax.broadcasted_iota(jnp.int32, (rows, LANES), 1)
    parts = []
    for first in range(0, heads, per):
        part = jnp.broadcast_to(cols[:, first : first + 1], (rows, LANES))
        for extra in range(1, per):
            part = jnp.where(lane < extra * size, part, cols[:, first + extra : first + extra + 1])
        parts.append(part)
    return jnp.concatenate(parts, axis=1)


def head_sums(values, heads, size):
    width = heads * size
    channel = lax.broadcasted_iota(jnp.int32, (width, LANES), 0)
    column = lax.broadcasted_iota(jnp.int32, (width, LANES), 1)
    first = column * size
    picks = jnp.where((channel >= first) & (channel < first + size), 1.0, 0.0).astype(BF16)
    high = values.astype(BF16)
    low = (values - high.astype(F32)).astype(BF16)
    return dot(high, picks) + dot(low, picks)


def widen(tile, width):
    return jnp.concatenate([tile] * (width // tile.shape[1]), axis=1)


def softplus(v):
    return jnp.maximum(v, 0.0) + jnp.log1p(jnp.exp(-jnp.abs(v)))


def sigmoid(v):
    return 1.0 / (1.0 + jnp.exp(-v))


def as_row(column):
    rows = column.shape[0]
    return jnp.broadcast_to(column, (rows, LANES)).T[:8]


def triangle(lower):
    row = lax.broadcasted_iota(jnp.int32, (Q, Q), 0)
    col = lax.broadcasted_iota(jnp.int32, (Q, Q), 1)
    return row >= col if lower else row <= col


def block_masks(window, seg_row):
    seg = window[HALO : HALO + Q]
    before = window[HALO - 1 : HALO]
    last = window[HALO + Q - 1 : HALO + Q]
    from_prev = (seg == before).astype(F32)
    same_last = (seg == last).astype(F32)
    passes = (last == before).astype(F32)
    keep = (widen(seg, Q) == seg_row) & triangle(True)
    bias = jnp.where(keep, 0.0, NEG)
    return seg, from_prev, same_last, passes, bias


def conv_forward(buffer, window, seg, kernel, conv_bias, width):
    total = conv_bias + kernel[CONV - 1 : CONV] * buffer[HALO : HALO + Q, :]
    for back in range(1, CONV):
        match = (window[HALO - back : HALO - back + Q] == seg).astype(F32)
        tap = kernel[CONV - 1 - back : CONV - back]
        total = total + tap * (buffer[HALO - back : HALO - back + Q, :] * widen(match, width))
    return total


def conv_backward(buffer, window, seg, kernel, values, width):
    here = buffer[0:Q, :]
    total = kernel[CONV - 1 : CONV] * here
    taps = [jnp.sum(values * here, axis=0, keepdims=True)]
    for ahead in range(1, CONV):
        match = (window[HALO + ahead : HALO + ahead + Q] == seg).astype(F32)
        moved = buffer[ahead : ahead + Q, :] * widen(match, width)
        total = total + kernel[CONV - 1 - ahead : CONV - ahead] * moved
        taps.append(jnp.sum(values * moved, axis=0, keepdims=True))
    return total, taps


def pick_block(place, near_refs, block):
    reach = len(near_refs) // 2
    away = pl.program_id(0) - place
    for index, ref in enumerate(near_refs):

        @pl.when(away == index - reach)
        def _():
            block[...] = ref[...]


def project_kernel(heads, size, near, place_ref, *refs):
    near_refs, refs = refs[:near], refs[near:]
    weights_ref, hidden_ref, tokens_ref, z_ref, x_ref, bcdt_ref, gain_ref = refs
    width = heads * size

    @pl.when(pl.program_id(0) == 0)
    def _():
        tail_columns = weights_ref[:, 3 * width + 2 * N :].astype(F32).T
        gain_ref[...] = jnp.broadcast_to(tail_columns[heads : heads + 1], gain_ref.shape)

    pick_block(place_ref[0], near_refs, hidden_ref)
    hidden = hidden_ref[...].astype(F32)
    inverse = lax.rsqrt(jnp.mean(hidden * hidden, axis=1, keepdims=True) + EPS)
    tokens = (hidden * inverse * gain_ref[0:1, :]).astype(BF16)
    tokens_ref[...] = tokens
    x_ref[...] = dot(tokens, weights_ref[:, width : 2 * width])
    z_ref[...] = dot(tokens, weights_ref[:, 2 * width : 3 * width])
    bcdt_ref[...] = dot(tokens, weights_ref[:, 3 * width :])


def forward_kernel(
    heads,
    size,
    window_ref,
    seg_row_ref,
    weights_ref,
    kernel_x_ref,
    kernel_bc_ref,
    head_ref,
    channel_ref,
    z_ref,
    x_ref,
    bcdt_ref,
    scaled_ref,
    part_ref,
    square_ref,
    state_ref,
    survive_ref,
    shape_ref,
    prob_ref,
    gated_ref,
    opened_ref,
    slope_z_ref,
    inner_ref,
    carried_ref,
    x_conv_ref,
    slope_x_ref,
    dt_ref,
    from_start_ref,
    to_end_ref,
    weighted_ref,
    weighted_end_ref,
    bc_ref,
    slope_bc_ref,
    decay_ref,
    slope_dt_ref,
    x_buffer,
    bc_buffer,
    carry,
):
    step = pl.program_id(0)
    width = heads * size

    @pl.when(step == 0)
    def _():
        x_buffer[0:HALO, :] = jnp.zeros((HALO, width), F32)
        bc_buffer[0:HALO, :] = jnp.zeros((HALO, 2 * N), F32)
        carry[...] = jnp.zeros((N, width), F32)

    window = window_ref[pl.ds(pl.multiple_of(step * Q, Q), Q + 2 * HALO), :]
    seg, from_prev, same_last, passes, bias = block_masks(window, seg_row_ref[0:1, :])
    bcdt = bcdt_ref[...]
    x_buffer[HALO : HALO + Q, :] = x_ref[...]
    bc_buffer[HALO : HALO + Q, :] = bcdt[:, : 2 * N]
    pre = conv_forward(
        x_buffer, window, seg, kernel_x_ref[...], kernel_x_ref[CONV : CONV + 1, :], width
    )
    pre_bc = conv_forward(
        bc_buffer, window, seg, kernel_bc_ref[...], kernel_bc_ref[CONV : CONV + 1, :], 2 * N
    )
    x_buffer[0:HALO, :] = x_buffer[Q : Q + HALO, :]
    bc_buffer[0:HALO, :] = bc_buffer[Q : Q + HALO, :]
    gate_x = sigmoid(pre)
    x_conv = pre * gate_x
    x_conv_ref[...] = x_conv
    slope_x_ref[...] = gate_x * (1.0 + pre * (1.0 - gate_x))
    gate_bc = sigmoid(pre_bc)
    bc_conv = (pre_bc * gate_bc).astype(BF16)
    bc_ref[...] = bc_conv
    slope_bc_ref[...] = gate_bc * (1.0 + pre_bc * (1.0 - gate_bc))
    b_in = bc_conv[:, :N]
    c_in = bc_conv[:, N:]

    raw = bcdt[:, 2 * N :] + head_ref[0:1, :]
    slope_dt_ref[...] = sigmoid(raw)
    dt = softplus(raw)
    decay = -dt * jnp.exp(head_ref[1:2, :])
    decay_ref[...] = decay
    total = dot_exact(triangle(True).astype(F32), decay)
    total_t = total.T
    dt_wide = spread(dt, heads, size)
    dt_ref[...] = dt_wide
    weighted = x_conv * dt_wide
    weighted_low = weighted.astype(BF16)
    weighted_ref[...] = weighted_low
    scores = dot_nt(c_in, b_in)
    before = carry[...]
    state_ref[0] = before

    per = LANES // size
    lane = lax.broadcasted_iota(jnp.int32, (Q, LANES), 1)
    none = jnp.zeros((Q, LANES), BF16)
    inner = []
    for first in range(0, heads, per):
        group = weighted_low[:, first * size : first * size + LANES]
        summed = jnp.zeros((Q, LANES), F32)
        for extra in range(per):
            h = first + extra
            shape = jnp.exp(total[:, h : h + 1] - total_t[h : h + 1, :] + bias)
            prob = (scores * shape).astype(BF16)
            shape_ref[:, h * Q : (h + 1) * Q] = shape.astype(BF16)
            prob_ref[:, h * Q : (h + 1) * Q] = prob
            mine = (lane >= extra * size) & (lane < (extra + 1) * size)
            summed = summed + dot(prob, jnp.where(mine, group, none))
        inner.append(summed)
    inner = jnp.concatenate(inner, axis=1)
    inner_ref[...] = inner
    carried = dot(c_in, before.astype(BF16))
    carried_ref[...] = carried
    from_start = spread(jnp.exp(total) * from_prev, heads, size)
    from_start_ref[...] = from_start
    last = total[Q - 1 : Q, :]
    to_end = spread(jnp.exp(last - total) * same_last, heads, size)
    to_end_ref[...] = to_end
    weighted_end = (weighted * to_end).astype(BF16)
    weighted_end_ref[...] = weighted_end
    survive = spread(jnp.exp(last) * passes, heads, size)
    survive_ref[0] = jnp.broadcast_to(survive, (8, width))
    carry[...] = dot_tn(b_in, weighted_end) + before * survive

    mixed = inner + carried * from_start + channel_ref[1:2, :] * x_conv
    z_proj = z_ref[...]
    gate = sigmoid(z_proj)
    opened = z_proj * gate
    opened_ref[...] = opened
    slope_z_ref[...] = mixed * (gate * (1.0 + z_proj * (1.0 - gate)))
    gated = mixed * opened
    gated_ref[...] = gated
    scaled = (gated * channel_ref[0:1, :]).astype(BF16)
    scaled_ref[...] = scaled
    part_ref[...] = dot_nt(scaled, weights_ref[...]).astype(BF16)
    square_ref[...] = as_row(jnp.sum(gated * gated, axis=1, keepdims=True))


def gradient_kernel(width, cot_ref, weights_ref, scaled_ref, window_ref, grad_ref, along_ref):
    step = pl.program_id(0)
    window = window_ref[pl.ds(pl.multiple_of(step * Q, Q), Q + 2 * HALO), :]
    live = (window[HALO : HALO + Q] > 0).astype(F32)
    grad = dot(cot_ref[...], weights_ref[...]) * widen(live, width)
    grad_ref[...] = grad
    along_ref[...] = as_row(jnp.sum(scaled_ref[...].astype(F32) * grad, axis=1, keepdims=True))


def backward_kernel(
    heads,
    size,
    full_inner,
    stat_ref,
    hidden_ref,
    window_ref,
    weights_ref,
    kernel_x_ref,
    kernel_bc_ref,
    head_ref,
    channel_ref,
    x_ref,
    bcdt_ref,
    grad_ref,
    state_ref,
    survive_ref,
    shape_ref,
    prob_ref,
    gated_ref,
    opened_ref,
    slope_z_ref,
    inner_ref,
    carried_ref,
    x_conv_ref,
    slope_x_ref,
    dt_ref,
    from_start_ref,
    to_end_ref,
    weighted_ref,
    weighted_end_ref,
    bc_ref,
    slope_bc_ref,
    decay_ref,
    slope_dt_ref,
    proj_ref,
    part_ref,
    out_ref,
    sum_x_ref,
    sum_bc_ref,
    sum_head_ref,
    sum_gain_ref,
    x_buffer,
    bc_buffer,
    carry,
    tail,
):
    turn = pl.program_id(0)
    step = pl.num_programs(0) - 1 - turn
    width = heads * size

    @pl.when(turn == 0)
    def _():
        x_buffer[...] = jnp.zeros((Q + HALO, width), F32)
        bc_buffer[...] = jnp.zeros((Q + HALO, 2 * N), F32)
        carry[...] = jnp.zeros((N, width), F32)
        tail[...] = jnp.zeros((8, LANES), F32)
        sum_x_ref[...] = jnp.zeros((8, width), F32)
        sum_bc_ref[...] = jnp.zeros((8, 2 * N), F32)
        sum_head_ref[...] = jnp.zeros((8, LANES), F32)
        sum_gain_ref[...] = jnp.zeros(sum_gain_ref.shape, F32)

    window = window_ref[pl.ds(pl.multiple_of(step * Q, Q), Q + 2 * HALO), :]
    seg = window[HALO : HALO + Q]
    live = (seg[:, 0:1] > 0).astype(F32)
    stat = stat_ref[...].T
    gate_inverse = lax.rsqrt(stat[:, 0:1] / full_inner + EPS)
    along = stat[:, 1:2] * (gate_inverse * gate_inverse * gate_inverse / full_inner)

    gain = channel_ref[0:1, :]
    skip = channel_ref[1:2, :]
    grad_out = grad_ref[...]
    gated = gated_ref[...]
    normal = gated * gate_inverse
    sum_gate = jnp.sum(grad_out * normal, axis=0, keepdims=True)
    out_ref[...] = (normal * gain * live).astype(BF16)
    grad_gated = grad_out * gain * gate_inverse - gated * along
    grad_z = (grad_gated * slope_z_ref[...]).astype(BF16)
    dy = grad_gated * opened_ref[...]
    dy_low = dy.astype(BF16)
    dy_start = (dy * from_start_ref[...]).astype(BF16)

    bc_conv = bc_ref[...]
    b_in = bc_conv[:, :N]
    c_in = bc_conv[:, N:]
    before = state_ref[0]
    before_low = before.astype(BF16)
    after_low = carry[...].astype(BF16)
    weighted_low = weighted_ref[...]
    weighted_end = weighted_end_ref[...]
    grad_c = dot_nt(dy_start, before_low)
    returned = dot(b_in, after_low)
    grad_b = dot_nt(weighted_end, after_low)
    new_after = dot_tn(c_in, dy_start) + carry[...] * survive_ref[0, 0:1, :]
    carry[...] = new_after

    per = LANES // size
    lane = lax.broadcasted_iota(jnp.int32, (Q, LANES), 1)
    grad_scores = jnp.zeros((Q, Q), F32)
    inner = []
    none = jnp.zeros((Q, LANES), BF16)
    for first in range(0, heads, per):
        at = first * size
        dy_group = dy_low[:, at : at + LANES]
        weighted_group = weighted_low[:, at : at + LANES]
        summed = jnp.zeros((Q, LANES), F32)
        for extra in range(per):
            h = first + extra
            mine = (lane >= extra * size) & (lane < (extra + 1) * size)
            dy_mine = jnp.where(mine, dy_group, none)
            shape = shape_ref[:, h * Q : (h + 1) * Q].astype(F32)
            grad_scores = grad_scores + dot_nt(dy_mine, weighted_group) * shape
            summed = summed + dot_tn(prob_ref[:, h * Q : (h + 1) * Q], dy_mine)
        inner.append(summed)
    grad_inner = jnp.concatenate(inner, axis=1)
    grad_weighted = to_end_ref[...] * returned + grad_inner
    grad_scores = grad_scores.astype(BF16)
    grad_c = grad_c + dot(grad_scores, b_in)
    grad_b = grad_b + dot_tn(grad_scores, c_in)

    x_conv = x_conv_ref[...]
    pairs = head_sums(
        dy_low.astype(F32) * inner_ref[...]
        + dy_start.astype(F32) * carried_ref[...]
        - weighted_low.astype(F32) * grad_inner
        - weighted_end.astype(F32) * returned,
        heads,
        size,
    )
    grad_decay = dot_exact(triangle(False).astype(F32), pairs) + tail[0:1, :]
    kept = jnp.sum(new_after.astype(BF16).astype(F32) * before, axis=0, keepdims=True)
    tail[...] = head_sums(jnp.broadcast_to(kept, (8, width)), heads, size)
    rate = jnp.exp(head_ref[1:2, :])
    grad_dt = head_sums(grad_weighted * x_conv, heads, size) - grad_decay * rate
    grad_raw = grad_dt * slope_dt_ref[...]
    sum_head_ref[0:1, :] += jnp.sum(grad_raw, axis=0, keepdims=True)
    sum_head_ref[1:2, :] += jnp.sum(grad_decay * decay_ref[...], axis=0, keepdims=True)

    sum_skip = jnp.sum(dy * x_conv, axis=0, keepdims=True)
    grad_pre = (grad_weighted * dt_ref[...] + skip * dy) * slope_x_ref[...]
    x_buffer[Q : Q + HALO, :] = x_buffer[0:HALO, :]
    x_buffer[0:Q, :] = grad_pre
    grad_proj, taps = conv_backward(
        x_buffer, window, seg, kernel_x_ref[...], x_ref[...], width
    )
    sum_bias = jnp.sum(grad_pre, axis=0, keepdims=True)
    blank = jnp.zeros((1, width), F32)
    sum_x_ref[...] += jnp.concatenate(
        [taps[3], taps[2], taps[1], taps[0], sum_bias, sum_gate, sum_skip, blank], axis=0
    )

    grad_pre_bc = jnp.concatenate([grad_b, grad_c], axis=1) * slope_bc_ref[...]
    bc_buffer[Q : Q + HALO, :] = bc_buffer[0:HALO, :]
    bc_buffer[0:Q, :] = grad_pre_bc
    grad_bc, taps_bc = conv_backward(
        bc_buffer, window, seg, kernel_bc_ref[...], bcdt_ref[:, : 2 * N], 2 * N
    )
    sum_bias_bc = jnp.sum(grad_pre_bc, axis=0, keepdims=True)
    blank_bc = jnp.zeros((3, 2 * N), F32)
    sum_bc_ref[...] += jnp.concatenate(
        [taps_bc[3], taps_bc[2], taps_bc[1], taps_bc[0], sum_bias_bc, blank_bc], axis=0
    )

    grads = jnp.concatenate(
        [grad_proj.astype(BF16), grad_z, grad_bc.astype(BF16), grad_raw.astype(BF16)], axis=1
    )
    proj_ref[...] = grads
    part = dot_nt(grads, weights_ref[:, width:])
    part_ref[...] = part.astype(BF16)
    hidden = hidden_ref[...].astype(F32)
    inverse = lax.rsqrt(jnp.mean(hidden * hidden, axis=1, keepdims=True) + EPS)
    sum_gain_ref[0:1, :] += jnp.sum(part * (hidden * inverse), axis=0, keepdims=True)


def pack_kernel(*refs):
    *parts, packed, sems = refs
    at = 0
    copies = []
    for index, part in enumerate(parts):
        columns = part.shape[1]
        copies.append(
            pltpu.make_async_copy(part, packed.at[:, pl.ds(at, columns)], sems.at[index])
        )
        at += columns
    for copy in copies:
        copy.start()
    for copy in copies:
        copy.wait()


def run_pack(*parts):
    rows = parts[0].shape[0]
    columns = sum(part.shape[1] for part in parts)
    return pl.pallas_call(
        pack_kernel,
        in_specs=[pl.BlockSpec(memory_space=pl.ANY)] * len(parts),
        out_specs=pl.BlockSpec(memory_space=pl.ANY),
        out_shape=jax.ShapeDtypeStruct((rows, columns), BF16),
        scratch_shapes=[pltpu.SemaphoreType.DMA((len(parts),))],
        compiler_params=pltpu.CompilerParams(vmem_limit_bytes=VMEM_LIMIT),
        name="pack",
    )(*parts)


def cost(micros):
    return pl.CostEstimate(flops=int(micros * 1e9), bytes_accessed=1 << 20, transcendentals=0)


def whole(shape):
    return pl.BlockSpec(shape, lambda i: (0,) * len(shape))


def scalar():
    return pl.BlockSpec(memory_space=pltpu.SMEM)


def run_project(heads, size, place, near, weights):
    features = near[0].shape[1]
    blocks = len(near) // 2 + 1
    length = blocks * Q
    width = heads * size
    rest = 2 * N + LANES

    def rows(columns):
        return pl.BlockSpec((Q, columns), lambda i: (i, 0))

    def made(columns, dtype):
        return jax.ShapeDtypeStruct((length, columns), dtype)

    return pl.pallas_call(
        functools.partial(project_kernel, heads, size, len(near)),
        grid=(blocks,),
        in_specs=[scalar(), *[whole(block.shape) for block in near], whole(weights.shape)],
        out_specs=[
            rows(features),
            rows(features),
            rows(width),
            rows(width),
            rows(rest),
            whole((8, features)),
        ],
        out_shape=[
            made(features, BF16),
            made(features, BF16),
            made(width, F32),
            made(width, F32),
            made(rest, F32),
            jax.ShapeDtypeStruct((8, features), F32),
        ],
        compiler_params=pltpu.CompilerParams(vmem_limit_bytes=VMEM_LIMIT),
        cost_estimate=cost(8),
        name="project",
    )(place, *near, weights)


def saved_rows(heads, size):
    width = heads * size
    return (
        [(heads * Q, BF16)] * 2
        + [(width, F32)] * 10
        + [(width, BF16)] * 2
        + [(2 * N, BF16), (2 * N, F32), (LANES, F32), (LANES, F32)]
    )


def saved_specs(heads, size, place):
    width = heads * size
    return [
        pl.BlockSpec((1, N, width), lambda i: (place(i), 0, 0)),
        pl.BlockSpec((1, 8, width), lambda i: (place(i), 0, 0)),
    ] + [
        pl.BlockSpec((Q, columns), lambda i: (place(i), 0))
        for columns, _ in saved_rows(heads, size)
    ]


def run_forward(
    heads, size, window, seg_row, weights, kernel_x, kernel_bc, head, channel, z_proj, x_proj, bcdt
):
    length, features = seg_row.shape[1], weights.shape[0]
    width = heads * size
    blocks = length // Q

    def rows(columns):
        return pl.BlockSpec((Q, columns), lambda i: (i, 0))

    def made(columns, dtype):
        return jax.ShapeDtypeStruct((length, columns), dtype)

    across = pl.BlockSpec((8, Q), lambda i: (0, i))
    return pl.pallas_call(
        functools.partial(forward_kernel, heads, size),
        grid=(blocks,),
        in_specs=[
            whole(window.shape),
            across,
            whole((features, width)),
            whole(kernel_x.shape),
            whole(kernel_bc.shape),
            whole(head.shape),
            whole(channel.shape),
            rows(width),
            rows(width),
            rows(bcdt.shape[1]),
        ],
        out_specs=[rows(width), rows(features), across, *saved_specs(heads, size, lambda i: i)],
        out_shape=[
            made(width, BF16),
            made(features, BF16),
            jax.ShapeDtypeStruct((8, length), F32),
            *[
                jax.ShapeDtypeStruct((blocks,) + shape, F32) for shape in ((N, width), (8, width))
            ],
            *[made(columns, dtype) for columns, dtype in saved_rows(heads, size)],
        ],
        scratch_shapes=[
            pltpu.VMEM((Q + HALO, width), F32),
            pltpu.VMEM((Q + HALO, 2 * N), F32),
            pltpu.VMEM((N, width), F32),
        ],
        compiler_params=pltpu.CompilerParams(vmem_limit_bytes=VMEM_LIMIT),
        cost_estimate=cost(14),
        name="forward",
    )(window, seg_row, weights, kernel_x, kernel_bc, head, channel, z_proj, x_proj, bcdt)


def run_gradient(cot, weights, scaled, window):
    length, features = cot.shape
    width = scaled.shape[1]
    return pl.pallas_call(
        functools.partial(gradient_kernel, width),
        grid=(length // Q,),
        in_specs=[
            pl.BlockSpec((Q, features), lambda i: (i, 0)),
            whole((features, width)),
            pl.BlockSpec((Q, width), lambda i: (i, 0)),
            whole(window.shape),
        ],
        out_specs=[
            pl.BlockSpec((Q, width), lambda i: (i, 0)),
            pl.BlockSpec((8, Q), lambda i: (0, i)),
        ],
        out_shape=[
            jax.ShapeDtypeStruct((length, width), F32),
            jax.ShapeDtypeStruct((8, length), F32),
        ],
        compiler_params=pltpu.CompilerParams(vmem_limit_bytes=VMEM_LIMIT),
        cost_estimate=cost(5),
        name="out_gradient",
    )(cot, weights, scaled, window)


def weights_kernel(width, cot_ref, normed_ref, tokens_ref, grads_ref, first_ref, second_ref):
    tokens = tokens_ref[...]
    first_ref[:, :width] = dot_tn(cot_ref[...], normed_ref[...]).astype(BF16)
    first_ref[:, width:] = dot_tn(tokens, grads_ref[:, 2 * width :]).astype(BF16)
    second_ref[...] = dot_tn(tokens, grads_ref[:, : 2 * width]).astype(BF16)


def run_weights(cot, normed, tokens, grads):
    length, features = tokens.shape
    width = normed.shape[1]
    columns = [grads.shape[1] - width, 2 * width]
    return pl.pallas_call(
        functools.partial(weights_kernel, width),
        grid=(features // Q,),
        in_specs=[
            pl.BlockSpec((length, Q), lambda i: (0, i)),
            whole(normed.shape),
            pl.BlockSpec((length, Q), lambda i: (0, i)),
            whole(grads.shape),
        ],
        out_specs=[pl.BlockSpec((Q, count), lambda i: (i, 0)) for count in columns],
        out_shape=[jax.ShapeDtypeStruct((features, count), BF16) for count in columns],
        compiler_params=pltpu.CompilerParams(vmem_limit_bytes=VMEM_LIMIT),
        cost_estimate=cost(7),
        name="weight_gradients",
    )(cot, normed, tokens, grads)


def run_backward(
    heads, size, full_inner, stat, hidden, window, weights, kernel_x, kernel_bc, head, channel,
    x_proj, bcdt, grad_out, saved,
):
    length, features = hidden.shape
    width = heads * size
    blocks = length // Q
    rest = 2 * N + LANES
    total = 2 * width + rest

    def rows(columns):
        return pl.BlockSpec((Q, columns), lambda i: (blocks - 1 - i, 0))

    def made(columns, dtype):
        return jax.ShapeDtypeStruct((length, columns), dtype)

    across = pl.BlockSpec((8, Q), lambda i: (0, blocks - 1 - i))
    sums = [(8, width), (8, 2 * N), (8, LANES), (8, features)]
    return pl.pallas_call(
        functools.partial(backward_kernel, heads, size, full_inner),
        grid=(blocks,),
        in_specs=[
            across,
            rows(features),
            whole(window.shape),
            whole(weights.shape),
            whole(kernel_x.shape),
            whole(kernel_bc.shape),
            whole(head.shape),
            whole(channel.shape),
            rows(width),
            rows(rest),
            rows(width),
            *saved_specs(heads, size, lambda i: blocks - 1 - i),
        ],
        out_specs=[rows(total), rows(features), rows(width)] + [whole(shape) for shape in sums],
        out_shape=[made(total, BF16), made(features, BF16), made(width, BF16)]
        + [jax.ShapeDtypeStruct(shape, F32) for shape in sums],
        scratch_shapes=[
            pltpu.VMEM((Q + HALO, width), F32),
            pltpu.VMEM((Q + HALO, 2 * N), F32),
            pltpu.VMEM((N, width), F32),
            pltpu.VMEM((8, LANES), F32),
        ],
        compiler_params=pltpu.CompilerParams(vmem_limit_bytes=VMEM_LIMIT),
        cost_estimate=cost(2),
        name="backward",
    )(
        stat, hidden, window, weights, kernel_x, kernel_bc, head, channel, x_proj, bcdt, grad_out,
        *saved,
    )


def finish_kernel(sum_ref, hidden_ref, cot_ref, gain_ref, out_ref):
    grad = sum_ref[...].astype(F32) * gain_ref[0:1, :]
    hidden = hidden_ref[...].astype(F32)
    inverse = lax.rsqrt(jnp.mean(hidden * hidden, axis=1, keepdims=True) + EPS)
    unit = hidden * inverse
    along = jnp.mean(grad * unit, axis=1, keepdims=True)
    out_ref[...] = (cot_ref[...].astype(F32) + inverse * (grad - unit * along)).astype(BF16)


def run_finish(in_sum, hidden, cot, gain):
    length, features = hidden.shape
    rows = pl.BlockSpec((length // 2, features), lambda i: (i, 0))
    return pl.pallas_call(
        finish_kernel,
        grid=(2,),
        in_specs=[rows, rows, rows, whole(gain.shape)],
        out_specs=rows,
        out_shape=jax.ShapeDtypeStruct(hidden.shape, BF16),
        compiler_params=pltpu.CompilerParams(vmem_limit_bytes=VMEM_LIMIT),
        name="finish",
    )(in_sum, hidden, cot, gain)


def pad_lanes(values):
    return jnp.pad(values, ((0, 0), (0, LANES - values.shape[1])))


def after(value, *others):
    return lax.optimization_barrier((value, *others))[0]


def line_step(right, left, step, axis):
    n = lax.axis_size(axis)
    return (
        lax.ppermute(right, axis, [(i, i + 1) for i in range(step - 1, n - 1)]),
        lax.ppermute(left, axis, [(i, i - 1) for i in range(1, n - step + 1)]),
    )


def line_order(block, moved):
    return [pair[0] for pair in moved[::-1]] + [block] + [pair[1] for pair in moved]


def line_gather(block, axis):
    right = left = block
    moved = []
    for step in range(1, lax.axis_size(axis)):
        right, left = line_step(right, left, step, axis)
        moved.append((right, left))
    return line_order(block, moved)


def cube_scatter(first, second, small, axis):
    n = lax.axis_size(axis)
    if n & (n - 1):
        sums = [
            lax.psum_scatter(part, axis, scatter_dimension=0, tiled=True).astype(F32)
            for part in (first, second)
        ]
        return (*sums, lax.psum(small, axis), sums)
    place = lax.axis_index(axis)
    bits = list(range(n.bit_length() - 1))
    orders = [bits, bits[:1] + bits[:0:-1]]
    parts = [part.reshape((2,) * len(bits) + (-1, part.shape[1])) for part in (first, second)]
    left = [bits[::-1], bits[::-1]]
    came = []
    for step in range(len(bits)):
        for index in range(2):
            part = parts[index]
            bit = orders[index][step]
            dim = left[index].index(bit)
            mine = (place >> bit) & 1
            keep = lax.dynamic_index_in_dim(part, mine, dim, keepdims=False)
            send = lax.dynamic_index_in_dim(part, 1 - mine, dim, keepdims=False)
            pairs = [(i, i ^ (1 << bit)) for i in range(n)]
            if index == 0:
                columns = part.shape[-1]
                rows = send.size // columns
                extra = -(-small.size // (16 * columns)) * 16
                small = lax.reduce_precision(small, 8, 7)
                rider = jnp.pad(
                    small.astype(BF16).reshape(-1), (0, extra * columns - small.size)
                ).reshape(extra, columns)
                moved = lax.ppermute(
                    jnp.concatenate([send.reshape(rows, columns), rider]), axis, pairs
                )
                other = moved[:rows].reshape(send.shape)
                rider = moved[rows:].reshape(-1)[: small.size].reshape(small.shape)
                small = small + rider.astype(F32)
            else:
                moved = other = lax.ppermute(send, axis, pairs)
            came.append(moved)
            part = keep.astype(F32) + other.astype(F32)
            left[index] = [other_bit for other_bit in left[index] if other_bit != bit]
            parts[index] = part.astype(BF16) if left[index] else part
    return (*parts, small, came)


def around(values, axis):
    n = lax.axis_size(axis)
    return [values] + [
        lax.ppermute(values, axis, [(i, (i - k) % n) for i in range(n)]) for k in range(1, n)
    ]


def sum_around(values, axis):
    return functools.reduce(jnp.add, around(values, axis))


def sum_around_low(values, axis):
    low = around(lax.reduce_precision(values, 8, 7).astype(BF16), axis)
    return functools.reduce(jnp.add, [share.astype(F32) for share in low])


def shards(
    hidden,
    seg_ids,
    cotangent,
    norm_gain,
    w_in_z,
    w_in_x,
    w_in_bc,
    w_in_dt,
    conv_x,
    conv_x_bias,
    conv_bc,
    conv_bc_bias,
    dt_bias,
    a_log,
    d_skip,
    gate_gain,
    w_out,
):
    heads = dt_bias.shape[0]
    width = gate_gain.shape[0]
    size = width // heads
    full_inner = width * lax.axis_size("tensor")
    features = hidden.shape[2]
    hidden_local = hidden[0]

    steps = jnp.pad(
        jnp.concatenate([w_in_dt, norm_gain[:, None]], axis=1), ((0, 0), (0, LANES - heads - 1))
    )
    packed = run_pack(w_out, w_in_x, w_in_z, w_in_bc, steps)
    n = lax.axis_size("tensor")
    axis_place = lax.axis_index("tensor")
    place = axis_place[None]
    near_hidden = line_gather(hidden_local, "tensor")
    weights = lax.all_gather(packed, "dp", axis=0, tiled=True)
    seg_stack = around(seg_ids[0], "tensor")
    count = seg_ids.shape[1]
    seg_full = lax.dynamic_slice_in_dim(
        jnp.concatenate(seg_stack + seg_stack), (n - axis_place) * count, n * count, 0
    )
    window = jnp.broadcast_to(
        jnp.pad(seg_full, (HALO, HALO), constant_values=-1)[:, None],
        (seg_full.shape[0] + 2 * HALO, LANES),
    )
    seg_row = jnp.broadcast_to(seg_full[None, :], (8, seg_full.shape[0]))
    kernel_x = jnp.concatenate([conv_x, conv_x_bias[None, :]], axis=0)
    kernel_bc = jnp.concatenate([conv_bc, conv_bc_bias[None, :]], axis=0)
    head = pad_lanes(jnp.stack([dt_bias, a_log]))
    channel = jnp.stack([gate_gain, jnp.repeat(d_skip, size)])

    hidden_full, tokens, z_proj, x_proj, bcdt, gain = run_project(
        heads, size, place, near_hidden, weights
    )
    cot_full = lax.all_gather(
        after(cotangent[0], near_hidden[1], near_hidden[-2]), "tensor", axis=0, tiled=True
    )
    scaled, out_part, square, *saved = run_forward(
        heads, size, window, seg_row, weights, kernel_x, kernel_bc, head, channel, z_proj, x_proj,
        bcdt,
    )
    grad_out, along = run_gradient(cot_full, weights, scaled, window)
    out_sum = lax.psum_scatter(
        out_part, "tensor", scatter_dimension=0, tiled=True
    )
    stat = sum_around(jnp.stack([square[0], along[0]]), "tensor")
    stat_full = jnp.pad(stat, ((0, 6), (0, 0)))
    out_scale = lax.rsqrt(stat[0] / full_inner + EPS) * (seg_full > 0).astype(F32)

    grads, in_part, normed_out, sum_x, sum_bc, sum_head, sum_gain = run_backward(
        heads, size, full_inner, stat_full, hidden_full, window, weights, kernel_x, kernel_bc, head,
        channel, x_proj, bcdt, grad_out, saved,
    )
    in_sum = lax.psum_scatter(in_part, "tensor", scatter_dimension=0, tiled=True)
    first, second = run_weights(cot_full, normed_out, tokens, grads)
    own = jnp.concatenate([sum_x.reshape(-1, LANES), sum_head])
    both = jnp.concatenate([sum_gain[0].reshape(-1, LANES), sum_bc.reshape(-1, LANES)])
    first, second, small, came = cube_scatter(first, second, jnp.concatenate([own, both]), "dp")
    sum_x = small[: own.shape[0] - 8].reshape(8, width)
    sum_head = small[own.shape[0] - 8 : own.shape[0]]
    grad_bc = first[:, width : width + 2 * N]
    shared = jnp.concatenate([small[own.shape[0] :], grad_bc.reshape(-1, LANES)])
    shared = sum_around_low(shared, "tensor")
    gain_rows = features // LANES
    sum_gain = shared[:gain_rows].reshape(features)
    sum_bc = shared[gain_rows : both.shape[0]].reshape(8, 2 * N)
    grad_bc = shared[both.shape[0] :].reshape(grad_bc.shape)
    local_features = norm_gain.shape[0]
    grad_norm_gain = lax.dynamic_slice_in_dim(
        sum_gain, lax.axis_index("dp") * local_features, local_features, 0
    )

    local = hidden_local.shape[0]
    hidden_rows = hidden_local.astype(F32)
    scale_here = lax.dynamic_slice_in_dim(out_scale, axis_place * local, local, 0)[:, None]
    layer_out = (hidden_rows + out_sum.astype(F32) * scale_here).astype(BF16)

    grad_hidden = run_finish(in_sum, hidden_local, cotangent[0], after(gain, shared))

    return (
        layer_out[None],
        grad_hidden[None],
        grad_norm_gain,
        second[:, width:],
        second[:, :width],
        grad_bc,
        first[:, width + 2 * N : width + 2 * N + heads],
        sum_x[0:CONV],
        sum_x[CONV],
        sum_bc[0:CONV],
        sum_bc[CONV],
        sum_head[0, :heads],
        sum_head[1, :heads],
        jnp.sum(sum_x[CONV + 2].reshape(heads, size), axis=1),
        sum_x[CONV + 1],
        first[:, :width],
    )


def solution(mesh):
    in_specs = (
        P("dp", "tensor", None),
        P("dp", "tensor"),
        P("dp", "tensor", None),
        P("dp"),
        P("dp", "tensor"),
        P("dp", "tensor"),
        P("dp", None),
        P("dp", "tensor"),
        P(None, "tensor"),
        P("tensor"),
        P(),
        P(),
        P("tensor"),
        P("tensor"),
        P("tensor"),
        P("tensor"),
        P("dp", "tensor"),
    )
    out_specs = (
        P("dp", "tensor", None),
        P("dp", "tensor", None),
        P("dp"),
        P("dp", "tensor"),
        P("dp", "tensor"),
        P("dp", None),
        P("dp", "tensor"),
        P(None, "tensor"),
        P("tensor"),
        P(),
        P(),
        P("tensor"),
        P("tensor"),
        P("tensor"),
        P("tensor"),
        P("dp", "tensor"),
    )
    return jax.shard_map(shards, mesh=mesh, in_specs=in_specs, out_specs=out_specs, check_vma=False)
```
